32 devices in a mesh: dp: 8 (over y, x, core), fsdp: 4 (over z).
Axes of the slice: x: 2, y: 2, z: 4, core: 2. Of those that a mesh axis runs over, the one named last changes fastest.
Arguments:
- hidden_in: bfloat16 [2, 12288, 768], P(None, ('dp', 'fsdp')), may hold values from -6 to 6
- grad_out: bfloat16 [2, 12288, 768], P(None, ('dp', 'fsdp')), may hold values from -6 to 6
- gain_attn: bfloat16 [768], P(('dp', 'fsdp')), may hold values from 0.099609375 to 1.8984375
- gain_ffn: bfloat16 [768], P(('dp', 'fsdp')), may hold values from 0.099609375 to 1.8984375
- rel_bias: bfloat16 [384], P(('dp', 'fsdp')), may hold values from -4 to 4
- w_query: bfloat16 [768, 768], P(('dp', 'fsdp')), may hold values from -0.046875 to 0.046875
- w_key: bfloat16 [768, 768], P(('dp', 'fsdp')), may hold values from -0.21875 to 0.21875
- w_value: bfloat16 [768, 768], P(('dp', 'fsdp')), may hold values from -0.21875 to 0.21875
- w_output: bfloat16 [768, 768], P(('dp', 'fsdp')), may hold values from -0.875 to 0.875
- w_inner: bfloat16 [768, 3072], P(('dp', 'fsdp')), may hold values from -0.21875 to 0.21875
- w_outer: bfloat16 [3072, 768], P(('dp', 'fsdp')), may hold values from -0.15625 to 0.15625
- dealing: int32 [2, 8, 1536], P(None, 'dp'), may hold values from 0 to 1535, as said below
- lengths: int32 [2, 8, 4], P(None, 'dp'), may hold values from 1 to 768, 1536 in all within a row
- bucket_table: int32 [257], replicated, may hold values from 0 to 31, as said below
Outputs:
- hidden_out: float32 [2, 12288, 768], P(None, ('dp', 'fsdp'))
- grad_in: float32 [2, 12288, 768], P(None, ('dp', 'fsdp'))
- grad_gain_attn: float32 [768], P(('dp', 'fsdp'))
- grad_gain_ffn: float32 [768], P(('dp', 'fsdp'))
- grad_rel_bias: float32 [384], P(('dp', 'fsdp'))
- grad_query: float32 [768, 768], P(('dp', 'fsdp'))
- grad_key: float32 [768, 768], P(('dp', 'fsdp'))
- grad_value: float32 [768, 768], P(('dp', 'fsdp'))
- grad_output: float32 [768, 768], P(('dp', 'fsdp'))
- grad_inner: float32 [768, 3072], P(('dp', 'fsdp'))
- grad_outer: float32 [3072, 768], P(('dp', 'fsdp'))
The draws below stay inside these ranges and needn't reach their ends.
Inputs may be any that keep to these rules, and one draw needn't show every extreme that they name: Each row dealing[m, g] is a permutation of 0 .. 1535. For t < 96, the entry at dealt place 384 * e + 96 * s + t lies in 384 * s .. 384 * s + 383. Each row lengths[m, g] sums to 1536; its longest entry is 768. `bucket_table`: entry 128 + r is the bucket of distance r. For r <= 0 it lies in 0 .. 15, for r > 0 in 17 .. 31, never falling as |r| grows on either side; distances |r| < 8 have buckets of their own, and every bucket but 32 / 2 is used.
All inputs are finite; a program needn't handle non-finite values.
Results may differ from the reference program's by a relative error of at most 0.019.
Values may be sent and summed in bfloat16 or wider, within the bound.
A program may use at most 256 MiB of HBM per device.

```python
import math
import jax
import jax.numpy as jnp
import numpy as np
from jax import lax

D = 768
H = 12
HD = 64
FF = 3072
BUCKETS = 32
RELSPAN = 128
MICRO = 2
SEQ_GRP = 4
TOK_DEV = 384
GROUPS = 8
GRP = 1536
SLOT = 96
MOST = 768
TOKENS = 12288
N_DP = 8


def draw_dealing(key, part):
    group_size = GRP // TOK_DEV
    subkeys = jax.random.split(key, MICRO * GROUPS * group_size)
    local = jax.vmap(lambda one_key: jax.random.permutation(one_key, TOK_DEV))(subkeys).astype(jnp.int32)
    local = local.reshape(MICRO, GROUPS, group_size, group_size, SLOT)
    source_base = (jnp.arange(group_size, dtype=jnp.int32) * TOK_DEV).reshape(1, 1, group_size, 1, 1)
    placed = jnp.transpose(local + source_base, (0, 1, 3, 2, 4))
    return placed.reshape(MICRO, GROUPS, GRP)


def draw_bucket_table(key, part):
    half_count = BUCKETS // 2
    exact_count = half_count // 2
    cut_count = half_count - exact_count - 1
    distance_signed = jnp.arange(2 * RELSPAN + 1, dtype=jnp.int32) - RELSPAN
    distance = jnp.abs(distance_signed)

    def one_side(side_key):
        pool = jax.random.permutation(side_key, RELSPAN - exact_count).astype(jnp.int32) + exact_count + 1
        cuts = pool[:cut_count]
        beyond = exact_count + jnp.sum((distance[:, None] >= cuts[None, :]).astype(jnp.int32), axis=1)
        return jnp.where(distance < exact_count, distance, beyond).astype(jnp.int32)
    below = one_side(jax.random.fold_in(key, 11))
    above = one_side(jax.random.fold_in(key, 23)) + half_count
    return jnp.where(distance_signed > 0, above, below).astype(jnp.int32)


def shard_levels(rng, shape, shards, least, largest):
    def one(axis_at, shards_of):
        heights = jax.random.uniform(jax.random.fold_in(jax.random.fold_in(rng, 6), axis_at), (shards_of,), jnp.float32, least / len(shards), largest / len(shards))
        return jnp.repeat(jnp.exp(heights), shape[axis_at] // shards_of).reshape((-1,) + (1,) * (len(shape) - axis_at - 1))

    gain = one(*shards[0])
    for cut in shards[1:]:
        gain = gain * one(*cut)
    return gain


def length_profile(number_of, total, limit, lean):
    portions = [(1 << 20) // math.isqrt(grade ** lean) + 1 for grade in range(2, number_of + 1)]
    spare, counts = total - limit - (number_of - 1), [1] * (number_of - 1)
    while spare > 0:
        movable = [i for i in range(number_of - 1) if counts[i] < limit]
        whole, remaining = sum([portions[i] for i in movable]), spare
        for i in movable:
            addition = min(limit - counts[i], max(1, remaining * portions[i] // whole), spare)
            counts[i] = counts[i] + addition
            spare = spare - addition
    return np.array([limit] + counts)


def ragged(own_key, number_of, total, bound, lean):
    if number_of == 2:
        one = jax.random.randint(own_key, (), max(1, total - bound), min(bound, total - 1) + 1)
        return jnp.stack([one, total - one])
    sizes = jnp.asarray(length_profile(number_of, total, bound, lean), jnp.int32)
    twos = (number_of - 1) // 2
    giver, receiver = sizes[1:1 + 2 * twos:2], sizes[2:2 + 2 * twos:2]
    room = jnp.minimum(giver - 1, bound - receiver)
    shifted = jax.random.randint(jax.random.fold_in(own_key, 1), (twos,), 0, 1 << 20) % (room + 1)
    sizes = sizes.at[1:1 + 2 * twos:2].set(giver - shifted).at[2:2 + 2 * twos:2].set(receiver + shifted)
    return sizes[jax.random.permutation(jax.random.fold_in(own_key, 2), number_of)]


def normal_values(own_key, shape, width, reach, cuts=(), held_as=jnp.bfloat16):
    factor_of = shard_levels(own_key, shape, cuts, -0.22, 0.18) if cuts else 1.0
    values = jax.random.normal(own_key, shape, jnp.float32) * width * factor_of
    return jnp.minimum(jnp.maximum(values, -reach), reach).astype(held_as)


def setup_inputs(seed: int = 0) -> dict:
    keys = jax.random.split(jax.random.key(seed), 15)
    return {
        "hidden_in": normal_values(keys[0], (MICRO, TOKENS, D), 1.0, 6.0, ((1, 32),)),
        "grad_out": normal_values(keys[1], (MICRO, TOKENS, D), 1.0, 6.0, ((1, 32),)),
        "gain_attn": jnp.clip(1.0 + 0.18 * jax.random.normal(keys[2], (D,), jnp.float32), 0.099609375, 1.8984375).astype(jnp.bfloat16),
        "gain_ffn": jnp.clip(1.0 + 0.18 * jax.random.normal(keys[3], (D,), jnp.float32), 0.099609375, 1.8984375).astype(jnp.bfloat16),
        "rel_bias": normal_values(keys[4], (BUCKETS * H,), 1.0, 4.0, ((0, 32),)),
        "w_query": normal_values(keys[5], (D, D), (25 * D) ** -0.5, 0.046875, ((0, 32),)),
        "w_key": normal_values(keys[6], (D, D), D ** -0.5, 0.21875, ((0, 32),)),
        "w_value": normal_values(keys[7], (D, D), D ** -0.5, 0.21875, ((0, 32),)),
        "w_output": normal_values(keys[8], (D, D), (D // 16) ** -0.5, 0.875, ((0, 32),)),
        "w_inner": normal_values(keys[9], (D, FF), D ** -0.5, 0.21875, ((0, 32),)),
        "w_outer": normal_values(keys[10], (FF, D), (FF // 2) ** -0.5, 0.15625, ((0, 32),)),
        "dealing": draw_dealing(jax.random.fold_in(keys[14], 71), 0),
        "lengths": jax.vmap(lambda own: ragged(own, SEQ_GRP, GRP, MOST, 2))(jax.random.split(keys[12], MICRO * GROUPS)).reshape((MICRO, GROUPS, SEQ_GRP)).astype(jnp.int32),
        "bucket_table": draw_bucket_table(jax.random.fold_in(keys[14], 71), 0),
    }


EPSILON = 1e-06
NEG_FILL = -1e+30

@jax.custom_vjp
def low(v):
    return lax.optimization_barrier(v.astype(jnp.bfloat16)).astype(jnp.float32)

@jax.custom_vjp
def low_back(v):
    return v

def low_keep(v):
    return (low(v), None)

def low_pass(kept, grad):
    return (grad,)

def back_keep(v):
    return (v, None)

def back_low(kept, grad):
    return (low(grad),)
low.defvjp(low_keep, low_pass)
low_back.defvjp(back_keep, back_low)

def matmul(left, right):
    return jnp.dot(left, right, precision=lax.Precision.HIGHEST, preferred_element_type=jnp.float32)

def token_places(deal_order, lengths):
    seq_ends = jnp.cumsum(lengths).astype(jnp.int32)
    starts = (seq_ends - lengths).astype(jnp.int32)
    inside = (deal_order[:, None] >= starts[None, :]).astype(jnp.int32)
    segment = (lax.optimization_barrier(jnp.sum(inside, axis=1)) - 1).astype(jnp.int32)
    picked = (segment[:, None] == jnp.arange(lengths.shape[0], dtype=jnp.int32)[None, :]).astype(jnp.int32)
    position = (deal_order - lax.optimization_barrier(jnp.sum(picked * starts[None, :], axis=1))).astype(jnp.int32)
    return (segment, position)

def rms_scale(rows_in):
    return lax.rsqrt(lax.optimization_barrier(jnp.mean(rows_in * rows_in, axis=1, keepdims=True)) + EPSILON)

def layer_group(block_in, deal_order, lengths, params, rel_heads):
    gain_one, gain_two, query_weight, key_weight, value_weight, output_weight, inner_weight, outer_weight = params
    dealt = jnp.take(block_in, deal_order, axis=0)
    segment, position = token_places(deal_order, lengths)
    normed1 = low(dealt * rms_scale(dealt) * gain_one)
    queries = low(low_back(matmul(normed1, query_weight))).reshape(GRP, H, HD)
    keys_all = low(low_back(matmul(normed1, key_weight))).reshape(GRP, H, HD)
    values_all = low(low_back(matmul(normed1, value_weight))).reshape(GRP, H, HD)
    block_rows = 512 if GRP % 512 == 0 else GRP
    blocks = GRP // block_rows

    def rows_out(block):
        query_block, seg_block, pos_block = block
        raw_scores = jnp.einsum('qhd,khd->hqk', query_block, keys_all, precision=lax.Precision.HIGHEST)
        offset_idx = (jnp.clip(position[None, :] - pos_block[:, None], -RELSPAN, RELSPAN) + RELSPAN).astype(jnp.int32)
        bias = jnp.take(rel_heads, offset_idx, axis=1)
        scores = low_back(raw_scores + bias)
        same_seq = (seg_block[:, None] == segment[None, :])[None]
        scores = jnp.where(same_seq, scores, NEG_FILL)
        log_total = jax.scipy.special.logsumexp(scores, axis=2, keepdims=True)
        probs = low(jnp.exp(scores - log_total))
        return jnp.einsum('hqk,khd->qhd', probs, values_all, precision=lax.Precision.HIGHEST)
    attended = lax.map(jax.checkpoint(rows_out), (queries.reshape(blocks, block_rows, H, HD), segment.reshape(blocks, block_rows), position.reshape(blocks, block_rows)))
    attended = low(low_back(attended.reshape(GRP, D)))
    mid = dealt + low_back(matmul(attended, output_weight))
    normed2 = low(mid * rms_scale(mid) * gain_two)
    inner = low_back(matmul(normed2, inner_weight))
    active = low(jax.nn.gelu(inner, approximate=False))
    return mid + matmul(active, outer_weight)

def reference(hidden_in, grad_out, gain_attn, gain_ffn, rel_bias, w_query, w_key, w_value, w_output, w_inner, w_outer, dealing, lengths, bucket_table):
    floats = tuple((item.astype(jnp.float32) for item in (hidden_in, gain_attn, gain_ffn, rel_bias, w_query, w_key, w_value, w_output, w_inner, w_outer)))
    picked = (bucket_table[:, None] == jnp.arange(BUCKETS, dtype=jnp.int32)[None, :]).astype(jnp.float32)
    orders = dealing.reshape(MICRO * N_DP, GRP)
    length_rows = lengths.reshape(MICRO * N_DP, SEQ_GRP)

    def forward(inputs, gain_one, gain_two, rel_flat, query_weight, key_weight, value_weight, output_weight, inner_weight, outer_weight):
        rel_heads = matmul(picked, rel_flat.reshape(BUCKETS, H)).T
        params = (gain_one, gain_two, query_weight, key_weight, value_weight, output_weight, inner_weight, outer_weight)

        def one_group(block):
            block_in, deal_order, group_lengths = block
            return layer_group(block_in, deal_order, group_lengths, params, rel_heads)
        result = lax.map(jax.checkpoint(one_group), (inputs.reshape(MICRO * N_DP, GRP, D), orders, length_rows))
        return result.reshape(MICRO, TOKENS, D)
    result, pullback = jax.vjp(forward, *floats)
    grads = pullback(grad_out.astype(jnp.float32))
    return (result, grads[0], grads[1], grads[2], grads[3], grads[4], grads[5], grads[6], grads[7], grads[8], grads[9])
```

```python
import functools
import math

import jax
import jax.numpy as jnp
from jax import lax
from jax.experimental import pallas as pl
from jax.experimental.pallas import tpu as pltpu
from jax.sharding import PartitionSpec as P

H = 12
BUCKETS = 32
EPSILON = 1e-06
NEG_FILL = -1e30
MESH = pl.DeviceIdType.MESH
TILE = 128
PAIRS = 6
OWN = 6
TILES = 12
FAR = 6
SEQS = 4


def lane_index(shape):
    return lax.broadcasted_iota(jnp.int32, shape, len(shape) - 1)


def row_index(shape):
    return lax.broadcasted_iota(jnp.int32, shape, len(shape) - 2)


def dot_nn(left, right):
    return lax.dot_general(left, right, (((1,), (0,)), ((), ())), preferred_element_type=jnp.float32)


def dot_nt(left, right):
    return lax.dot_general(left, right, (((1,), (1,)), ((), ())), preferred_element_type=jnp.float32)


def dot_tn(left, right):
    return lax.dot_general(left, right, (((0,), (0,)), ((), ())), preferred_element_type=jnp.float32)


def segments_of(places, lens_ref, count):
    edge = jnp.int32(0)
    found = jnp.zeros(places.shape, jnp.int32)
    for s in range(count - 1):
        edge = edge + lens_ref[0, s]
        found = found + (places >= edge).astype(jnp.int32)
    return found


def segment_tags(places, lens_ref, count, of_key):
    lane = lane_index(places.shape)
    hit = segments_of(places, lens_ref, count) == lane
    if of_key:
        return jnp.where((lane < count) & jnp.logical_not(hit), NEG_FILL, 0.0).astype(jnp.bfloat16)
    return jnp.where(hit, 1.0, 0.0).astype(jnp.bfloat16)


def key_range(i):
    return max(0, 2 * i - FAR), min(TILES, 2 * i + FAR + 2)


def fill_bias(rows_ref, tiles_ref, heads):
    def one_head(h, carry):
        for cls in range(3):
            row = rows_ref[cls, h]
            wide = pltpu.roll(
                jnp.broadcast_to(row, (TILE, 2 * TILE)), 0, 1, stride=1, stride_axis=0
            )
            tiles_ref[h, cls + 1] = wide[:, :TILE]
        left = rows_ref[3, h, :, :TILE]
        right = rows_ref[4, h, :, :TILE]
        tiles_ref[h, 0] = jnp.broadcast_to(left, (TILE, TILE))
        tiles_ref[h, 4] = jnp.broadcast_to(right, (TILE, TILE))
        return carry

    lax.fori_loop(0, heads, one_head, 0)


def bias_class(kt, i, core):
    return jnp.clip(kt - 2 * i - core, -2, 2) + 2


def attn_fwd(
    lens_ref, x_ref, gain_ref, wq_ref, wk_ref, wv_ref, rows_ref,
    q_ref, k_ref, v_ref, o_ref, log_ref,
    bias_ref, ext_q, ext_k, s_ref, log_acc, send_sem, recv_sem,
):
    dp, z = lax.axis_index("dp"), lax.axis_index("fsdp")
    core = lax.rem(dp, 2)
    other = dp + 1 - 2 * core
    barrier = pltpu.get_barrier_semaphore()
    pl.semaphore_signal(barrier, inc=1, device_id=(other, z), device_id_type=MESH)

    rows = x_ref[...].astype(jnp.float32)
    scale = lax.rsqrt(jnp.mean(rows * rows, axis=1, keepdims=True) + EPSILON)
    normed = (rows * scale * gain_ref[0:1, :]).astype(jnp.bfloat16)

    def project(w_ref):
        return dot_nn(normed, w_ref[...]).astype(jnp.bfloat16)

    copies = []
    for n, (w_ref, all_ref) in enumerate(((wk_ref, k_ref), (wv_ref, v_ref))):
        made = project(w_ref)
        for hp in range(PAIRS):
            for i in range(OWN):
                all_ref[hp, i, core] = made[TILE * i : TILE * (i + 1), 128 * hp : 128 * (hp + 1)]
        if n == 0:
            pl.semaphore_wait(barrier, 1)
        copy = pltpu.make_async_remote_copy(
            all_ref.at[:, :, core], all_ref.at[:, :, core], send_sem.at[n], recv_sem.at[n],
            device_id=(other, z), device_id_type=MESH,
        )
        copy.start()
        copies.append(copy)
    made = project(wq_ref)
    for hp in range(PAIRS):
        for i in range(OWN):
            q_ref[hp, i] = made[TILE * i : TILE * (i + 1), 128 * hp : 128 * (hp + 1)]
    count = SEQS
    for t in range(TILES):
        ext_k[t] = segment_tags(TILE * t + row_index((TILE, 128)), lens_ref, count, True)
    for i in range(OWN):
        ext_q[i] = segment_tags(TILE * (2 * i + core) + row_index((TILE, 128)), lens_ref, count, False)
        log_acc[i] = jnp.zeros((TILE, 128), jnp.float32)
    fill_bias(rows_ref, bias_ref, 2 * PAIRS)
    for n, all_ref in enumerate((k_ref, v_ref)):
        pltpu.make_async_remote_copy(
            all_ref.at[:, :, 1 - core], all_ref.at[:, :, 1 - core], send_sem.at[n], recv_sem.at[n],
            device_id=(other, z), device_id_type=MESH,
        ).wait_recv()

    lane = lane_index((TILE, 128))

    def one_pair(hp, carry):
        for i in range(OWN):
            lo, hi = key_range(i)
            width = (hi - lo) * TILE
            pair = q_ref[hp, i]
            tags = ext_q[i]
            zero = jnp.zeros_like(pair)
            left = jnp.concatenate(
                [
                    jnp.concatenate([jnp.where(lane < 64, pair, zero), tags], axis=1),
                    jnp.concatenate([jnp.where(lane < 64, zero, pair), tags], axis=1),
                ],
                axis=0,
            )
            keys = k_ref[hp, lo // 2 : hi // 2].reshape(width, 128)
            right = jnp.concatenate([keys, ext_k[lo:hi].reshape(width, 128)], axis=1)
            raw = dot_nt(left, right)
            tops = []
            for e in range(2):
                top = None
                for kt in range(lo, hi):
                    at = (kt - lo) * TILE
                    part = raw[e * TILE : (e + 1) * TILE, at : at + TILE]
                    if -1 <= kt - 2 * i <= 2:
                        part = part + bias_ref[2 * hp + e, bias_class(kt, i, core)]
                    else:
                        part = part + rows_ref[3 if kt < 2 * i else 4, 2 * hp + e, :, :TILE]
                    s_ref[e, :, at : at + TILE] = part
                    top = part if top is None else jnp.maximum(top, part)
                tops.append(jnp.max(top, axis=1, keepdims=True))
            outs = []
            for e in range(2):
                total = None
                pieces = []
                for kt in range(lo, hi):
                    at = (kt - lo) * TILE
                    weight = jnp.exp(s_ref[e, :, at : at + TILE] - tops[e])
                    total = weight if total is None else total + weight
                    pieces.append(weight.astype(jnp.bfloat16))
                total = jnp.sum(total, axis=1, keepdims=True)
                probs = jnp.concatenate(pieces, axis=1)
                values = v_ref[hp, lo // 2 : hi // 2].reshape(width, 128)
                outs.append(dot_nn(probs, values) / total)
                log_acc[i] = jnp.where(lane == 2 * hp + e, tops[e] + jnp.log(total), log_acc[i])
            o_ref[hp, i] = jnp.where(lane < 64, outs[0], outs[1])
        return carry

    lax.fori_loop(0, PAIRS, one_pair, 0)
    for i in range(OWN):
        turned = log_acc[i].T
        for h in range(2 * PAIRS):
            log_ref[i, h] = turned[h : h + 1, :]
    for copy in copies:
        copy.wait_send()


def attn_bwd(
    lens_ref, q_ref, k_ref, v_ref, log_ref, do_ref, delta_ref, rows_ref,
    dq_ref, dk_ref, dv_ref, hist_ref,
    bias_ref, acc_ref, ext_q, ext_k, dk_acc, dv_acc, out_k, out_v, got_k, got_v, send_sem, recv_sem,
):
    dp, z = lax.axis_index("dp"), lax.axis_index("fsdp")
    core = lax.rem(dp, 2)
    other = dp + 1 - 2 * core
    barrier = pltpu.get_barrier_semaphore()
    pl.semaphore_signal(barrier, inc=1, device_id=(other, z), device_id_type=MESH)
    count = SEQS
    for t in range(TILES):
        ext_k[t] = segment_tags(TILE * t + row_index((TILE, 128)), lens_ref, count, True)
    for i in range(OWN):
        ext_q[i] = segment_tags(TILE * (2 * i + core) + row_index((TILE, 128)), lens_ref, count, False)
    fill_bias(rows_ref, bias_ref, 2 * PAIRS)
    acc_ref[...] = jnp.zeros_like(acc_ref)
    pl.semaphore_wait(barrier, 1)
    lane = lane_index((TILE, 128))

    def one_pair(hp, carry):
        dk_acc[...] = jnp.zeros_like(dk_acc)
        dv_acc[...] = jnp.zeros_like(dv_acc)
        for i in range(OWN):
            lo, hi = key_range(i)
            width = (hi - lo) * TILE
            pair, d_pair = q_ref[hp, i], do_ref[hp, i]
            tags = ext_q[i]
            zero = jnp.zeros_like(pair)
            q_two = jnp.concatenate([jnp.where(lane < 64, pair, zero), jnp.where(lane < 64, zero, pair)], axis=0)
            d_two = jnp.concatenate([jnp.where(lane < 64, d_pair, zero), jnp.where(lane < 64, zero, d_pair)], axis=0)
            q_ext = jnp.concatenate([q_two, jnp.concatenate([tags, tags], axis=0)], axis=1)
            keys = k_ref[hp, lo // 2 : hi // 2].reshape(width, 128)
            values = v_ref[hp, lo // 2 : hi // 2].reshape(width, 128)
            k_ext = jnp.concatenate([keys, ext_k[lo:hi].reshape(width, 128)], axis=1)
            raw = dot_nt(k_ext, q_ext)
            d_probs = dot_nt(values, d_two)
            p_rows, s_rows = [], []
            for kt in range(lo, hi):
                at = (kt - lo) * TILE
                p_two, s_two = [], []
                for e in range(2):
                    head = 2 * hp + e
                    part = raw[at : at + TILE, e * TILE : (e + 1) * TILE]
                    near = -1 <= kt - 2 * i <= 2
                    cls = bias_class(kt, i, core) if near else (0 if kt < 2 * i else 4)
                    if near:
                        part = part + bias_ref[head, cls]
                    else:
                        part = part + rows_ref[3 if kt < 2 * i else 4, head, :, :TILE]
                    probs = jnp.exp(part - log_ref[i, head])
                    slope = probs * (
                        d_probs[at : at + TILE, e * TILE : (e + 1) * TILE] - delta_ref[i, head]
                    )
                    acc_ref[head, cls] += slope
                    p_two.append(probs.astype(jnp.bfloat16))
                    s_two.append(slope.astype(jnp.bfloat16))
                p_rows.append(jnp.concatenate(p_two, axis=1))
                s_rows.append(jnp.concatenate(s_two, axis=1))
            probs_t = jnp.concatenate(p_rows, axis=0)
            slopes_t = jnp.concatenate(s_rows, axis=0)
            dv_acc[lo * TILE : hi * TILE, :] += dot_nn(probs_t, d_two)
            dk_acc[lo * TILE : hi * TILE, :] += dot_nn(slopes_t, q_two)
            d_q = dot_tn(slopes_t, keys)
            dq_ref[hp, i] = jnp.where(lane < 64, d_q[:TILE], d_q[TILE:]).astype(jnp.bfloat16)
        for acc, own, out in ((dk_acc, dk_ref, out_k), (dv_acc, dv_ref, out_v)):
            for i in range(OWN):
                own[hp, i] = acc[pl.ds((2 * i + core) * TILE, TILE), :].astype(jnp.bfloat16)
                out[hp, i] = acc[pl.ds((2 * i + 1 - core) * TILE, TILE), :].astype(jnp.bfloat16)
        for n, (out, got) in enumerate(((out_k, got_k), (out_v, got_v))):
            pltpu.make_async_remote_copy(
                out.at[hp], got.at[hp], send_sem.at[n, hp], recv_sem.at[n, hp],
                device_id=(other, z), device_id_type=MESH,
            ).start()
        return carry

    lax.fori_loop(0, PAIRS, one_pair, 0)
    flip = (row_index((TILE, TILE)) + lane == TILE - 1).astype(jnp.float32)

    def one_head(h, carry):
        for cls in range(3):
            tile = jnp.dot(flip, acc_ref[h, cls + 1], precision=lax.Precision.HIGHEST)
            wide = jnp.concatenate([tile, jnp.zeros((TILE, TILE), jnp.float32)], axis=1)
            wide = pltpu.roll(wide, 0, 1, stride=1, stride_axis=0)
            hist_ref[cls, h] = jnp.sum(wide, axis=0, keepdims=True)
        for n, cls in ((3, 0), (4, 4)):
            row = jnp.sum(acc_ref[h, cls], axis=0, keepdims=True)
            hist_ref[n, h] = jnp.concatenate([row, jnp.zeros_like(row)], axis=1)
        return carry

    lax.fori_loop(0, 2 * PAIRS, one_head, 0)

    def finish(hp, carry):
        for n, (out, got, own) in enumerate(((out_k, got_k, dk_ref), (out_v, got_v, dv_ref))):
            copy = pltpu.make_async_remote_copy(
                out.at[hp], got.at[hp], send_sem.at[n, hp], recv_sem.at[n, hp],
                device_id=(other, z), device_id_type=MESH,
            )
            copy.wait_send()
            copy.wait_recv()
            own[hp] = (own[hp].astype(jnp.float32) + got[hp].astype(jnp.float32)).astype(jnp.bfloat16)
        return carry

    lax.fori_loop(0, PAIRS, finish, 0)


def norm_back(rows_in, scale, gain, grad_normed):
    scaled = grad_normed * gain
    grad_gain = jnp.sum(grad_normed * rows_in * scale, axis=0, keepdims=True)
    shared = jnp.mean(scaled * rows_in, axis=1, keepdims=True)
    return scale * scaled - rows_in * (scale * scale * scale * shared), grad_gain


def join_pairs(pairs_ref, joined_ref):
    for hp in range(PAIRS):
        joined_ref[:, 128 * hp : 128 * (hp + 1)] = (
            pairs_ref[hp].reshape(OWN * TILE, 128).astype(joined_ref.dtype)
        )


def ffn_kernel(
    deal_ref, x_ref, o_ref, g_ref, wo_ref, gain_ref, wi_ref, wu_ref,
    out_ref, dmid_ref, datt_ref, delta_ref, gwo_ref, gwi_ref, gwu_ref, ggain_ref,
    att_ref, grad_ref, mid_ref, normed_ref, total_ref, back_ref,
):
    step = pl.program_id(0)
    tok = OWN * TILE

    @pl.when(step == 0)
    def _():
        core = lax.rem(lax.axis_index("dp"), 2)
        for i in range(OWN):
            places = (2 * i + core) * TILE + row_index((TILE, TILES * TILE))
            pick = jnp.where(deal_ref[...] == places, 1.0, 0.0).astype(jnp.bfloat16)
            grad_ref[TILE * i : TILE * (i + 1), :] = dot_nn(pick, g_ref[...]).astype(jnp.bfloat16)
        join_pairs(o_ref, att_ref)
        mid = x_ref[...].astype(jnp.float32) + dot_nn(att_ref[...], wo_ref[...])
        mid_ref[...] = mid
        scale = lax.rsqrt(jnp.mean(mid * mid, axis=1, keepdims=True) + EPSILON)
        normed_ref[...] = (mid * scale * gain_ref[0:1, :]).astype(jnp.bfloat16)
        total_ref[...] = jnp.zeros_like(total_ref)
        back_ref[...] = jnp.zeros_like(back_ref)

    normed = normed_ref[...]
    grad = grad_ref[...]
    inner = dot_nn(normed, wi_ref[...])
    cdf = 0.5 * (1.0 + lax.erf(inner * (1.0 / math.sqrt(2.0))))
    active = (inner * cdf).astype(jnp.bfloat16)
    slope = cdf + inner * (jnp.exp(-0.5 * inner * inner) * (1.0 / math.sqrt(2.0 * math.pi)))
    total_ref[...] += dot_nn(active, wu_ref[...])
    d_inner = (dot_nt(grad, wu_ref[...]) * slope).astype(jnp.bfloat16)
    gwu_ref[...] = dot_tn(active, grad).astype(gwu_ref.dtype)
    gwi_ref[...] = dot_tn(normed, d_inner).astype(gwi_ref.dtype)
    back_ref[...] += dot_nt(d_inner, wi_ref[...])

    @pl.when(step == pl.num_programs(0) - 1)
    def _():
        mid = mid_ref[...]
        out_ref[...] = (mid + total_ref[...]).astype(out_ref.dtype)
        scale = lax.rsqrt(jnp.mean(mid * mid, axis=1, keepdims=True) + EPSILON)
        d_rows, d_gain = norm_back(mid, scale, gain_ref[0:1, :], back_ref[...])
        ggain_ref[...] = jnp.broadcast_to(d_gain, ggain_ref.shape)
        d_mid = grad_ref[...].astype(jnp.float32) + d_rows
        dmid_ref[...] = d_mid
        branch = d_mid.astype(jnp.bfloat16)
        gwo_ref[...] = dot_tn(att_ref[...], branch).astype(gwo_ref.dtype)
        d_att = dot_nt(branch, wo_ref[...]).astype(jnp.bfloat16)
        pick = (lane_index((16, PAIRS * 128)) // 64 == row_index((16, PAIRS * 128))).astype(jnp.float32)
        sums = None
        for hp in range(PAIRS):
            part = d_att[:, 128 * hp : 128 * (hp + 1)]
            datt_ref[hp] = part.reshape(OWN, TILE, 128)
            prod = part.astype(jnp.float32) * o_ref[hp].reshape(tok, 128)
            term = lax.dot_general(
                pick[:, 128 * hp : 128 * (hp + 1)], prod, (((1,), (1,)), ((), ())),
                precision=lax.Precision.HIGHEST, preferred_element_type=jnp.float32,
            )
            sums = term if sums is None else sums + term
        for i in range(OWN):
            for h in range(2 * PAIRS):
                delta_ref[i, h] = sums[h : h + 1, TILE * i : TILE * (i + 1)]


def qkv_back_kernel(
    x_ref, gain_ref, dmid_ref, dq_ref, dk_ref, dv_ref, wq_ref, wk_ref, wv_ref,
    gq_ref, gk_ref, gv_ref, ddealt_ref, ggain_ref, join_ref,
):
    rows = x_ref[...].astype(jnp.float32)
    scale = lax.rsqrt(jnp.mean(rows * rows, axis=1, keepdims=True) + EPSILON)
    normed_t = (rows * scale * gain_ref[0:1, :]).astype(jnp.bfloat16).T
    back = None
    for pairs, w_ref, g_ref in ((dq_ref, wq_ref, gq_ref), (dk_ref, wk_ref, gk_ref), (dv_ref, wv_ref, gv_ref)):
        join_pairs(pairs, join_ref)
        grad = join_ref[...]
        g_ref[...] = dot_nn(normed_t, grad).astype(g_ref.dtype)
        term = dot_nt(grad, w_ref[...])
        back = term if back is None else back + term
    d_rows, d_gain = norm_back(rows, scale, gain_ref[0:1, :], back)
    ggain_ref[...] = jnp.broadcast_to(d_gain, ggain_ref.shape)
    ddealt_ref[...] = (dmid_ref[...] + d_rows).astype(ddealt_ref.dtype)


def coordinates():
    dp, z = lax.axis_index("dp"), lax.axis_index("fsdp")
    return dp // 4, lax.rem(dp // 2, 2), lax.rem(dp, 2), z


def place(y, x, c, z):
    return (4 * y + 2 * x + c, z)


def column(y, x, c):
    return 16 * y + 8 * x + 4 * c


def greet(barrier):
    y, x, c, z = coordinates()
    partners = [place(1 - y, x, c, z), place(y, 1 - x, c, z)]
    for dc in range(2):
        for dz in range(4):
            if dc or dz:
                partners.append(place(y, x, lax.rem(c + dc, 2), lax.rem(z + dz, 4)))
    for partner in partners:
        pl.semaphore_signal(barrier, inc=1, device_id=partner, device_id_type=MESH)
    pl.semaphore_wait(barrier, len(partners))


def remote(src, dst, send, recv, target):
    return pltpu.make_async_remote_copy(
        src, dst, send, recv, device_id=target, device_id_type=MESH
    )


def send_or_keep(src, dst, send, recv, target, here):
    @pl.when(jnp.logical_not(here))
    def _():
        remote(src, dst, send, recv, target).start()

    @pl.when(here)
    def _():
        pltpu.make_async_copy(src, dst, recv).start()


def sent(src, dst, send, recv, target, here):
    @pl.when(jnp.logical_not(here))
    def _():
        remote(src, dst, send, recv, target).wait_send()


def gather_kernel(first_axis, *refs):
    count = len(first_axis)
    lens_in, deal_in, hid_in, grd_in = refs[:4]
    shards = refs[4 : 4 + count]
    lens_u, deal_u, x_own, g_all = refs[4 + count : 8 + count]
    outs = refs[8 + count : 8 + 2 * count]
    w_send, w_recv, w_local, x_send, x_recv, g_send, g_recv, p_send, p_recv = refs[8 + 2 * count :]
    y, x, c, z = coordinates()
    sibling = place(y, x, 1 - c, z)
    greet(pltpu.get_barrier_semaphore())

    def token_sends():
        for m in range(2):
            for l in range(3):
                t = 3 * z + l
                core_to, z_to = lax.rem(t, 2), 2 * c + m
                yield (
                    hid_in.at[m, l], x_own.at[t // 2], x_send.at[m, l], x_recv.at[t // 2],
                    place(y, x, core_to, z_to), (core_to == c) & (z_to == z),
                )

    def grad_sends():
        for m in range(2):
            for half in range(2):
                z_to = 2 * c + m
                yield (
                    grd_in.at[m, half], g_all.at[2 * z + half], g_send.at[0, m, half], g_recv.at[0, z],
                    place(y, x, half, z_to), (half == c) & (z_to == z),
                )

    for item in token_sends():
        send_or_keep(*item)
    owner, micro = z // 2, lax.rem(z, 2)
    plans = []
    for n, (src, dst) in enumerate(((lens_in, lens_u), (deal_in, deal_u))):
        plans.append((src.at[micro], dst, p_send.at[n], p_recv.at[n]))

    @pl.when(owner == c)
    def _():
        for src, dst, send, recv in plans:
            remote(src, dst, send, recv, sibling).start()
            pltpu.make_async_copy(src, dst, recv).start()

    own = column(y, x, c) + z

    def start(w):
        pltpu.make_async_copy(shards[w], outs[w].at[own], w_local.at[w]).start()
        for dz in range(1, 4):
            remote(
                shards[w], outs[w].at[own], w_send.at[w, dz - 1], w_recv.at[w, dz - 1],
                place(y, x, c, lax.rem(z + dz, 4)),
            ).start()

    def sides(w):
        if first_axis[w] == "x":
            return place(y, 1 - x, c, z), place(1 - y, x, c, z), column(y, 1 - x, c), column(1 - y, x, c)
        return place(1 - y, x, c, z), place(y, 1 - x, c, z), column(1 - y, x, c), column(y, 1 - x, c)

    def push(w, k, base, target):
        block = outs[w].at[pl.ds(base, 4)]
        return remote(block, block, w_send.at[w, k], w_recv.at[w, k], target)

    far_column = column(1 - y, 1 - x, c)

    def spread_own(w):
        near, side, _, _ = sides(w)
        pltpu.make_async_copy(shards[w], outs[w].at[own], w_local.at[w]).wait()
        for dz in range(1, 4):
            came = column(y, x, c) + lax.rem(z + 4 - dz, 4)
            remote(
                shards[w], outs[w].at[came], w_send.at[w, dz - 1], w_recv.at[w, dz - 1], sibling
            ).wait_recv()
        mine = column(y, x, c)
        for k, target in ((3, near), (4, side), (6, sibling)):
            push(w, k, mine, target).start()

    def spread_near(w):
        _, side, near_column, _ = sides(w)
        push(w, 3, near_column, sibling).wait_recv()
        push(w, 5, near_column, side).start()
        push(w, 7, near_column, sibling).start()

    def spread_side(w):
        _, _, _, side_column = sides(w)
        push(w, 4, side_column, sibling).wait_recv()
        push(w, 8, side_column, sibling).start()
        push(w, 5, far_column, sibling).wait_recv()
        push(w, 9, far_column, sibling).start()

    def finish(w):
        _, _, near_column, side_column = sides(w)
        for k, base in ((6, column(y, x, c)), (7, near_column), (8, side_column), (9, far_column)):
            push(w, k, base + 4 - 8 * c, sibling).wait_recv()
        for dz in range(1, 4):
            remote(
                shards[w], outs[w].at[own], w_send.at[w, dz - 1], w_recv.at[w, dz - 1], sibling
            ).wait_send()
        for k in range(3, 10):
            push(w, k, column(y, x, c), sibling).wait_send()

    ahead = 4
    for w in range(min(ahead, count)):
        start(w)
    for item in grad_sends():
        send_or_keep(*item)
    for n in range(count + 3):
        for back, stage in enumerate((spread_own, spread_near, spread_side, finish)):
            if 0 <= n - back < count:
                stage(n - back)
        if n + ahead < count:
            start(n + ahead)

    for zs in range(4):
        block = g_all.at[2 * zs + c]
        remote(block, block, g_send.at[1, 0, 0], g_recv.at[0, zs], sibling).wait_recv()
        remote(block, block, g_send.at[1, zs // 2, zs % 2], g_recv.at[1, zs], sibling).start()
    for item in token_sends():
        sent(*item)
    for item in grad_sends():
        sent(*item)
    for i in range(OWN):
        remote(hid_in.at[0, 0], x_own.at[i], x_send.at[0, 0], x_recv.at[i], sibling).wait_recv()
    for zs in range(4):
        block = g_all.at[2 * zs + 1 - c]
        remote(block, block, g_send.at[1, zs // 2, zs % 2], g_recv.at[1, zs], sibling).wait_recv()
        remote(block, block, g_send.at[1, zs // 2, zs % 2], g_recv.at[1, zs], sibling).wait_send()
    for src, dst, send, recv in plans:
        remote(src, dst, send, recv, sibling).wait_recv()

    @pl.when(owner == c)
    def _():
        for src, dst, send, recv in plans:
            remote(src, dst, send, recv, sibling).wait_send()


def scatter_kernel(first_axis, *refs):
    count = len(first_axis)
    deal_ref, res_in, back_in = refs[:3]
    grads = refs[3 : 3 + count]
    hid_out, gin_out = refs[3 + count : 5 + count]
    outs = refs[5 + count : 5 + 2 * count]
    scratch = refs[5 + 2 * count :]
    r1, r2, r3, r4 = (scratch[n * count : (n + 1) * count] for n in range(4))
    res_all, dealt, w_send, w_recv, b_send, b_recv, h_send, h_recv, e_send, e_recv = scratch[4 * count :]
    y, x, c, z = coordinates()
    sibling = place(y, x, 1 - c, z)
    owner, micro = z // 2, lax.rem(z, 2)
    greet(pltpu.get_barrier_semaphore())

    def core_copy(w, k):
        return remote(
            grads[w].at[pl.ds(8 * k + 4 * (1 - c), 4)], r1[w].at[k], w_send.at[w, k], w_recv.at[w, k], sibling
        )

    res_copy = remote(res_in, res_all.at[:, c], e_send, e_recv, sibling)
    res_copy.start()

    def back_sends():
        for i in range(OWN):
            t = 2 * i + c
            z_to, l = t // 3, lax.rem(t, 3)
            yield (
                back_in.at[i], gin_out.at[micro, l], b_send.at[i], b_recv.at[micro, l],
                place(y, x, owner, z_to), (owner == c) & (z_to == z),
            )

    for item in back_sends():
        send_or_keep(*item)
    for w in range(count):
        for k in range(4):
            core_copy(w, k).start()

    def sides(w):
        near, side = place(y, 1 - x, c, z), place(1 - y, x, c, z)
        index = lambda s, f: 2 * s + f
        s, f = y, x
        if first_axis[w] == "y":
            near, side = side, near
            index = lambda s, f: 2 * f + s
            s, f = x, y
        return near, side, index, s, f

    def add_into(dst, k, src):
        def one(n, carry):
            dst[k, n] = dst[k, n] + src[n]
            return carry

        lax.fori_loop(0, 4, one, 0)

    def side_copy(w, f_at):
        near, side, index, s, f = sides(w)
        return remote(
            r1[w].at[index(1 - s, f_at)], r2[w].at[f_at], w_send.at[w, 4 + f_at], w_recv.at[w, 4 + f_at], side
        )

    def near_copy(w):
        near, side, index, s, f = sides(w)
        return remote(r1[w].at[index(s, 1 - f)], r3[w], w_send.at[w, 6], w_recv.at[w, 6], near)

    def z_copy(w, dz):
        near, side, index, s, f = sides(w)
        z_to = lax.rem(z + dz, 4)
        return remote(
            r1[w].at[index(s, f), z_to], r4[w].at[dz - 1], w_send.at[w, 6 + dz], w_recv.at[w, 6 + dz],
            place(y, x, c, z_to),
        )

    def stage_core(w):
        for k in range(4):
            core_copy(w, k).wait_recv()
            add_into(r1[w], k, grads[w].at[pl.ds(8 * k + 4 * c, 4)])
        for f_at in range(2):
            side_copy(w, f_at).start()

    def stage_side(w):
        near, side, index, s, f = sides(w)
        for f_at in range(2):
            side_copy(w, f_at).wait_recv()
            add_into(r1[w], index(s, f_at), r2[w].at[f_at])
        near_copy(w).start()

    def stage_near(w):
        near, side, index, s, f = sides(w)
        near_copy(w).wait_recv()
        add_into(r1[w], index(s, f), r3[w])
        for dz in range(1, 4):
            z_copy(w, dz).start()

    def stage_z(w):
        near, side, index, s, f = sides(w)
        total = r1[w][index(s, f), z].astype(jnp.float32)
        for dz in range(1, 4):
            z_copy(w, dz).wait_recv()
            total = total + r4[w][dz - 1].astype(jnp.float32)
        outs[w][...] = total
        for k in range(4):
            core_copy(w, k).wait_send()
        for f_at in range(2):
            side_copy(w, f_at).wait_send()
        near_copy(w).wait_send()
        for dz in range(1, 4):
            z_copy(w, dz).wait_send()

    def dealt_sends():
        for e in range(2):
            z_to = 2 * c + e
            yield (
                dealt.at[e], hid_out.at[micro], h_send.at[e], h_recv.at[micro],
                place(y, x, owner, z_to), (owner == c) & (z_to == z),
            )

    def deal_result():
        for i in range(OWN):
            res_all[i, c] = res_in[i]
        remote(res_in, res_all.at[:, 1 - c], e_send, e_recv, sibling).wait_recv()
        pick = jnp.where(
            row_index((TILES * TILE, TILES * TILE // 2)) == deal_ref[c], 1.0, 0.0
        ).astype(jnp.bfloat16)
        rows = dot_tn(pick, res_all[...].reshape(TILES * TILE, -1))
        dealt[...] = rows.astype(jnp.bfloat16).reshape(dealt.shape)
        for item in dealt_sends():
            send_or_keep(*item)

    for n in range(count + 3):
        for back, stage in enumerate((stage_core, stage_side, stage_near, stage_z)):
            if 0 <= n - back < count:
                stage(n - back)
        if n == 0:
            deal_result()
    res_copy.wait_send()
    for item in back_sends():
        sent(*item)
    for item in dealt_sends():
        sent(*item)
    for m in range(2):
        remote(dealt.at[0], hid_out.at[m], h_send.at[0], h_recv.at[m], sibling).wait_recv()
        for l in range(3):
            remote(back_in.at[0], gin_out.at[m, l], b_send.at[0], b_recv.at[m, l], sibling).wait_recv()


def token_places(deal_order, lengths):
    seq_ends = jnp.cumsum(lengths)
    starts = seq_ends - lengths
    inside = (deal_order[:, None] >= starts[None, :]).astype(jnp.int32)
    segment = jnp.sum(inside, axis=1) - 1
    picked = (segment[:, None] == jnp.arange(lengths.shape[0], dtype=jnp.int32)[None, :]).astype(
        jnp.int32
    )
    position = deal_order - jnp.sum(picked * starts[None, :], axis=1)
    return (segment, position)


def rms_scale(rows_in):
    return lax.rsqrt(jnp.mean(rows_in * rows_in, axis=1, keepdims=True) + EPSILON)


def gelu_slope(values):
    normal_cdf = 0.5 * (1.0 + jax.scipy.special.erf(values * (1.0 / math.sqrt(2.0))))
    normal_pdf = jnp.exp(-0.5 * values * values) * (1.0 / math.sqrt(2.0 * math.pi))
    return normal_cdf + values * normal_pdf


def norm_back_rows(rows_in, scale, gain, grad_normed):
    scaled_grad = grad_normed * gain
    grad_gain = jnp.sum(grad_normed * rows_in * scale, axis=0)
    grad_rows = scale * scaled_grad - rows_in * scale * scale * scale * jnp.mean(
        scaled_grad * rows_in, axis=1, keepdims=True
    )
    return (grad_rows, grad_gain)


def key_layout(key_all, value_all, segment, position, head_count):
    rows_all = key_all.shape[0]
    block_rows = 512
    blocks = rows_all // block_rows
    return (
        key_all.reshape(blocks, block_rows, head_count, -1),
        value_all.reshape(blocks, block_rows, head_count, -1),
        segment.reshape(blocks, block_rows),
        position.reshape(blocks, block_rows),
    )


def block_scores(
    queries,
    key_block,
    seg_query,
    pos_query,
    seg_block,
    pos_block,
    rel_bucket,
    bucket_edges,
    max_offset,
):
    lower_edge, upper_edge = bucket_edges
    raw_scores = jnp.einsum("qhd,khd->hqk", queries, key_block, preferred_element_type=jnp.float32)
    offset = jnp.clip(pos_block[None, :] - pos_query[:, None], -max_offset, max_offset)
    bucket_hit = (
        (offset[:, :, None] >= lower_edge[None, None, :])
        & (offset[:, :, None] <= upper_edge[None, None, :])
    ).astype(jnp.float32)
    bias = jnp.einsum(
        "qkb,bh->hqk",
        bucket_hit,
        rel_bucket,
        precision=lax.Precision.HIGHEST,
        preferred_element_type=jnp.float32,
    )
    same_seq = (seg_query[:, None] == seg_block[None, :])[None]
    return (raw_scores + bias, same_seq, bucket_hit)


def attend(queries, layout, seg_query, pos_query, rel_bucket, bucket_edges, max_offset):
    key_blocks, value_blocks, seg_blocks, pos_blocks = layout
    query_count, head_count, head_size = queries.shape

    def measure(carry, block):
        row_top, row_total = carry
        key_block, seg_block, pos_block = block
        scores, same_seq, _ = block_scores(
            queries,
            key_block,
            seg_query,
            pos_query,
            seg_block,
            pos_block,
            rel_bucket,
            bucket_edges,
            max_offset,
        )
        scores = jnp.where(same_seq, scores, NEG_FILL)
        new_top = jnp.maximum(row_top, jnp.max(scores, axis=2))
        weights_now = jnp.where(same_seq, jnp.exp(scores - new_top[:, :, None]), 0.0)
        row_total = row_total * jnp.exp(row_top - new_top) + jnp.sum(weights_now, axis=2)
        return ((new_top, row_total), None)

    start = (
        jnp.full((head_count, query_count), NEG_FILL, jnp.float32),
        jnp.zeros((head_count, query_count), jnp.float32),
    )
    (row_top, row_total), _ = lax.scan(measure, start, (key_blocks, seg_blocks, pos_blocks))
    log_total = row_top + jnp.log(row_total)

    def collect(summed, block):
        key_block, value_block, seg_block, pos_block = block
        scores, same_seq, _ = block_scores(
            queries,
            key_block,
            seg_query,
            pos_query,
            seg_block,
            pos_block,
            rel_bucket,
            bucket_edges,
            max_offset,
        )
        probs = jnp.where(same_seq, jnp.exp(scores - log_total[:, :, None]), 0.0).astype(
            jnp.bfloat16
        )
        return (
            summed
            + jnp.einsum("hqk,khd->qhd", probs, value_block, preferred_element_type=jnp.float32),
            None,
        )

    attended_f, _ = lax.scan(
        collect, jnp.zeros((query_count, head_count, head_size), jnp.float32), layout
    )
    return (attended_f, log_total)


def attend_back(
    queries,
    layout,
    seg_query,
    pos_query,
    rel_bucket,
    bucket_edges,
    max_offset,
    log_total,
    d_attended,
    row_delta,
):

    def step(carry, block):
        d_queries, d_buckets = carry
        key_block, value_block, seg_block, pos_block = block
        scores, same_seq, bucket_hit = block_scores(
            queries,
            key_block,
            seg_query,
            pos_query,
            seg_block,
            pos_block,
            rel_bucket,
            bucket_edges,
            max_offset,
        )
        probs_f = jnp.where(same_seq, jnp.exp(scores - log_total[:, :, None]), 0.0)
        d_probs = jnp.einsum(
            "qhd,khd->hqk", d_attended, value_block, preferred_element_type=jnp.float32
        )
        d_scores = (probs_f * (d_probs - row_delta[:, :, None])).astype(jnp.bfloat16)
        d_queries = d_queries + jnp.einsum(
            "hqk,khd->qhd", d_scores, key_block, preferred_element_type=jnp.float32
        )
        d_buckets = d_buckets + jnp.einsum(
            "hqk,qkb->bh",
            d_scores,
            bucket_hit.astype(jnp.bfloat16),
            preferred_element_type=jnp.float32,
        )
        d_values = jnp.einsum(
            "hqk,qhd->khd",
            probs_f.astype(jnp.bfloat16),
            d_attended,
            preferred_element_type=jnp.float32,
        )
        d_keys = jnp.einsum("hqk,qhd->khd", d_scores, queries, preferred_element_type=jnp.float32)
        return ((d_queries, d_buckets), (d_keys, d_values))

    start = (jnp.zeros(queries.shape, jnp.float32), jnp.zeros(rel_bucket.shape, jnp.float32))
    (d_queries, d_buckets), key_terms = lax.scan(step, start, layout)
    return (d_queries, key_terms, d_buckets)


def on_device(
    hidden_in,
    grad_out,
    gain_attn,
    gain_ffn,
    rel_bias,
    w_query,
    w_key,
    w_value,
    w_output,
    w_inner,
    w_outer,
    dealing,
    lengths,
    bucket_table,
):
    micro_count, tok_rows, model_width = hidden_in.shape
    group_size = lax.axis_size("fsdp")
    slot_rows = tok_rows // group_size
    own_index = lax.axis_index("fsdp")
    max_offset = (bucket_table.shape[0] - 1) // 2
    bucket_count = BUCKETS
    head_count = H
    offsets_all = jnp.arange(bucket_table.shape[0], dtype=jnp.int32) - max_offset
    matches = bucket_table[:, None] == jnp.arange(bucket_count, dtype=jnp.int32)[None, :]
    lower_edge = jnp.min(jnp.where(matches, offsets_all[:, None], 2 * max_offset + 2), axis=0)
    upper_edge = jnp.max(jnp.where(matches, offsets_all[:, None], -2 * max_offset - 2), axis=0)
    bucket_edges = (lower_edge, upper_edge)
    hidden_units = w_inner.shape[1]
    acc_gain_one = jnp.zeros((model_width,), jnp.float32)
    acc_gain_two = jnp.zeros((model_width,), jnp.float32)
    acc_buckets = jnp.zeros((bucket_count, head_count), jnp.float32)
    acc_query = jnp.zeros((model_width, model_width), jnp.float32)
    acc_key = jnp.zeros((model_width, model_width), jnp.float32)
    acc_value = jnp.zeros((model_width, model_width), jnp.float32)
    acc_output = jnp.zeros((model_width, model_width), jnp.float32)
    acc_inner = jnp.zeros((model_width, hidden_units), jnp.float32)
    acc_outer = jnp.zeros((hidden_units, model_width), jnp.float32)
    outputs_list = []
    grads_list = []
    for micro_idx in range(micro_count):
        weights_now = (
            lax.all_gather(gain_attn, ("dp", "fsdp"), axis=0, tiled=True),
            lax.all_gather(gain_ffn, ("dp", "fsdp"), axis=0, tiled=True),
            lax.all_gather(rel_bias, ("dp", "fsdp"), axis=0, tiled=True),
            lax.all_gather(w_query, ("dp", "fsdp"), axis=0, tiled=True),
            lax.all_gather(w_key, ("dp", "fsdp"), axis=0, tiled=True),
            lax.all_gather(w_value, ("dp", "fsdp"), axis=0, tiled=True),
            lax.all_gather(w_output, ("dp", "fsdp"), axis=0, tiled=True),
            lax.all_gather(w_inner, ("dp", "fsdp"), axis=0, tiled=True),
            lax.all_gather(w_outer, ("dp", "fsdp"), axis=0, tiled=True),
        )
        gain_one = weights_now[0].astype(jnp.float32)
        gain_two = weights_now[1].astype(jnp.float32)
        rel_bucket = weights_now[2].astype(jnp.float32).reshape(bucket_count, head_count)
        query_weight, key_weight, value_weight, output_weight, inner_weight, outer_weight = (
            weights_now[3:]
        )
        deal_order = dealing[micro_idx, 0]
        segment, position = token_places(deal_order, lengths[micro_idx, 0])
        seg_query = lax.dynamic_slice_in_dim(segment, own_index * tok_rows, tok_rows)
        pos_query = lax.dynamic_slice_in_dim(position, own_index * tok_rows, tok_rows)
        take_rows = (
            lax.dynamic_slice_in_dim(
                deal_order.reshape(group_size, tok_rows), own_index * slot_rows, slot_rows, 1
            )
            - own_index * tok_rows
        ).reshape(tok_rows)
        dealt = lax.all_to_all(
            jnp.take(hidden_in[micro_idx], take_rows, axis=0),
            "fsdp",
            split_axis=0,
            concat_axis=0,
            tiled=True,
        )
        dealt_rows = dealt.astype(jnp.float32)
        scale_one = rms_scale(dealt_rows)
        normed1 = (dealt_rows * scale_one * gain_one).astype(jnp.bfloat16)
        queries = jnp.dot(normed1, query_weight, preferred_element_type=jnp.float32).astype(
            jnp.bfloat16
        )
        key_rows = jnp.dot(normed1, key_weight, preferred_element_type=jnp.float32).astype(
            jnp.bfloat16
        )
        value_rows = jnp.dot(normed1, value_weight, preferred_element_type=jnp.float32).astype(
            jnp.bfloat16
        )
        key_all, value_all = (
            lax.all_gather(key_rows, "fsdp", axis=0, tiled=True),
            lax.all_gather(value_rows, "fsdp", axis=0, tiled=True),
        )
        layout = key_layout(key_all, value_all, segment, position, head_count)
        queries_heads = queries.reshape(tok_rows, head_count, -1)
        attended_f, log_total = attend(
            queries_heads, layout, seg_query, pos_query, rel_bucket, bucket_edges, max_offset
        )
        attended = attended_f.reshape(tok_rows, model_width).astype(jnp.bfloat16)
        mid = dealt_rows + jnp.dot(attended, output_weight, preferred_element_type=jnp.float32)
        scale_two = rms_scale(mid)
        normed2 = (mid * scale_two * gain_two).astype(jnp.bfloat16)
        inner_act = jnp.dot(normed2, inner_weight, preferred_element_type=jnp.float32)
        active = jax.nn.gelu(inner_act, approximate=False).astype(jnp.bfloat16)
        result = mid + jnp.dot(active, outer_weight, preferred_element_type=jnp.float32)
        outputs_list.append(result)
        weights_back = (
            lax.all_gather(gain_attn, ("dp", "fsdp"), axis=0, tiled=True),
            lax.all_gather(gain_ffn, ("dp", "fsdp"), axis=0, tiled=True),
            lax.all_gather(rel_bias, ("dp", "fsdp"), axis=0, tiled=True),
            lax.all_gather(w_query, ("dp", "fsdp"), axis=0, tiled=True),
            lax.all_gather(w_key, ("dp", "fsdp"), axis=0, tiled=True),
            lax.all_gather(w_value, ("dp", "fsdp"), axis=0, tiled=True),
            lax.all_gather(w_output, ("dp", "fsdp"), axis=0, tiled=True),
            lax.all_gather(w_inner, ("dp", "fsdp"), axis=0, tiled=True),
            lax.all_gather(w_outer, ("dp", "fsdp"), axis=0, tiled=True),
        )
        query_weight, key_weight, value_weight, output_weight, inner_weight, outer_weight = (
            weights_back[3:]
        )
        grad_top = grad_out[micro_idx]
        acc_outer = acc_outer + jnp.einsum(
            "tf,td->fd", active, grad_top, preferred_element_type=jnp.float32
        )
        d_active = jnp.einsum(
            "td,fd->tf", grad_top, outer_weight, preferred_element_type=jnp.float32
        )
        d_inner = (d_active * gelu_slope(inner_act)).astype(jnp.bfloat16)
        acc_inner = acc_inner + jnp.einsum(
            "td,tf->df", normed2, d_inner, preferred_element_type=jnp.float32
        )
        d_normed2 = jnp.einsum(
            "tf,df->td", d_inner, inner_weight, preferred_element_type=jnp.float32
        )
        d_mid_norm, d_gain_two = norm_back_rows(mid, scale_two, gain_two, d_normed2)
        acc_gain_two = acc_gain_two + d_gain_two
        d_mid = grad_top.astype(jnp.float32) + d_mid_norm
        d_branch = d_mid.astype(jnp.bfloat16)
        acc_output = acc_output + jnp.einsum(
            "td,te->de", attended, d_branch, preferred_element_type=jnp.float32
        )
        d_attended = jnp.einsum(
            "te,de->td", d_branch, output_weight, preferred_element_type=jnp.float32
        ).astype(jnp.bfloat16)
        d_attended_heads = d_attended.reshape(tok_rows, head_count, -1)
        row_delta = jnp.sum(d_attended_heads.astype(jnp.float32) * attended_f, axis=2).T
        key_back, value_back = (
            lax.all_gather(key_rows, "fsdp", axis=0, tiled=True),
            lax.all_gather(value_rows, "fsdp", axis=0, tiled=True),
        )
        layout_back = key_layout(key_back, value_back, segment, position, head_count)
        d_queries, key_terms, d_buckets = attend_back(
            queries_heads,
            layout_back,
            seg_query,
            pos_query,
            rel_bucket,
            bucket_edges,
            max_offset,
            log_total,
            d_attended_heads,
            row_delta,
        )
        d_keys, d_values = key_terms
        group_rows = d_keys.shape[0] * d_keys.shape[1]
        d_keys_own, d_values_own = (
            lax.psum_scatter(
                d_keys.reshape(group_rows, model_width).astype(jnp.bfloat16),
                "fsdp",
                scatter_dimension=0,
                tiled=True,
            ).astype(jnp.float32),
            lax.psum_scatter(
                d_values.reshape(group_rows, model_width).astype(jnp.bfloat16),
                "fsdp",
                scatter_dimension=0,
                tiled=True,
            ).astype(jnp.float32),
        )
        acc_buckets = acc_buckets + d_buckets
        d_queries_low = d_queries.reshape(tok_rows, model_width).astype(jnp.bfloat16)
        d_keys_low = d_keys_own.astype(jnp.bfloat16)
        d_values_low = d_values_own.astype(jnp.bfloat16)
        acc_query = acc_query + jnp.einsum(
            "td,te->de", normed1, d_queries_low, preferred_element_type=jnp.float32
        )
        acc_key = acc_key + jnp.einsum(
            "td,te->de", normed1, d_keys_low, preferred_element_type=jnp.float32
        )
        acc_value = acc_value + jnp.einsum(
            "td,te->de", normed1, d_values_low, preferred_element_type=jnp.float32
        )
        d_normed1 = (
            jnp.einsum("te,de->td", d_queries_low, query_weight, preferred_element_type=jnp.float32)
            + jnp.einsum("te,de->td", d_keys_low, key_weight, preferred_element_type=jnp.float32)
            + jnp.einsum(
                "te,de->td", d_values_low, value_weight, preferred_element_type=jnp.float32
            )
        )
        d_rows_norm, d_gain_one = norm_back_rows(dealt_rows, scale_one, gain_one, d_normed1)
        acc_gain_one = acc_gain_one + d_gain_one
        d_dealt = d_mid + d_rows_norm
        returned = lax.all_to_all(
            d_dealt.astype(jnp.bfloat16), "fsdp", split_axis=0, concat_axis=0, tiled=True
        ).astype(d_dealt.dtype)
        grads_list.append(jnp.zeros_like(returned).at[take_rows].set(returned))
    acc_rel = acc_buckets.reshape(-1)
    summed = (
        lax.psum_scatter(acc_gain_one, ("dp", "fsdp"), scatter_dimension=0, tiled=True),
        lax.psum_scatter(acc_gain_two, ("dp", "fsdp"), scatter_dimension=0, tiled=True),
        lax.psum_scatter(acc_rel, ("dp", "fsdp"), scatter_dimension=0, tiled=True),
        lax.psum_scatter(acc_query, ("dp", "fsdp"), scatter_dimension=0, tiled=True),
        lax.psum_scatter(acc_key, ("dp", "fsdp"), scatter_dimension=0, tiled=True),
        lax.psum_scatter(acc_value, ("dp", "fsdp"), scatter_dimension=0, tiled=True),
        lax.psum_scatter(acc_output, ("dp", "fsdp"), scatter_dimension=0, tiled=True),
        lax.psum_scatter(acc_inner, ("dp", "fsdp"), scatter_dimension=0, tiled=True),
        lax.psum_scatter(acc_outer, ("dp", "fsdp"), scatter_dimension=0, tiled=True),
    )
    return (
        jnp.stack(outputs_list),
        jnp.stack(grads_list),
        summed[0],
        summed[1],
        summed[2],
        summed[3],
        summed[4],
        summed[5],
        summed[6],
        summed[7],
        summed[8],
    )


VMEM = pl.BlockSpec(memory_space=pltpu.VMEM)
SMEM = pl.BlockSpec(memory_space=pltpu.SMEM)
ANYWHERE = pl.BlockSpec(memory_space=pl.ANY)
LIMIT = 56 * 1024 * 1024
FIRST_AXIS = ("x", "x", "y", "x", "y", "x", "y")


def shaped(*shape, dtype=jnp.bfloat16):
    return jax.ShapeDtypeStruct(shape, dtype)


def params(collective_id=None):
    if collective_id is None:
        return pltpu.CompilerParams(vmem_limit_bytes=LIMIT)
    return pltpu.CompilerParams(
        collective_id=collective_id, has_side_effects=True, vmem_limit_bytes=LIMIT
    )


def dma(*shape):
    return pltpu.SemaphoreType.DMA(shape)


def gather_all(lens, deal, hid, grd, shards):
    count = len(shards)
    return pl.pallas_call(
        functools.partial(gather_kernel, FIRST_AXIS),
        name="gather_all",
        out_shape=[
            shaped(*lens.shape[1:], dtype=jnp.int32),
            shaped(*deal.shape[1:], dtype=jnp.int32),
            shaped(OWN, TILE, hid.shape[-1]),
            shaped(8, *grd.shape[2:]),
        ]
        + [shaped(32, *s.shape) for s in shards],
        in_specs=[ANYWHERE] * (4 + count),
        out_specs=[ANYWHERE] * (4 + count),
        scratch_shapes=[
            dma(count, 10), dma(count, 10), dma(count), dma(2, 3), dma(OWN), dma(2, 2, 2), dma(2, 4), dma(2), dma(2),
        ],
        compiler_params=params(0),
    )(lens, deal, hid, grd, *shards)


def scatter_all(deal, res, back, grads):
    count = len(grads)
    width = res.shape[-1]
    blocks = [g.shape[1:] for g in grads]
    return pl.pallas_call(
        functools.partial(scatter_kernel, FIRST_AXIS),
        name="scatter_all",
        out_shape=[shaped(2, 3 * TILE, width), shaped(2, 3, TILE, width)]
        + [shaped(*b, dtype=jnp.float32) for b in blocks],
        in_specs=[VMEM] * (3 + count),
        out_specs=[VMEM] * (2 + count),
        scratch_shapes=[pltpu.VMEM((4, 4, *b), jnp.bfloat16) for b in blocks]
        + [pltpu.VMEM((2, 4, *b), jnp.bfloat16) for b in blocks]
        + [pltpu.VMEM((4, *b), jnp.bfloat16) for b in blocks]
        + [pltpu.VMEM((3, *b), jnp.bfloat16) for b in blocks]
        + [
            pltpu.VMEM((OWN, 2, TILE, width), jnp.bfloat16),
            pltpu.VMEM((2, 3 * TILE, width), jnp.bfloat16),
            dma(count, 10), dma(count, 10), dma(OWN), dma(2, 3), dma(2), dma(2),
            pltpu.SemaphoreType.DMA, pltpu.SemaphoreType.DMA,
        ],
        compiler_params=params(3),
    )(deal, res, back, *grads)


def attention_forward(lens, x, gain, wq, wk, wv, rows):
    heads, keys = (PAIRS, OWN, TILE, 128), (PAIRS, OWN, 2, TILE, 128)
    return pl.pallas_call(
        attn_fwd,
        name="attn_fwd",
        out_shape=[
            shaped(*heads), shaped(*keys), shaped(*keys), shaped(*heads, dtype=jnp.float32),
            shaped(OWN, 2 * PAIRS, 1, TILE, dtype=jnp.float32),
        ],
        in_specs=[SMEM] + [VMEM] * 6,
        out_specs=[VMEM] * 5,
        scratch_shapes=[
            pltpu.VMEM((2 * PAIRS, 5, TILE, TILE), jnp.float32),
            pltpu.VMEM((OWN, TILE, 128), jnp.bfloat16),
            pltpu.VMEM((TILES, TILE, 128), jnp.bfloat16),
            pltpu.VMEM((2, TILE, TILES * TILE), jnp.float32),
            pltpu.VMEM((OWN, TILE, 128), jnp.float32),
            dma(2), dma(2),
        ],
        compiler_params=params(1),
    )(lens, x, gain, wq, wk, wv, rows)


def attention_backward(lens, q, k, v, log_total, d_att, delta, rows):
    heads = (PAIRS, OWN, TILE, 128)
    return pl.pallas_call(
        attn_bwd,
        name="attn_bwd",
        out_shape=[shaped(*heads)] * 3 + [shaped(5, 2 * PAIRS, 1, 2 * TILE, dtype=jnp.float32)],
        in_specs=[SMEM] + [VMEM] * 7,
        out_specs=[VMEM] * 4,
        scratch_shapes=[pltpu.VMEM((2 * PAIRS, 5, TILE, TILE), jnp.float32)] * 2
        + [pltpu.VMEM((OWN, TILE, 128), jnp.bfloat16), pltpu.VMEM((TILES, TILE, 128), jnp.bfloat16)]
        + [pltpu.VMEM((TILES * TILE, 128), jnp.float32)] * 2
        + [pltpu.VMEM(heads, jnp.bfloat16)] * 4
        + [dma(2, PAIRS), dma(2, PAIRS)],
        compiler_params=params(2),
    )(lens, q, k, v, log_total, d_att, delta, rows)


def feed_forward(deal, x, o, g, wo, gain, wi, wu):
    tok, width, hidden = x.shape[0], x.shape[1], wi.shape[1]
    chunk = 512
    f32 = jnp.float32

    def full(*shape):
        return pl.BlockSpec(shape, lambda j: (0,) * len(shape))

    columns = pl.BlockSpec((width, chunk), lambda j: (0, j))
    lines = pl.BlockSpec((chunk, width), lambda j: (j, 0))
    heads, stats = (PAIRS, OWN, TILE, 128), (OWN, 2 * PAIRS, 1, TILE)
    return pl.pallas_call(
        ffn_kernel,
        name="feed_forward",
        grid=(hidden // chunk,),
        out_shape=[
            shaped(tok, width), shaped(tok, width, dtype=f32), shaped(*heads), shaped(*stats, dtype=f32),
            shaped(width, width), shaped(width, hidden), shaped(hidden, width), shaped(8, width, dtype=f32),
        ],
        in_specs=[
            full(*deal.shape), full(tok, width), full(*heads), full(2 * tok, width), full(width, width),
            full(8, width), columns, lines,
        ],
        out_specs=[
            full(tok, width), full(tok, width), full(*heads), full(*stats), full(width, width),
            columns, lines, full(8, width),
        ],
        scratch_shapes=[
            pltpu.VMEM((tok, width), jnp.bfloat16), pltpu.VMEM((tok, width), jnp.bfloat16),
            pltpu.VMEM((tok, width), f32), pltpu.VMEM((tok, width), jnp.bfloat16),
            pltpu.VMEM((tok, width), f32), pltpu.VMEM((tok, width), f32),
        ],
        compiler_params=params(),
    )(deal, x, o, g, wo, gain, wi, wu)


def qkv_backward(x, gain, d_mid, dq, dk, dv, wq, wk, wv):
    tok, width = x.shape
    return pl.pallas_call(
        qkv_back_kernel,
        name="qkv_back",
        out_shape=[shaped(width, width)] * 3 + [shaped(tok, width), shaped(8, width, dtype=jnp.float32)],
        in_specs=[VMEM] * 9,
        out_specs=[VMEM] * 5,
        scratch_shapes=[pltpu.VMEM((tok, width), jnp.bfloat16)],
        compiler_params=params(),
    )(x, gain, d_mid, dq, dk, dv, wq, wk, wv)


def bias_rows(rel, turned=False):
    first, last = rel[:, :1], rel[:, 256:]
    low, high = rel[:, :128], rel[:, 128:256]
    spread = lambda one: jnp.broadcast_to(one, low.shape)
    rows = [
        jnp.concatenate(pair, axis=1)
        for pair in (
            (low, spread(first)), (high, low), (spread(last), high),
            (spread(first), spread(first)), (spread(last), spread(last)),
        )
    ]
    if turned:
        rows = [rows[2], rows[1], rows[0], rows[4], rows[3]]
    return jnp.stack(rows)[:, :, None, :]


def on_device_packed(
    hidden_in, grad_out, gain_attn, gain_ffn, rel_bias,
    w_query, w_key, w_value, w_output, w_inner, w_outer,
    dealing, lengths, bucket_table,
):
    micro_count, tok_rows, width = hidden_in.shape
    f32 = jnp.float32
    line = lambda v: jnp.pad(v, (0, 128 - v.shape[0]))[None]
    small = jnp.concatenate(
        [line(gain_attn), line(gain_ffn), line(rel_bias), jnp.zeros((13, 128), jnp.bfloat16)], axis=0
    )
    lens = jnp.pad(lengths, ((0, 0), (0, 0), (0, 128 - lengths.shape[2])))
    gathered = gather_all(
        lens,
        dealing,
        hidden_in.reshape(2, 3, TILE, width),
        grad_out.reshape(2, 2, tok_rows // 2, width),
        (small, w_query, w_key, w_value, w_output, w_inner, w_outer),
    )
    lens_u, deal_u, x_own, g_all, small_all = gathered[:5]
    wq, wk, wv, wo, wi, wu = (w.reshape(-1, w.shape[-1]) for w in gathered[5:])
    gains = [
        jnp.broadcast_to(small_all[:, n, :24].reshape(1, width).astype(f32), (8, width)) for n in range(2)
    ]
    picked = (bucket_table[None, :] == jnp.arange(BUCKETS, dtype=jnp.int32)[:, None]).astype(f32)
    rel = lax.dot_general(
        small_all[:, 2, :H].astype(f32), picked, (((0,), (0,)), ((), ())),
        precision=lax.Precision.HIGHEST, preferred_element_type=f32,
    )
    x_rows = x_own.reshape(-1, width)
    q, k, v, o, log_total = attention_forward(lens_u, x_rows, gains[0], wq, wk, wv, bias_rows(rel))
    result, d_mid, d_att, delta, g_wo, g_wi, g_wu, g_two = feed_forward(
        deal_u, x_rows, o, g_all.reshape(-1, width), wo, gains[1], wi, wu
    )
    dq, dk, dv, hist = attention_backward(
        lens_u, q, k, v, log_total, d_att, delta, bias_rows(rel[:, ::-1], True)
    )
    g_wq, g_wk, g_wv, d_dealt, g_one = qkv_backward(x_rows, gains[0], d_mid, dq, dk, dv, wq, wk, wv)

    hist = hist[:, :, 0, :]
    turned = hist[:3, :, ::-1]
    by_distance = jnp.concatenate([turned[1], jnp.zeros((H, 1), f32)], axis=1)
    by_distance = by_distance.at[:, 128:256].add(turned[2][:, :128])
    by_distance = by_distance.at[:, 256].add(jnp.sum(turned[2][:, 128:], axis=1) + jnp.sum(hist[4], axis=1))
    by_distance = by_distance.at[:, :128].add(turned[0][:, 128:])
    by_distance = by_distance.at[:, 0].add(jnp.sum(turned[0][:, :128], axis=1) + jnp.sum(hist[3], axis=1))
    g_rel = lax.dot_general(
        picked, by_distance, (((1,), (1,)), ((), ())), precision=lax.Precision.HIGHEST, preferred_element_type=f32
    )
    wide = lambda v: jnp.pad(v, ((0, 0), (0, 128 - v.shape[1])))[:, None]
    g_small = jnp.concatenate(
        [wide(g_one[0].reshape(32, 24)), wide(g_two[0].reshape(32, 24)), wide(g_rel), jnp.zeros((32, 13, 128), f32)],
        axis=1,
    ).astype(jnp.bfloat16)
    split = lambda g: g.reshape(32, -1, g.shape[-1])
    done = scatter_all(
        deal_u.reshape(2, 1, -1),
        result.reshape(OWN, TILE, width),
        d_dealt.reshape(OWN, TILE, width),
        (g_small, split(g_wq), split(g_wk), split(g_wv), split(g_wo), split(g_wi), split(g_wu)),
    )
    hid, gin, s_small = done[:3]
    return (
        hid.astype(f32),
        gin.reshape(2, tok_rows, width).astype(f32),
        s_small[0, :24],
        s_small[1, :24],
        s_small[2, :H],
        *done[3:],
    )


def solution(mesh):
    axes = ("dp", "fsdp")
    tokens, matrix, vector = P(None, axes, None), P(axes, None), P(axes)
    packed = mesh.shape["fsdp"] == 4 and mesh.shape["dp"] == 8
    return jax.shard_map(
        on_device_packed if packed else on_device,
        mesh=mesh,
        in_specs=(tokens, tokens, vector, vector, vector)
        + (matrix,) * 6
        + (P(None, "dp", None), P(None, "dp", None), P()),
        out_specs=(tokens, tokens, vector, vector, vector) + (matrix,) * 6,
        check_vma=False,
    )
```

```python
import functools
import math

import jax
import jax.numpy as jnp
from jax import lax
from jax.experimental import pallas as pl
from jax.experimental.pallas import tpu as pltpu
from jax.sharding import PartitionSpec as P

H = 12
BUCKETS = 32
EPSILON = 1e-06
NEG_FILL = -1e30
MESH = pl.DeviceIdType.MESH
TILE = 128
PAIRS = 6
OWN = 6
TILES = 12
FAR = 6
SEQS = 4


def lane_index(shape):
    return lax.broadcasted_iota(jnp.int32, shape, len(shape) - 1)


def row_index(shape):
    return lax.broadcasted_iota(jnp.int32, shape, len(shape) - 2)


def dot_nn(left, right):
    return lax.dot_general(left, right, (((1,), (0,)), ((), ())), preferred_element_type=jnp.float32)


def dot_nt(left, right):
    return lax.dot_general(left, right, (((1,), (1,)), ((), ())), preferred_element_type=jnp.float32)


def dot_tn(left, right):
    return lax.dot_general(left, right, (((0,), (0,)), ((), ())), preferred_element_type=jnp.float32)


def segments_of(places, lens_ref, count):
    edge = jnp.int32(0)
    found = jnp.zeros(places.shape, jnp.int32)
    for s in range(count - 1):
        edge = edge + lens_ref[0, s]
        found = found + (places >= edge).astype(jnp.int32)
    return found


def segment_tags(places, lens_ref, count, of_key):
    lane = lane_index(places.shape)
    hit = segments_of(places, lens_ref, count) == lane
    if of_key:
        return jnp.where((lane < count) & jnp.logical_not(hit), NEG_FILL, 0.0).astype(jnp.bfloat16)
    return jnp.where(hit, 1.0, 0.0).astype(jnp.bfloat16)


def key_range(i):
    return max(0, 2 * i - FAR), min(TILES, 2 * i + FAR + 2)


def fill_bias(rows_ref, tiles_ref, heads):
    def one_head(h, carry):
        for cls in range(3):
            row = rows_ref[cls, h]
            wide = pltpu.roll(
                jnp.broadcast_to(row, (TILE, 2 * TILE)), 0, 1, stride=1, stride_axis=0
            )
            tiles_ref[h, cls + 1] = wide[:, :TILE]
        left = rows_ref[3, h, :, :TILE]
        right = rows_ref[4, h, :, :TILE]
        tiles_ref[h, 0] = jnp.broadcast_to(left, (TILE, TILE))
        tiles_ref[h, 4] = jnp.broadcast_to(right, (TILE, TILE))
        return carry

    lax.fori_loop(0, heads, one_head, 0)


def bias_class(kt, i, core):
    return jnp.clip(kt - 2 * i - core, -2, 2) + 2


def attn_fwd(
    lens_ref, x_ref, gain_ref, wq_ref, wk_ref, wv_ref, rows_ref, grd_in, wo_in, wi_in, wu_in,
    q_ref, k_ref, v_ref, o_ref, log_ref, g_all, wo_all, wi_all, wu_all,
    bias_ref, ext_q, ext_k, s_ref, log_acc, send_sem, recv_sem,
    w_send, w_recv, w_local, g_send, g_recv,
):
    y, x, core, z = coordinates()
    sibling = place(y, x, 1 - core, z)
    greet()
    hidden = wi_in.shape[1] // 2
    lines = wu_in.shape[0] // 2
    gather = Gather(
        [
            (wo_in, wo_all, None, "x"),
            (wi_in, wi_all, ("columns", 0, hidden), "y"),
            (wu_in, wu_all, ("rows", 0, lines), "x"),
            (wi_in, wi_all, ("columns", hidden, hidden), "y"),
            (wu_in, wu_all, ("rows", lines, lines), "x"),
        ],
        w_send, w_recv, w_local,
    )
    pieces = range(len(gather.pieces))
    grads = list(grad_sends(grd_in, g_all, g_send, g_recv))
    events = {}

    def plan(at, step, *args):
        events.setdefault(at, []).append(functools.partial(step, *args))

    def start_grads():
        for item in grads:
            send_or_keep(*item)

    for n in pieces:
        plan(FWD_OWN[n], gather.spread_own, n)
        plan(FWD_NEAR[n], gather.spread_near, n)
        plan(FWD_SIDE[n], gather.spread_side, n)
    plan(FWD_GRADS, start_grads)

    rows = x_ref[...].astype(jnp.float32)
    scale = lax.rsqrt(jnp.mean(rows * rows, axis=1, keepdims=True) + EPSILON)
    normed = (rows * scale * gain_ref[0:1, :]).astype(jnp.bfloat16)

    def project(w_ref):
        return dot_nn(normed, w_ref[...]).astype(jnp.bfloat16)

    copies = []
    for n, (w_ref, all_ref) in enumerate(((wk_ref, k_ref), (wv_ref, v_ref))):
        made = project(w_ref)
        for hp in range(PAIRS):
            for i in range(OWN):
                all_ref[hp, i, core] = made[TILE * i : TILE * (i + 1), 128 * hp : 128 * (hp + 1)]
        if n == 0:
            greeted()
            for piece in pieces:
                gather.start(piece)
        copy = pltpu.make_async_remote_copy(
            all_ref.at[:, :, core], all_ref.at[:, :, core], send_sem.at[n], recv_sem.at[n],
            device_id=sibling, device_id_type=MESH,
        )
        copy.start()
        copies.append(copy)
    made = project(wq_ref)
    for hp in range(PAIRS):
        for i in range(OWN):
            q_ref[hp, i] = made[TILE * i : TILE * (i + 1), 128 * hp : 128 * (hp + 1)]
    count = SEQS
    for t in range(TILES):
        ext_k[t] = segment_tags(TILE * t + row_index((TILE, 128)), lens_ref, count, True)
    for i in range(OWN):
        ext_q[i] = segment_tags(TILE * (2 * i + core) + row_index((TILE, 128)), lens_ref, count, False)
        log_acc[i] = jnp.zeros((TILE, 128), jnp.float32)
    fill_bias(rows_ref, bias_ref, 2 * PAIRS)
    for n, all_ref in enumerate((k_ref, v_ref)):
        pltpu.make_async_remote_copy(
            all_ref.at[:, :, 1 - core], all_ref.at[:, :, 1 - core], send_sem.at[n], recv_sem.at[n],
            device_id=sibling, device_id_type=MESH,
        ).wait_recv()

    lane = lane_index((TILE, 128))

    def one_pair(hp, carry):
        for i in range(OWN):
            run_events(events, hp, i)
            lo, hi = key_range(i)
            width = (hi - lo) * TILE
            pair = q_ref[hp, i]
            tags = ext_q[i]
            zero = jnp.zeros_like(pair)
            left = jnp.concatenate(
                [
                    jnp.concatenate([jnp.where(lane < 64, pair, zero), tags], axis=1),
                    jnp.concatenate([jnp.where(lane < 64, zero, pair), tags], axis=1),
                ],
                axis=0,
            )
            keys = k_ref[hp, lo // 2 : hi // 2].reshape(width, 128)
            right = jnp.concatenate([keys, ext_k[lo:hi].reshape(width, 128)], axis=1)
            raw = dot_nt(left, right)
            tops = []
            for e in range(2):
                top = None
                for kt in range(lo, hi):
                    at = (kt - lo) * TILE
                    part = raw[e * TILE : (e + 1) * TILE, at : at + TILE]
                    if -1 <= kt - 2 * i <= 2:
                        part = part + bias_ref[2 * hp + e, bias_class(kt, i, core)]
                    else:
                        part = part + rows_ref[3 if kt < 2 * i else 4, 2 * hp + e, :, :TILE]
                    s_ref[e, :, at : at + TILE] = part
                    top = part if top is None else jnp.maximum(top, part)
                tops.append(jnp.max(top, axis=1, keepdims=True))
            outs = []
            for e in range(2):
                total = None
                pieces = []
                for kt in range(lo, hi):
                    at = (kt - lo) * TILE
                    weight = jnp.exp(s_ref[e, :, at : at + TILE] - tops[e])
                    total = weight if total is None else total + weight
                    pieces.append(weight.astype(jnp.bfloat16))
                total = jnp.sum(total, axis=1, keepdims=True)
                probs = jnp.concatenate(pieces, axis=1)
                values = v_ref[hp, lo // 2 : hi // 2].reshape(width, 128)
                outs.append(dot_nn(probs, values) / total)
                log_acc[i] = jnp.where(lane == 2 * hp + e, tops[e] + jnp.log(total), log_acc[i])
            o_ref[hp, i] = jnp.where(lane < 64, outs[0], outs[1])
        return carry

    lax.fori_loop(0, PAIRS, one_pair, 0)
    for i in range(OWN):
        turned = log_acc[i].T
        for h in range(2 * PAIRS):
            log_ref[i, h] = turned[h : h + 1, :]
    late(events)
    for zs in range(4):
        block = g_all.at[2 * zs + core]
        remote(block, block, g_send.at[1, 0, 0], g_recv.at[0, zs], sibling).wait_recv()
        remote(block, block, g_send.at[1, zs // 2, zs % 2], g_recv.at[1, zs], sibling).start()
    for n in pieces:
        gather.finish(n)
    for zs in range(4):
        block = g_all.at[2 * zs + 1 - core]
        remote(block, block, g_send.at[1, zs // 2, zs % 2], g_recv.at[1, zs], sibling).wait_recv()
        remote(block, block, g_send.at[1, zs // 2, zs % 2], g_recv.at[1, zs], sibling).wait_send()
    for item in grads:
        sent(*item)
    for copy in copies:
        copy.wait_send()


def attn_bwd(
    lens_ref, q_ref, k_ref, v_ref, log_ref, do_ref, delta_ref, rows_ref, deal_ref, res_in, gwo, gwi, gwu,
    dq_ref, dk_ref, dv_ref, hist_ref, hid_out, two, twi, twu,
    bias_ref, acc_ref, ext_q, ext_k, dk_acc, dv_acc, out_k, out_v, got_k, got_v, send_sem, recv_sem,
    res_all, dealt, *scratch,
):
    y, x, core, z = coordinates()
    sibling = place(y, x, 1 - core, z)
    greet()
    owner, micro = z // 2, lax.rem(z, 2)
    hidden = gwi.shape[2] // 2
    lines = gwu.shape[1] // 2
    plain = [
        (gwu, twu, ("rows", 0, lines), "x"),
        (gwi, twi, ("columns", 0, hidden), "y"),
        (gwu, twu, ("rows", lines, lines), "x"),
        (gwi, twi, ("columns", hidden, hidden), "y"),
        (gwo, two, None, "x"),
    ]
    count = len(plain)
    w_send, w_recv, w_local, h_send, h_recv, e_send, e_recv = scratch[3 * count :]
    scatter = Scatter(
        [item + tuple(scratch[3 * n : 3 * n + 3]) for n, item in enumerate(plain)], w_send, w_recv, w_local
    )
    res_copy = remote(res_in, res_all.at[:, core], e_send, e_recv, sibling)

    def dealt_sends():
        for e in range(2):
            z_to = 2 * core + e
            yield (
                dealt.at[e], hid_out.at[micro], h_send.at[e], h_recv.at[micro],
                place(y, x, owner, z_to), (owner == core) & (z_to == z),
            )

    def deal_result():
        for i in range(OWN):
            res_all[i, core] = res_in[i]
        remote(res_in, res_all.at[:, 1 - core], e_send, e_recv, sibling).wait_recv()
        pick = jnp.where(
            row_index((TILES * TILE, TILES * TILE // 2)) == deal_ref[core], 1.0, 0.0
        ).astype(jnp.bfloat16)
        made = dot_tn(pick, res_all[...].reshape(TILES * TILE, -1))
        dealt[...] = made.astype(jnp.bfloat16).reshape(dealt.shape)
        for item in dealt_sends():
            send_or_keep(*item)

    events = {}

    def plan(at, step, *args):
        events.setdefault(at, []).append(functools.partial(step, *args))

    plan(BWD_DEAL, deal_result)
    for n in range(count):
        plan(BWD_CORE[n], scatter.sum_core, n)
        plan(BWD_SIDE[n], scatter.sum_side, n)
        plan(BWD_NEAR[n], scatter.sum_near, n)
    for t in range(TILES):
        ext_k[t] = segment_tags(TILE * t + row_index((TILE, 128)), lens_ref, SEQS, True)
    for i in range(OWN):
        ext_q[i] = segment_tags(TILE * (2 * i + core) + row_index((TILE, 128)), lens_ref, SEQS, False)
    fill_bias(rows_ref, bias_ref, 2 * PAIRS)
    acc_ref[...] = jnp.zeros_like(acc_ref)
    greeted()
    for n in range(count):
        scatter.start(n)
        if n == 0:
            res_copy.start()
    lane = lane_index((TILE, 128))

    def one_pair(hp, carry):
        dk_acc[...] = jnp.zeros_like(dk_acc)
        dv_acc[...] = jnp.zeros_like(dv_acc)
        for i in range(OWN):
            run_events(events, hp, i)
            lo, hi = key_range(i)
            width = (hi - lo) * TILE
            pair, d_pair = q_ref[hp, i], do_ref[hp, i]
            tags = ext_q[i]
            zero = jnp.zeros_like(pair)
            q_two = jnp.concatenate([jnp.where(lane < 64, pair, zero), jnp.where(lane < 64, zero, pair)], axis=0)
            d_two = jnp.concatenate([jnp.where(lane < 64, d_pair, zero), jnp.where(lane < 64, zero, d_pair)], axis=0)
            q_ext = jnp.concatenate([q_two, jnp.concatenate([tags, tags], axis=0)], axis=1)
            keys = k_ref[hp, lo // 2 : hi // 2].reshape(width, 128)
            values = v_ref[hp, lo // 2 : hi // 2].reshape(width, 128)
            k_ext = jnp.concatenate([keys, ext_k[lo:hi].reshape(width, 128)], axis=1)
            raw = dot_nt(k_ext, q_ext)
            d_probs = dot_nt(values, d_two)
            p_rows, s_rows = [], []
            for kt in range(lo, hi):
                at = (kt - lo) * TILE
                p_two, s_two = [], []
                for e in range(2):
                    head = 2 * hp + e
                    part = raw[at : at + TILE, e * TILE : (e + 1) * TILE]
                    near = -1 <= kt - 2 * i <= 2
                    cls = bias_class(kt, i, core) if near else (0 if kt < 2 * i else 4)
                    if near:
                        part = part + bias_ref[head, cls]
                    else:
                        part = part + rows_ref[3 if kt < 2 * i else 4, head, :, :TILE]
                    probs = jnp.exp(part - log_ref[i, head])
                    slope = probs * (
                        d_probs[at : at + TILE, e * TILE : (e + 1) * TILE] - delta_ref[i, head]
                    )
                    acc_ref[head, cls] += slope
                    p_two.append(probs.astype(jnp.bfloat16))
                    s_two.append(slope.astype(jnp.bfloat16))
                p_rows.append(jnp.concatenate(p_two, axis=1))
                s_rows.append(jnp.concatenate(s_two, axis=1))
            probs_t = jnp.concatenate(p_rows, axis=0)
            slopes_t = jnp.concatenate(s_rows, axis=0)
            dv_acc[lo * TILE : hi * TILE, :] += dot_nn(probs_t, d_two)
            dk_acc[lo * TILE : hi * TILE, :] += dot_nn(slopes_t, q_two)
            d_q = dot_tn(slopes_t, keys)
            dq_ref[hp, i] = jnp.where(lane < 64, d_q[:TILE], d_q[TILE:]).astype(jnp.bfloat16)
        for acc, own, out in ((dk_acc, dk_ref, out_k), (dv_acc, dv_ref, out_v)):
            for i in range(OWN):
                own[hp, i] = acc[pl.ds((2 * i + core) * TILE, TILE), :].astype(jnp.bfloat16)
                out[hp, i] = acc[pl.ds((2 * i + 1 - core) * TILE, TILE), :].astype(jnp.bfloat16)
        for n, (out, got) in enumerate(((out_k, got_k), (out_v, got_v))):
            pltpu.make_async_remote_copy(
                out.at[hp], got.at[hp], send_sem.at[n, hp], recv_sem.at[n, hp],
                device_id=sibling, device_id_type=MESH,
            ).start()
        return carry

    lax.fori_loop(0, PAIRS, one_pair, 0)
    flip = (row_index((TILE, TILE)) + lane == TILE - 1).astype(jnp.float32)

    def one_head(h, carry):
        for cls in range(3):
            tile = jnp.dot(flip, acc_ref[h, cls + 1], precision=lax.Precision.HIGHEST)
            wide = jnp.concatenate([tile, jnp.zeros((TILE, TILE), jnp.float32)], axis=1)
            wide = pltpu.roll(wide, 0, 1, stride=1, stride_axis=0)
            hist_ref[cls, h] = jnp.sum(wide, axis=0, keepdims=True)
        for n, cls in ((3, 0), (4, 4)):
            row = jnp.sum(acc_ref[h, cls], axis=0, keepdims=True)
            hist_ref[n, h] = jnp.concatenate([row, jnp.zeros_like(row)], axis=1)
        return carry

    lax.fori_loop(0, 2 * PAIRS, one_head, 0)

    def finish(hp, carry):
        for n, (out, got, own) in enumerate(((out_k, got_k, dk_ref), (out_v, got_v, dv_ref))):
            copy = pltpu.make_async_remote_copy(
                out.at[hp], got.at[hp], send_sem.at[n, hp], recv_sem.at[n, hp],
                device_id=sibling, device_id_type=MESH,
            )
            copy.wait_send()
            copy.wait_recv()
            own[hp] = (own[hp].astype(jnp.float32) + got[hp].astype(jnp.float32)).astype(jnp.bfloat16)
        return carry

    lax.fori_loop(0, PAIRS, finish, 0)
    late(events)
    for n in range(count):
        scatter.finish(n)
    res_copy.wait_send()
    for item in dealt_sends():
        sent(*item)
    for m in range(2):
        remote(dealt.at[0], hid_out.at[m], h_send.at[0], h_recv.at[m], sibling).wait_recv()


def norm_back(rows_in, scale, gain, grad_normed):
    scaled = grad_normed * gain
    grad_gain = jnp.sum(grad_normed * rows_in * scale, axis=0, keepdims=True)
    shared = jnp.mean(scaled * rows_in, axis=1, keepdims=True)
    return scale * scaled - rows_in * (scale * scale * scale * shared), grad_gain


def join_pairs(pairs_ref, joined_ref):
    for hp in range(PAIRS):
        joined_ref[:, 128 * hp : 128 * (hp + 1)] = (
            pairs_ref[hp].reshape(OWN * TILE, 128).astype(joined_ref.dtype)
        )


def gain_block(row):
    width = row.shape[1]
    lines = jnp.where(lane_index((32, width)) // 24 == row_index((32, width)), row, 0.0)
    pick = (lax.rem(row_index((width, 128)), 24) == lane_index((width, 128))).astype(jnp.float32)
    return jnp.dot(lines, pick, precision=lax.Precision.HIGHEST)


def ffn_kernel(
    deal_ref, x_ref, o_ref, g_ref, wo_ref, gain_ref, wi_ref, wu_ref,
    out_ref, dmid_ref, datt_ref, delta_ref, gwo_ref, gwi_ref, gwu_ref, ggain_ref,
    att_ref, grad_ref, mid_ref, normed_ref, total_ref, back_ref,
):
    step = pl.program_id(0)
    tok = OWN * TILE

    @pl.when(step == 0)
    def _():
        core = lax.rem(lax.axis_index("dp"), 2)
        for i in range(OWN):
            places = (2 * i + core) * TILE + row_index((TILE, TILES * TILE))
            pick = jnp.where(deal_ref[...] == places, 1.0, 0.0).astype(jnp.bfloat16)
            grad_ref[TILE * i : TILE * (i + 1), :] = dot_nn(pick, g_ref[...]).astype(jnp.bfloat16)
        join_pairs(o_ref, att_ref)
        mid = x_ref[...].astype(jnp.float32) + dot_nn(att_ref[...], wo_ref[...])
        mid_ref[...] = mid
        scale = lax.rsqrt(jnp.mean(mid * mid, axis=1, keepdims=True) + EPSILON)
        normed_ref[...] = (mid * scale * gain_ref[0:1, :]).astype(jnp.bfloat16)
        total_ref[...] = jnp.zeros_like(total_ref)
        back_ref[...] = jnp.zeros_like(back_ref)

    normed = normed_ref[...]
    grad = grad_ref[...]
    inner = dot_nn(normed, wi_ref[...])
    cdf = 0.5 * (1.0 + lax.erf(inner * (1.0 / math.sqrt(2.0))))
    active = (inner * cdf).astype(jnp.bfloat16)
    slope = cdf + inner * (jnp.exp(-0.5 * inner * inner) * (1.0 / math.sqrt(2.0 * math.pi)))
    total_ref[...] += dot_nn(active, wu_ref[...])
    d_inner = (dot_nt(grad, wu_ref[...]) * slope).astype(jnp.bfloat16)
    gwu_ref[...] = dot_tn(active, grad).astype(gwu_ref.dtype)
    gwi_ref[...] = dot_tn(normed, d_inner).astype(gwi_ref.dtype)
    back_ref[...] += dot_nt(d_inner, wi_ref[...])

    @pl.when(step == pl.num_programs(0) - 1)
    def _():
        mid = mid_ref[...]
        out_ref[...] = (mid + total_ref[...]).astype(out_ref.dtype)
        scale = lax.rsqrt(jnp.mean(mid * mid, axis=1, keepdims=True) + EPSILON)
        d_rows, d_gain = norm_back(mid, scale, gain_ref[0:1, :], back_ref[...])
        ggain_ref[...] = gain_block(d_gain)
        d_mid = grad_ref[...].astype(jnp.float32) + d_rows
        dmid_ref[...] = d_mid
        branch = d_mid.astype(jnp.bfloat16)
        gwo_ref[...] = dot_tn(att_ref[...], branch).astype(gwo_ref.dtype)
        d_att = dot_nt(branch, wo_ref[...]).astype(jnp.bfloat16)
        pick = (lane_index((16, PAIRS * 128)) // 64 == row_index((16, PAIRS * 128))).astype(jnp.float32)
        sums = None
        for hp in range(PAIRS):
            part = d_att[:, 128 * hp : 128 * (hp + 1)]
            datt_ref[hp] = part.reshape(OWN, TILE, 128)
            prod = part.astype(jnp.float32) * o_ref[hp].reshape(tok, 128)
            term = lax.dot_general(
                pick[:, 128 * hp : 128 * (hp + 1)], prod, (((1,), (1,)), ((), ())),
                precision=lax.Precision.HIGHEST, preferred_element_type=jnp.float32,
            )
            sums = term if sums is None else sums + term
        for i in range(OWN):
            for h in range(2 * PAIRS):
                delta_ref[i, h] = sums[h : h + 1, TILE * i : TILE * (i + 1)]


def tail_kernel(
    x_ref, gain_ref, dmid_ref, dq_ref, dk_ref, dv_ref, wq_ref, wk_ref, wv_ref, g_two, g_rel,
    gin_out, tsmall, tq, tk, tv,
    join_ref, back_out, small, gq, gk, gv, *scratch,
):
    y, x, c, z = coordinates()
    sibling = place(y, x, 1 - c, z)
    owner, micro = z // 2, lax.rem(z, 2)
    greet()
    plain = [(gk, tk, None, "x"), (gv, tv, None, "y"), (gq, tq, None, "x"), (small, tsmall, None, "y")]
    count = len(plain)
    w_send, w_recv, w_local, b_send, b_recv = scratch[3 * count :]
    scatter = Scatter(
        [item + tuple(scratch[3 * n : 3 * n + 3]) for n, item in enumerate(plain)], w_send, w_recv, w_local
    )
    rows = x_ref[...].astype(jnp.float32)
    scale = lax.rsqrt(jnp.mean(rows * rows, axis=1, keepdims=True) + EPSILON)
    back = None
    for n, (pairs, w_ref) in enumerate(((dq_ref, wq_ref), (dk_ref, wk_ref), (dv_ref, wv_ref))):
        join_pairs(pairs, join_ref.at[n])
        term = dot_nt(join_ref[n], w_ref[...])
        back = term if back is None else back + term
    d_rows, d_gain = norm_back(rows, scale, gain_ref[0:1, :], back)
    d_dealt = (dmid_ref[...] + d_rows).astype(jnp.bfloat16)
    back_out[...] = d_dealt.reshape(back_out.shape)
    greeted()

    def back_sends():
        for i in range(OWN):
            t = 2 * i + c
            z_to, l = t // 3, lax.rem(t, 3)
            yield (
                back_out.at[i], gin_out.at[micro, l], b_send.at[i], b_recv.at[micro, l],
                place(y, x, owner, z_to), (owner == c) & (z_to == z),
            )

    sends = list(back_sends())
    for item in sends:
        send_or_keep(*item)
    normed_t = (rows * scale * gain_ref[0:1, :]).astype(jnp.bfloat16).T
    for n, (at, grad_ref) in enumerate(((1, gk), (2, gv), (0, gq))):
        made = dot_nn(normed_t, join_ref[at])
        for r in range(32):
            grad_ref[r] = made[24 * r : 24 * (r + 1), :].astype(jnp.bfloat16)
        scatter.start(n)
    g_one = gain_block(d_gain)
    shape = (32, 16, 128)
    kind = lax.broadcasted_iota(jnp.int32, shape, 1)
    spread = lambda v: jnp.broadcast_to(v[:, None, :], shape)
    small[...] = jnp.where(
        kind == 0, spread(g_one), jnp.where(kind == 1, spread(g_two[...]), spread(g_rel[...]))
    ).astype(jnp.bfloat16)
    scatter.start(3)
    for n in range(count + 2):
        for back_by, stage in enumerate((scatter.sum_core, scatter.sum_side, scatter.sum_near)):
            if 0 <= n - back_by < count:
                stage(n - back_by)
    for n in range(count):
        scatter.finish(n)
    for item in sends:
        sent(*item)
    for m in range(2):
        for l in range(3):
            remote(back_out.at[0], gin_out.at[m, l], b_send.at[0], b_recv.at[m, l], sibling).wait_recv()


def coordinates():
    dp, z = lax.axis_index("dp"), lax.axis_index("fsdp")
    return dp // 4, lax.rem(dp // 2, 2), lax.rem(dp, 2), z


def place(y, x, c, z):
    return (4 * y + 2 * x + c, z)


def column(y, x, c):
    return 16 * y + 8 * x + 4 * c


def partners():
    y, x, c, z = coordinates()
    found = [place(1 - y, x, c, z), place(y, 1 - x, c, z)]
    for dc in range(2):
        for dz in range(4):
            if dc or dz:
                found.append(place(y, x, lax.rem(c + dc, 2), lax.rem(z + dz, 4)))
    return found


def greet():
    for partner in partners():
        pl.semaphore_signal(pltpu.get_barrier_semaphore(), inc=1, device_id=partner, device_id_type=MESH)


def greeted():
    pl.semaphore_wait(pltpu.get_barrier_semaphore(), len(partners()))


def remote(src, dst, send, recv, target):
    return pltpu.make_async_remote_copy(
        src, dst, send, recv, device_id=target, device_id_type=MESH
    )


def send_or_keep(src, dst, send, recv, target, here):
    @pl.when(jnp.logical_not(here))
    def _():
        remote(src, dst, send, recv, target).start()

    @pl.when(here)
    def _():
        pltpu.make_async_copy(src, dst, recv).start()


def sent(src, dst, send, recv, target, here):
    @pl.when(jnp.logical_not(here))
    def _():
        remote(src, dst, send, recv, target).wait_send()


def cut(ref, lead, part):
    if part is None:
        return ref.at[lead]
    kind, start, size = part
    if kind == "rows":
        return ref.at[lead, pl.ds(start, size)]
    return ref.at[lead, slice(None), pl.ds(start, size)]


def cut_shard(ref, part):
    if part is None:
        return ref
    kind, start, size = part
    return ref.at[pl.ds(start, size)] if kind == "rows" else ref.at[:, pl.ds(start, size)]


class Gather:
    def __init__(self, pieces, send, recv, local):
        self.pieces, self.send, self.recv, self.local = pieces, send, recv, local
        self.y, self.x, self.c, self.z = coordinates()
        y, x, c, z = self.y, self.x, self.c, self.z
        self.sibling = place(y, x, 1 - c, z)
        self.mine = column(y, x, c)
        self.far = column(1 - y, 1 - x, c)
        by_x = (place(y, 1 - x, c, z), column(y, 1 - x, c))
        by_y = (place(1 - y, x, c, z), column(1 - y, x, c))
        self.sides = {"x": by_x + by_y, "y": by_y + by_x}

    def own_copy(self, n):
        shard, whole, part, _ = self.pieces[n]
        return pltpu.make_async_copy(
            cut_shard(shard, part), cut(whole, self.mine + self.z, part), self.local.at[n]
        )

    def z_copy(self, n, dz, came=False):
        shard, whole, part, _ = self.pieces[n]
        entry = self.mine + (lax.rem(self.z + 4 - dz, 4) if came else self.z)
        return remote(
            cut_shard(shard, part), cut(whole, entry, part), self.send.at[n, dz - 1], self.recv.at[n, dz - 1],
            place(self.y, self.x, self.c, lax.rem(self.z + dz, 4)),
        )

    def push(self, n, k, base, target):
        _, whole, part, _ = self.pieces[n]
        block = cut(whole, pl.ds(base, 4), part)
        return remote(block, block, self.send.at[n, k], self.recv.at[n, k], target)

    def start(self, n):
        self.own_copy(n).start()
        for dz in range(1, 4):
            self.z_copy(n, dz).start()

    def spread_own(self, n):
        near, _, side, _ = self.sides[self.pieces[n][3]]
        self.own_copy(n).wait()
        for dz in range(1, 4):
            self.z_copy(n, dz, True).wait_recv()
        for k, target in ((3, near), (4, side), (6, self.sibling)):
            self.push(n, k, self.mine, target).start()

    def spread_near(self, n):
        _, near_column, side, _ = self.sides[self.pieces[n][3]]
        self.push(n, 3, near_column, self.sibling).wait_recv()
        self.push(n, 5, near_column, side).start()
        self.push(n, 7, near_column, self.sibling).start()

    def spread_side(self, n):
        side_column = self.sides[self.pieces[n][3]][3]
        self.push(n, 4, side_column, self.sibling).wait_recv()
        self.push(n, 8, side_column, self.sibling).start()
        self.push(n, 5, self.far, self.sibling).wait_recv()
        self.push(n, 9, self.far, self.sibling).start()

    def finish(self, n):
        _, near_column, _, side_column = self.sides[self.pieces[n][3]]
        for k, base in ((6, self.mine), (7, near_column), (8, side_column), (9, self.far)):
            self.push(n, k, base + 4 - 8 * self.c, self.sibling).wait_recv()
        for dz in range(1, 4):
            self.z_copy(n, dz).wait_send()
        for k in range(3, 10):
            self.push(n, k, self.mine, self.sibling).wait_send()


class Scatter:
    def __init__(self, pieces, send, recv, local):
        self.pieces, self.send, self.recv, self.local = pieces, send, recv, local
        self.y, self.x, self.c, self.z = coordinates()
        y, x, c, z = self.y, self.x, self.c, self.z
        self.sibling = place(y, x, 1 - c, z)

    def sides(self, n):
        y, x, c, z = self.y, self.x, self.c, self.z
        by_x, by_y = place(y, 1 - x, c, z), place(1 - y, x, c, z)
        if self.pieces[n][3] == "x":
            return by_x, by_y, (lambda s, f: 2 * s + f), y, x
        return by_y, by_x, (lambda s, f: 2 * f + s), x, y

    def core_copy(self, n, k):
        grad, _, part, _, r1 = self.pieces[n][:5]
        return remote(
            cut(grad, pl.ds(8 * k + 4 * (1 - self.c), 4), part), r1.at[k],
            self.send.at[n, k], self.recv.at[n, k], self.sibling,
        )

    def side_copy(self, n, f_at):
        _, side, index, s, _ = self.sides(n)
        _, _, _, _, r1, r2, _ = self.pieces[n]
        return remote(
            r1.at[index(1 - s, f_at)], r2.at[f_at], self.send.at[n, 4 + f_at], self.recv.at[n, 4 + f_at], side
        )

    def near_copy(self, n):
        near, _, index, s, f = self.sides(n)
        _, _, _, _, r1, _, r3 = self.pieces[n]
        return remote(r1.at[index(s, 1 - f)], r3, self.send.at[n, 6], self.recv.at[n, 6], near)

    def z_copy(self, n, dz):
        _, _, index, s, f = self.sides(n)
        _, terms, part, _, r1, _, _ = self.pieces[n]
        z_to = lax.rem(self.z + dz, 4)
        return remote(
            r1.at[index(s, f), z_to], cut(terms, dz, part), self.send.at[n, 6 + dz], self.recv.at[n, 6 + dz],
            place(self.y, self.x, self.c, z_to),
        )

    def own_copy(self, n):
        _, _, index, s, f = self.sides(n)
        _, terms, part, _, r1, _, _ = self.pieces[n]
        return pltpu.make_async_copy(r1.at[index(s, f), self.z], cut(terms, 0, part), self.local.at[n])

    def start(self, n):
        for k in range(4):
            self.core_copy(n, k).start()

    def sum_core(self, n):
        grad, _, part, _, r1 = self.pieces[n][:5]
        for k in range(4):
            self.core_copy(n, k).wait_recv()

            def one(j, carry, k=k):
                r1[k, j] = r1[k, j] + cut(grad, 8 * k + 4 * self.c + j, part)[...]
                return carry

            lax.fori_loop(0, 4, one, 0)
        for f_at in range(2):
            self.side_copy(n, f_at).start()

    def sum_side(self, n):
        _, _, index, s, _ = self.sides(n)
        _, _, _, _, r1, r2, _ = self.pieces[n]
        for f_at in range(2):
            self.side_copy(n, f_at).wait_recv()
            k = index(s, f_at)

            def one(j, carry, k=k, f_at=f_at):
                r1[k, j] = r1[k, j] + r2[f_at, j]
                return carry

            lax.fori_loop(0, 4, one, 0)
        self.near_copy(n).start()

    def sum_near(self, n):
        _, _, index, s, f = self.sides(n)
        _, _, _, _, r1, _, r3 = self.pieces[n]
        self.near_copy(n).wait_recv()
        k = index(s, f)

        def one(j, carry):
            r1[k, j] = r1[k, j] + r3[j]
            return carry

        lax.fori_loop(0, 4, one, 0)
        for dz in range(1, 4):
            self.z_copy(n, dz).start()
        self.own_copy(n).start()

    def finish(self, n):
        self.own_copy(n).wait()
        for dz in range(1, 4):
            self.z_copy(n, dz).wait_recv()
        for k in range(4):
            self.core_copy(n, k).wait_send()
        for f_at in range(2):
            self.side_copy(n, f_at).wait_send()
        self.near_copy(n).wait_send()
        for dz in range(1, 4):
            self.z_copy(n, dz).wait_send()


def run_events(events, hp, i):
    for at in range(PAIRS):
        todo = events.get(at * OWN + i, ())
        if todo:

            @pl.when(hp == at)
            def _(todo=todo):
                for step in todo:
                    step()


def late(events):
    for at in sorted(events):
        if at >= PAIRS * OWN:
            for step in events[at]:
                step()


def token_sends(hid_in, x_own, x_send, x_recv):
    y, x, c, z = coordinates()
    for m in range(2):
        for l in range(3):
            t = 3 * z + l
            core_to, z_to = lax.rem(t, 2), 2 * c + m
            yield (
                hid_in.at[m, l], x_own.at[t // 2], x_send.at[m, l], x_recv.at[t // 2],
                place(y, x, core_to, z_to), (core_to == c) & (z_to == z),
            )


def grad_sends(grd_in, g_all, g_send, g_recv):
    y, x, c, z = coordinates()
    for m in range(2):
        for half in range(2):
            z_to = 2 * c + m
            yield (
                grd_in.at[m, half], g_all.at[2 * z + half], g_send.at[0, m, half], g_recv.at[0, z],
                place(y, x, half, z_to), (half == c) & (z_to == z),
            )


def gather_kernel(first_axis, *refs):
    count = len(first_axis)
    lens_in, deal_in, hid_in = refs[:3]
    shards = refs[3 : 3 + count]
    lens_u, deal_u, x_own = refs[3 + count : 6 + count]
    outs = refs[6 + count : 6 + 2 * count]
    w_send, w_recv, w_local, x_send, x_recv, p_send, p_recv = refs[6 + 2 * count :]
    y, x, c, z = coordinates()
    sibling = place(y, x, 1 - c, z)
    greet()
    greeted()
    gather = Gather(
        [(s, o, None, a) for s, o, a in zip(shards, outs, first_axis)], w_send, w_recv, w_local
    )
    for n in range(count):
        gather.start(n)
    sends = list(token_sends(hid_in, x_own, x_send, x_recv))
    for item in sends:
        send_or_keep(*item)
    owner, micro = z // 2, lax.rem(z, 2)
    plans = []
    for n, (src, dst) in enumerate(((lens_in, lens_u), (deal_in, deal_u))):
        plans.append((src.at[micro], dst, p_send.at[n], p_recv.at[n]))

    @pl.when(owner == c)
    def _():
        for src, dst, send, recv in plans:
            remote(src, dst, send, recv, sibling).start()
            pltpu.make_async_copy(src, dst, recv).start()

    for n in range(count):
        gather.spread_own(n)
    for n in range(count):
        gather.spread_near(n)
    for n in range(count):
        gather.spread_side(n)
    for n in range(count):
        gather.finish(n)
    for item in sends:
        sent(*item)
    for i in range(OWN):
        remote(hid_in.at[0, 0], x_own.at[i], x_send.at[0, 0], x_recv.at[i], sibling).wait_recv()
    for src, dst, send, recv in plans:
        remote(src, dst, send, recv, sibling).wait_recv()

    @pl.when(owner == c)
    def _():
        for src, dst, send, recv in plans:
            remote(src, dst, send, recv, sibling).wait_send()


def sum_kernel(count, *refs):
    hid_in, gin_in = refs[:2]
    terms = refs[2 : 2 + count]
    hid_out, gin_out = refs[2 + count : 4 + count]
    outs = refs[4 + count :]
    hid_out[...] = hid_in[...].astype(jnp.float32)
    gin_out[...] = gin_in[...].astype(jnp.float32)
    for term, out in zip(terms, outs):
        total = term[0].astype(jnp.float32)
        for dz in range(1, 4):
            total = total + term[dz].astype(jnp.float32)
        out[...] = total


def token_places(deal_order, lengths):
    seq_ends = jnp.cumsum(lengths)
    starts = seq_ends - lengths
    inside = (deal_order[:, None] >= starts[None, :]).astype(jnp.int32)
    segment = jnp.sum(inside, axis=1) - 1
    picked = (segment[:, None] == jnp.arange(lengths.shape[0], dtype=jnp.int32)[None, :]).astype(
        jnp.int32
    )
    position = deal_order - jnp.sum(picked * starts[None, :], axis=1)
    return (segment, position)


def rms_scale(rows_in):
    return lax.rsqrt(jnp.mean(rows_in * rows_in, axis=1, keepdims=True) + EPSILON)


def gelu_slope(values):
    normal_cdf = 0.5 * (1.0 + jax.scipy.special.erf(values * (1.0 / math.sqrt(2.0))))
    normal_pdf = jnp.exp(-0.5 * values * values) * (1.0 / math.sqrt(2.0 * math.pi))
    return normal_cdf + values * normal_pdf


def norm_back_rows(rows_in, scale, gain, grad_normed):
    scaled_grad = grad_normed * gain
    grad_gain = jnp.sum(grad_normed * rows_in * scale, axis=0)
    grad_rows = scale * scaled_grad - rows_in * scale * scale * scale * jnp.mean(
        scaled_grad * rows_in, axis=1, keepdims=True
    )
    return (grad_rows, grad_gain)


def key_layout(key_all, value_all, segment, position, head_count):
    rows_all = key_all.shape[0]
    block_rows = 512
    blocks = rows_all // block_rows
    return (
        key_all.reshape(blocks, block_rows, head_count, -1),
        value_all.reshape(blocks, block_rows, head_count, -1),
        segment.reshape(blocks, block_rows),
        position.reshape(blocks, block_rows),
    )


def block_scores(
    queries,
    key_block,
    seg_query,
    pos_query,
    seg_block,
    pos_block,
    rel_bucket,
    bucket_edges,
    max_offset,
):
    lower_edge, upper_edge = bucket_edges
    raw_scores = jnp.einsum("qhd,khd->hqk", queries, key_block, preferred_element_type=jnp.float32)
    offset = jnp.clip(pos_block[None, :] - pos_query[:, None], -max_offset, max_offset)
    bucket_hit = (
        (offset[:, :, None] >= lower_edge[None, None, :])
        & (offset[:, :, None] <= upper_edge[None, None, :])
    ).astype(jnp.float32)
    bias = jnp.einsum(
        "qkb,bh->hqk",
        bucket_hit,
        rel_bucket,
        precision=lax.Precision.HIGHEST,
        preferred_element_type=jnp.float32,
    )
    same_seq = (seg_query[:, None] == seg_block[None, :])[None]
    return (raw_scores + bias, same_seq, bucket_hit)


def attend(queries, layout, seg_query, pos_query, rel_bucket, bucket_edges, max_offset):
    key_blocks, value_blocks, seg_blocks, pos_blocks = layout
    query_count, head_count, head_size = queries.shape

    def measure(carry, block):
        row_top, row_total = carry
        key_block, seg_block, pos_block = block
        scores, same_seq, _ = block_scores(
            queries,
            key_block,
            seg_query,
            pos_query,
            seg_block,
            pos_block,
            rel_bucket,
            bucket_edges,
            max_offset,
        )
        scores = jnp.where(same_seq, scores, NEG_FILL)
        new_top = jnp.maximum(row_top, jnp.max(scores, axis=2))
        weights_now = jnp.where(same_seq, jnp.exp(scores - new_top[:, :, None]), 0.0)
        row_total = row_total * jnp.exp(row_top - new_top) + jnp.sum(weights_now, axis=2)
        return ((new_top, row_total), None)

    start = (
        jnp.full((head_count, query_count), NEG_FILL, jnp.float32),
        jnp.zeros((head_count, query_count), jnp.float32),
    )
    (row_top, row_total), _ = lax.scan(measure, start, (key_blocks, seg_blocks, pos_blocks))
    log_total = row_top + jnp.log(row_total)

    def collect(summed, block):
        key_block, value_block, seg_block, pos_block = block
        scores, same_seq, _ = block_scores(
            queries,
            key_block,
            seg_query,
            pos_query,
            seg_block,
            pos_block,
            rel_bucket,
            bucket_edges,
            max_offset,
        )
        probs = jnp.where(same_seq, jnp.exp(scores - log_total[:, :, None]), 0.0).astype(
            jnp.bfloat16
        )
        return (
            summed
            + jnp.einsum("hqk,khd->qhd", probs, value_block, preferred_element_type=jnp.float32),
            None,
        )

    attended_f, _ = lax.scan(
        collect, jnp.zeros((query_count, head_count, head_size), jnp.float32), layout
    )
    return (attended_f, log_total)


def attend_back(
    queries,
    layout,
    seg_query,
    pos_query,
    rel_bucket,
    bucket_edges,
    max_offset,
    log_total,
    d_attended,
    row_delta,
):

    def step(carry, block):
        d_queries, d_buckets = carry
        key_block, value_block, seg_block, pos_block = block
        scores, same_seq, bucket_hit = block_scores(
            queries,
            key_block,
            seg_query,
            pos_query,
            seg_block,
            pos_block,
            rel_bucket,
            bucket_edges,
            max_offset,
        )
        probs_f = jnp.where(same_seq, jnp.exp(scores - log_total[:, :, None]), 0.0)
        d_probs = jnp.einsum(
            "qhd,khd->hqk", d_attended, value_block, preferred_element_type=jnp.float32
        )
        d_scores = (probs_f * (d_probs - row_delta[:, :, None])).astype(jnp.bfloat16)
        d_queries = d_queries + jnp.einsum(
            "hqk,khd->qhd", d_scores, key_block, preferred_element_type=jnp.float32
        )
        d_buckets = d_buckets + jnp.einsum(
            "hqk,qkb->bh",
            d_scores,
            bucket_hit.astype(jnp.bfloat16),
            preferred_element_type=jnp.float32,
        )
        d_values = jnp.einsum(
            "hqk,qhd->khd",
            probs_f.astype(jnp.bfloat16),
            d_attended,
            preferred_element_type=jnp.float32,
        )
        d_keys = jnp.einsum("hqk,qhd->khd", d_scores, queries, preferred_element_type=jnp.float32)
        return ((d_queries, d_buckets), (d_keys, d_values))

    start = (jnp.zeros(queries.shape, jnp.float32), jnp.zeros(rel_bucket.shape, jnp.float32))
    (d_queries, d_buckets), key_terms = lax.scan(step, start, layout)
    return (d_queries, key_terms, d_buckets)


def on_device(
    hidden_in,
    grad_out,
    gain_attn,
    gain_ffn,
    rel_bias,
    w_query,
    w_key,
    w_value,
    w_output,
    w_inner,
    w_outer,
    dealing,
    lengths,
    bucket_table,
):
    micro_count, tok_rows, model_width = hidden_in.shape
    group_size = lax.axis_size("fsdp")
    slot_rows = tok_rows // group_size
    own_index = lax.axis_index("fsdp")
    max_offset = (bucket_table.shape[0] - 1) // 2
    bucket_count = BUCKETS
    head_count = H
    offsets_all = jnp.arange(bucket_table.shape[0], dtype=jnp.int32) - max_offset
    matches = bucket_table[:, None] == jnp.arange(bucket_count, dtype=jnp.int32)[None, :]
    lower_edge = jnp.min(jnp.where(matches, offsets_all[:, None], 2 * max_offset + 2), axis=0)
    upper_edge = jnp.max(jnp.where(matches, offsets_all[:, None], -2 * max_offset - 2), axis=0)
    bucket_edges = (lower_edge, upper_edge)
    hidden_units = w_inner.shape[1]
    acc_gain_one = jnp.zeros((model_width,), jnp.float32)
    acc_gain_two = jnp.zeros((model_width,), jnp.float32)
    acc_buckets = jnp.zeros((bucket_count, head_count), jnp.float32)
    acc_query = jnp.zeros((model_width, model_width), jnp.float32)
    acc_key = jnp.zeros((model_width, model_width), jnp.float32)
    acc_value = jnp.zeros((model_width, model_width), jnp.float32)
    acc_output = jnp.zeros((model_width, model_width), jnp.float32)
    acc_inner = jnp.zeros((model_width, hidden_units), jnp.float32)
    acc_outer = jnp.zeros((hidden_units, model_width), jnp.float32)
    outputs_list = []
    grads_list = []
    for micro_idx in range(micro_count):
        weights_now = (
            lax.all_gather(gain_attn, ("dp", "fsdp"), axis=0, tiled=True),
            lax.all_gather(gain_ffn, ("dp", "fsdp"), axis=0, tiled=True),
            lax.all_gather(rel_bias, ("dp", "fsdp"), axis=0, tiled=True),
            lax.all_gather(w_query, ("dp", "fsdp"), axis=0, tiled=True),
            lax.all_gather(w_key, ("dp", "fsdp"), axis=0, tiled=True),
            lax.all_gather(w_value, ("dp", "fsdp"), axis=0, tiled=True),
            lax.all_gather(w_output, ("dp", "fsdp"), axis=0, tiled=True),
            lax.all_gather(w_inner, ("dp", "fsdp"), axis=0, tiled=True),
            lax.all_gather(w_outer, ("dp", "fsdp"), axis=0, tiled=True),
        )
        gain_one = weights_now[0].astype(jnp.float32)
        gain_two = weights_now[1].astype(jnp.float32)
        rel_bucket = weights_now[2].astype(jnp.float32).reshape(bucket_count, head_count)
        query_weight, key_weight, value_weight, output_weight, inner_weight, outer_weight = (
            weights_now[3:]
        )
        deal_order = dealing[micro_idx, 0]
        segment, position = token_places(deal_order, lengths[micro_idx, 0])
        seg_query = lax.dynamic_slice_in_dim(segment, own_index * tok_rows, tok_rows)
        pos_query = lax.dynamic_slice_in_dim(position, own_index * tok_rows, tok_rows)
        take_rows = (
            lax.dynamic_slice_in_dim(
                deal_order.reshape(group_size, tok_rows), own_index * slot_rows, slot_rows, 1
            )
            - own_index * tok_rows
        ).reshape(tok_rows)
        dealt = lax.all_to_all(
            jnp.take(hidden_in[micro_idx], take_rows, axis=0),
            "fsdp",
            split_axis=0,
            concat_axis=0,
            tiled=True,
        )
        dealt_rows = dealt.astype(jnp.float32)
        scale_one = rms_scale(dealt_rows)
        normed1 = (dealt_rows * scale_one * gain_one).astype(jnp.bfloat16)
        queries = jnp.dot(normed1, query_weight, preferred_element_type=jnp.float32).astype(
            jnp.bfloat16
        )
        key_rows = jnp.dot(normed1, key_weight, preferred_element_type=jnp.float32).astype(
            jnp.bfloat16
        )
        value_rows = jnp.dot(normed1, value_weight, preferred_element_type=jnp.float32).astype(
            jnp.bfloat16
        )
        key_all, value_all = (
            lax.all_gather(key_rows, "fsdp", axis=0, tiled=True),
            lax.all_gather(value_rows, "fsdp", axis=0, tiled=True),
        )
        layout = key_layout(key_all, value_all, segment, position, head_count)
        queries_heads = queries.reshape(tok_rows, head_count, -1)
        attended_f, log_total = attend(
            queries_heads, layout, seg_query, pos_query, rel_bucket, bucket_edges, max_offset
        )
        attended = attended_f.reshape(tok_rows, model_width).astype(jnp.bfloat16)
        mid = dealt_rows + jnp.dot(attended, output_weight, preferred_element_type=jnp.float32)
        scale_two = rms_scale(mid)
        normed2 = (mid * scale_two * gain_two).astype(jnp.bfloat16)
        inner_act = jnp.dot(normed2, inner_weight, preferred_element_type=jnp.float32)
        active = jax.nn.gelu(inner_act, approximate=False).astype(jnp.bfloat16)
        result = mid + jnp.dot(active, outer_weight, preferred_element_type=jnp.float32)
        outputs_list.append(result)
        weights_back = (
            lax.all_gather(gain_attn, ("dp", "fsdp"), axis=0, tiled=True),
            lax.all_gather(gain_ffn, ("dp", "fsdp"), axis=0, tiled=True),
            lax.all_gather(rel_bias, ("dp", "fsdp"), axis=0, tiled=True),
            lax.all_gather(w_query, ("dp", "fsdp"), axis=0, tiled=True),
            lax.all_gather(w_key, ("dp", "fsdp"), axis=0, tiled=True),
            lax.all_gather(w_value, ("dp", "fsdp"), axis=0, tiled=True),
            lax.all_gather(w_output, ("dp", "fsdp"), axis=0, tiled=True),
            lax.all_gather(w_inner, ("dp", "fsdp"), axis=0, tiled=True),
            lax.all_gather(w_outer, ("dp", "fsdp"), axis=0, tiled=True),
        )
        query_weight, key_weight, value_weight, output_weight, inner_weight, outer_weight = (
            weights_back[3:]
        )
        grad_top = grad_out[micro_idx]
        acc_outer = acc_outer + jnp.einsum(
            "tf,td->fd", active, grad_top, preferred_element_type=jnp.float32
        )
        d_active = jnp.einsum(
            "td,fd->tf", grad_top, outer_weight, preferred_element_type=jnp.float32
        )
        d_inner = (d_active * gelu_slope(inner_act)).astype(jnp.bfloat16)
        acc_inner = acc_inner + jnp.einsum(
            "td,tf->df", normed2, d_inner, preferred_element_type=jnp.float32
        )
        d_normed2 = jnp.einsum(
            "tf,df->td", d_inner, inner_weight, preferred_element_type=jnp.float32
        )
        d_mid_norm, d_gain_two = norm_back_rows(mid, scale_two, gain_two, d_normed2)
        acc_gain_two = acc_gain_two + d_gain_two
        d_mid = grad_top.astype(jnp.float32) + d_mid_norm
        d_branch = d_mid.astype(jnp.bfloat16)
        acc_output = acc_output + jnp.einsum(
            "td,te->de", attended, d_branch, preferred_element_type=jnp.float32
        )
        d_attended = jnp.einsum(
            "te,de->td", d_branch, output_weight, preferred_element_type=jnp.float32
        ).astype(jnp.bfloat16)
        d_attended_heads = d_attended.reshape(tok_rows, head_count, -1)
        row_delta = jnp.sum(d_attended_heads.astype(jnp.float32) * attended_f, axis=2).T
        key_back, value_back = (
            lax.all_gather(key_rows, "fsdp", axis=0, tiled=True),
            lax.all_gather(value_rows, "fsdp", axis=0, tiled=True),
        )
        layout_back = key_layout(key_back, value_back, segment, position, head_count)
        d_queries, key_terms, d_buckets = attend_back(
            queries_heads,
            layout_back,
            seg_query,
            pos_query,
            rel_bucket,
            bucket_edges,
            max_offset,
            log_total,
            d_attended_heads,
            row_delta,
        )
        d_keys, d_values = key_terms
        group_rows = d_keys.shape[0] * d_keys.shape[1]
        d_keys_own, d_values_own = (
            lax.psum_scatter(
                d_keys.reshape(group_rows, model_width).astype(jnp.bfloat16),
                "fsdp",
                scatter_dimension=0,
                tiled=True,
            ).astype(jnp.float32),
            lax.psum_scatter(
                d_values.reshape(group_rows, model_width).astype(jnp.bfloat16),
                "fsdp",
                scatter_dimension=0,
                tiled=True,
            ).astype(jnp.float32),
        )
        acc_buckets = acc_buckets + d_buckets
        d_queries_low = d_queries.reshape(tok_rows, model_width).astype(jnp.bfloat16)
        d_keys_low = d_keys_own.astype(jnp.bfloat16)
        d_values_low = d_values_own.astype(jnp.bfloat16)
        acc_query = acc_query + jnp.einsum(
            "td,te->de", normed1, d_queries_low, preferred_element_type=jnp.float32
        )
        acc_key = acc_key + jnp.einsum(
            "td,te->de", normed1, d_keys_low, preferred_element_type=jnp.float32
        )
        acc_value = acc_value + jnp.einsum(
            "td,te->de", normed1, d_values_low, preferred_element_type=jnp.float32
        )
        d_normed1 = (
            jnp.einsum("te,de->td", d_queries_low, query_weight, preferred_element_type=jnp.float32)
            + jnp.einsum("te,de->td", d_keys_low, key_weight, preferred_element_type=jnp.float32)
            + jnp.einsum(
                "te,de->td", d_values_low, value_weight, preferred_element_type=jnp.float32
            )
        )
        d_rows_norm, d_gain_one = norm_back_rows(dealt_rows, scale_one, gain_one, d_normed1)
        acc_gain_one = acc_gain_one + d_gain_one
        d_dealt = d_mid + d_rows_norm
        returned = lax.all_to_all(
            d_dealt.astype(jnp.bfloat16), "fsdp", split_axis=0, concat_axis=0, tiled=True
        ).astype(d_dealt.dtype)
        grads_list.append(jnp.zeros_like(returned).at[take_rows].set(returned))
    acc_rel = acc_buckets.reshape(-1)
    summed = (
        lax.psum_scatter(acc_gain_one, ("dp", "fsdp"), scatter_dimension=0, tiled=True),
        lax.psum_scatter(acc_gain_two, ("dp", "fsdp"), scatter_dimension=0, tiled=True),
        lax.psum_scatter(acc_rel, ("dp", "fsdp"), scatter_dimension=0, tiled=True),
        lax.psum_scatter(acc_query, ("dp", "fsdp"), scatter_dimension=0, tiled=True),
        lax.psum_scatter(acc_key, ("dp", "fsdp"), scatter_dimension=0, tiled=True),
        lax.psum_scatter(acc_value, ("dp", "fsdp"), scatter_dimension=0, tiled=True),
        lax.psum_scatter(acc_output, ("dp", "fsdp"), scatter_dimension=0, tiled=True),
        lax.psum_scatter(acc_inner, ("dp", "fsdp"), scatter_dimension=0, tiled=True),
        lax.psum_scatter(acc_outer, ("dp", "fsdp"), scatter_dimension=0, tiled=True),
    )
    return (
        jnp.stack(outputs_list),
        jnp.stack(grads_list),
        summed[0],
        summed[1],
        summed[2],
        summed[3],
        summed[4],
        summed[5],
        summed[6],
        summed[7],
        summed[8],
    )


VMEM = pl.BlockSpec(memory_space=pltpu.VMEM)
SMEM = pl.BlockSpec(memory_space=pltpu.SMEM)
ANYWHERE = pl.BlockSpec(memory_space=pl.ANY)
LIMIT = 56 * 1024 * 1024
FIRST_AXIS = ("x", "x", "y", "x")
FWD_OWN = (0, 2, 8, 16, 24)
FWD_NEAR = (9, 12, 18, 26, 34)
FWD_SIDE = (20, 24, 30, 38, 44)
FWD_GRADS = 14
BWD_DEAL = 2
BWD_CORE = (3, 6, 9, 12, 15)
BWD_SIDE = (8, 13, 18, 23, 28)
BWD_NEAR = (13, 19, 24, 29, 34)


def shaped(*shape, dtype=jnp.bfloat16):
    return jax.ShapeDtypeStruct(shape, dtype)


def params(collective_id=None):
    if collective_id is None:
        return pltpu.CompilerParams(vmem_limit_bytes=LIMIT)
    return pltpu.CompilerParams(
        collective_id=collective_id, has_side_effects=True, vmem_limit_bytes=LIMIT
    )


def dma(*shape):
    return pltpu.SemaphoreType.DMA(shape)


def gather_all(lens, deal, hid, shards):
    count = len(shards)
    return pl.pallas_call(
        functools.partial(gather_kernel, FIRST_AXIS),
        name="gather_all",
        out_shape=[
            shaped(*lens.shape[1:], dtype=jnp.int32),
            shaped(*deal.shape[1:], dtype=jnp.int32),
            shaped(OWN, TILE, hid.shape[-1]),
        ]
        + [shaped(32, *s.shape) for s in shards],
        in_specs=[ANYWHERE] * (3 + count),
        out_specs=[ANYWHERE] * (3 + count),
        scratch_shapes=[
            dma(count, 10), dma(count, 10), dma(count), dma(2, 3), dma(OWN), dma(2), dma(2),
        ],
        compiler_params=params(0),
    )(lens, deal, hid, *shards)


def attention_forward(lens, x, gain, wq, wk, wv, rows, grd, wo, wi, wu):
    heads, keys = (PAIRS, OWN, TILE, 128), (PAIRS, OWN, 2, TILE, 128)
    count = len(FWD_OWN)
    return pl.pallas_call(
        attn_fwd,
        name="attn_fwd",
        out_shape=[
            shaped(*heads), shaped(*keys), shaped(*keys), shaped(*heads, dtype=jnp.float32),
            shaped(OWN, 2 * PAIRS, 1, TILE, dtype=jnp.float32),
            shaped(8, *grd.shape[2:]),
        ]
        + [shaped(32, *w.shape) for w in (wo, wi, wu)],
        in_specs=[SMEM] + [VMEM] * 6 + [ANYWHERE] * 4,
        out_specs=[VMEM] * 5 + [ANYWHERE] * 4,
        scratch_shapes=[
            pltpu.VMEM((2 * PAIRS, 5, TILE, TILE), jnp.float32),
            pltpu.VMEM((OWN, TILE, 128), jnp.bfloat16),
            pltpu.VMEM((TILES, TILE, 128), jnp.bfloat16),
            pltpu.VMEM((2, TILE, TILES * TILE), jnp.float32),
            pltpu.VMEM((OWN, TILE, 128), jnp.float32),
            dma(2), dma(2),
            dma(count, 10), dma(count, 10), dma(count), dma(2, 2, 2), dma(2, 4),
        ],
        compiler_params=params(1),
    )(lens, x, gain, wq, wk, wv, rows, grd, wo, wi, wu)


def landing(shapes):
    found = []
    for b in shapes:
        found += [
            pltpu.VMEM((4, 4, *b), jnp.bfloat16), pltpu.VMEM((2, 4, *b), jnp.bfloat16), pltpu.VMEM((4, *b), jnp.bfloat16)
        ]
    return found


def attention_backward(lens, q, k, v, log_total, d_att, delta, rows, deal, res, gwo, gwi, gwu):
    heads = (PAIRS, OWN, TILE, 128)
    width = res.shape[-1]
    half_u, half_i = (gwu.shape[1] // 2, width), (gwi.shape[1], gwi.shape[2] // 2)
    blocks = [half_u, half_i, half_u, half_i, gwo.shape[1:]]
    count = len(blocks)
    return pl.pallas_call(
        attn_bwd,
        name="attn_bwd",
        out_shape=[shaped(*heads)] * 3
        + [shaped(5, 2 * PAIRS, 1, 2 * TILE, dtype=jnp.float32), shaped(2, 3 * TILE, width)]
        + [shaped(4, *g.shape[1:]) for g in (gwo, gwi, gwu)],
        in_specs=[SMEM] + [VMEM] * 12,
        out_specs=[VMEM] * 4 + [ANYWHERE] * 4,
        scratch_shapes=[pltpu.VMEM((2 * PAIRS, 5, TILE, TILE), jnp.float32)] * 2
        + [pltpu.VMEM((OWN, TILE, 128), jnp.bfloat16), pltpu.VMEM((TILES, TILE, 128), jnp.bfloat16)]
        + [pltpu.VMEM((TILES * TILE, 128), jnp.float32)] * 2
        + [pltpu.VMEM(heads, jnp.bfloat16)] * 4
        + [dma(2, PAIRS), dma(2, PAIRS)]
        + [pltpu.VMEM((OWN, 2, TILE, width), jnp.bfloat16), pltpu.VMEM((2, 3 * TILE, width), jnp.bfloat16)]
        + landing(blocks)
        + [
            dma(count, 10), dma(count, 10), dma(count), dma(2), dma(2),
            pltpu.SemaphoreType.DMA, pltpu.SemaphoreType.DMA,
        ],
        compiler_params=params(2),
    )(lens, q, k, v, log_total, d_att, delta, rows, deal, res, gwo, gwi, gwu)


def feed_forward(deal, x, o, g, wo, gain, wi, wu):
    tok, width, hidden = x.shape[0], x.shape[1], wi.shape[1]
    chunk = 512
    f32 = jnp.float32

    def full(*shape):
        return pl.BlockSpec(shape, lambda j: (0,) * len(shape))

    columns = pl.BlockSpec((width, chunk), lambda j: (0, j))
    lines = pl.BlockSpec((chunk, width), lambda j: (j, 0))
    heads, stats = (PAIRS, OWN, TILE, 128), (OWN, 2 * PAIRS, 1, TILE)
    return pl.pallas_call(
        ffn_kernel,
        name="feed_forward",
        grid=(hidden // chunk,),
        out_shape=[
            shaped(tok, width), shaped(tok, width, dtype=f32), shaped(*heads), shaped(*stats, dtype=f32),
            shaped(width, width), shaped(width, hidden), shaped(hidden, width), shaped(32, 128, dtype=f32),
        ],
        in_specs=[
            full(*deal.shape), full(tok, width), full(*heads), full(2 * tok, width), full(width, width),
            full(8, width), columns, lines,
        ],
        out_specs=[
            full(tok, width), full(tok, width), full(*heads), full(*stats), full(width, width),
            columns, lines, full(32, 128),
        ],
        scratch_shapes=[
            pltpu.VMEM((tok, width), jnp.bfloat16), pltpu.VMEM((tok, width), jnp.bfloat16),
            pltpu.VMEM((tok, width), f32), pltpu.VMEM((tok, width), jnp.bfloat16),
            pltpu.VMEM((tok, width), f32), pltpu.VMEM((tok, width), f32),
        ],
        compiler_params=params(),
    )(deal, x, o, g, wo, gain, wi, wu)


def tail(x, gain, d_mid, dq, dk, dv, wq, wk, wv, g_two, g_rel):
    tok, width = x.shape
    block = (width // 32, width)
    blocks = [block, block, block, (16, 128)]
    count = len(blocks)
    return pl.pallas_call(
        tail_kernel,
        name="tail",
        out_shape=[shaped(2, 3, TILE, width), shaped(4, 16, 128)] + [shaped(4, *block)] * 3,
        in_specs=[VMEM] * 11,
        out_specs=[ANYWHERE] * 5,
        scratch_shapes=[
            pltpu.VMEM((3, tok, width), jnp.bfloat16), pltpu.VMEM((OWN, TILE, width), jnp.bfloat16),
            pltpu.VMEM((32, 16, 128), jnp.bfloat16),
        ]
        + [pltpu.VMEM((32, *block), jnp.bfloat16)] * 3
        + landing(blocks)
        + [dma(count, 10), dma(count, 10), dma(count), dma(OWN), dma(2, 3)],
        compiler_params=params(3),
    )(x, gain, d_mid, dq, dk, dv, wq, wk, wv, g_two, g_rel)


def last_sums(hid, gin, terms):
    f32 = jnp.float32
    return pl.pallas_call(
        functools.partial(sum_kernel, len(terms)),
        name="last_sums",
        out_shape=[shaped(*hid.shape, dtype=f32), shaped(*gin.shape, dtype=f32)]
        + [shaped(*t.shape[1:], dtype=f32) for t in terms],
        in_specs=[VMEM] * (2 + len(terms)),
        out_specs=[VMEM] * (2 + len(terms)),
        compiler_params=params(),
    )(hid, gin, *terms)


def bias_rows(rel, turned=False):
    first, last = rel[:, :1], rel[:, 256:]
    low, high = rel[:, :128], rel[:, 128:256]
    spread = lambda one: jnp.broadcast_to(one, low.shape)
    rows = [
        jnp.concatenate(pair, axis=1)
        for pair in (
            (low, spread(first)), (high, low), (spread(last), high),
            (spread(first), spread(first)), (spread(last), spread(last)),
        )
    ]
    if turned:
        rows = [rows[2], rows[1], rows[0], rows[4], rows[3]]
    return jnp.stack(rows)[:, :, None, :]


def on_device_packed(
    hidden_in, grad_out, gain_attn, gain_ffn, rel_bias,
    w_query, w_key, w_value, w_output, w_inner, w_outer,
    dealing, lengths, bucket_table,
):
    micro_count, tok_rows, width = hidden_in.shape
    f32 = jnp.float32
    line = lambda v: jnp.pad(v, (0, 128 - v.shape[0]))[None]
    small = jnp.concatenate(
        [line(gain_attn), line(gain_ffn), line(rel_bias), jnp.zeros((13, 128), jnp.bfloat16)], axis=0
    )
    lens = jnp.pad(lengths, ((0, 0), (0, 0), (0, 128 - lengths.shape[2])))
    gathered = gather_all(
        lens, dealing, hidden_in.reshape(2, 3, TILE, width), (small, w_query, w_key, w_value)
    )
    lens_u, deal_u, x_own, small_all = gathered[:4]
    matrix = lambda w: w.reshape(-1, w.shape[-1])
    wq, wk, wv = map(matrix, gathered[4:])
    gains = [
        jnp.broadcast_to(small_all[:, n, :24].reshape(1, width).astype(f32), (8, width)) for n in range(2)
    ]
    picked = (bucket_table[None, :] == jnp.arange(BUCKETS, dtype=jnp.int32)[:, None]).astype(f32)
    rel = lax.dot_general(
        small_all[:, 2, :H].astype(f32), picked, (((0,), (0,)), ((), ())),
        precision=lax.Precision.HIGHEST, preferred_element_type=f32,
    )
    x_rows = x_own.reshape(-1, width)
    q, k, v, o, log_total, g_all, wo, wi, wu = attention_forward(
        lens_u, x_rows, gains[0], wq, wk, wv, bias_rows(rel),
        grad_out.reshape(2, 2, tok_rows // 2, width), w_output, w_inner, w_outer,
    )
    result, d_mid, d_att, delta, g_wo, g_wi, g_wu, g_two = feed_forward(
        deal_u, x_rows, o, matrix(g_all), matrix(wo), gains[1], matrix(wi), matrix(wu)
    )
    split = lambda g: g.reshape(32, -1, g.shape[-1])
    dq, dk, dv, hist, hid, t_wo, t_wi, t_wu = attention_backward(
        lens_u, q, k, v, log_total, d_att, delta, bias_rows(rel[:, ::-1], True),
        deal_u.reshape(2, 1, -1), result.reshape(OWN, TILE, width), split(g_wo), split(g_wi), split(g_wu),
    )

    hist = hist[:, :, 0, :]
    turned = hist[:3, :, ::-1]
    by_distance = jnp.concatenate([turned[1], jnp.zeros((H, 1), f32)], axis=1)
    by_distance = by_distance.at[:, 128:256].add(turned[2][:, :128])
    by_distance = by_distance.at[:, 256].add(jnp.sum(turned[2][:, 128:], axis=1) + jnp.sum(hist[4], axis=1))
    by_distance = by_distance.at[:, :128].add(turned[0][:, 128:])
    by_distance = by_distance.at[:, 0].add(jnp.sum(turned[0][:, :128], axis=1) + jnp.sum(hist[3], axis=1))
    g_rel = lax.dot_general(
        picked, by_distance, (((1,), (1,)), ((), ())), precision=lax.Precision.HIGHEST, preferred_element_type=f32
    )
    gin, t_small, t_wq, t_wk, t_wv = tail(
        x_rows, gains[0], d_mid, dq, dk, dv, wq, wk, wv, g_two, jnp.pad(g_rel, ((0, 0), (0, 128 - H)))
    )
    hid, gin, s_small, *grads = last_sums(hid, gin, (t_small, t_wq, t_wk, t_wv, t_wo, t_wi, t_wu))
    return (
        hid, gin.reshape(2, tok_rows, width), s_small[0, :24], s_small[1, :24], s_small[2, :H], *grads
    )


def solution(mesh):
    axes = ("dp", "fsdp")
    tokens, matrix, vector = P(None, axes, None), P(axes, None), P(axes)
    packed = mesh.shape["fsdp"] == 4 and mesh.shape["dp"] == 8
    return jax.shard_map(
        on_device_packed if packed else on_device,
        mesh=mesh,
        in_specs=(tokens, tokens, vector, vector, vector)
        + (matrix,) * 6
        + (P(None, "dp", None), P(None, "dp", None), P()),
        out_specs=(tokens, tokens, vector, vector, vector) + (matrix,) * 6,
        check_vma=False,
    )
```

```python
import functools
import math

import jax
import jax.numpy as jnp
from jax import lax
from jax.experimental import pallas as pl
from jax.experimental.pallas import tpu as pltpu
from jax.sharding import PartitionSpec as P

H = 12
BUCKETS = 32
EPSILON = 1e-06
NEG_FILL = -1e30
MESH = pl.DeviceIdType.MESH
TILE = 128
PAIRS = 6
OWN = 6
TILES = 12
FAR = 6
SEQS = 4


def lane_index(shape):
    return lax.broadcasted_iota(jnp.int32, shape, len(shape) - 1)


def row_index(shape):
    return lax.broadcasted_iota(jnp.int32, shape, len(shape) - 2)


def dot_nn(left, right):
    return lax.dot_general(left, right, (((1,), (0,)), ((), ())), preferred_element_type=jnp.float32)


def dot_nt(left, right):
    return lax.dot_general(left, right, (((1,), (1,)), ((), ())), preferred_element_type=jnp.float32)


def dot_tn(left, right):
    return lax.dot_general(left, right, (((0,), (0,)), ((), ())), preferred_element_type=jnp.float32)


def segments_of(places, lens_ref, count):
    edge = jnp.int32(0)
    found = jnp.zeros(places.shape, jnp.int32)
    for s in range(count - 1):
        edge = edge + lens_ref[0, s]
        found = found + (places >= edge).astype(jnp.int32)
    return found


def segment_tags(places, lens_ref, count, of_key):
    lane = lane_index(places.shape)
    hit = segments_of(places, lens_ref, count) == lane
    if of_key:
        return jnp.where((lane < count) & jnp.logical_not(hit), NEG_FILL, 0.0).astype(jnp.bfloat16)
    return jnp.where(hit, 1.0, 0.0).astype(jnp.bfloat16)


def one_hot(rows, columns):
    return jnp.where(rows == columns, 1.0, 0.0).astype(jnp.bfloat16)


def small_lines(small_ref, kind):
    flat = small_ref[...].reshape(32 * 16, 128)
    pick = one_hot(16 * row_index((32, 512)) + kind, lane_index((32, 512)))
    return dot_nn(pick, flat).astype(jnp.bfloat16)


def gain_row(small_ref, kind, width):
    lines = dot_nn(
        small_lines(small_ref, kind), one_hot(row_index((128, width)), lax.rem(lane_index((128, width)), 24))
    )
    own = lane_index((32, width)) // 24 == row_index((32, width))
    return jnp.sum(jnp.where(own, lines, 0.0), axis=0, keepdims=True)


def bucket_picks(table_ref, places):
    span = table_ref.shape[1]
    picked = one_hot(row_index((BUCKETS, span)), jnp.broadcast_to(table_ref[...], (BUCKETS, span)))
    places = jnp.clip(places, 0, span - 1)
    return dot_nn(picked, one_hot(row_index((span, 256)), jnp.broadcast_to(places, (span, 256)))).astype(jnp.bfloat16)


def class_places(cls, sign):
    lane = lane_index((1, 256))
    if cls >= 3:
        return jnp.full((1, 256), 0 if cls == 3 else 2 * TILE, jnp.int32)
    turn = jnp.where(lane < TILE, lane, lane - 2 * TILE)
    return TILE * (cls - 1) + sign * turn + TILE


def fill_rows(small_ref, table_ref, rows_ref, sign):
    rel = small_lines(small_ref, 2)
    for cls in range(5):
        made = dot_tn(rel, bucket_picks(table_ref, class_places(cls, sign)))
        for h in range(2 * PAIRS):
            rows_ref[cls, h] = made[h : h + 1, :]


def bucket_sums(hist_ref, table_ref):
    total = None
    for cls in range(5):
        if cls >= 3:
            places = class_places(cls, 1)
        else:
            places = TILE * (cls - 1) + 2 * TILE - 1 - lane_index((1, 256))
        hist = jnp.concatenate([hist_ref[cls, h] for h in range(2 * PAIRS)] + [jnp.zeros((4, 256), jnp.float32)], axis=0)
        term = lax.dot_general(
            bucket_picks(table_ref, places).astype(jnp.float32), hist, (((1,), (1,)), ((), ())),
            precision=lax.Precision.HIGHEST, preferred_element_type=jnp.float32,
        )
        total = term if total is None else total + term
    return total


def key_range(i):
    return max(0, 2 * i - FAR), min(TILES, 2 * i + FAR + 2)


def fill_bias(rows_ref, tiles_ref, heads):
    def one_head(h, carry):
        for cls in range(3):
            row = rows_ref[cls, h]
            wide = pltpu.roll(
                jnp.broadcast_to(row, (TILE, 2 * TILE)), 0, 1, stride=1, stride_axis=0
            )
            tiles_ref[h, cls + 1] = wide[:, :TILE]
        left = rows_ref[3, h, :, :TILE]
        right = rows_ref[4, h, :, :TILE]
        tiles_ref[h, 0] = jnp.broadcast_to(left, (TILE, TILE))
        tiles_ref[h, 4] = jnp.broadcast_to(right, (TILE, TILE))
        return carry

    lax.fori_loop(0, heads, one_head, 0)


def bias_class(kt, i, core):
    return jnp.clip(kt - 2 * i - core, -2, 2) + 2


def make_tags(lens_ref, ext_q, ext_k):
    core = lax.rem(lax.axis_index("dp"), 2)
    for t in range(TILES):
        ext_k[t] = segment_tags(TILE * t + row_index((TILE, 128)), lens_ref, SEQS, True)
    for i in range(OWN):
        ext_q[i] = segment_tags(TILE * (2 * i + core) + row_index((TILE, 128)), lens_ref, SEQS, False)


def attn_fwd(
    lens_ref, x_ref, small_ref, table_ref, wq_ref, wk_ref, wv_ref, grd_in, wo_in, wi_in, wu_in,
    q_ref, k_ref, v_ref, att_ref, log_ref, g_low, wo_all, wi_all, wu_all,
    rows_ref, bias_ref, ext_q, ext_k, s_ref, log_acc, send_sem, recv_sem,
    w_send, w_recv, w_local, g_send, g_recv,
):
    y, x, core, z = coordinates()
    sibling = place(y, x, 1 - core, z)
    greet()
    pieces = [(wo_in, wo_all, None, "x")]
    part_i, part_u = wi_in.shape[1] // FWD_PARTS, wu_in.shape[1] // FWD_PARTS
    for n in range(FWD_PARTS):
        pieces.append((wi_in, wi_all, (n * part_i, part_i), "xy"[(n + 1) % 2]))
        pieces.append((wu_in, wu_all, (n * part_u, part_u), "xy"[n % 2]))
    gather = Gather(pieces, w_send, w_recv, w_local)
    grads = list(grad_sends(grd_in, g_low, 0, g_send, g_recv))
    events = {}

    def plan(at, step, *args):
        events.setdefault(at, []).append(functools.partial(step, *args))

    for n in range(len(pieces)):
        plan(FWD_OWN[n], gather.spread_own, n)
        if n + FWD_AHEAD < len(pieces):
            plan(FWD_OWN[n], gather.start, n + FWD_AHEAD)
        plan(FWD_NEAR[n], gather.spread_near, n)
        plan(FWD_SIDE[n], gather.spread_side, n)
    plan(FWD_GRADS, start_all, grads)

    greeted()
    for n in range(FWD_AHEAD):
        gather.start(n)
    rows = x_ref[...].astype(jnp.float32)
    scale = lax.rsqrt(jnp.mean(rows * rows, axis=1, keepdims=True) + EPSILON)
    normed = (rows * scale * gain_row(small_ref, 0, rows.shape[1])).astype(jnp.bfloat16)

    def project(w_ref):
        return dot_nn(normed, w_ref[...]).astype(jnp.bfloat16)

    copies = []
    for n, (w_ref, all_ref) in enumerate(((wk_ref, k_ref), (wv_ref, v_ref))):
        made = project(w_ref)
        for hp in range(PAIRS):
            for i in range(OWN):
                all_ref[hp, i, core] = made[TILE * i : TILE * (i + 1), 128 * hp : 128 * (hp + 1)]
        copy = remote(all_ref.at[:, :, core], all_ref.at[:, :, core], send_sem.at[n], recv_sem.at[n], sibling)
        copy.start()
        copies.append(copy)
    made = project(wq_ref)
    for hp in range(PAIRS):
        for i in range(OWN):
            q_ref[hp, i] = made[TILE * i : TILE * (i + 1), 128 * hp : 128 * (hp + 1)]
    make_tags(lens_ref, ext_q, ext_k)
    for i in range(OWN):
        log_acc[i] = jnp.zeros((TILE, 128), jnp.float32)
    for step in events.pop(-1, ()):
        step()
    fill_rows(small_ref, table_ref, rows_ref, 1)
    fill_bias(rows_ref, bias_ref, 2 * PAIRS)
    for n, all_ref in enumerate((k_ref, v_ref)):
        block = all_ref.at[:, :, 1 - core]
        remote(block, block, send_sem.at[n], recv_sem.at[n], sibling).wait_recv()

    lane = lane_index((TILE, 128))

    def one_pair(hp, carry):
        for i in range(OWN):
            run_events(events, hp, i)
            lo, hi = key_range(i)
            width = (hi - lo) * TILE
            pair = q_ref[hp, i]
            tags = ext_q[i]
            zero = jnp.zeros_like(pair)
            left = jnp.concatenate(
                [
                    jnp.concatenate([jnp.where(lane < 64, pair, zero), tags], axis=1),
                    jnp.concatenate([jnp.where(lane < 64, zero, pair), tags], axis=1),
                ],
                axis=0,
            )
            keys = k_ref[hp, lo // 2 : hi // 2].reshape(width, 128)
            right = jnp.concatenate([keys, ext_k[lo:hi].reshape(width, 128)], axis=1)
            raw = dot_nt(left, right)
            tops = []
            for e in range(2):
                top = None
                for kt in range(lo, hi):
                    at = (kt - lo) * TILE
                    part = raw[e * TILE : (e + 1) * TILE, at : at + TILE]
                    if -1 <= kt - 2 * i <= 2:
                        part = part + bias_ref[2 * hp + e, bias_class(kt, i, core)]
                    else:
                        part = part + rows_ref[3 if kt < 2 * i else 4, 2 * hp + e, :, :TILE]
                    s_ref[e, :, at : at + TILE] = part
                    top = part if top is None else jnp.maximum(top, part)
                tops.append(jnp.max(top, axis=1, keepdims=True))
            outs = []
            for e in range(2):
                total = None
                found = []
                for kt in range(lo, hi):
                    at = (kt - lo) * TILE
                    weight = jnp.exp(s_ref[e, :, at : at + TILE] - tops[e])
                    total = weight if total is None else total + weight
                    found.append(weight.astype(jnp.bfloat16))
                total = jnp.sum(total, axis=1, keepdims=True)
                probs = jnp.concatenate(found, axis=1)
                values = v_ref[hp, lo // 2 : hi // 2].reshape(width, 128)
                outs.append(dot_nn(probs, values) / total)
                log_acc[i] = jnp.where(lane == 2 * hp + e, tops[e] + jnp.log(total), log_acc[i])
            att_ref[TILE * i : TILE * (i + 1), pl.ds(pl.multiple_of(128 * hp, 128), 128)] = jnp.where(
                lane < 64, outs[0], outs[1]
            ).astype(jnp.bfloat16)
        return carry

    lax.fori_loop(0, PAIRS, one_pair, 0)
    for i in range(OWN):
        turned = log_acc[i].T
        for h in range(2 * PAIRS):
            log_ref[i, h] = turned[h : h + 1, :]
    late(events)
    share_grads(g_low, g_send, g_recv)
    for n in range(len(pieces)):
        gather.finish(n)
    end_grads(grads, g_low, g_send, g_recv)
    for copy in copies:
        copy.wait_send()


def attn_bwd(
    lens_ref, q_ref, k_ref, v_ref, log_ref, do_ref, delta_ref, small_ref, table_ref, gwo, gwi, gwu,
    dq_ref, dk_ref, dv_ref, rel_ref, two, twi, twu,
    rows_ref, hist_ref, bias_ref, acc_ref, ext_q, ext_k, dk_acc, dv_acc, out_k, out_v, got_k, got_v, send_sem, recv_sem,
    w_send, w_recv, w_local, *landed,
):
    y, x, core, z = coordinates()
    sibling = place(y, x, 1 - core, z)
    greet()
    plain = []
    part_i, part_u = gwi.shape[3] // BWD_PARTS, gwu.shape[3] // BWD_PARTS
    for n in range(BWD_PARTS):
        plain.append((gwi, twi, (n * part_i, part_i), "xy"[n % 2]))
        plain.append((gwu, twu, (n * part_u, part_u), "xy"[(n + 1) % 2]))
    plain.append((gwo, two, None, "x"))
    count = len(plain)
    scatter = LateScatter(
        [item + tuple(landed[3 * n : 3 * n + 3]) for n, item in enumerate(plain)], w_send, w_recv, w_local
    )
    events = {}

    def plan(at, step, *args):
        events.setdefault(at, []).append(functools.partial(step, *args))

    for n in range(count):
        plan(BWD_SIDE[n], scatter.sum_side, n)
        if n + BWD_AHEAD < count:
            plan(BWD_SIDE[n], scatter.start, n + BWD_AHEAD)
        plan(BWD_NEAR[n], scatter.sum_near, n)
    make_tags(lens_ref, ext_q, ext_k)
    greeted()
    for n in range(BWD_AHEAD):
        scatter.start(n)
    acc_ref[...] = jnp.zeros_like(acc_ref)
    fill_rows(small_ref, table_ref, rows_ref, -1)
    fill_bias(rows_ref, bias_ref, 2 * PAIRS)
    for step in events.pop(-1, ()):
        step()
    lane = lane_index((TILE, 128))

    def one_pair(hp, carry):
        dk_acc[...] = jnp.zeros_like(dk_acc)
        dv_acc[...] = jnp.zeros_like(dv_acc)
        for i in range(OWN):
            run_events(events, hp, i)
            lo, hi = key_range(i)
            width = (hi - lo) * TILE
            pair, d_pair = q_ref[hp, i], do_ref[hp, i]
            tags = ext_q[i]
            zero = jnp.zeros_like(pair)
            q_two = jnp.concatenate([jnp.where(lane < 64, pair, zero), jnp.where(lane < 64, zero, pair)], axis=0)
            d_two = jnp.concatenate([jnp.where(lane < 64, d_pair, zero), jnp.where(lane < 64, zero, d_pair)], axis=0)
            q_ext = jnp.concatenate([q_two, jnp.concatenate([tags, tags], axis=0)], axis=1)
            keys = k_ref[hp, lo // 2 : hi // 2].reshape(width, 128)
            values = v_ref[hp, lo // 2 : hi // 2].reshape(width, 128)
            k_ext = jnp.concatenate([keys, ext_k[lo:hi].reshape(width, 128)], axis=1)
            raw = dot_nt(k_ext, q_ext)
            d_probs = dot_nt(values, d_two)
            p_rows, s_rows = [], []
            for kt in range(lo, hi):
                at = (kt - lo) * TILE
                p_two, s_two = [], []
                for e in range(2):
                    head = 2 * hp + e
                    part = raw[at : at + TILE, e * TILE : (e + 1) * TILE]
                    near = -1 <= kt - 2 * i <= 2
                    cls = bias_class(kt, i, core) if near else (0 if kt < 2 * i else 4)
                    if near:
                        part = part + bias_ref[head, cls]
                    else:
                        part = part + rows_ref[3 if kt < 2 * i else 4, head, :, :TILE]
                    probs = jnp.exp(part - log_ref[i, head])
                    slope = probs * (
                        d_probs[at : at + TILE, e * TILE : (e + 1) * TILE] - delta_ref[i, head]
                    )
                    acc_ref[head, cls] += slope
                    p_two.append(probs.astype(jnp.bfloat16))
                    s_two.append(slope.astype(jnp.bfloat16))
                p_rows.append(jnp.concatenate(p_two, axis=1))
                s_rows.append(jnp.concatenate(s_two, axis=1))
            probs_t = jnp.concatenate(p_rows, axis=0)
            slopes_t = jnp.concatenate(s_rows, axis=0)
            dv_acc[lo * TILE : hi * TILE, :] += dot_nn(probs_t, d_two)
            dk_acc[lo * TILE : hi * TILE, :] += dot_nn(slopes_t, q_two)
            d_q = dot_tn(slopes_t, keys)
            dq_ref[hp, i] = jnp.where(lane < 64, d_q[:TILE], d_q[TILE:]).astype(jnp.bfloat16)
        for acc, own, out in ((dk_acc, dk_ref, out_k), (dv_acc, dv_ref, out_v)):
            for i in range(OWN):
                own[hp, i] = acc[pl.ds((2 * i + core) * TILE, TILE), :].astype(jnp.bfloat16)
                out[hp, i] = acc[pl.ds((2 * i + 1 - core) * TILE, TILE), :].astype(jnp.bfloat16)
        for n, (out, got) in enumerate(((out_k, got_k), (out_v, got_v))):
            pltpu.make_async_remote_copy(
                out.at[hp], got.at[hp], send_sem.at[n, hp], recv_sem.at[n, hp],
                device_id=sibling, device_id_type=MESH,
            ).start()
        return carry

    lax.fori_loop(0, PAIRS, one_pair, 0)
    flip = (row_index((TILE, TILE)) + lane == TILE - 1).astype(jnp.float32)

    def one_head(h, carry):
        for cls in range(3):
            tile = jnp.dot(flip, acc_ref[h, cls + 1], precision=lax.Precision.HIGHEST)
            wide = jnp.concatenate([tile, jnp.zeros((TILE, TILE), jnp.float32)], axis=1)
            wide = pltpu.roll(wide, 0, 1, stride=1, stride_axis=0)
            hist_ref[cls, h] = jnp.sum(wide, axis=0, keepdims=True)
        for n, cls in ((3, 0), (4, 4)):
            row = jnp.sum(acc_ref[h, cls], axis=0, keepdims=True)
            hist_ref[n, h] = jnp.concatenate([row, jnp.zeros_like(row)], axis=1)
        return carry

    lax.fori_loop(0, 2 * PAIRS, one_head, 0)

    rel_ref[...] = jnp.zeros_like(rel_ref)
    rel_ref[:, :16] = bucket_sums(hist_ref, table_ref)

    def finish(hp, carry):
        for n, (out, got, own) in enumerate(((out_k, got_k, dk_ref), (out_v, got_v, dv_ref))):
            copy = pltpu.make_async_remote_copy(
                out.at[hp], got.at[hp], send_sem.at[n, hp], recv_sem.at[n, hp],
                device_id=sibling, device_id_type=MESH,
            )
            copy.wait_send()
            copy.wait_recv()
            own[hp] = (own[hp].astype(jnp.float32) + got[hp].astype(jnp.float32)).astype(jnp.bfloat16)
        return carry

    lax.fori_loop(0, PAIRS, finish, 0)
    late(events)
    for n in range(count):
        scatter.finish(n)


def norm_back(rows_in, scale, gain, grad_normed):
    scaled = grad_normed * gain
    grad_gain = jnp.sum(grad_normed * rows_in * scale, axis=0, keepdims=True)
    shared = jnp.mean(scaled * rows_in, axis=1, keepdims=True)
    return scale * scaled - rows_in * (scale * scale * scale * shared), grad_gain


def join_pairs(pairs_ref, joined_ref):
    for hp in range(PAIRS):
        joined_ref[:, 128 * hp : 128 * (hp + 1)] = (
            pairs_ref[hp].reshape(OWN * TILE, 128).astype(joined_ref.dtype)
        )


def gain_block(row):
    width = row.shape[1]
    lines = jnp.where(lane_index((32, width)) // 24 == row_index((32, width)), row, 0.0)
    pick = (lax.rem(row_index((width, 128)), 24) == lane_index((width, 128))).astype(jnp.float32)
    return jnp.dot(lines, pick, precision=lax.Precision.HIGHEST)


def ffn_kernel(
    deal_ref, x_ref, att_ref, wo_ref, small_ref, g_low, grd_in, wi_in, wu_in,
    dmid_ref, datt_ref, delta_ref, gwo_ref, two_ref, gwi, gwu, hid_out,
    grad_ref, mid_ref, normed_ref, total_ref, active_ref, slope_ref, wi_ref, wu_ref, gwi_two, gwu_two, g_high,
    res_ref, res_all, dealt, got_i, got_u, gwo_own, in_sem, out_sem, g_send, g_recv, h_send, h_recv, e_send, e_recv,
    c_send, c_recv,
):
    y, x, core, z = coordinates()
    sibling = place(y, x, 1 - core, z)
    owner, micro = z // 2, lax.rem(z, 2)
    greet()
    width = x_ref.shape[1]
    half = width // 2
    chunk = FFN_CHUNK
    chunks = wi_ref.shape[1] // chunk

    def bring(j):
        span = pl.ds(chunk * j, chunk)
        return (
            pltpu.make_async_copy(wi_in.at[:, span], wi_ref.at[:, span], in_sem.at[0, j]),
            pltpu.make_async_copy(wu_in.at[span], wu_ref.at[span], in_sem.at[1, j]),
        )

    for j in range(chunks):
        for copy in bring(j):
            copy.start()
    grads = list(grad_sends(grd_in, g_high, half, g_send, g_recv))
    gain = gain_row(small_ref, 1, width)
    mid = x_ref[...].astype(jnp.float32) + dot_nn(att_ref[...], wo_ref[...])
    mid_ref[...] = mid
    scale = lax.rsqrt(jnp.mean(mid * mid, axis=1, keepdims=True) + EPSILON)
    normed_ref[...] = (mid * scale * gain).astype(jnp.bfloat16)
    greeted()
    start_all(grads)

    def rows_of(i):
        return slice(TILE * i, TILE * (i + 1))

    picks = []
    for i in range(OWN):
        picks.append(one_hot((2 * i + core) * TILE + row_index((TILE, TILES * TILE)), deal_ref[...]))
        grad_ref[rows_of(i), :half] = dot_nn(
            picks[i], g_low[...].reshape(TILES * TILE, half)
        ).astype(jnp.bfloat16)
    for j in range(chunks):
        span = slice(chunk * j, chunk * (j + 1))
        for copy in bring(j):
            copy.wait()
        inner = dot_nn(normed_ref[...], wi_ref[:, span])
        cdf = 0.5 * (1.0 + lax.erf(inner * (1.0 / math.sqrt(2.0))))
        active_ref[:, span] = (inner * cdf).astype(jnp.bfloat16)
        slope = cdf + inner * (jnp.exp(-0.5 * inner * inner) * (1.0 / math.sqrt(2.0 * math.pi)))
        slope_ref[:, span] = slope.astype(jnp.bfloat16)
        term = dot_nn(active_ref[:, span], wu_ref[span, :])
        total_ref[...] = term if j == 0 else total_ref[...] + term
    result = (mid_ref[...] + total_ref[...]).astype(jnp.bfloat16).reshape(OWN, TILE, width)
    res_ref[...] = result
    res_copy = remote(res_ref, res_all.at[:, core], e_send, e_recv, sibling)
    res_copy.start()
    for i in range(OWN):
        res_all[i, core] = result[i]
    share_grads(g_high, g_send, g_recv)

    def dealt_sends():
        for e in range(2):
            z_to = 2 * core + e
            yield (
                dealt.at[e], hid_out.at[micro], h_send.at[e], h_recv.at[micro],
                place(y, x, owner, z_to), (owner == core) & (z_to == z),
            )

    remote(res_ref, res_all.at[:, 1 - core], e_send, e_recv, sibling).wait_recv()
    lane = lane_index((TILE, TILE))
    for b in range(OWN):
        at = pl.multiple_of((OWN * core + b) * TILE, TILE)
        turned = jnp.broadcast_to(deal_ref[:, pl.ds(at, TILE)].astype(jnp.float32), (TILE, TILE)).T
        turned = turned.astype(jnp.int32)
        pick = jnp.concatenate([one_hot(turned, TILE * t + lane) for t in range(TILES)], axis=1)
        made = dot_nn(pick, res_all[...].reshape(TILES * TILE, width)).astype(jnp.bfloat16)
        dealt[b // 3, TILE * (b % 3) : TILE * (b % 3 + 1)] = made
    deals = list(dealt_sends())
    start_all(deals)
    end_grads(grads, g_high, g_send, g_recv)
    for i in range(OWN):
        grad_ref[rows_of(i), half:] = dot_nn(
            picks[i], g_high[...].reshape(TILES * TILE, half)
        ).astype(jnp.bfloat16)

    def swap(j):
        slot, there = j % 2, 4 * (1 - core)
        copies = [remote(gwu_two.at[slot, pl.ds(there, 4)], got_u.at[j], c_send.at[j, 4], c_recv.at[j, 4], sibling)]
        for k in range(4):
            copies.append(
                remote(
                    gwi_two.at[slot, pl.ds(8 * k + there, 4)], got_i.at[j, k],
                    c_send.at[j, k], c_recv.at[j, k], sibling,
                )
            )
        return copies

    def take(j):
        return (
            pltpu.make_async_copy(got_i.at[j], gwi.at[:, :, :, pl.ds(chunk * j, chunk)], out_sem.at[0, j]),
            pltpu.make_async_copy(got_u.at[j], gwu.at[j], out_sem.at[1, j]),
        )

    def combine(j):
        slot, here = j % 2, 4 * core
        for copy in swap(j):
            copy.wait_recv()
        for n in range(4):
            got_u[j, n] = got_u[j, n] + gwu_two[slot, here + n]
            for k in range(4):
                got_i[j, k, n] = got_i[j, k, n] + gwi_two[slot, 8 * k + here + n]
        for copy in take(j):
            copy.start()
        for copy in swap(j):
            copy.wait_send()

    for j in range(chunks):
        span = slice(chunk * j, chunk * (j + 1))
        d_inner = (
            dot_nt(grad_ref[...], wu_ref[span, :]) * slope_ref[:, span].astype(jnp.float32)
        ).astype(jnp.bfloat16)
        made = dot_tn(active_ref[:, span], grad_ref[...])
        gwu_two[j % 2] = made.astype(jnp.bfloat16).reshape(gwu_two.shape[1:])
        made = dot_tn(normed_ref[...], d_inner)
        gwi_two[j % 2] = made.reshape(32, -1, chunk).astype(jnp.bfloat16)
        for copy in swap(j):
            copy.start()
        term = dot_nt(d_inner, wi_ref[:, span])
        total_ref[...] = term if j == 0 else total_ref[...] + term
        if j:
            combine(j - 1)

    mid = mid_ref[...]
    scale = lax.rsqrt(jnp.mean(mid * mid, axis=1, keepdims=True) + EPSILON)
    d_rows, d_gain = norm_back(mid, scale, gain, total_ref[...])
    two_ref[...] = gain_block(d_gain)
    d_mid = grad_ref[...].astype(jnp.float32) + d_rows
    dmid_ref[...] = d_mid
    branch = d_mid.astype(jnp.bfloat16)
    made = dot_tn(att_ref[...], branch)
    gwo_own[...] = made.reshape(32, -1, width).astype(jnp.bfloat16)
    swaps = [
        remote(
            gwo_own.at[pl.ds(8 * k + 4 * (1 - core), 4)], gwo_ref.at[k], c_send.at[chunks, k], c_recv.at[chunks, k], sibling
        )
        for k in range(4)
    ]
    for copy in swaps:
        copy.start()
    combine(chunks - 1)
    d_att = dot_nt(branch, wo_ref[...]).astype(jnp.bfloat16)
    pick = (lane_index((16, width)) // 64 == row_index((16, width))).astype(jnp.float32)
    prod = d_att.astype(jnp.float32) * att_ref[...].astype(jnp.float32)
    sums = lax.dot_general(
        pick, prod, (((1,), (1,)), ((), ())), precision=lax.Precision.HIGHEST, preferred_element_type=jnp.float32
    )
    for hp in range(PAIRS):
        datt_ref[hp] = d_att[:, 128 * hp : 128 * (hp + 1)].reshape(OWN, TILE, 128)
    for i in range(OWN):
        for h in range(2 * PAIRS):
            delta_ref[i, h] = sums[h : h + 1, TILE * i : TILE * (i + 1)]
    for k, copy in enumerate(swaps):
        copy.wait_recv()
        for n in range(4):
            gwo_ref[k, n] = gwo_ref[k, n] + gwo_own[8 * k + 4 * core + n]
        copy.wait_send()
    for j in range(chunks):
        for copy in take(j):
            copy.wait()
    res_copy.wait_send()
    for item in deals:
        sent(*item)
    for m in range(2):
        remote(dealt.at[0], hid_out.at[m], h_send.at[0], h_recv.at[m], sibling).wait_recv()


def tail_kernel(
    x_ref, small_ref, dmid_ref, dq_ref, dk_ref, dv_ref, wq_ref, wk_ref, wv_ref, g_two, g_rel,
    gin_out, tsmall, tq, tk, tv,
    join_ref, back_out, small, gq, gk, gv, *scratch,
):
    y, x, c, z = coordinates()
    sibling = place(y, x, 1 - c, z)
    owner, micro = z // 2, lax.rem(z, 2)
    greet()
    plain = [(gk, tk, None, "x"), (gv, tv, None, "y"), (gq, tq, None, "x"), (small, tsmall, None, "y")]
    count = len(plain)
    w_send, w_recv, w_local, b_send, b_recv = scratch[3 * count :]
    scatter = Scatter(
        [item + tuple(scratch[3 * n : 3 * n + 3]) for n, item in enumerate(plain)], w_send, w_recv, w_local
    )
    rows = x_ref[...].astype(jnp.float32)
    scale = lax.rsqrt(jnp.mean(rows * rows, axis=1, keepdims=True) + EPSILON)
    back = None
    for n, (pairs, w_ref) in enumerate(((dq_ref, wq_ref), (dk_ref, wk_ref), (dv_ref, wv_ref))):
        join_pairs(pairs, join_ref.at[n])
        term = dot_nt(join_ref[n], w_ref[...])
        back = term if back is None else back + term
    gain = gain_row(small_ref, 0, rows.shape[1])
    d_rows, d_gain = norm_back(rows, scale, gain, back)
    d_dealt = (dmid_ref[...] + d_rows).astype(jnp.bfloat16)
    back_out[...] = d_dealt.reshape(back_out.shape)
    greeted()

    def back_sends():
        for i in range(OWN):
            t = 2 * i + c
            z_to, l = t // 3, lax.rem(t, 3)
            yield (
                back_out.at[i], gin_out.at[micro, l], b_send.at[i], b_recv.at[micro, l],
                place(y, x, owner, z_to), (owner == c) & (z_to == z),
            )

    sends = list(back_sends())
    for item in sends:
        send_or_keep(*item)
    normed_t = (rows * scale * gain).astype(jnp.bfloat16).T
    for n, (at, grad_ref) in enumerate(((1, gk), (2, gv), (0, gq))):
        made = dot_nn(normed_t, join_ref[at])
        for r in range(32):
            grad_ref[r] = made[24 * r : 24 * (r + 1), :].astype(jnp.bfloat16)
        scatter.start(n)
    g_one = gain_block(d_gain)
    shape = (32, 16, 128)
    kind = lax.broadcasted_iota(jnp.int32, shape, 1)
    spread = lambda v: jnp.broadcast_to(v[:, None, :], shape)
    small[...] = jnp.where(
        kind == 0, spread(g_one), jnp.where(kind == 1, spread(g_two[...]), spread(g_rel[...]))
    ).astype(jnp.bfloat16)
    scatter.start(3)
    for n in range(count + 2):
        for back_by, stage in enumerate((scatter.sum_core, scatter.sum_side, scatter.sum_near)):
            if 0 <= n - back_by < count:
                stage(n - back_by)
    for n in range(count):
        scatter.finish(n)
    for item in sends:
        sent(*item)
    for m in range(2):
        for l in range(3):
            remote(back_out.at[0], gin_out.at[m, l], b_send.at[0], b_recv.at[m, l], sibling).wait_recv()


def coordinates():
    dp, z = lax.axis_index("dp"), lax.axis_index("fsdp")
    return dp // 4, lax.rem(dp // 2, 2), lax.rem(dp, 2), z


def place(y, x, c, z):
    return (4 * y + 2 * x + c, z)


def column(y, x, c):
    return 16 * y + 8 * x + 4 * c


def partners():
    y, x, c, z = coordinates()
    found = [place(1 - y, x, c, z), place(y, 1 - x, c, z)]
    for dc in range(2):
        for dz in range(4):
            if dc or dz:
                found.append(place(y, x, lax.rem(c + dc, 2), lax.rem(z + dz, 4)))
    return found


def greet():
    for partner in partners():
        pl.semaphore_signal(pltpu.get_barrier_semaphore(), inc=1, device_id=partner, device_id_type=MESH)


def greeted():
    pl.semaphore_wait(pltpu.get_barrier_semaphore(), len(partners()))


def remote(src, dst, send, recv, target):
    return pltpu.make_async_remote_copy(
        src, dst, send, recv, device_id=target, device_id_type=MESH
    )


def send_or_keep(src, dst, send, recv, target, here):
    @pl.when(jnp.logical_not(here))
    def _():
        remote(src, dst, send, recv, target).start()

    @pl.when(here)
    def _():
        pltpu.make_async_copy(src, dst, recv).start()


def sent(src, dst, send, recv, target, here):
    @pl.when(jnp.logical_not(here))
    def _():
        remote(src, dst, send, recv, target).wait_send()


def cut(ref, lead, part):
    return ref.at[lead] if part is None else ref.at[lead, slice(None), pl.ds(*part)]


def cut_shard(ref, part):
    return ref if part is None else ref.at[:, pl.ds(*part)]


class Gather:
    def __init__(self, pieces, send, recv, local):
        self.pieces, self.send, self.recv, self.local = pieces, send, recv, local
        self.y, self.x, self.c, self.z = coordinates()
        y, x, c, z = self.y, self.x, self.c, self.z
        self.sibling = place(y, x, 1 - c, z)
        self.mine = column(y, x, c)
        self.far = column(1 - y, 1 - x, c)
        by_x = (place(y, 1 - x, c, z), column(y, 1 - x, c))
        by_y = (place(1 - y, x, c, z), column(1 - y, x, c))
        self.sides = {"x": by_x + by_y, "y": by_y + by_x}

    def own_copy(self, n):
        shard, whole, part, _ = self.pieces[n]
        return pltpu.make_async_copy(
            cut_shard(shard, part), cut(whole, self.mine + self.z, part), self.local.at[n]
        )

    def z_copy(self, n, dz, came=False):
        shard, whole, part, _ = self.pieces[n]
        entry = self.mine + (lax.rem(self.z + 4 - dz, 4) if came else self.z)
        return remote(
            cut_shard(shard, part), cut(whole, entry, part), self.send.at[n, dz - 1], self.recv.at[n, dz - 1],
            place(self.y, self.x, self.c, lax.rem(self.z + dz, 4)),
        )

    def push(self, n, k, base, target):
        _, whole, part, _ = self.pieces[n]
        block = cut(whole, pl.ds(base, 4), part)
        return remote(block, block, self.send.at[n, k], self.recv.at[n, k], target)

    def start(self, n):
        self.own_copy(n).start()
        for dz in range(1, 4):
            self.z_copy(n, dz).start()

    def spread_own(self, n):
        near, _, side, _ = self.sides[self.pieces[n][3]]
        self.own_copy(n).wait()
        for dz in range(1, 4):
            self.z_copy(n, dz, True).wait_recv()
        for k, target in ((3, near), (4, side), (6, self.sibling)):
            self.push(n, k, self.mine, target).start()

    def spread_near(self, n):
        _, near_column, side, _ = self.sides[self.pieces[n][3]]
        self.push(n, 3, near_column, self.sibling).wait_recv()
        self.push(n, 5, near_column, side).start()
        self.push(n, 7, near_column, self.sibling).start()

    def spread_side(self, n):
        side_column = self.sides[self.pieces[n][3]][3]
        self.push(n, 4, side_column, self.sibling).wait_recv()
        self.push(n, 8, side_column, self.sibling).start()
        self.push(n, 5, self.far, self.sibling).wait_recv()
        self.push(n, 9, self.far, self.sibling).start()

    def finish(self, n):
        _, near_column, _, side_column = self.sides[self.pieces[n][3]]
        for k, base in ((6, self.mine), (7, near_column), (8, side_column), (9, self.far)):
            self.push(n, k, base + 4 - 8 * self.c, self.sibling).wait_recv()
        for dz in range(1, 4):
            self.z_copy(n, dz).wait_send()
        for k in range(3, 10):
            self.push(n, k, self.mine, self.sibling).wait_send()


class Scatter:
    def __init__(self, pieces, send, recv, local):
        self.pieces, self.send, self.recv, self.local = pieces, send, recv, local
        self.y, self.x, self.c, self.z = coordinates()
        y, x, c, z = self.y, self.x, self.c, self.z
        self.sibling = place(y, x, 1 - c, z)

    def sides(self, n):
        y, x, c, z = self.y, self.x, self.c, self.z
        by_x, by_y = place(y, 1 - x, c, z), place(1 - y, x, c, z)
        if self.pieces[n][3] == "x":
            return by_x, by_y, (lambda s, f: 2 * s + f), y, x
        return by_y, by_x, (lambda s, f: 2 * f + s), x, y

    def core_copy(self, n, k):
        grad, _, part, _, r1 = self.pieces[n][:5]
        return remote(
            cut(grad, pl.ds(8 * k + 4 * (1 - self.c), 4), part), r1.at[k],
            self.send.at[n, k], self.recv.at[n, k], self.sibling,
        )

    def side_copy(self, n, f_at):
        _, side, index, s, _ = self.sides(n)
        _, _, _, _, r1, r2, _ = self.pieces[n]
        return remote(
            r1.at[index(1 - s, f_at)], r2.at[f_at], self.send.at[n, 4 + f_at], self.recv.at[n, 4 + f_at], side
        )

    def near_copy(self, n):
        near, _, index, s, f = self.sides(n)
        _, _, _, _, r1, _, r3 = self.pieces[n]
        return remote(r1.at[index(s, 1 - f)], r3, self.send.at[n, 6], self.recv.at[n, 6], near)

    def z_copy(self, n, dz):
        _, _, index, s, f = self.sides(n)
        _, terms, part, _, r1, _, _ = self.pieces[n]
        z_to = lax.rem(self.z + dz, 4)
        return remote(
            r1.at[index(s, f), z_to], cut(terms, dz, part), self.send.at[n, 6 + dz], self.recv.at[n, 6 + dz],
            place(self.y, self.x, self.c, z_to),
        )

    def own_copy(self, n):
        _, _, index, s, f = self.sides(n)
        _, terms, part, _, r1, _, _ = self.pieces[n]
        return pltpu.make_async_copy(r1.at[index(s, f), self.z], cut(terms, 0, part), self.local.at[n, 0])

    def start(self, n):
        for k in range(4):
            self.core_copy(n, k).start()

    def sum_core(self, n):
        grad, _, part, _, r1 = self.pieces[n][:5]
        for k in range(4):
            self.core_copy(n, k).wait_recv()

            def one(j, carry, k=k):
                r1[k, j] = r1[k, j] + cut(grad, 8 * k + 4 * self.c + j, part)[...]
                return carry

            lax.fori_loop(0, 4, one, 0)
        for f_at in range(2):
            self.side_copy(n, f_at).start()

    def sum_side(self, n):
        _, _, index, s, _ = self.sides(n)
        _, _, _, _, r1, r2, _ = self.pieces[n]
        for f_at in range(2):
            self.side_copy(n, f_at).wait_recv()
            k = index(s, f_at)

            def one(j, carry, k=k, f_at=f_at):
                r1[k, j] = r1[k, j] + r2[f_at, j]
                return carry

            lax.fori_loop(0, 4, one, 0)
        self.near_copy(n).start()

    def sum_near(self, n):
        _, _, index, s, f = self.sides(n)
        _, _, _, _, r1, _, r3 = self.pieces[n]
        self.near_copy(n).wait_recv()
        k = index(s, f)

        def one(j, carry):
            r1[k, j] = r1[k, j] + r3[j]
            return carry

        lax.fori_loop(0, 4, one, 0)
        for dz in range(1, 4):
            self.z_copy(n, dz).start()
        self.own_copy(n).start()

    def finish(self, n):
        self.own_copy(n).wait()
        for dz in range(1, 4):
            self.z_copy(n, dz).wait_recv()
        for k in range(4):
            self.core_copy(n, k).wait_send()
        for f_at in range(2):
            self.side_copy(n, f_at).wait_send()
        self.near_copy(n).wait_send()
        for dz in range(1, 4):
            self.z_copy(n, dz).wait_send()


class LateScatter(Scatter):
    def side_copy(self, n, f_at):
        _, side, index, s, _ = self.sides(n)
        summed, _, part, _, _, r2, _ = self.pieces[n]
        return remote(
            cut(summed.at[index(1 - s, f_at)], pl.ds(0, 4), part), r2.at[f_at],
            self.send.at[n, 4 + f_at], self.recv.at[n, 4 + f_at], side,
        )

    def fetch(self, n, f_at):
        _, _, index, s, _ = self.sides(n)
        summed, _, part, _, own, _, _ = self.pieces[n]
        return pltpu.make_async_copy(
            cut(summed.at[index(s, f_at)], pl.ds(0, 4), part), own.at[f_at], self.local.at[n, 1 + f_at]
        )

    def near_copy(self, n):
        near, _, _, _, f = self.sides(n)
        _, _, _, _, _, r2, r3 = self.pieces[n]
        return remote(r2.at[1 - f], r3, self.send.at[n, 6], self.recv.at[n, 6], near)

    def z_copy(self, n, dz):
        f = self.sides(n)[4]
        _, terms, part, _, _, r2, _ = self.pieces[n]
        z_to = lax.rem(self.z + dz, 4)
        return remote(
            r2.at[f, z_to], cut(terms, dz, part), self.send.at[n, 6 + dz], self.recv.at[n, 6 + dz],
            place(self.y, self.x, self.c, z_to),
        )

    def own_copy(self, n):
        f = self.sides(n)[4]
        _, terms, part, _, _, r2, _ = self.pieces[n]
        return pltpu.make_async_copy(r2.at[f, self.z], cut(terms, 0, part), self.local.at[n, 0])

    def start(self, n):
        for f_at in range(2):
            self.side_copy(n, f_at).start()
            self.fetch(n, f_at).start()

    def sum_side(self, n):
        _, _, _, _, own, r2, _ = self.pieces[n]
        for f_at in range(2):
            self.side_copy(n, f_at).wait_recv()
            self.fetch(n, f_at).wait()

            def one(j, carry, f_at=f_at):
                r2[f_at, j] = r2[f_at, j] + own[f_at, j]
                return carry

            lax.fori_loop(0, 4, one, 0)
        self.near_copy(n).start()

    def sum_near(self, n):
        f = self.sides(n)[4]
        _, _, _, _, _, r2, r3 = self.pieces[n]
        self.near_copy(n).wait_recv()

        def one(j, carry):
            r2[f, j] = r2[f, j] + r3[j]
            return carry

        lax.fori_loop(0, 4, one, 0)
        for dz in range(1, 4):
            self.z_copy(n, dz).start()
        self.own_copy(n).start()

    def finish(self, n):
        self.own_copy(n).wait()
        for dz in range(1, 4):
            self.z_copy(n, dz).wait_recv()
        for f_at in range(2):
            self.side_copy(n, f_at).wait_send()
        self.near_copy(n).wait_send()
        for dz in range(1, 4):
            self.z_copy(n, dz).wait_send()


def run_events(events, hp, i):
    for at in range(PAIRS):
        todo = events.get(at * OWN + i, ())
        if todo:

            @pl.when(hp == at)
            def _(todo=todo):
                for step in todo:
                    step()


def late(events):
    for at in sorted(events):
        if at >= PAIRS * OWN:
            for step in events[at]:
                step()


def token_sends(hid_in, x_own, x_send, x_recv):
    y, x, c, z = coordinates()
    for m in range(2):
        for l in range(3):
            t = 3 * z + l
            core_to, z_to = lax.rem(t, 2), 2 * c + m
            yield (
                hid_in.at[m, l], x_own.at[t // 2], x_send.at[m, l], x_recv.at[t // 2],
                place(y, x, core_to, z_to), (core_to == c) & (z_to == z),
            )


def start_all(items):
    for item in items:
        send_or_keep(*item)


def grad_sends(grd_in, g_part, first, g_send, g_recv):
    y, x, c, z = coordinates()
    width = g_part.shape[2]
    for m in range(2):
        for half in range(2):
            z_to = 2 * c + m
            yield (
                grd_in.at[m, half, :, pl.ds(first, width)], g_part.at[2 * z + half], g_send.at[0, m, half],
                g_recv.at[0, z], place(y, x, half, z_to), (half == c) & (z_to == z),
            )


def share_copy(g_part, zs, core, g_send, g_recv):
    y, x, c, z = coordinates()
    block = g_part.at[2 * zs + core]
    return remote(
        block, block, g_send.at[1, zs // 2, zs % 2], g_recv.at[1, zs], place(y, x, 1 - c, z)
    )


def share_grads(g_part, g_send, g_recv):
    y, x, c, z = coordinates()
    for zs in range(4):
        block = g_part.at[2 * zs + c]
        remote(block, block, g_send.at[1, 0, 0], g_recv.at[0, zs], place(y, x, 1 - c, z)).wait_recv()
        share_copy(g_part, zs, c, g_send, g_recv).start()


def end_grads(items, g_part, g_send, g_recv):
    c = coordinates()[2]
    for zs in range(4):
        share_copy(g_part, zs, 1 - c, g_send, g_recv).wait_recv()
        share_copy(g_part, zs, c, g_send, g_recv).wait_send()
    for item in items:
        sent(*item)


def gather_kernel(first_axis, *refs):
    count = len(first_axis)
    lens_in, deal_in, hid_in, one_in, two_in, rel_in = refs[:6]
    shards = refs[6 : 5 + count]
    rest = refs[5 + count :]
    lens_u, deal_u, x_own = rest[:3]
    outs = rest[3 : 3 + count]
    lens_wide, rows_f, small, w_send, w_recv, w_local, x_send, x_recv, p_send, p_recv = rest[3 + count :]
    y, x, c, z = coordinates()
    sibling = place(y, x, 1 - c, z)
    greet()
    rows_f[...] = jnp.zeros_like(rows_f)
    rows_f[0:1, : one_in.shape[1]] = one_in[...].astype(jnp.float32)
    rows_f[1:2, : two_in.shape[1]] = two_in[...].astype(jnp.float32)
    rows_f[2:3, : rel_in.shape[1]] = rel_in[...].astype(jnp.float32)
    small[...] = rows_f[...].astype(jnp.bfloat16)
    lens_wide[...] = jnp.zeros_like(lens_wide)
    lens_wide[:, :, : lens_in.shape[2]] = lens_in[...]
    greeted()
    gather = Gather(
        [(s, o, None, a) for s, o, a in zip((small,) + tuple(shards), outs, first_axis)], w_send, w_recv, w_local
    )
    for n in range(count):
        gather.start(n)
    sends = list(token_sends(hid_in, x_own, x_send, x_recv))
    for item in sends:
        send_or_keep(*item)
    owner, micro = z // 2, lax.rem(z, 2)
    plans = []
    for n, (src, dst) in enumerate(((lens_wide, lens_u), (deal_in, deal_u))):
        plans.append((src.at[micro], dst, p_send.at[n], p_recv.at[n]))

    @pl.when(owner == c)
    def _():
        for src, dst, send, recv in plans:
            remote(src, dst, send, recv, sibling).start()
            pltpu.make_async_copy(src, dst, recv).start()

    for n in range(count):
        gather.spread_own(n)
    for n in range(count):
        gather.spread_near(n)
    for n in range(count):
        gather.spread_side(n)
    for n in range(count):
        gather.finish(n)
    for item in sends:
        sent(*item)
    for i in range(OWN):
        remote(hid_in.at[0, 0], x_own.at[i], x_send.at[0, 0], x_recv.at[i], sibling).wait_recv()
    for src, dst, send, recv in plans:
        remote(src, dst, send, recv, sibling).wait_recv()

    @pl.when(owner == c)
    def _():
        for src, dst, send, recv in plans:
            remote(src, dst, send, recv, sibling).wait_send()


def sum_terms(term):
    total = term[0].astype(jnp.float32)
    for dz in range(1, 4):
        total = total + term[dz].astype(jnp.float32)
    return total


def sum_kernel(
    hid_in, gin_in, tsmall, tq, tk, tv, two, twi, twu,
    hid_out, gin_out, one_out, two_out, rel_out, gq, gk, gv, gwo, gwi, gwu,
):
    hid_out[...] = hid_in[...].astype(jnp.float32)
    gin_out[...] = gin_in[...].astype(jnp.float32)
    small = sum_terms(tsmall)
    one_out[...] = small[0:1, : one_out.shape[1]]
    two_out[...] = small[1:2, : two_out.shape[1]]
    rel_out[...] = small[2:3, : rel_out.shape[1]]
    for term, out in ((tq, gq), (tk, gk), (tv, gv), (two, gwo), (twi, gwi), (twu, gwu)):
        out[...] = sum_terms(term)


def token_places(deal_order, lengths):
    seq_ends = jnp.cumsum(lengths)
    starts = seq_ends - lengths
    inside = (deal_order[:, None] >= starts[None, :]).astype(jnp.int32)
    segment = jnp.sum(inside, axis=1) - 1
    picked = (segment[:, None] == jnp.arange(lengths.shape[0], dtype=jnp.int32)[None, :]).astype(
        jnp.int32
    )
    position = deal_order - jnp.sum(picked * starts[None, :], axis=1)
    return (segment, position)


def rms_scale(rows_in):
    return lax.rsqrt(jnp.mean(rows_in * rows_in, axis=1, keepdims=True) + EPSILON)


def gelu_slope(values):
    normal_cdf = 0.5 * (1.0 + jax.scipy.special.erf(values * (1.0 / math.sqrt(2.0))))
    normal_pdf = jnp.exp(-0.5 * values * values) * (1.0 / math.sqrt(2.0 * math.pi))
    return normal_cdf + values * normal_pdf


def norm_back_rows(rows_in, scale, gain, grad_normed):
    scaled_grad = grad_normed * gain
    grad_gain = jnp.sum(grad_normed * rows_in * scale, axis=0)
    grad_rows = scale * scaled_grad - rows_in * scale * scale * scale * jnp.mean(
        scaled_grad * rows_in, axis=1, keepdims=True
    )
    return (grad_rows, grad_gain)


def key_layout(key_all, value_all, segment, position, head_count):
    rows_all = key_all.shape[0]
    block_rows = 512
    blocks = rows_all // block_rows
    return (
        key_all.reshape(blocks, block_rows, head_count, -1),
        value_all.reshape(blocks, block_rows, head_count, -1),
        segment.reshape(blocks, block_rows),
        position.reshape(blocks, block_rows),
    )


def block_scores(
    queries,
    key_block,
    seg_query,
    pos_query,
    seg_block,
    pos_block,
    rel_bucket,
    bucket_edges,
    max_offset,
):
    lower_edge, upper_edge = bucket_edges
    raw_scores = jnp.einsum("qhd,khd->hqk", queries, key_block, preferred_element_type=jnp.float32)
    offset = jnp.clip(pos_block[None, :] - pos_query[:, None], -max_offset, max_offset)
    bucket_hit = (
        (offset[:, :, None] >= lower_edge[None, None, :])
        & (offset[:, :, None] <= upper_edge[None, None, :])
    ).astype(jnp.float32)
    bias = jnp.einsum(
        "qkb,bh->hqk",
        bucket_hit,
        rel_bucket,
        precision=lax.Precision.HIGHEST,
        preferred_element_type=jnp.float32,
    )
    same_seq = (seg_query[:, None] == seg_block[None, :])[None]
    return (raw_scores + bias, same_seq, bucket_hit)


def attend(queries, layout, seg_query, pos_query, rel_bucket, bucket_edges, max_offset):
    key_blocks, value_blocks, seg_blocks, pos_blocks = layout
    query_count, head_count, head_size = queries.shape

    def measure(carry, block):
        row_top, row_total = carry
        key_block, seg_block, pos_block = block
        scores, same_seq, _ = block_scores(
            queries,
            key_block,
            seg_query,
            pos_query,
            seg_block,
            pos_block,
            rel_bucket,
            bucket_edges,
            max_offset,
        )
        scores = jnp.where(same_seq, scores, NEG_FILL)
        new_top = jnp.maximum(row_top, jnp.max(scores, axis=2))
        weights_now = jnp.where(same_seq, jnp.exp(scores - new_top[:, :, None]), 0.0)
        row_total = row_total * jnp.exp(row_top - new_top) + jnp.sum(weights_now, axis=2)
        return ((new_top, row_total), None)

    start = (
        jnp.full((head_count, query_count), NEG_FILL, jnp.float32),
        jnp.zeros((head_count, query_count), jnp.float32),
    )
    (row_top, row_total), _ = lax.scan(measure, start, (key_blocks, seg_blocks, pos_blocks))
    log_total = row_top + jnp.log(row_total)

    def collect(summed, block):
        key_block, value_block, seg_block, pos_block = block
        scores, same_seq, _ = block_scores(
            queries,
            key_block,
            seg_query,
            pos_query,
            seg_block,
            pos_block,
            rel_bucket,
            bucket_edges,
            max_offset,
        )
        probs = jnp.where(same_seq, jnp.exp(scores - log_total[:, :, None]), 0.0).astype(
            jnp.bfloat16
        )
        return (
            summed
            + jnp.einsum("hqk,khd->qhd", probs, value_block, preferred_element_type=jnp.float32),
            None,
        )

    attended_f, _ = lax.scan(
        collect, jnp.zeros((query_count, head_count, head_size), jnp.float32), layout
    )
    return (attended_f, log_total)


def attend_back(
    queries,
    layout,
    seg_query,
    pos_query,
    rel_bucket,
    bucket_edges,
    max_offset,
    log_total,
    d_attended,
    row_delta,
):

    def step(carry, block):
        d_queries, d_buckets = carry
        key_block, value_block, seg_block, pos_block = block
        scores, same_seq, bucket_hit = block_scores(
            queries,
            key_block,
            seg_query,
            pos_query,
            seg_block,
            pos_block,
            rel_bucket,
            bucket_edges,
            max_offset,
        )
        probs_f = jnp.where(same_seq, jnp.exp(scores - log_total[:, :, None]), 0.0)
        d_probs = jnp.einsum(
            "qhd,khd->hqk", d_attended, value_block, preferred_element_type=jnp.float32
        )
        d_scores = (probs_f * (d_probs - row_delta[:, :, None])).astype(jnp.bfloat16)
        d_queries = d_queries + jnp.einsum(
            "hqk,khd->qhd", d_scores, key_block, preferred_element_type=jnp.float32
        )
        d_buckets = d_buckets + jnp.einsum(
            "hqk,qkb->bh",
            d_scores,
            bucket_hit.astype(jnp.bfloat16),
            preferred_element_type=jnp.float32,
        )
        d_values = jnp.einsum(
            "hqk,qhd->khd",
            probs_f.astype(jnp.bfloat16),
            d_attended,
            preferred_element_type=jnp.float32,
        )
        d_keys = jnp.einsum("hqk,qhd->khd", d_scores, queries, preferred_element_type=jnp.float32)
        return ((d_queries, d_buckets), (d_keys, d_values))

    start = (jnp.zeros(queries.shape, jnp.float32), jnp.zeros(rel_bucket.shape, jnp.float32))
    (d_queries, d_buckets), key_terms = lax.scan(step, start, layout)
    return (d_queries, key_terms, d_buckets)


def on_device(
    hidden_in,
    grad_out,
    gain_attn,
    gain_ffn,
    rel_bias,
    w_query,
    w_key,
    w_value,
    w_output,
    w_inner,
    w_outer,
    dealing,
    lengths,
    bucket_table,
):
    micro_count, tok_rows, model_width = hidden_in.shape
    group_size = lax.axis_size("fsdp")
    slot_rows = tok_rows // group_size
    own_index = lax.axis_index("fsdp")
    max_offset = (bucket_table.shape[0] - 1) // 2
    bucket_count = BUCKETS
    head_count = H
    offsets_all = jnp.arange(bucket_table.shape[0], dtype=jnp.int32) - max_offset
    matches = bucket_table[:, None] == jnp.arange(bucket_count, dtype=jnp.int32)[None, :]
    lower_edge = jnp.min(jnp.where(matches, offsets_all[:, None], 2 * max_offset + 2), axis=0)
    upper_edge = jnp.max(jnp.where(matches, offsets_all[:, None], -2 * max_offset - 2), axis=0)
    bucket_edges = (lower_edge, upper_edge)
    hidden_units = w_inner.shape[1]
    acc_gain_one = jnp.zeros((model_width,), jnp.float32)
    acc_gain_two = jnp.zeros((model_width,), jnp.float32)
    acc_buckets = jnp.zeros((bucket_count, head_count), jnp.float32)
    acc_query = jnp.zeros((model_width, model_width), jnp.float32)
    acc_key = jnp.zeros((model_width, model_width), jnp.float32)
    acc_value = jnp.zeros((model_width, model_width), jnp.float32)
    acc_output = jnp.zeros((model_width, model_width), jnp.float32)
    acc_inner = jnp.zeros((model_width, hidden_units), jnp.float32)
    acc_outer = jnp.zeros((hidden_units, model_width), jnp.float32)
    outputs_list = []
    grads_list = []
    for micro_idx in range(micro_count):
        weights_now = (
            lax.all_gather(gain_attn, ("dp", "fsdp"), axis=0, tiled=True),
            lax.all_gather(gain_ffn, ("dp", "fsdp"), axis=0, tiled=True),
            lax.all_gather(rel_bias, ("dp", "fsdp"), axis=0, tiled=True),
            lax.all_gather(w_query, ("dp", "fsdp"), axis=0, tiled=True),
            lax.all_gather(w_key, ("dp", "fsdp"), axis=0, tiled=True),
            lax.all_gather(w_value, ("dp", "fsdp"), axis=0, tiled=True),
            lax.all_gather(w_output, ("dp", "fsdp"), axis=0, tiled=True),
            lax.all_gather(w_inner, ("dp", "fsdp"), axis=0, tiled=True),
            lax.all_gather(w_outer, ("dp", "fsdp"), axis=0, tiled=True),
        )
        gain_one = weights_now[0].astype(jnp.float32)
        gain_two = weights_now[1].astype(jnp.float32)
        rel_bucket = weights_now[2].astype(jnp.float32).reshape(bucket_count, head_count)
        query_weight, key_weight, value_weight, output_weight, inner_weight, outer_weight = (
            weights_now[3:]
        )
        deal_order = dealing[micro_idx, 0]
        segment, position = token_places(deal_order, lengths[micro_idx, 0])
        seg_query = lax.dynamic_slice_in_dim(segment, own_index * tok_rows, tok_rows)
        pos_query = lax.dynamic_slice_in_dim(position, own_index * tok_rows, tok_rows)
        take_rows = (
            lax.dynamic_slice_in_dim(
                deal_order.reshape(group_size, tok_rows), own_index * slot_rows, slot_rows, 1
            )
            - own_index * tok_rows
        ).reshape(tok_rows)
        dealt = lax.all_to_all(
            jnp.take(hidden_in[micro_idx], take_rows, axis=0),
            "fsdp",
            split_axis=0,
            concat_axis=0,
            tiled=True,
        )
        dealt_rows = dealt.astype(jnp.float32)
        scale_one = rms_scale(dealt_rows)
        normed1 = (dealt_rows * scale_one * gain_one).astype(jnp.bfloat16)
        queries = jnp.dot(normed1, query_weight, preferred_element_type=jnp.float32).astype(
            jnp.bfloat16
        )
        key_rows = jnp.dot(normed1, key_weight, preferred_element_type=jnp.float32).astype(
            jnp.bfloat16
        )
        value_rows = jnp.dot(normed1, value_weight, preferred_element_type=jnp.float32).astype(
            jnp.bfloat16
        )
        key_all, value_all = (
            lax.all_gather(key_rows, "fsdp", axis=0, tiled=True),
            lax.all_gather(value_rows, "fsdp", axis=0, tiled=True),
        )
        layout = key_layout(key_all, value_all, segment, position, head_count)
        queries_heads = queries.reshape(tok_rows, head_count, -1)
        attended_f, log_total = attend(
            queries_heads, layout, seg_query, pos_query, rel_bucket, bucket_edges, max_offset
        )
        attended = attended_f.reshape(tok_rows, model_width).astype(jnp.bfloat16)
        mid = dealt_rows + jnp.dot(attended, output_weight, preferred_element_type=jnp.float32)
        scale_two = rms_scale(mid)
        normed2 = (mid * scale_two * gain_two).astype(jnp.bfloat16)
        inner_act = jnp.dot(normed2, inner_weight, preferred_element_type=jnp.float32)
        active = jax.nn.gelu(inner_act, approximate=False).astype(jnp.bfloat16)
        result = mid + jnp.dot(active, outer_weight, preferred_element_type=jnp.float32)
        outputs_list.append(result)
        weights_back = (
            lax.all_gather(gain_attn, ("dp", "fsdp"), axis=0, tiled=True),
            lax.all_gather(gain_ffn, ("dp", "fsdp"), axis=0, tiled=True),
            lax.all_gather(rel_bias, ("dp", "fsdp"), axis=0, tiled=True),
            lax.all_gather(w_query, ("dp", "fsdp"), axis=0, tiled=True),
            lax.all_gather(w_key, ("dp", "fsdp"), axis=0, tiled=True),
            lax.all_gather(w_value, ("dp", "fsdp"), axis=0, tiled=True),
            lax.all_gather(w_output, ("dp", "fsdp"), axis=0, tiled=True),
            lax.all_gather(w_inner, ("dp", "fsdp"), axis=0, tiled=True),
            lax.all_gather(w_outer, ("dp", "fsdp"), axis=0, tiled=True),
        )
        query_weight, key_weight, value_weight, output_weight, inner_weight, outer_weight = (
            weights_back[3:]
        )
        grad_top = grad_out[micro_idx]
        acc_outer = acc_outer + jnp.einsum(
            "tf,td->fd", active, grad_top, preferred_element_type=jnp.float32
        )
        d_active = jnp.einsum(
            "td,fd->tf", grad_top, outer_weight, preferred_element_type=jnp.float32
        )
        d_inner = (d_active * gelu_slope(inner_act)).astype(jnp.bfloat16)
        acc_inner = acc_inner + jnp.einsum(
            "td,tf->df", normed2, d_inner, preferred_element_type=jnp.float32
        )
        d_normed2 = jnp.einsum(
            "tf,df->td", d_inner, inner_weight, preferred_element_type=jnp.float32
        )
        d_mid_norm, d_gain_two = norm_back_rows(mid, scale_two, gain_two, d_normed2)
        acc_gain_two = acc_gain_two + d_gain_two
        d_mid = grad_top.astype(jnp.float32) + d_mid_norm
        d_branch = d_mid.astype(jnp.bfloat16)
        acc_output = acc_output + jnp.einsum(
            "td,te->de", attended, d_branch, preferred_element_type=jnp.float32
        )
        d_attended = jnp.einsum(
            "te,de->td", d_branch, output_weight, preferred_element_type=jnp.float32
        ).astype(jnp.bfloat16)
        d_attended_heads = d_attended.reshape(tok_rows, head_count, -1)
        row_delta = jnp.sum(d_attended_heads.astype(jnp.float32) * attended_f, axis=2).T
        key_back, value_back = (
            lax.all_gather(key_rows, "fsdp", axis=0, tiled=True),
            lax.all_gather(value_rows, "fsdp", axis=0, tiled=True),
        )
        layout_back = key_layout(key_back, value_back, segment, position, head_count)
        d_queries, key_terms, d_buckets = attend_back(
            queries_heads,
            layout_back,
            seg_query,
            pos_query,
            rel_bucket,
            bucket_edges,
            max_offset,
            log_total,
            d_attended_heads,
            row_delta,
        )
        d_keys, d_values = key_terms
        group_rows = d_keys.shape[0] * d_keys.shape[1]
        d_keys_own, d_values_own = (
            lax.psum_scatter(
                d_keys.reshape(group_rows, model_width).astype(jnp.bfloat16),
                "fsdp",
                scatter_dimension=0,
                tiled=True,
            ).astype(jnp.float32),
            lax.psum_scatter(
                d_values.reshape(group_rows, model_width).astype(jnp.bfloat16),
                "fsdp",
                scatter_dimension=0,
                tiled=True,
            ).astype(jnp.float32),
        )
        acc_buckets = acc_buckets + d_buckets
        d_queries_low = d_queries.reshape(tok_rows, model_width).astype(jnp.bfloat16)
        d_keys_low = d_keys_own.astype(jnp.bfloat16)
        d_values_low = d_values_own.astype(jnp.bfloat16)
        acc_query = acc_query + jnp.einsum(
            "td,te->de", normed1, d_queries_low, preferred_element_type=jnp.float32
        )
        acc_key = acc_key + jnp.einsum(
            "td,te->de", normed1, d_keys_low, preferred_element_type=jnp.float32
        )
        acc_value = acc_value + jnp.einsum(
            "td,te->de", normed1, d_values_low, preferred_element_type=jnp.float32
        )
        d_normed1 = (
            jnp.einsum("te,de->td", d_queries_low, query_weight, preferred_element_type=jnp.float32)
            + jnp.einsum("te,de->td", d_keys_low, key_weight, preferred_element_type=jnp.float32)
            + jnp.einsum(
                "te,de->td", d_values_low, value_weight, preferred_element_type=jnp.float32
            )
        )
        d_rows_norm, d_gain_one = norm_back_rows(dealt_rows, scale_one, gain_one, d_normed1)
        acc_gain_one = acc_gain_one + d_gain_one
        d_dealt = d_mid + d_rows_norm
        returned = lax.all_to_all(
            d_dealt.astype(jnp.bfloat16), "fsdp", split_axis=0, concat_axis=0, tiled=True
        ).astype(d_dealt.dtype)
        grads_list.append(jnp.zeros_like(returned).at[take_rows].set(returned))
    acc_rel = acc_buckets.reshape(-1)
    summed = (
        lax.psum_scatter(acc_gain_one, ("dp", "fsdp"), scatter_dimension=0, tiled=True),
        lax.psum_scatter(acc_gain_two, ("dp", "fsdp"), scatter_dimension=0, tiled=True),
        lax.psum_scatter(acc_rel, ("dp", "fsdp"), scatter_dimension=0, tiled=True),
        lax.psum_scatter(acc_query, ("dp", "fsdp"), scatter_dimension=0, tiled=True),
        lax.psum_scatter(acc_key, ("dp", "fsdp"), scatter_dimension=0, tiled=True),
        lax.psum_scatter(acc_value, ("dp", "fsdp"), scatter_dimension=0, tiled=True),
        lax.psum_scatter(acc_output, ("dp", "fsdp"), scatter_dimension=0, tiled=True),
        lax.psum_scatter(acc_inner, ("dp", "fsdp"), scatter_dimension=0, tiled=True),
        lax.psum_scatter(acc_outer, ("dp", "fsdp"), scatter_dimension=0, tiled=True),
    )
    return (
        jnp.stack(outputs_list),
        jnp.stack(grads_list),
        summed[0],
        summed[1],
        summed[2],
        summed[3],
        summed[4],
        summed[5],
        summed[6],
        summed[7],
        summed[8],
    )


VMEM = pl.BlockSpec(memory_space=pltpu.VMEM)
SMEM = pl.BlockSpec(memory_space=pltpu.SMEM)
ANYWHERE = pl.BlockSpec(memory_space=pl.ANY)
LIMIT = 58 * 1024 * 1024
FIRST_AXIS = ("x", "x", "y", "x")
FWD_PARTS = 3
FWD_AHEAD = 2
FWD_OWN = (-1, 2, 8, 14, 20, 27, 34)
FWD_NEAR = (8, 14, 20, 26, 32, 38, 40)
FWD_SIDE = (41, 41, 41, 41, 41, 41, 41)
FWD_GRADS = 34
FFN_CHUNK = 768
BWD_PARTS = 3
BWD_AHEAD = 4
BWD_SIDE = (12, 14, 20, 20, 24, 26, 28)
BWD_NEAR = (18, 22, 26, 24, 28, 30, 34)


def shaped(*shape, dtype=jnp.bfloat16):
    return jax.ShapeDtypeStruct(shape, dtype)


def params(collective_id=None):
    if collective_id is None:
        return pltpu.CompilerParams(vmem_limit_bytes=LIMIT)
    return pltpu.CompilerParams(
        collective_id=collective_id, has_side_effects=True, vmem_limit_bytes=LIMIT
    )


def dma(*shape):
    return pltpu.SemaphoreType.DMA(shape)


def gather_all(lens, deal, hid, one, two, rel, shards):
    count = len(shards) + 1
    return pl.pallas_call(
        functools.partial(gather_kernel, FIRST_AXIS),
        name="gather_all",
        out_shape=[
            shaped(1, 128, dtype=jnp.int32),
            shaped(*deal.shape[1:], dtype=jnp.int32),
            shaped(OWN, TILE, hid.shape[-1]),
            shaped(32, 16, 128),
        ]
        + [shaped(32, *s.shape) for s in shards],
        in_specs=[VMEM] + [ANYWHERE] * 2 + [VMEM] * 3 + [ANYWHERE] * (count - 1),
        out_specs=[ANYWHERE] * (3 + count),
        scratch_shapes=[
            pltpu.VMEM((2, 1, 128), jnp.int32), pltpu.VMEM((16, 128), jnp.float32), pltpu.VMEM((16, 128), jnp.bfloat16),
            dma(count, 10), dma(count, 10), dma(count), dma(2, 3), dma(OWN), dma(2), dma(2),
        ],
        compiler_params=params(0),
    )(lens, deal, hid, one, two, rel, *shards)


def attention_forward(lens, x, small, table, wq, wk, wv, grd, wo, wi, wu):
    heads, keys = (PAIRS, OWN, TILE, 128), (PAIRS, OWN, 2, TILE, 128)
    count = len(FWD_OWN)
    return pl.pallas_call(
        attn_fwd,
        name="attn_fwd",
        out_shape=[
            shaped(*heads), shaped(*keys), shaped(*keys), shaped(*x.shape),
            shaped(OWN, 2 * PAIRS, 1, TILE, dtype=jnp.float32),
            shaped(8, grd.shape[2], grd.shape[3] // 2),
            shaped(32, *wo.shape), shaped(32, *wi.shape), shaped(32, *wu.shape),
        ],
        in_specs=[SMEM] + [VMEM] * 6 + [ANYWHERE] * 4,
        out_specs=[VMEM] * 5 + [ANYWHERE] * 4,
        scratch_shapes=[
            pltpu.VMEM((5, 2 * PAIRS, 1, 2 * TILE), jnp.float32),
            pltpu.VMEM((2 * PAIRS, 5, TILE, TILE), jnp.float32),
            pltpu.VMEM((OWN, TILE, 128), jnp.bfloat16),
            pltpu.VMEM((TILES, TILE, 128), jnp.bfloat16),
            pltpu.VMEM((2, TILE, TILES * TILE), jnp.float32),
            pltpu.VMEM((OWN, TILE, 128), jnp.float32),
            dma(2), dma(2),
            dma(count, 10), dma(count, 10), dma(count), dma(2, 2, 2), dma(2, 4),
        ],
        compiler_params=params(1),
    )(lens, x, small, table, wq, wk, wv, grd, wo, wi, wu)


def landing(shapes, leads=((4, 4), (2, 4), (4,))):
    return [pltpu.VMEM((*lead, *b), jnp.bfloat16) for b in shapes for lead in leads]


def attention_backward(lens, q, k, v, log_total, d_att, delta, small, table, gwo, gwi, gwu):
    heads = (PAIRS, OWN, TILE, 128)
    block_i, block_u = (gwi.shape[2], gwi.shape[3] // BWD_PARTS), (gwu.shape[2], gwu.shape[3] // BWD_PARTS)
    blocks = [block_i, block_u] * BWD_PARTS + [gwo.shape[2:]]
    count = len(blocks)
    return pl.pallas_call(
        attn_bwd,
        name="attn_bwd",
        out_shape=[shaped(*heads)] * 3
        + [shaped(32, 128, dtype=jnp.float32)]
        + [shaped(4, *g.shape[2:]) for g in (gwo, gwi, gwu)],
        in_specs=[SMEM] + [VMEM] * 8 + [ANYWHERE] * 3,
        out_specs=[VMEM] * 4 + [ANYWHERE] * 3,
        scratch_shapes=[pltpu.VMEM((5, 2 * PAIRS, 1, 2 * TILE), jnp.float32)] * 2
        + [pltpu.VMEM((2 * PAIRS, 5, TILE, TILE), jnp.float32)] * 2
        + [pltpu.VMEM((OWN, TILE, 128), jnp.bfloat16), pltpu.VMEM((TILES, TILE, 128), jnp.bfloat16)]
        + [pltpu.VMEM((TILES * TILE, 128), jnp.float32)] * 2
        + [pltpu.VMEM(heads, jnp.bfloat16)] * 4
        + [dma(2, PAIRS), dma(2, PAIRS), dma(count, 10), dma(count, 10), dma(count, 3)]
        + landing(blocks, ((2, 4), (2, 4), (4,))),
        compiler_params=params(2),
    )(lens, q, k, v, log_total, d_att, delta, small, table, gwo, gwi, gwu)


def feed_forward(deal, x, att, wo, small, g_low, grd, wi, wu):
    tok, width = x.shape
    hidden = wi.shape[1]
    f32, bf16 = jnp.float32, jnp.bfloat16
    heads, stats = (PAIRS, OWN, TILE, 128), (OWN, 2 * PAIRS, 1, TILE)
    block_i, block_u = (32, width // 32, hidden), (32, hidden // 32, width)
    chunks = hidden // FFN_CHUNK
    return pl.pallas_call(
        ffn_kernel,
        name="feed_forward",
        out_shape=[
            shaped(tok, width, dtype=f32), shaped(*heads), shaped(*stats, dtype=f32),
            shaped(4, 4, width // 32, width), shaped(32, 128, dtype=f32), shaped(4, 4, *block_i[1:]), shaped(4, 4, *block_u[1:]),
            shaped(2, 3 * TILE, width),
        ],
        in_specs=[VMEM] * 6 + [ANYWHERE] * 3,
        out_specs=[VMEM] * 5 + [ANYWHERE] * 3,
        scratch_shapes=[
            pltpu.VMEM((tok, width), bf16), pltpu.VMEM((tok, width), f32), pltpu.VMEM((tok, width), bf16),
            pltpu.VMEM((tok, width), f32), pltpu.VMEM((tok, hidden), bf16), pltpu.VMEM((tok, hidden), bf16),
            pltpu.VMEM((width, hidden), bf16), pltpu.VMEM((hidden, width), bf16),
            pltpu.VMEM((2, 32, width // 32, FFN_CHUNK), bf16), pltpu.VMEM((2, 32 // chunks, hidden // 32, width), bf16),
            pltpu.VMEM(g_low.shape, bf16),
            pltpu.VMEM((OWN, TILE, width), bf16), pltpu.VMEM((OWN, 2, TILE, width), bf16),
            pltpu.VMEM((2, 3 * TILE, width), bf16),
            pltpu.VMEM((chunks, 4, 4, width // 32, FFN_CHUNK), bf16), pltpu.VMEM((chunks, 4, hidden // 32, width), bf16),
            pltpu.VMEM((32, width // 32, width), bf16),
            dma(2, chunks), dma(2, chunks), dma(2, 2, 2), dma(2, 4), dma(2), dma(2),
            pltpu.SemaphoreType.DMA, pltpu.SemaphoreType.DMA, dma(chunks + 1, 5), dma(chunks + 1, 5),
        ],
        compiler_params=params(4),
    )(deal, x, att, wo, small, g_low, grd, wi, wu)


def tail(x, small, d_mid, dq, dk, dv, wq, wk, wv, g_two, g_rel):
    tok, width = x.shape
    block = (width // 32, width)
    blocks = [block, block, block, (16, 128)]
    count = len(blocks)
    return pl.pallas_call(
        tail_kernel,
        name="tail",
        out_shape=[shaped(2, 3, TILE, width), shaped(4, 16, 128)] + [shaped(4, *block)] * 3,
        in_specs=[VMEM] * 11,
        out_specs=[ANYWHERE] * 5,
        scratch_shapes=[
            pltpu.VMEM((3, tok, width), jnp.bfloat16), pltpu.VMEM((OWN, TILE, width), jnp.bfloat16),
            pltpu.VMEM((32, 16, 128), jnp.bfloat16),
        ]
        + [pltpu.VMEM((32, *block), jnp.bfloat16)] * 3
        + landing(blocks)
        + [dma(count, 10), dma(count, 10), dma(count, 1), dma(OWN), dma(2, 3)],
        compiler_params=params(3),
    )(x, small, d_mid, dq, dk, dv, wq, wk, wv, g_two, g_rel)


def last_sums(hid, gin, terms):
    f32 = jnp.float32
    lines = lambda n: shaped(1, n, dtype=f32)
    return pl.pallas_call(
        sum_kernel,
        name="last_sums",
        out_shape=[shaped(*hid.shape, dtype=f32), shaped(*gin.shape, dtype=f32), lines(24), lines(24), lines(H)]
        + [shaped(*t.shape[1:], dtype=f32) for t in terms[1:]],
        in_specs=[VMEM] * (2 + len(terms)),
        out_specs=[VMEM] * (4 + len(terms)),
        compiler_params=params(),
    )(hid, gin, *terms)


def on_device_packed(
    hidden_in, grad_out, gain_attn, gain_ffn, rel_bias,
    w_query, w_key, w_value, w_output, w_inner, w_outer,
    dealing, lengths, bucket_table,
):
    micro_count, tok_rows, width = hidden_in.shape
    matrix = lambda w: w.reshape(-1, w.shape[-1])
    table = bucket_table[None]
    grd = grad_out.reshape(2, 2, tok_rows // 2, width)
    lens_u, deal_u, x_own, small, wq, wk, wv = gather_all(
        lengths, dealing, hidden_in.reshape(2, 3, TILE, width),
        gain_attn[None], gain_ffn[None], rel_bias[None], (w_query, w_key, w_value),
    )
    wq, wk, wv = map(matrix, (wq, wk, wv))
    x_rows = matrix(x_own)
    q, k, v, att, log_total, g_low, wo, wi, wu = attention_forward(
        lens_u, x_rows, small, table, wq, wk, wv, grd, w_output, w_inner, w_outer
    )
    d_mid, d_att, delta, g_wo, g_two, g_wi, g_wu, hid = feed_forward(
        deal_u, x_rows, att, matrix(wo), small, g_low, grd, matrix(wi), matrix(wu)
    )
    dq, dk, dv, g_rel, t_wo, t_wi, t_wu = attention_backward(
        lens_u, q, k, v, log_total, d_att, delta, small, table, g_wo, g_wi, g_wu
    )
    gin, t_small, t_wq, t_wk, t_wv = tail(x_rows, small, d_mid, dq, dk, dv, wq, wk, wv, g_two, g_rel)
    hid, gin, s_one, s_two, s_rel, *grads = last_sums(hid, gin, (t_small, t_wq, t_wk, t_wv, t_wo, t_wi, t_wu))
    return (hid, gin.reshape(2, tok_rows, width), s_one[0], s_two[0], s_rel[0], *grads)


def solution(mesh):
    axes = ("dp", "fsdp")
    tokens, matrix, vector = P(None, axes, None), P(axes, None), P(axes)
    packed = mesh.shape["fsdp"] == 4 and mesh.shape["dp"] == 8
    return jax.shard_map(
        on_device_packed if packed else on_device,
        mesh=mesh,
        in_specs=(tokens, tokens, vector, vector, vector)
        + (matrix,) * 6
        + (P(None, "dp", None), P(None, "dp", None), P()),
        out_specs=(tokens, tokens, vector, vector, vector) + (matrix,) * 6,
        check_vma=False,
    )
```

```python
import functools
import math

import jax
import jax.numpy as jnp
from jax import lax
from jax.experimental import pallas as pl
from jax.experimental.pallas import tpu as pltpu
from jax.sharding import PartitionSpec as P

H = 12
BUCKETS = 32
EPSILON = 1e-06
NEG_FILL = -1e30
MESH = pl.DeviceIdType.MESH
TILE = 128
PAIRS = 6
OWN = 6
TILES = 12
FAR = 6
SEQS = 4


def lane_index(shape):
    return lax.broadcasted_iota(jnp.int32, shape, len(shape) - 1)


def row_index(shape):
    return lax.broadcasted_iota(jnp.int32, shape, len(shape) - 2)


def dot_nn(left, right):
    return lax.dot_general(left, right, (((1,), (0,)), ((), ())), preferred_element_type=jnp.float32)


def dot_nt(left, right):
    return lax.dot_general(left, right, (((1,), (1,)), ((), ())), preferred_element_type=jnp.float32)


def dot_tn(left, right):
    return lax.dot_general(left, right, (((0,), (0,)), ((), ())), preferred_element_type=jnp.float32)


def segments_of(places, lens_ref, count):
    edge = jnp.int32(0)
    found = jnp.zeros(places.shape, jnp.int32)
    for s in range(count - 1):
        edge = edge + lens_ref[0, s]
        found = found + (places >= edge).astype(jnp.int32)
    return found


def segment_tags(places, lens_ref, count, of_key):
    lane = lane_index(places.shape)
    hit = segments_of(places, lens_ref, count) == lane
    if of_key:
        return jnp.where((lane < count) & jnp.logical_not(hit), NEG_FILL, 0.0).astype(jnp.bfloat16)
    return jnp.where(hit, 1.0, 0.0).astype(jnp.bfloat16)


def one_hot(rows, columns):
    return jnp.where(rows == columns, 1.0, 0.0).astype(jnp.bfloat16)


def small_lines(small_ref, kind):
    flat = small_ref[...].reshape(32 * 16, 128)
    pick = one_hot(16 * row_index((32, 512)) + kind, lane_index((32, 512)))
    return dot_nn(pick, flat).astype(jnp.bfloat16)


def gain_row(small_ref, kind, width):
    lines = dot_nn(
        small_lines(small_ref, kind), one_hot(row_index((128, width)), lax.rem(lane_index((128, width)), 24))
    )
    own = lane_index((32, width)) // 24 == row_index((32, width))
    return jnp.sum(jnp.where(own, lines, 0.0), axis=0, keepdims=True)


def bucket_picks(table_ref, places):
    span = table_ref.shape[1]
    picked = one_hot(row_index((BUCKETS, span)), jnp.broadcast_to(table_ref[...], (BUCKETS, span)))
    places = jnp.clip(places, 0, span - 1)
    return dot_nn(picked, one_hot(row_index((span, 256)), jnp.broadcast_to(places, (span, 256)))).astype(jnp.bfloat16)


def class_places(cls, sign):
    lane = lane_index((1, 256))
    if cls >= 3:
        return jnp.full((1, 256), 0 if cls == 3 else 2 * TILE, jnp.int32)
    turn = jnp.where(lane < TILE, lane, lane - 2 * TILE)
    return TILE * (cls - 1) + sign * turn + TILE


def fill_rows(small_ref, table_ref, rows_ref, sign):
    rel = small_lines(small_ref, 2)
    for cls in range(5):
        made = dot_tn(rel, bucket_picks(table_ref, class_places(cls, sign)))
        for h in range(2 * PAIRS):
            rows_ref[cls, h] = made[h : h + 1, :]


def bucket_sums(hist_ref, table_ref):
    total = None
    for cls in range(5):
        if cls >= 3:
            places = class_places(cls, 1)
        else:
            places = TILE * (cls - 1) + 2 * TILE - 1 - lane_index((1, 256))
        hist = jnp.concatenate([hist_ref[cls, h] for h in range(2 * PAIRS)] + [jnp.zeros((4, 256), jnp.float32)], axis=0)
        term = lax.dot_general(
            bucket_picks(table_ref, places).astype(jnp.float32), hist, (((1,), (1,)), ((), ())),
            precision=lax.Precision.HIGHEST, preferred_element_type=jnp.float32,
        )
        total = term if total is None else total + term
    return total


def key_range(i):
    return max(0, 2 * i - FAR), min(TILES, 2 * i + FAR + 2)


def fill_bias(rows_ref, tiles_ref, heads):
    def one_head(h, carry):
        for cls in range(3):
            row = rows_ref[cls, h]
            wide = pltpu.roll(
                jnp.broadcast_to(row, (TILE, 2 * TILE)), 0, 1, stride=1, stride_axis=0
            )
            tiles_ref[h, cls + 1] = wide[:, :TILE]
        left = rows_ref[3, h, :, :TILE]
        right = rows_ref[4, h, :, :TILE]
        tiles_ref[h, 0] = jnp.broadcast_to(left, (TILE, TILE))
        tiles_ref[h, 4] = jnp.broadcast_to(right, (TILE, TILE))
        return carry

    lax.fori_loop(0, heads, one_head, 0)


def bias_class(kt, i, core):
    return jnp.clip(kt - 2 * i - core, -2, 2) + 2


def make_tags(lens_ref, ext_q, ext_k):
    core = lax.rem(lax.axis_index("dp"), 2)
    for t in range(TILES):
        ext_k[t] = segment_tags(TILE * t + row_index((TILE, 128)), lens_ref, SEQS, True)
    for i in range(OWN):
        ext_q[i] = segment_tags(TILE * (2 * i + core) + row_index((TILE, 128)), lens_ref, SEQS, False)


def attn_fwd(
    lens_ref, x_ref, small_ref, table_ref, wq_ref, wk_ref, wv_ref, grd_in, wi_in, wu_in,
    q_ref, k_ref, v_ref, att_ref, log_ref, g_low, wi_all, wu_all,
    rows_ref, bias_ref, ext_q, ext_k, s_ref, log_acc, send_sem, recv_sem,
    w_send, w_recv, w_local, g_send, g_recv,
):
    y, x, core, z = coordinates()
    sibling = place(y, x, 1 - core, z)
    greet()
    pieces = []
    part_i, part_u = wi_in.shape[1] // FWD_PARTS, wu_in.shape[1] // FWD_PARTS
    for n in range(FWD_PARTS):
        pieces.append((wi_in, wi_all, (n * part_i, part_i), "xy"[(n + 1) % 2]))
        pieces.append((wu_in, wu_all, (n * part_u, part_u), "xy"[n % 2]))
    gather = Gather(pieces, w_send, w_recv, w_local)
    grads = list(grad_sends(grd_in, g_low, 0, g_send, g_recv))
    events = {}

    def plan(at, step, *args):
        events.setdefault(at, []).append(functools.partial(step, *args))

    for n in range(len(pieces)):
        plan(FWD_OWN[n], gather.spread_own, n)
        if n + FWD_AHEAD < len(pieces):
            plan(FWD_OWN[n], gather.start, n + FWD_AHEAD)
        plan(FWD_NEAR[n], gather.spread_near, n)
        plan(FWD_SIDE[n], gather.spread_side, n)
    plan(FWD_GRADS, start_all, grads)

    greeted()
    for n in range(FWD_AHEAD):
        gather.start(n)
    rows = x_ref[...].astype(jnp.float32)
    scale = lax.rsqrt(jnp.mean(rows * rows, axis=1, keepdims=True) + EPSILON)
    normed = (rows * scale * gain_row(small_ref, 0, rows.shape[1])).astype(jnp.bfloat16)

    def project(w_ref):
        return dot_nn(normed, w_ref[...]).astype(jnp.bfloat16)

    copies = []
    for n, (w_ref, all_ref) in enumerate(((wk_ref, k_ref), (wv_ref, v_ref))):
        made = project(w_ref)
        for hp in range(PAIRS):
            for i in range(OWN):
                all_ref[hp, i, core] = made[TILE * i : TILE * (i + 1), 128 * hp : 128 * (hp + 1)]
        copy = remote(all_ref.at[:, :, core], all_ref.at[:, :, core], send_sem.at[n], recv_sem.at[n], sibling)
        copy.start()
        copies.append(copy)
    made = project(wq_ref)
    for hp in range(PAIRS):
        for i in range(OWN):
            q_ref[hp, i] = made[TILE * i : TILE * (i + 1), 128 * hp : 128 * (hp + 1)]
    make_tags(lens_ref, ext_q, ext_k)
    for i in range(OWN):
        log_acc[i] = jnp.zeros((TILE, 128), jnp.float32)
    for step in events.pop(-1, ()):
        step()
    fill_rows(small_ref, table_ref, rows_ref, 1)
    fill_bias(rows_ref, bias_ref, 2 * PAIRS)
    for n, all_ref in enumerate((k_ref, v_ref)):
        block = all_ref.at[:, :, 1 - core]
        remote(block, block, send_sem.at[n], recv_sem.at[n], sibling).wait_recv()

    lane = lane_index((TILE, 128))

    def one_pair(hp, carry):
        for i in range(OWN):
            run_events(events, hp, i)
            lo, hi = key_range(i)
            width = (hi - lo) * TILE
            pair = q_ref[hp, i]
            tags = ext_q[i]
            zero = jnp.zeros_like(pair)
            left = jnp.concatenate(
                [
                    jnp.concatenate([jnp.where(lane < 64, pair, zero), tags], axis=1),
                    jnp.concatenate([jnp.where(lane < 64, zero, pair), tags], axis=1),
                ],
                axis=0,
            )
            keys = k_ref[hp, lo // 2 : hi // 2].reshape(width, 128)
            right = jnp.concatenate([keys, ext_k[lo:hi].reshape(width, 128)], axis=1)
            raw = dot_nt(left, right)
            tops = []
            for e in range(2):
                top = None
                for kt in range(lo, hi):
                    at = (kt - lo) * TILE
                    part = raw[e * TILE : (e + 1) * TILE, at : at + TILE]
                    if -1 <= kt - 2 * i <= 2:
                        part = part + bias_ref[2 * hp + e, bias_class(kt, i, core)]
                    else:
                        part = part + rows_ref[3 if kt < 2 * i else 4, 2 * hp + e, :, :TILE]
                    s_ref[e, :, at : at + TILE] = part
                    top = part if top is None else jnp.maximum(top, part)
                tops.append(jnp.max(top, axis=1, keepdims=True))
            outs = []
            for e in range(2):
                total = None
                found = []
                for kt in range(lo, hi):
                    at = (kt - lo) * TILE
                    weight = jnp.exp(s_ref[e, :, at : at + TILE] - tops[e])
                    total = weight if total is None else total + weight
                    found.append(weight.astype(jnp.bfloat16))
                total = jnp.sum(total, axis=1, keepdims=True)
                probs = jnp.concatenate(found, axis=1)
                values = v_ref[hp, lo // 2 : hi // 2].reshape(width, 128)
                outs.append(dot_nn(probs, values) / total)
                log_acc[i] = jnp.where(lane == 2 * hp + e, tops[e] + jnp.log(total), log_acc[i])
            att_ref[TILE * i : TILE * (i + 1), pl.ds(pl.multiple_of(128 * hp, 128), 128)] = jnp.where(
                lane < 64, outs[0], outs[1]
            ).astype(jnp.bfloat16)
        return carry

    lax.fori_loop(0, PAIRS, one_pair, 0)
    for i in range(OWN):
        turned = log_acc[i].T
        for h in range(2 * PAIRS):
            log_ref[i, h] = turned[h : h + 1, :]
    late(events)
    share_grads(g_low, g_send, g_recv)
    for n in range(len(pieces)):
        gather.finish(n)
    end_grads(grads, g_low, g_send, g_recv)
    for copy in copies:
        copy.wait_send()


def attn_bwd(
    lens_ref, q_ref, k_ref, v_ref, log_ref, do_ref, delta_ref, small_ref, table_ref, gwo, gwi, gwu, dealt,
    dq_ref, dk_ref, dv_ref, rel_ref, two, twi, twu, hid_out,
    rows_ref, hist_ref, bias_ref, acc_ref, ext_q, ext_k, dk_acc, dv_acc, out_k, out_v, got_k, got_v, send_sem, recv_sem,
    w_send, w_recv, w_local, h_send, h_recv, *landed,
):
    y, x, core, z = coordinates()
    sibling = place(y, x, 1 - core, z)
    greet()
    plain = []
    part_i, part_u = gwi.shape[3] // BWD_PARTS, gwu.shape[3] // BWD_PARTS
    for n in range(BWD_PARTS):
        plain.append((gwi, twi, (n * part_i, part_i), "xy"[n % 2]))
        plain.append((gwu, twu, (n * part_u, part_u), "xy"[(n + 1) % 2]))
    plain.append((gwo, two, None, "x"))
    count = len(plain)
    scatter = LateScatter(
        [item + tuple(landed[3 * n : 3 * n + 3]) for n, item in enumerate(plain)], w_send, w_recv, w_local
    )
    events = {}

    def plan(at, step, *args):
        events.setdefault(at, []).append(functools.partial(step, *args))

    for n in range(count):
        plan(BWD_SIDE[n], scatter.sum_side, n)
        if n + BWD_AHEAD < count:
            plan(BWD_SIDE[n], scatter.start, n + BWD_AHEAD)
        plan(BWD_NEAR[n], scatter.sum_near, n)
    make_tags(lens_ref, ext_q, ext_k)
    greeted()
    for n in range(BWD_AHEAD):
        scatter.start(n)
    deals = list(dealt_sends(dealt, hid_out, hid_out.shape[2], h_send, h_recv))
    start_all(deals)
    acc_ref[...] = jnp.zeros_like(acc_ref)
    fill_rows(small_ref, table_ref, rows_ref, -1)
    fill_bias(rows_ref, bias_ref, 2 * PAIRS)
    for step in events.pop(-1, ()):
        step()
    lane = lane_index((TILE, 128))

    def one_pair(hp, carry):
        dk_acc[...] = jnp.zeros_like(dk_acc)
        dv_acc[...] = jnp.zeros_like(dv_acc)
        for i in range(OWN):
            run_events(events, hp, i)
            lo, hi = key_range(i)
            width = (hi - lo) * TILE
            pair, d_pair = q_ref[hp, i], do_ref[hp, i]
            tags = ext_q[i]
            zero = jnp.zeros_like(pair)
            q_two = jnp.concatenate([jnp.where(lane < 64, pair, zero), jnp.where(lane < 64, zero, pair)], axis=0)
            d_two = jnp.concatenate([jnp.where(lane < 64, d_pair, zero), jnp.where(lane < 64, zero, d_pair)], axis=0)
            q_ext = jnp.concatenate([q_two, jnp.concatenate([tags, tags], axis=0)], axis=1)
            keys = k_ref[hp, lo // 2 : hi // 2].reshape(width, 128)
            values = v_ref[hp, lo // 2 : hi // 2].reshape(width, 128)
            k_ext = jnp.concatenate([keys, ext_k[lo:hi].reshape(width, 128)], axis=1)
            raw = dot_nt(k_ext, q_ext)
            d_probs = dot_nt(values, d_two)
            p_rows, s_rows = [], []
            for kt in range(lo, hi):
                at = (kt - lo) * TILE
                p_two, s_two = [], []
                for e in range(2):
                    head = 2 * hp + e
                    part = raw[at : at + TILE, e * TILE : (e + 1) * TILE]
                    near = -1 <= kt - 2 * i <= 2
                    cls = bias_class(kt, i, core) if near else (0 if kt < 2 * i else 4)
                    if near:
                        part = part + bias_ref[head, cls]
                    else:
                        part = part + rows_ref[3 if kt < 2 * i else 4, head, :, :TILE]
                    probs = jnp.exp(part - log_ref[i, head])
                    slope = probs * (
                        d_probs[at : at + TILE, e * TILE : (e + 1) * TILE] - delta_ref[i, head]
                    )
                    acc_ref[head, cls] += slope
                    p_two.append(probs.astype(jnp.bfloat16))
                    s_two.append(slope.astype(jnp.bfloat16))
                p_rows.append(jnp.concatenate(p_two, axis=1))
                s_rows.append(jnp.concatenate(s_two, axis=1))
            probs_t = jnp.concatenate(p_rows, axis=0)
            slopes_t = jnp.concatenate(s_rows, axis=0)
            dv_acc[lo * TILE : hi * TILE, :] += dot_nn(probs_t, d_two)
            dk_acc[lo * TILE : hi * TILE, :] += dot_nn(slopes_t, q_two)
            d_q = dot_tn(slopes_t, keys)
            dq_ref[hp, i] = jnp.where(lane < 64, d_q[:TILE], d_q[TILE:]).astype(jnp.bfloat16)
        for acc, own, out in ((dk_acc, dk_ref, out_k), (dv_acc, dv_ref, out_v)):
            for i in range(OWN):
                own[hp, i] = acc[pl.ds((2 * i + core) * TILE, TILE), :].astype(jnp.bfloat16)
                out[hp, i] = acc[pl.ds((2 * i + 1 - core) * TILE, TILE), :].astype(jnp.bfloat16)
        for n, (out, got) in enumerate(((out_k, got_k), (out_v, got_v))):
            pltpu.make_async_remote_copy(
                out.at[hp], got.at[hp], send_sem.at[n, hp], recv_sem.at[n, hp],
                device_id=sibling, device_id_type=MESH,
            ).start()
        return carry

    lax.fori_loop(0, PAIRS, one_pair, 0)
    flip = (row_index((TILE, TILE)) + lane == TILE - 1).astype(jnp.float32)

    def one_head(h, carry):
        for cls in range(3):
            tile = jnp.dot(flip, acc_ref[h, cls + 1], precision=lax.Precision.HIGHEST)
            wide = jnp.concatenate([tile, jnp.zeros((TILE, TILE), jnp.float32)], axis=1)
            wide = pltpu.roll(wide, 0, 1, stride=1, stride_axis=0)
            hist_ref[cls, h] = jnp.sum(wide, axis=0, keepdims=True)
        for n, cls in ((3, 0), (4, 4)):
            row = jnp.sum(acc_ref[h, cls], axis=0, keepdims=True)
            hist_ref[n, h] = jnp.concatenate([row, jnp.zeros_like(row)], axis=1)
        return carry

    lax.fori_loop(0, 2 * PAIRS, one_head, 0)

    rel_ref[...] = jnp.zeros_like(rel_ref)
    rel_ref[:, :16] = bucket_sums(hist_ref, table_ref)

    def finish(hp, carry):
        for n, (out, got, own) in enumerate(((out_k, got_k, dk_ref), (out_v, got_v, dv_ref))):
            copy = pltpu.make_async_remote_copy(
                out.at[hp], got.at[hp], send_sem.at[n, hp], recv_sem.at[n, hp],
                device_id=sibling, device_id_type=MESH,
            )
            copy.wait_send()
            copy.wait_recv()
            own[hp] = (own[hp].astype(jnp.float32) + got[hp].astype(jnp.float32)).astype(jnp.bfloat16)
        return carry

    lax.fori_loop(0, PAIRS, finish, 0)
    late(events)
    for n in range(count):
        scatter.finish(n)
    for item in deals:
        sent(*item)
    for m in range(2):
        remote(hid_out.at[m], hid_out.at[m], h_send.at[0], h_recv.at[m], sibling).wait_recv()


def norm_back(rows_in, scale, gain, grad_normed):
    scaled = grad_normed * gain
    grad_gain = jnp.sum(grad_normed * rows_in * scale, axis=0, keepdims=True)
    shared = jnp.mean(scaled * rows_in, axis=1, keepdims=True)
    return scale * scaled - rows_in * (scale * scale * scale * shared), grad_gain


def join_pairs(pairs_ref, joined_ref):
    for hp in range(PAIRS):
        joined_ref[:, 128 * hp : 128 * (hp + 1)] = (
            pairs_ref[hp].reshape(OWN * TILE, 128).astype(joined_ref.dtype)
        )


def gain_block(row):
    width = row.shape[1]
    lines = jnp.where(lane_index((32, width)) // 24 == row_index((32, width)), row, 0.0)
    pick = (lax.rem(row_index((width, 128)), 24) == lane_index((width, 128))).astype(jnp.float32)
    return jnp.dot(lines, pick, precision=lax.Precision.HIGHEST)


def ffn_kernel(
    deal_ref, x_ref, att_ref, wo_ref, small_ref, g_low, grd_in, wi_in, wu_in,
    dmid_ref, datt_ref, delta_ref, gwo_ref, two_ref, dealt, gwi, gwu, hid_out,
    grad_ref, mid_ref, normed_ref, total_ref, active_ref, slope_ref, wi_ref, wu_ref, gwi_two, gwu_two, g_high,
    res_ref, res_all, got_i, got_u, gwo_own, in_sem, out_sem, g_send, g_recv, h_send, h_recv, e_send, e_recv,
    c_send, c_recv, pick_ref,
):
    y, x, core, z = coordinates()
    sibling = place(y, x, 1 - core, z)
    greet()
    width = x_ref.shape[1]
    half = width // 2
    chunk = FFN_CHUNK
    chunks = wi_ref.shape[1] // chunk

    def bring(j):
        span = pl.ds(chunk * j, chunk)
        return (
            pltpu.make_async_copy(wi_in.at[:, span], wi_ref.at[:, span], in_sem.at[0, j]),
            pltpu.make_async_copy(wu_in.at[span], wu_ref.at[span], in_sem.at[1, j]),
        )

    for j in range(chunks):
        for copy in bring(j):
            copy.start()
    grads = list(grad_sends(grd_in, g_high, half, g_send, g_recv))
    gain = gain_row(small_ref, 1, width)
    mid = x_ref[...].astype(jnp.float32) + dot_nn(att_ref[...], wo_ref[...])
    mid_ref[...] = mid
    scale = lax.rsqrt(jnp.mean(mid * mid, axis=1, keepdims=True) + EPSILON)
    normed_ref[...] = (mid * scale * gain).astype(jnp.bfloat16)
    greeted()
    start_all(grads)

    def rows_of(i):
        return slice(TILE * i, TILE * (i + 1))

    for i in range(OWN):
        pick_ref[rows_of(i), :] = one_hot((2 * i + core) * TILE + row_index((TILE, TILES * TILE)), deal_ref[...])
    grad_ref[:, :half] = dot_nn(pick_ref[...], g_low[...].reshape(TILES * TILE, half)).astype(jnp.bfloat16)
    for j in range(chunks):
        span = slice(chunk * j, chunk * (j + 1))
        for copy in bring(j):
            copy.wait()
        inner = dot_nn(normed_ref[...], wi_ref[:, span])
        cdf = 0.5 * (1.0 + lax.erf(inner * (1.0 / math.sqrt(2.0))))
        active = (inner * cdf).astype(jnp.bfloat16)
        active_ref[:, span] = active
        slope = cdf + inner * (jnp.exp(-0.5 * inner * inner) * (1.0 / math.sqrt(2.0 * math.pi)))
        slope_ref[:, span] = slope.astype(jnp.bfloat16)
        term = dot_nn(active, wu_ref[span, :])
        total_ref[...] = term if j == 0 else total_ref[...] + term
    result = (mid_ref[...] + total_ref[...]).astype(jnp.bfloat16).reshape(OWN, TILE, width)
    res_ref[...] = result
    res_copy = remote(res_ref, res_all.at[:, core], e_send, e_recv, sibling)
    res_copy.start()
    for i in range(OWN):
        res_all[i, core] = result[i]
    share_grads(g_high, g_send, g_recv)

    end_grads(grads, g_high, g_send, g_recv)
    grad_ref[:, half:] = dot_nn(pick_ref[...], g_high[...].reshape(TILES * TILE, half)).astype(jnp.bfloat16)
    remote(res_ref, res_all.at[:, 1 - core], e_send, e_recv, sibling).wait_recv()
    lane = lane_index((TILE, TILE))
    for b in range(OWN):
        at = pl.multiple_of((OWN * core + b) * TILE, TILE)
        turned = jnp.broadcast_to(deal_ref[:, pl.ds(at, TILE)].astype(jnp.float32), (TILE, TILE)).T
        turned = turned.astype(jnp.int32)
        for t in range(TILES):
            pick_ref[rows_of(b), TILE * t : TILE * (t + 1)] = one_hot(turned, TILE * t + lane)
    made = dot_nn(pick_ref[...], res_all[...].reshape(TILES * TILE, width)).astype(jnp.bfloat16)
    dealt[...] = made.reshape(dealt.shape)
    deals = list(dealt_sends(dealt, hid_out, 0, h_send, h_recv))
    start_all(deals)

    def swap(j):
        slot, there = j % 2, 4 * (1 - core)
        copies = [remote(gwu_two.at[slot, pl.ds(there, 4)], got_u.at[j], c_send.at[j, 4], c_recv.at[j, 4], sibling)]
        for k in range(4):
            copies.append(
                remote(
                    gwi_two.at[slot, pl.ds(8 * k + there, 4)], got_i.at[j, k],
                    c_send.at[j, k], c_recv.at[j, k], sibling,
                )
            )
        return copies

    def take(j):
        return (
            pltpu.make_async_copy(got_i.at[j], gwi.at[:, :, :, pl.ds(chunk * j, chunk)], out_sem.at[0, j]),
            pltpu.make_async_copy(got_u.at[j], gwu.at[j], out_sem.at[1, j]),
        )

    def combine(j):
        slot, here = j % 2, 4 * core
        for copy in swap(j):
            copy.wait_recv()
        for n in range(4):
            got_u[j, n] = got_u[j, n] + gwu_two[slot, here + n]
            for k in range(4):
                got_i[j, k, n] = got_i[j, k, n] + gwi_two[slot, 8 * k + here + n]
        for copy in take(j):
            copy.start()
        for copy in swap(j):
            copy.wait_send()

    for j in range(chunks):
        span = slice(chunk * j, chunk * (j + 1))
        d_inner = (
            dot_nt(grad_ref[...], wu_ref[span, :]) * slope_ref[:, span].astype(jnp.float32)
        ).astype(jnp.bfloat16)
        made = dot_tn(active_ref[:, span], grad_ref[...])
        gwu_two[j % 2] = made.astype(jnp.bfloat16).reshape(gwu_two.shape[1:])
        made = dot_tn(normed_ref[...], d_inner)
        gwi_two[j % 2] = made.reshape(32, -1, chunk).astype(jnp.bfloat16)
        for copy in swap(j):
            copy.start()
        term = dot_nt(d_inner, wi_ref[:, span])
        total_ref[...] = term if j == 0 else total_ref[...] + term
        if j:
            combine(j - 1)

    mid = mid_ref[...]
    scale = lax.rsqrt(jnp.mean(mid * mid, axis=1, keepdims=True) + EPSILON)
    d_rows, d_gain = norm_back(mid, scale, gain, total_ref[...])
    two_ref[...] = gain_block(d_gain)
    d_mid = grad_ref[...].astype(jnp.float32) + d_rows
    dmid_ref[...] = d_mid
    branch = d_mid.astype(jnp.bfloat16)
    made = dot_tn(att_ref[...], branch)
    gwo_own[...] = made.reshape(32, -1, width).astype(jnp.bfloat16)
    swaps = [
        remote(
            gwo_own.at[pl.ds(8 * k + 4 * (1 - core), 4)], gwo_ref.at[k], c_send.at[chunks, k], c_recv.at[chunks, k], sibling
        )
        for k in range(4)
    ]
    for copy in swaps:
        copy.start()
    combine(chunks - 1)
    d_att = dot_nt(branch, wo_ref[...]).astype(jnp.bfloat16)
    pick = (lane_index((16, width)) // 64 == row_index((16, width))).astype(jnp.float32)
    prod = d_att.astype(jnp.float32) * att_ref[...].astype(jnp.float32)
    sums = lax.dot_general(
        pick, prod, (((1,), (1,)), ((), ())), precision=lax.Precision.HIGHEST, preferred_element_type=jnp.float32
    )
    for hp in range(PAIRS):
        datt_ref[hp] = d_att[:, 128 * hp : 128 * (hp + 1)].reshape(OWN, TILE, 128)
    for i in range(OWN):
        for h in range(2 * PAIRS):
            delta_ref[i, h] = sums[h : h + 1, TILE * i : TILE * (i + 1)]
    for k, copy in enumerate(swaps):
        copy.wait_recv()
        for n in range(4):
            gwo_ref[k, n] = gwo_ref[k, n] + gwo_own[8 * k + 4 * core + n]
        copy.wait_send()
    for j in range(chunks):
        for copy in take(j):
            copy.wait()
    res_copy.wait_send()
    for item in deals:
        sent(*item)
    for m in range(2):
        remote(hid_out.at[m], hid_out.at[m], h_send.at[0], h_recv.at[m], sibling).wait_recv()


def tail_kernel(
    x_ref, small_ref, g_two, g_rel, dmid_in, dq_in, dk_in, dv_in, wq_in, wk_in, wv_in,
    gin_out, tsmall, tq, tk, tv,
    dmid_ref, w_ref, join_ref, normed_ref, back_out, small, gq, gk, gv, *scratch,
):
    y, x, c, z = coordinates()
    sibling = place(y, x, 1 - c, z)
    owner, micro = z // 2, lax.rem(z, 2)
    greet()
    plain = [(gk, tk, None, "x"), (gv, tv, None, "y"), (gq, tq, None, "x"), (small, tsmall, None, "y")]
    count = len(plain)
    w_send, w_recv, w_local, b_send, b_recv, in_sem = scratch[3 * count :]
    scatter = Scatter(
        [item + tuple(scratch[3 * n : 3 * n + 3]) for n, item in enumerate(plain)], w_send, w_recv, w_local
    )
    grads_in = []
    for n, (w_in, pairs) in enumerate(((wq_in, dq_in), (wk_in, dk_in), (wv_in, dv_in))):
        copies = [pltpu.make_async_copy(w_in, w_ref.at[n], in_sem.at[n, PAIRS])]
        for hp in range(PAIRS):
            copies.append(
                pltpu.make_async_copy(
                    pairs.at[hp], join_ref.at[n, :, :, pl.ds(128 * hp, 128)], in_sem.at[n, hp]
                )
            )
        for copy in copies:
            copy.start()
        grads_in.append(copies)
    dmid_copy = pltpu.make_async_copy(dmid_in, dmid_ref, in_sem.at[3, 0])
    dmid_copy.start()

    def back_sends():
        for i in range(OWN):
            t = 2 * i + c
            z_to, l = t // 3, lax.rem(t, 3)
            yield (
                back_out.at[i], gin_out.at[micro, l], b_send.at[i], b_recv.at[micro, l],
                place(y, x, owner, z_to), (owner == c) & (z_to == z),
            )

    sends = list(back_sends())
    gain = gain_row(small_ref, 0, x_ref.shape[1])
    width = x_ref.shape[1]
    d_gain = None
    for half in range(2):
        tiles = slice(OWN // 2 * half, OWN // 2 * (half + 1))
        span = slice(TILE * tiles.start, TILE * tiles.stop)
        rows = x_ref[span, :].astype(jnp.float32)
        scale = lax.rsqrt(jnp.mean(rows * rows, axis=1, keepdims=True) + EPSILON)
        normed_ref[span, :] = (rows * scale * gain).astype(jnp.bfloat16)
        back = None
        for n in range(3):
            if half == 0:
                for copy in grads_in[n]:
                    copy.wait()
            term = dot_nt(join_ref[n, tiles].reshape(-1, width), w_ref[n])
            back = term if back is None else back + term
        d_rows, part = norm_back(rows, scale, gain, back)
        d_gain = part if d_gain is None else d_gain + part
        if half == 0:
            dmid_copy.wait()
        back_out[tiles] = (dmid_ref[span, :] + d_rows).astype(jnp.bfloat16).reshape(-1, TILE, width)
        if half == 0:
            greeted()
        start_all(sends[tiles])
    normed_t = normed_ref[...].T
    for n, (at, grad_ref) in enumerate(((1, gk), (2, gv), (0, gq))):
        made = dot_nn(normed_t, join_ref[at].reshape(-1, width))
        for r in range(32):
            grad_ref[r] = made[24 * r : 24 * (r + 1), :].astype(jnp.bfloat16)
        scatter.start(n)
    g_one = gain_block(d_gain)
    shape = (32, 16, 128)
    kind = lax.broadcasted_iota(jnp.int32, shape, 1)
    spread = lambda v: jnp.broadcast_to(v[:, None, :], shape)
    small[...] = jnp.where(
        kind == 0, spread(g_one), jnp.where(kind == 1, spread(g_two[...]), spread(g_rel[...]))
    ).astype(jnp.bfloat16)
    scatter.start(3)
    for n in range(count + 2):
        for back_by, stage in enumerate((scatter.sum_core, scatter.sum_side, scatter.sum_near)):
            if 0 <= n - back_by < count:
                stage(n - back_by)
    for n in range(count):
        scatter.finish(n)
    for item in sends:
        sent(*item)
    for m in range(2):
        for l in range(3):
            remote(back_out.at[0], gin_out.at[m, l], b_send.at[0], b_recv.at[m, l], sibling).wait_recv()


def coordinates():
    dp, z = lax.axis_index("dp"), lax.axis_index("fsdp")
    return dp // 4, lax.rem(dp // 2, 2), lax.rem(dp, 2), z


def place(y, x, c, z):
    return (4 * y + 2 * x + c, z)


def column(y, x, c):
    return 16 * y + 8 * x + 4 * c


def partners():
    y, x, c, z = coordinates()
    found = [place(1 - y, x, c, z), place(y, 1 - x, c, z)]
    for dc in range(2):
        for dz in range(4):
            if dc or dz:
                found.append(place(y, x, lax.rem(c + dc, 2), lax.rem(z + dz, 4)))
    return found


def greet():
    for partner in partners():
        pl.semaphore_signal(pltpu.get_barrier_semaphore(), inc=1, device_id=partner, device_id_type=MESH)


def greeted():
    pl.semaphore_wait(pltpu.get_barrier_semaphore(), len(partners()))


def remote(src, dst, send, recv, target):
    return pltpu.make_async_remote_copy(
        src, dst, send, recv, device_id=target, device_id_type=MESH
    )


def send_or_keep(src, dst, send, recv, target, here):
    @pl.when(jnp.logical_not(here))
    def _():
        remote(src, dst, send, recv, target).start()

    @pl.when(here)
    def _():
        pltpu.make_async_copy(src, dst, recv).start()


def sent(src, dst, send, recv, target, here):
    @pl.when(jnp.logical_not(here))
    def _():
        remote(src, dst, send, recv, target).wait_send()


def cut(ref, lead, part):
    return ref.at[lead] if part is None else ref.at[lead, slice(None), pl.ds(*part)]


def cut_shard(ref, part):
    return ref if part is None else ref.at[:, pl.ds(*part)]


class Gather:
    def __init__(self, pieces, send, recv, local):
        self.pieces, self.send, self.recv, self.local = pieces, send, recv, local
        self.y, self.x, self.c, self.z = coordinates()
        y, x, c, z = self.y, self.x, self.c, self.z
        self.sibling = place(y, x, 1 - c, z)
        self.mine = column(y, x, c)
        self.far = column(1 - y, 1 - x, c)
        by_x = (place(y, 1 - x, c, z), column(y, 1 - x, c))
        by_y = (place(1 - y, x, c, z), column(1 - y, x, c))
        self.sides = {"x": by_x + by_y, "y": by_y + by_x}

    def own_copy(self, n):
        shard, whole, part, _ = self.pieces[n]
        return pltpu.make_async_copy(
            cut_shard(shard, part), cut(whole, self.mine + self.z, part), self.local.at[n]
        )

    def z_copy(self, n, dz, came=False):
        shard, whole, part, _ = self.pieces[n]
        entry = self.mine + (lax.rem(self.z + 4 - dz, 4) if came else self.z)
        return remote(
            cut_shard(shard, part), cut(whole, entry, part), self.send.at[n, dz - 1], self.recv.at[n, dz - 1],
            place(self.y, self.x, self.c, lax.rem(self.z + dz, 4)),
        )

    def push(self, n, k, base, target):
        _, whole, part, _ = self.pieces[n]
        block = cut(whole, pl.ds(base, 4), part)
        return remote(block, block, self.send.at[n, k], self.recv.at[n, k], target)

    def start(self, n):
        self.own_copy(n).start()
        for dz in range(1, 4):
            self.z_copy(n, dz).start()

    def spread_own(self, n):
        near, _, side, _ = self.sides[self.pieces[n][3]]
        self.own_copy(n).wait()
        for dz in range(1, 4):
            self.z_copy(n, dz, True).wait_recv()
        for k, target in ((3, near), (4, side), (6, self.sibling)):
            self.push(n, k, self.mine, target).start()

    def spread_near(self, n):
        _, near_column, side, _ = self.sides[self.pieces[n][3]]
        self.push(n, 3, near_column, self.sibling).wait_recv()
        self.push(n, 5, near_column, side).start()
        self.push(n, 7, near_column, self.sibling).start()

    def spread_side(self, n):
        side_column = self.sides[self.pieces[n][3]][3]
        self.push(n, 4, side_column, self.sibling).wait_recv()
        self.push(n, 8, side_column, self.sibling).start()
        self.push(n, 5, self.far, self.sibling).wait_recv()
        self.push(n, 9, self.far, self.sibling).start()

    def finish(self, n):
        _, near_column, _, side_column = self.sides[self.pieces[n][3]]
        for k, base in ((6, self.mine), (7, near_column), (8, side_column), (9, self.far)):
            self.push(n, k, base + 4 - 8 * self.c, self.sibling).wait_recv()
        for dz in range(1, 4):
            self.z_copy(n, dz).wait_send()
        for k in range(3, 10):
            self.push(n, k, self.mine, self.sibling).wait_send()


class Scatter:
    def __init__(self, pieces, send, recv, local):
        self.pieces, self.send, self.recv, self.local = pieces, send, recv, local
        self.y, self.x, self.c, self.z = coordinates()
        y, x, c, z = self.y, self.x, self.c, self.z
        self.sibling = place(y, x, 1 - c, z)

    def sides(self, n):
        y, x, c, z = self.y, self.x, self.c, self.z
        by_x, by_y = place(y, 1 - x, c, z), place(1 - y, x, c, z)
        if self.pieces[n][3] == "x":
            return by_x, by_y, (lambda s, f: 2 * s + f), y, x
        return by_y, by_x, (lambda s, f: 2 * f + s), x, y

    def core_copy(self, n, k):
        grad, _, part, _, r1 = self.pieces[n][:5]
        return remote(
            cut(grad, pl.ds(8 * k + 4 * (1 - self.c), 4), part), r1.at[k],
            self.send.at[n, k], self.recv.at[n, k], self.sibling,
        )

    def side_copy(self, n, f_at):
        _, side, index, s, _ = self.sides(n)
        _, _, _, _, r1, r2, _ = self.pieces[n]
        return remote(
            r1.at[index(1 - s, f_at)], r2.at[f_at], self.send.at[n, 4 + f_at], self.recv.at[n, 4 + f_at], side
        )

    def near_copy(self, n):
        near, _, index, s, f = self.sides(n)
        _, _, _, _, r1, _, r3 = self.pieces[n]
        return remote(r1.at[index(s, 1 - f)], r3, self.send.at[n, 6], self.recv.at[n, 6], near)

    def z_copy(self, n, dz):
        _, _, index, s, f = self.sides(n)
        _, terms, part, _, r1, _, _ = self.pieces[n]
        z_to = lax.rem(self.z + dz, 4)
        return remote(
            r1.at[index(s, f), z_to], cut(terms, dz, part), self.send.at[n, 6 + dz], self.recv.at[n, 6 + dz],
            place(self.y, self.x, self.c, z_to),
        )

    def own_copy(self, n):
        _, _, index, s, f = self.sides(n)
        _, terms, part, _, r1, _, _ = self.pieces[n]
        return pltpu.make_async_copy(r1.at[index(s, f), self.z], cut(terms, 0, part), self.local.at[n, 0])

    def start(self, n):
        for k in range(4):
            self.core_copy(n, k).start()

    def sum_core(self, n):
        grad, _, part, _, r1 = self.pieces[n][:5]
        for k in range(4):
            self.core_copy(n, k).wait_recv()

            def one(j, carry, k=k):
                r1[k, j] = r1[k, j] + cut(grad, 8 * k + 4 * self.c + j, part)[...]
                return carry

            lax.fori_loop(0, 4, one, 0)
        for f_at in range(2):
            self.side_copy(n, f_at).start()

    def sum_side(self, n):
        _, _, index, s, _ = self.sides(n)
        _, _, _, _, r1, r2, _ = self.pieces[n]
        for f_at in range(2):
            self.side_copy(n, f_at).wait_recv()
            k = index(s, f_at)

            def one(j, carry, k=k, f_at=f_at):
                r1[k, j] = r1[k, j] + r2[f_at, j]
                return carry

            lax.fori_loop(0, 4, one, 0)
        self.near_copy(n).start()

    def sum_near(self, n):
        _, _, index, s, f = self.sides(n)
        _, _, _, _, r1, _, r3 = self.pieces[n]
        self.near_copy(n).wait_recv()
        k = index(s, f)

        def one(j, carry):
            r1[k, j] = r1[k, j] + r3[j]
            return carry

        lax.fori_loop(0, 4, one, 0)
        for dz in range(1, 4):
            self.z_copy(n, dz).start()
        self.own_copy(n).start()

    def finish(self, n):
        self.own_copy(n).wait()
        for dz in range(1, 4):
            self.z_copy(n, dz).wait_recv()
        for k in range(4):
            self.core_copy(n, k).wait_send()
        for f_at in range(2):
            self.side_copy(n, f_at).wait_send()
        self.near_copy(n).wait_send()
        for dz in range(1, 4):
            self.z_copy(n, dz).wait_send()


class LateScatter(Scatter):
    def side_copy(self, n, f_at):
        _, side, index, s, _ = self.sides(n)
        summed, _, part, _, _, r2, _ = self.pieces[n]
        return remote(
            cut(summed.at[index(1 - s, f_at)], pl.ds(0, 4), part), r2.at[f_at],
            self.send.at[n, 4 + f_at], self.recv.at[n, 4 + f_at], side,
        )

    def fetch(self, n, f_at):
        _, _, index, s, _ = self.sides(n)
        summed, _, part, _, own, _, _ = self.pieces[n]
        return pltpu.make_async_copy(
            cut(summed.at[index(s, f_at)], pl.ds(0, 4), part), own.at[f_at], self.local.at[n, 1 + f_at]
        )

    def near_copy(self, n):
        near, _, _, _, f = self.sides(n)
        _, _, _, _, _, r2, r3 = self.pieces[n]
        return remote(r2.at[1 - f], r3, self.send.at[n, 6], self.recv.at[n, 6], near)

    def z_copy(self, n, dz):
        f = self.sides(n)[4]
        _, terms, part, _, _, r2, _ = self.pieces[n]
        z_to = lax.rem(self.z + dz, 4)
        return remote(
            r2.at[f, z_to], cut(terms, dz, part), self.send.at[n, 6 + dz], self.recv.at[n, 6 + dz],
            place(self.y, self.x, self.c, z_to),
        )

    def own_copy(self, n):
        f = self.sides(n)[4]
        _, terms, part, _, _, r2, _ = self.pieces[n]
        return pltpu.make_async_copy(r2.at[f, self.z], cut(terms, 0, part), self.local.at[n, 0])

    def start(self, n):
        for f_at in range(2):
            self.side_copy(n, f_at).start()
            self.fetch(n, f_at).start()

    def sum_side(self, n):
        _, _, _, _, own, r2, _ = self.pieces[n]
        for f_at in range(2):
            self.side_copy(n, f_at).wait_recv()
            self.fetch(n, f_at).wait()

            def one(j, carry, f_at=f_at):
                r2[f_at, j] = r2[f_at, j] + own[f_at, j]
                return carry

            lax.fori_loop(0, 4, one, 0)
        self.near_copy(n).start()

    def sum_near(self, n):
        f = self.sides(n)[4]
        _, _, _, _, _, r2, r3 = self.pieces[n]
        self.near_copy(n).wait_recv()

        def one(j, carry):
            r2[f, j] = r2[f, j] + r3[j]
            return carry

        lax.fori_loop(0, 4, one, 0)
        for dz in range(1, 4):
            self.z_copy(n, dz).start()
        self.own_copy(n).start()

    def finish(self, n):
        self.own_copy(n).wait()
        for dz in range(1, 4):
            self.z_copy(n, dz).wait_recv()
        for f_at in range(2):
            self.side_copy(n, f_at).wait_send()
        self.near_copy(n).wait_send()
        for dz in range(1, 4):
            self.z_copy(n, dz).wait_send()


def run_events(events, hp, i):
    for at in range(PAIRS):
        todo = events.get(at * OWN + i, ())
        if todo:

            @pl.when(hp == at)
            def _(todo=todo):
                for step in todo:
                    step()


def late(events):
    for at in sorted(events):
        if at >= PAIRS * OWN:
            for step in events[at]:
                step()


def token_sends(hid_in, x_own, x_send, x_recv):
    y, x, c, z = coordinates()
    for m in range(2):
        for l in range(3):
            t = 3 * z + l
            core_to, z_to = lax.rem(t, 2), 2 * c + m
            yield (
                hid_in.at[m, l], x_own.at[t // 2], x_send.at[m, l], x_recv.at[t // 2],
                place(y, x, core_to, z_to), (core_to == c) & (z_to == z),
            )


def start_all(items):
    for item in items:
        send_or_keep(*item)


def grad_sends(grd_in, g_part, first, g_send, g_recv):
    y, x, c, z = coordinates()
    width = g_part.shape[2]
    for m in range(2):
        for half in range(2):
            z_to = 2 * c + m
            yield (
                grd_in.at[m, half, :, pl.ds(first, width)], g_part.at[2 * z + half], g_send.at[0, m, half],
                g_recv.at[0, z], place(y, x, half, z_to), (half == c) & (z_to == z),
            )


def dealt_sends(dealt, hid_part, first, h_send, h_recv):
    y, x, c, z = coordinates()
    owner, micro = z // 2, lax.rem(z, 2)
    for e in range(2):
        z_to = 2 * c + e
        yield (
            dealt.at[e, :, pl.ds(first, hid_part.shape[2])], hid_part.at[micro], h_send.at[e], h_recv.at[micro],
            place(y, x, owner, z_to), (owner == c) & (z_to == z),
        )


def share_copy(g_part, zs, core, g_send, g_recv):
    y, x, c, z = coordinates()
    block = g_part.at[2 * zs + core]
    return remote(
        block, block, g_send.at[1, zs // 2, zs % 2], g_recv.at[1, zs], place(y, x, 1 - c, z)
    )


def share_grads(g_part, g_send, g_recv):
    y, x, c, z = coordinates()
    for zs in range(4):
        block = g_part.at[2 * zs + c]
        remote(block, block, g_send.at[1, 0, 0], g_recv.at[0, zs], place(y, x, 1 - c, z)).wait_recv()
        share_copy(g_part, zs, c, g_send, g_recv).start()


def end_grads(items, g_part, g_send, g_recv):
    c = coordinates()[2]
    for zs in range(4):
        share_copy(g_part, zs, 1 - c, g_send, g_recv).wait_recv()
        share_copy(g_part, zs, c, g_send, g_recv).wait_send()
    for item in items:
        sent(*item)


def gather_kernel(first_axis, *refs):
    count = len(first_axis)
    lens_in, deal_in, hid_in, one_in, two_in, rel_in = refs[:6]
    shards = refs[6 : 5 + count]
    rest = refs[5 + count :]
    lens_u, deal_u, x_own = rest[:3]
    outs = rest[3 : 3 + count]
    lens_wide, rows_f, small, w_send, w_recv, w_local, x_send, x_recv, p_send, p_recv = rest[3 + count :]
    y, x, c, z = coordinates()
    sibling = place(y, x, 1 - c, z)
    greet()
    rows_f[...] = jnp.zeros_like(rows_f)
    rows_f[0:1, : one_in.shape[1]] = one_in[...].astype(jnp.float32)
    rows_f[1:2, : two_in.shape[1]] = two_in[...].astype(jnp.float32)
    rows_f[2:3, : rel_in.shape[1]] = rel_in[...].astype(jnp.float32)
    small[...] = rows_f[...].astype(jnp.bfloat16)
    lens_wide[...] = jnp.zeros_like(lens_wide)
    lens_wide[:, :, : lens_in.shape[2]] = lens_in[...]
    greeted()
    gather = Gather(
        [(s, o, None, a) for s, o, a in zip((small,) + tuple(shards), outs, first_axis)], w_send, w_recv, w_local
    )
    for n in range(count):
        gather.start(n)
    sends = list(token_sends(hid_in, x_own, x_send, x_recv))
    for item in sends:
        send_or_keep(*item)
    owner, micro = z // 2, lax.rem(z, 2)
    plans = []
    for n, (src, dst) in enumerate(((lens_wide, lens_u), (deal_in, deal_u))):
        plans.append((src.at[micro], dst, p_send.at[n], p_recv.at[n]))

    @pl.when(owner == c)
    def _():
        for src, dst, send, recv in plans:
            remote(src, dst, send, recv, sibling).start()
            pltpu.make_async_copy(src, dst, recv).start()

    for n in range(count):
        gather.spread_own(n)
    for n in range(count):
        gather.spread_near(n)
    for n in range(count):
        gather.spread_side(n)
    for n in range(count):
        gather.finish(n)
    for item in sends:
        sent(*item)
    for i in range(OWN):
        remote(hid_in.at[0, 0], x_own.at[i], x_send.at[0, 0], x_recv.at[i], sibling).wait_recv()
    for src, dst, send, recv in plans:
        remote(src, dst, send, recv, sibling).wait_recv()

    @pl.when(owner == c)
    def _():
        for src, dst, send, recv in plans:
            remote(src, dst, send, recv, sibling).wait_send()


def sum_terms(term):
    total = term[0].astype(jnp.float32)
    for dz in range(1, 4):
        total = total + term[dz].astype(jnp.float32)
    return total


def sum_kernel(
    hid_low, hid_high, gin_in, tsmall, tq, tk, tv, two, twi, twu,
    hid_out, gin_out, one_out, two_out, rel_out, gq, gk, gv, gwo, gwi, gwu,
):
    half = hid_low.shape[2]
    hid_out[:, :, :half] = hid_low[...].astype(jnp.float32)
    hid_out[:, :, half:] = hid_high[...].astype(jnp.float32)
    gin_out[...] = gin_in[...].astype(jnp.float32)
    small = sum_terms(tsmall)
    one_out[...] = small[0:1, : one_out.shape[1]]
    two_out[...] = small[1:2, : two_out.shape[1]]
    rel_out[...] = small[2:3, : rel_out.shape[1]]
    for term, out in ((tq, gq), (tk, gk), (tv, gv), (two, gwo), (twi, gwi), (twu, gwu)):
        out[...] = sum_terms(term)


def token_places(deal_order, lengths):
    seq_ends = jnp.cumsum(lengths)
    starts = seq_ends - lengths
    inside = (deal_order[:, None] >= starts[None, :]).astype(jnp.int32)
    segment = jnp.sum(inside, axis=1) - 1
    picked = (segment[:, None] == jnp.arange(lengths.shape[0], dtype=jnp.int32)[None, :]).astype(
        jnp.int32
    )
    position = deal_order - jnp.sum(picked * starts[None, :], axis=1)
    return (segment, position)


def rms_scale(rows_in):
    return lax.rsqrt(jnp.mean(rows_in * rows_in, axis=1, keepdims=True) + EPSILON)


def gelu_slope(values):
    normal_cdf = 0.5 * (1.0 + jax.scipy.special.erf(values * (1.0 / math.sqrt(2.0))))
    normal_pdf = jnp.exp(-0.5 * values * values) * (1.0 / math.sqrt(2.0 * math.pi))
    return normal_cdf + values * normal_pdf


def norm_back_rows(rows_in, scale, gain, grad_normed):
    scaled_grad = grad_normed * gain
    grad_gain = jnp.sum(grad_normed * rows_in * scale, axis=0)
    grad_rows = scale * scaled_grad - rows_in * scale * scale * scale * jnp.mean(
        scaled_grad * rows_in, axis=1, keepdims=True
    )
    return (grad_rows, grad_gain)


def key_layout(key_all, value_all, segment, position, head_count):
    rows_all = key_all.shape[0]
    block_rows = 512
    blocks = rows_all // block_rows
    return (
        key_all.reshape(blocks, block_rows, head_count, -1),
        value_all.reshape(blocks, block_rows, head_count, -1),
        segment.reshape(blocks, block_rows),
        position.reshape(blocks, block_rows),
    )


def block_scores(
    queries,
    key_block,
    seg_query,
    pos_query,
    seg_block,
    pos_block,
    rel_bucket,
    bucket_edges,
    max_offset,
):
    lower_edge, upper_edge = bucket_edges
    raw_scores = jnp.einsum("qhd,khd->hqk", queries, key_block, preferred_element_type=jnp.float32)
    offset = jnp.clip(pos_block[None, :] - pos_query[:, None], -max_offset, max_offset)
    bucket_hit = (
        (offset[:, :, None] >= lower_edge[None, None, :])
        & (offset[:, :, None] <= upper_edge[None, None, :])
    ).astype(jnp.float32)
    bias = jnp.einsum(
        "qkb,bh->hqk",
        bucket_hit,
        rel_bucket,
        precision=lax.Precision.HIGHEST,
        preferred_element_type=jnp.float32,
    )
    same_seq = (seg_query[:, None] == seg_block[None, :])[None]
    return (raw_scores + bias, same_seq, bucket_hit)


def attend(queries, layout, seg_query, pos_query, rel_bucket, bucket_edges, max_offset):
    key_blocks, value_blocks, seg_blocks, pos_blocks = layout
    query_count, head_count, head_size = queries.shape

    def measure(carry, block):
        row_top, row_total = carry
        key_block, seg_block, pos_block = block
        scores, same_seq, _ = block_scores(
            queries,
            key_block,
            seg_query,
            pos_query,
            seg_block,
            pos_block,
            rel_bucket,
            bucket_edges,
            max_offset,
        )
        scores = jnp.where(same_seq, scores, NEG_FILL)
        new_top = jnp.maximum(row_top, jnp.max(scores, axis=2))
        weights_now = jnp.where(same_seq, jnp.exp(scores - new_top[:, :, None]), 0.0)
        row_total = row_total * jnp.exp(row_top - new_top) + jnp.sum(weights_now, axis=2)
        return ((new_top, row_total), None)

    start = (
        jnp.full((head_count, query_count), NEG_FILL, jnp.float32),
        jnp.zeros((head_count, query_count), jnp.float32),
    )
    (row_top, row_total), _ = lax.scan(measure, start, (key_blocks, seg_blocks, pos_blocks))
    log_total = row_top + jnp.log(row_total)

    def collect(summed, block):
        key_block, value_block, seg_block, pos_block = block
        scores, same_seq, _ = block_scores(
            queries,
            key_block,
            seg_query,
            pos_query,
            seg_block,
            pos_block,
            rel_bucket,
            bucket_edges,
            max_offset,
        )
        probs = jnp.where(same_seq, jnp.exp(scores - log_total[:, :, None]), 0.0).astype(
            jnp.bfloat16
        )
        return (
            summed
            + jnp.einsum("hqk,khd->qhd", probs, value_block, preferred_element_type=jnp.float32),
            None,
        )

    attended_f, _ = lax.scan(
        collect, jnp.zeros((query_count, head_count, head_size), jnp.float32), layout
    )
    return (attended_f, log_total)


def attend_back(
    queries,
    layout,
    seg_query,
    pos_query,
    rel_bucket,
    bucket_edges,
    max_offset,
    log_total,
    d_attended,
    row_delta,
):

    def step(carry, block):
        d_queries, d_buckets = carry
        key_block, value_block, seg_block, pos_block = block
        scores, same_seq, bucket_hit = block_scores(
            queries,
            key_block,
            seg_query,
            pos_query,
            seg_block,
            pos_block,
            rel_bucket,
            bucket_edges,
            max_offset,
        )
        probs_f = jnp.where(same_seq, jnp.exp(scores - log_total[:, :, None]), 0.0)
        d_probs = jnp.einsum(
            "qhd,khd->hqk", d_attended, value_block, preferred_element_type=jnp.float32
        )
        d_scores = (probs_f * (d_probs - row_delta[:, :, None])).astype(jnp.bfloat16)
        d_queries = d_queries + jnp.einsum(
            "hqk,khd->qhd", d_scores, key_block, preferred_element_type=jnp.float32
        )
        d_buckets = d_buckets + jnp.einsum(
            "hqk,qkb->bh",
            d_scores,
            bucket_hit.astype(jnp.bfloat16),
            preferred_element_type=jnp.float32,
        )
        d_values = jnp.einsum(
            "hqk,qhd->khd",
            probs_f.astype(jnp.bfloat16),
            d_attended,
            preferred_element_type=jnp.float32,
        )
        d_keys = jnp.einsum("hqk,qhd->khd", d_scores, queries, preferred_element_type=jnp.float32)
        return ((d_queries, d_buckets), (d_keys, d_values))

    start = (jnp.zeros(queries.shape, jnp.float32), jnp.zeros(rel_bucket.shape, jnp.float32))
    (d_queries, d_buckets), key_terms = lax.scan(step, start, layout)
    return (d_queries, key_terms, d_buckets)


def on_device(
    hidden_in,
    grad_out,
    gain_attn,
    gain_ffn,
    rel_bias,
    w_query,
    w_key,
    w_value,
    w_output,
    w_inner,
    w_outer,
    dealing,
    lengths,
    bucket_table,
):
    micro_count, tok_rows, model_width = hidden_in.shape
    group_size = lax.axis_size("fsdp")
    slot_rows = tok_rows // group_size
    own_index = lax.axis_index("fsdp")
    max_offset = (bucket_table.shape[0] - 1) // 2
    bucket_count = BUCKETS
    head_count = H
    offsets_all = jnp.arange(bucket_table.shape[0], dtype=jnp.int32) - max_offset
    matches = bucket_table[:, None] == jnp.arange(bucket_count, dtype=jnp.int32)[None, :]
    lower_edge = jnp.min(jnp.where(matches, offsets_all[:, None], 2 * max_offset + 2), axis=0)
    upper_edge = jnp.max(jnp.where(matches, offsets_all[:, None], -2 * max_offset - 2), axis=0)
    bucket_edges = (lower_edge, upper_edge)
    hidden_units = w_inner.shape[1]
    acc_gain_one = jnp.zeros((model_width,), jnp.float32)
    acc_gain_two = jnp.zeros((model_width,), jnp.float32)
    acc_buckets = jnp.zeros((bucket_count, head_count), jnp.float32)
    acc_query = jnp.zeros((model_width, model_width), jnp.float32)
    acc_key = jnp.zeros((model_width, model_width), jnp.float32)
    acc_value = jnp.zeros((model_width, model_width), jnp.float32)
    acc_output = jnp.zeros((model_width, model_width), jnp.float32)
    acc_inner = jnp.zeros((model_width, hidden_units), jnp.float32)
    acc_outer = jnp.zeros((hidden_units, model_width), jnp.float32)
    outputs_list = []
    grads_list = []
    for micro_idx in range(micro_count):
        weights_now = (
            lax.all_gather(gain_attn, ("dp", "fsdp"), axis=0, tiled=True),
            lax.all_gather(gain_ffn, ("dp", "fsdp"), axis=0, tiled=True),
            lax.all_gather(rel_bias, ("dp", "fsdp"), axis=0, tiled=True),
            lax.all_gather(w_query, ("dp", "fsdp"), axis=0, tiled=True),
            lax.all_gather(w_key, ("dp", "fsdp"), axis=0, tiled=True),
            lax.all_gather(w_value, ("dp", "fsdp"), axis=0, tiled=True),
            lax.all_gather(w_output, ("dp", "fsdp"), axis=0, tiled=True),
            lax.all_gather(w_inner, ("dp", "fsdp"), axis=0, tiled=True),
            lax.all_gather(w_outer, ("dp", "fsdp"), axis=0, tiled=True),
        )
        gain_one = weights_now[0].astype(jnp.float32)
        gain_two = weights_now[1].astype(jnp.float32)
        rel_bucket = weights_now[2].astype(jnp.float32).reshape(bucket_count, head_count)
        query_weight, key_weight, value_weight, output_weight, inner_weight, outer_weight = (
            weights_now[3:]
        )
        deal_order = dealing[micro_idx, 0]
        segment, position = token_places(deal_order, lengths[micro_idx, 0])
        seg_query = lax.dynamic_slice_in_dim(segment, own_index * tok_rows, tok_rows)
        pos_query = lax.dynamic_slice_in_dim(position, own_index * tok_rows, tok_rows)
        take_rows = (
            lax.dynamic_slice_in_dim(
                deal_order.reshape(group_size, tok_rows), own_index * slot_rows, slot_rows, 1
            )
            - own_index * tok_rows
        ).reshape(tok_rows)
        dealt = lax.all_to_all(
            jnp.take(hidden_in[micro_idx], take_rows, axis=0),
            "fsdp",
            split_axis=0,
            concat_axis=0,
            tiled=True,
        )
        dealt_rows = dealt.astype(jnp.float32)
        scale_one = rms_scale(dealt_rows)
        normed1 = (dealt_rows * scale_one * gain_one).astype(jnp.bfloat16)
        queries = jnp.dot(normed1, query_weight, preferred_element_type=jnp.float32).astype(
            jnp.bfloat16
        )
        key_rows = jnp.dot(normed1, key_weight, preferred_element_type=jnp.float32).astype(
            jnp.bfloat16
        )
        value_rows = jnp.dot(normed1, value_weight, preferred_element_type=jnp.float32).astype(
            jnp.bfloat16
        )
        key_all, value_all = (
            lax.all_gather(key_rows, "fsdp", axis=0, tiled=True),
            lax.all_gather(value_rows, "fsdp", axis=0, tiled=True),
        )
        layout = key_layout(key_all, value_all, segment, position, head_count)
        queries_heads = queries.reshape(tok_rows, head_count, -1)
        attended_f, log_total = attend(
            queries_heads, layout, seg_query, pos_query, rel_bucket, bucket_edges, max_offset
        )
        attended = attended_f.reshape(tok_rows, model_width).astype(jnp.bfloat16)
        mid = dealt_rows + jnp.dot(attended, output_weight, preferred_element_type=jnp.float32)
        scale_two = rms_scale(mid)
        normed2 = (mid * scale_two * gain_two).astype(jnp.bfloat16)
        inner_act = jnp.dot(normed2, inner_weight, preferred_element_type=jnp.float32)
        active = jax.nn.gelu(inner_act, approximate=False).astype(jnp.bfloat16)
        result = mid + jnp.dot(active, outer_weight, preferred_element_type=jnp.float32)
        outputs_list.append(result)
        weights_back = (
            lax.all_gather(gain_attn, ("dp", "fsdp"), axis=0, tiled=True),
            lax.all_gather(gain_ffn, ("dp", "fsdp"), axis=0, tiled=True),
            lax.all_gather(rel_bias, ("dp", "fsdp"), axis=0, tiled=True),
            lax.all_gather(w_query, ("dp", "fsdp"), axis=0, tiled=True),
            lax.all_gather(w_key, ("dp", "fsdp"), axis=0, tiled=True),
            lax.all_gather(w_value, ("dp", "fsdp"), axis=0, tiled=True),
            lax.all_gather(w_output, ("dp", "fsdp"), axis=0, tiled=True),
            lax.all_gather(w_inner, ("dp", "fsdp"), axis=0, tiled=True),
            lax.all_gather(w_outer, ("dp", "fsdp"), axis=0, tiled=True),
        )
        query_weight, key_weight, value_weight, output_weight, inner_weight, outer_weight = (
            weights_back[3:]
        )
        grad_top = grad_out[micro_idx]
        acc_outer = acc_outer + jnp.einsum(
            "tf,td->fd", active, grad_top, preferred_element_type=jnp.float32
        )
        d_active = jnp.einsum(
            "td,fd->tf", grad_top, outer_weight, preferred_element_type=jnp.float32
        )
        d_inner = (d_active * gelu_slope(inner_act)).astype(jnp.bfloat16)
        acc_inner = acc_inner + jnp.einsum(
            "td,tf->df", normed2, d_inner, preferred_element_type=jnp.float32
        )
        d_normed2 = jnp.einsum(
            "tf,df->td", d_inner, inner_weight, preferred_element_type=jnp.float32
        )
        d_mid_norm, d_gain_two = norm_back_rows(mid, scale_two, gain_two, d_normed2)
        acc_gain_two = acc_gain_two + d_gain_two
        d_mid = grad_top.astype(jnp.float32) + d_mid_norm
        d_branch = d_mid.astype(jnp.bfloat16)
        acc_output = acc_output + jnp.einsum(
            "td,te->de", attended, d_branch, preferred_element_type=jnp.float32
        )
        d_attended = jnp.einsum(
            "te,de->td", d_branch, output_weight, preferred_element_type=jnp.float32
        ).astype(jnp.bfloat16)
        d_attended_heads = d_attended.reshape(tok_rows, head_count, -1)
        row_delta = jnp.sum(d_attended_heads.astype(jnp.float32) * attended_f, axis=2).T
        key_back, value_back = (
            lax.all_gather(key_rows, "fsdp", axis=0, tiled=True),
            lax.all_gather(value_rows, "fsdp", axis=0, tiled=True),
        )
        layout_back = key_layout(key_back, value_back, segment, position, head_count)
        d_queries, key_terms, d_buckets = attend_back(
            queries_heads,
            layout_back,
            seg_query,
            pos_query,
            rel_bucket,
            bucket_edges,
            max_offset,
            log_total,
            d_attended_heads,
            row_delta,
        )
        d_keys, d_values = key_terms
        group_rows = d_keys.shape[0] * d_keys.shape[1]
        d_keys_own, d_values_own = (
            lax.psum_scatter(
                d_keys.reshape(group_rows, model_width).astype(jnp.bfloat16),
                "fsdp",
                scatter_dimension=0,
                tiled=True,
            ).astype(jnp.float32),
            lax.psum_scatter(
                d_values.reshape(group_rows, model_width).astype(jnp.bfloat16),
                "fsdp",
                scatter_dimension=0,
                tiled=True,
            ).astype(jnp.float32),
        )
        acc_buckets = acc_buckets + d_buckets
        d_queries_low = d_queries.reshape(tok_rows, model_width).astype(jnp.bfloat16)
        d_keys_low = d_keys_own.astype(jnp.bfloat16)
        d_values_low = d_values_own.astype(jnp.bfloat16)
        acc_query = acc_query + jnp.einsum(
            "td,te->de", normed1, d_queries_low, preferred_element_type=jnp.float32
        )
        acc_key = acc_key + jnp.einsum(
            "td,te->de", normed1, d_keys_low, preferred_element_type=jnp.float32
        )
        acc_value = acc_value + jnp.einsum(
            "td,te->de", normed1, d_values_low, preferred_element_type=jnp.float32
        )
        d_normed1 = (
            jnp.einsum("te,de->td", d_queries_low, query_weight, preferred_element_type=jnp.float32)
            + jnp.einsum("te,de->td", d_keys_low, key_weight, preferred_element_type=jnp.float32)
            + jnp.einsum(
                "te,de->td", d_values_low, value_weight, preferred_element_type=jnp.float32
            )
        )
        d_rows_norm, d_gain_one = norm_back_rows(dealt_rows, scale_one, gain_one, d_normed1)
        acc_gain_one = acc_gain_one + d_gain_one
        d_dealt = d_mid + d_rows_norm
        returned = lax.all_to_all(
            d_dealt.astype(jnp.bfloat16), "fsdp", split_axis=0, concat_axis=0, tiled=True
        ).astype(d_dealt.dtype)
        grads_list.append(jnp.zeros_like(returned).at[take_rows].set(returned))
    acc_rel = acc_buckets.reshape(-1)
    summed = (
        lax.psum_scatter(acc_gain_one, ("dp", "fsdp"), scatter_dimension=0, tiled=True),
        lax.psum_scatter(acc_gain_two, ("dp", "fsdp"), scatter_dimension=0, tiled=True),
        lax.psum_scatter(acc_rel, ("dp", "fsdp"), scatter_dimension=0, tiled=True),
        lax.psum_scatter(acc_query, ("dp", "fsdp"), scatter_dimension=0, tiled=True),
        lax.psum_scatter(acc_key, ("dp", "fsdp"), scatter_dimension=0, tiled=True),
        lax.psum_scatter(acc_value, ("dp", "fsdp"), scatter_dimension=0, tiled=True),
        lax.psum_scatter(acc_output, ("dp", "fsdp"), scatter_dimension=0, tiled=True),
        lax.psum_scatter(acc_inner, ("dp", "fsdp"), scatter_dimension=0, tiled=True),
        lax.psum_scatter(acc_outer, ("dp", "fsdp"), scatter_dimension=0, tiled=True),
    )
    return (
        jnp.stack(outputs_list),
        jnp.stack(grads_list),
        summed[0],
        summed[1],
        summed[2],
        summed[3],
        summed[4],
        summed[5],
        summed[6],
        summed[7],
        summed[8],
    )


VMEM = pl.BlockSpec(memory_space=pltpu.VMEM)
SMEM = pl.BlockSpec(memory_space=pltpu.SMEM)
ANYWHERE = pl.BlockSpec(memory_space=pl.ANY)
LIMIT = 58 * 1024 * 1024
FIRST_AXIS = ("x", "x", "y", "x", "y")
FWD_PARTS = 3
FWD_AHEAD = 2
FWD_OWN = (-1, 0, 6, 12, 15, 21)
FWD_NEAR = (9, 12, 18, 24, 27, 33)
FWD_SIDE = (21, 24, 30, 36, 41, 41)
FWD_GRADS = 15
FFN_CHUNK = 768
BWD_PARTS = 3
BWD_AHEAD = 4
BWD_SIDE = (12, 14, 20, 20, 24, 26, 28)
BWD_NEAR = (18, 22, 26, 24, 28, 30, 34)


def shaped(*shape, dtype=jnp.bfloat16):
    return jax.ShapeDtypeStruct(shape, dtype)


def params(collective_id=None):
    if collective_id is None:
        return pltpu.CompilerParams(vmem_limit_bytes=LIMIT)
    return pltpu.CompilerParams(
        collective_id=collective_id, has_side_effects=True, vmem_limit_bytes=LIMIT
    )


def dma(*shape):
    return pltpu.SemaphoreType.DMA(shape)


def gather_all(lens, deal, hid, one, two, rel, shards):
    count = len(shards) + 1
    return pl.pallas_call(
        functools.partial(gather_kernel, FIRST_AXIS),
        name="gather_all",
        out_shape=[
            shaped(1, 128, dtype=jnp.int32),
            shaped(*deal.shape[1:], dtype=jnp.int32),
            shaped(OWN, TILE, hid.shape[-1]),
            shaped(32, 16, 128),
        ]
        + [shaped(32, *s.shape) for s in shards],
        in_specs=[VMEM] + [ANYWHERE] * 2 + [VMEM] * 3 + [ANYWHERE] * (count - 1),
        out_specs=[ANYWHERE] * (3 + count),
        scratch_shapes=[
            pltpu.VMEM((2, 1, 128), jnp.int32), pltpu.VMEM((16, 128), jnp.float32), pltpu.VMEM((16, 128), jnp.bfloat16),
            dma(count, 10), dma(count, 10), dma(count), dma(2, 3), dma(OWN), dma(2), dma(2),
        ],
        compiler_params=params(0),
    )(lens, deal, hid, one, two, rel, *shards)


def attention_forward(lens, x, small, table, wq, wk, wv, grd, wi, wu):
    heads, keys = (PAIRS, OWN, TILE, 128), (PAIRS, OWN, 2, TILE, 128)
    count = len(FWD_OWN)
    return pl.pallas_call(
        attn_fwd,
        name="attn_fwd",
        out_shape=[
            shaped(*heads), shaped(*keys), shaped(*keys), shaped(*x.shape),
            shaped(OWN, 2 * PAIRS, 1, TILE, dtype=jnp.float32),
            shaped(8, grd.shape[2], grd.shape[3] // 2),
            shaped(32, *wi.shape), shaped(32, *wu.shape),
        ],
        in_specs=[SMEM] + [VMEM] * 6 + [ANYWHERE] * 3,
        out_specs=[VMEM] * 5 + [ANYWHERE] * 3,
        scratch_shapes=[
            pltpu.VMEM((5, 2 * PAIRS, 1, 2 * TILE), jnp.float32),
            pltpu.VMEM((2 * PAIRS, 5, TILE, TILE), jnp.float32),
            pltpu.VMEM((OWN, TILE, 128), jnp.bfloat16),
            pltpu.VMEM((TILES, TILE, 128), jnp.bfloat16),
            pltpu.VMEM((2, TILE, TILES * TILE), jnp.float32),
            pltpu.VMEM((OWN, TILE, 128), jnp.float32),
            dma(2), dma(2),
            dma(count, 10), dma(count, 10), dma(count), dma(2, 2, 2), dma(2, 4),
        ],
        compiler_params=params(1),
    )(lens, x, small, table, wq, wk, wv, grd, wi, wu)


def landing(shapes, leads=((4, 4), (2, 4), (4,))):
    return [pltpu.VMEM((*lead, *b), jnp.bfloat16) for b in shapes for lead in leads]


def attention_backward(lens, q, k, v, log_total, d_att, delta, small, table, gwo, gwi, gwu, dealt):
    heads = (PAIRS, OWN, TILE, 128)
    block_i, block_u = (gwi.shape[2], gwi.shape[3] // BWD_PARTS), (gwu.shape[2], gwu.shape[3] // BWD_PARTS)
    blocks = [block_i, block_u] * BWD_PARTS + [gwo.shape[2:]]
    count = len(blocks)
    return pl.pallas_call(
        attn_bwd,
        name="attn_bwd",
        out_shape=[shaped(*heads)] * 3
        + [shaped(32, 128, dtype=jnp.float32)]
        + [shaped(4, *g.shape[2:]) for g in (gwo, gwi, gwu)]
        + [shaped(*dealt.shape[:2], dealt.shape[2] // 2)],
        in_specs=[SMEM] + [VMEM] * 8 + [ANYWHERE] * 4,
        out_specs=[VMEM] * 4 + [ANYWHERE] * 4,
        scratch_shapes=[pltpu.VMEM((5, 2 * PAIRS, 1, 2 * TILE), jnp.float32)] * 2
        + [pltpu.VMEM((2 * PAIRS, 5, TILE, TILE), jnp.float32)] * 2
        + [pltpu.VMEM((OWN, TILE, 128), jnp.bfloat16), pltpu.VMEM((TILES, TILE, 128), jnp.bfloat16)]
        + [pltpu.VMEM((TILES * TILE, 128), jnp.float32)] * 2
        + [pltpu.VMEM(heads, jnp.bfloat16)] * 4
        + [dma(2, PAIRS), dma(2, PAIRS), dma(count, 10), dma(count, 10), dma(count, 3), dma(2), dma(2)]
        + landing(blocks, ((2, 4), (2, 4), (4,))),
        compiler_params=params(2),
    )(lens, q, k, v, log_total, d_att, delta, small, table, gwo, gwi, gwu, dealt)


def feed_forward(deal, x, att, wo, small, g_low, grd, wi, wu):
    tok, width = x.shape
    hidden = wi.shape[1]
    f32, bf16 = jnp.float32, jnp.bfloat16
    heads, stats = (PAIRS, OWN, TILE, 128), (OWN, 2 * PAIRS, 1, TILE)
    block_i, block_u = (32, width // 32, hidden), (32, hidden // 32, width)
    chunks = hidden // FFN_CHUNK
    return pl.pallas_call(
        ffn_kernel,
        name="feed_forward",
        out_shape=[
            shaped(tok, width, dtype=f32), shaped(*heads), shaped(*stats, dtype=f32),
            shaped(4, 4, width // 32, width), shaped(32, 128, dtype=f32), shaped(2, 3 * TILE, width),
            shaped(4, 4, *block_i[1:]), shaped(4, 4, *block_u[1:]), shaped(2, 3 * TILE, width // 2),
        ],
        in_specs=[VMEM] * 6 + [ANYWHERE] * 3,
        out_specs=[VMEM] * 6 + [ANYWHERE] * 3,
        scratch_shapes=[
            pltpu.VMEM((tok, width), bf16), pltpu.VMEM((tok, width), f32), pltpu.VMEM((tok, width), bf16),
            pltpu.VMEM((tok, width), f32), pltpu.VMEM((tok, hidden), bf16), pltpu.VMEM((tok, hidden), bf16),
            pltpu.VMEM((width, hidden), bf16), pltpu.VMEM((hidden, width), bf16),
            pltpu.VMEM((2, 32, width // 32, FFN_CHUNK), bf16), pltpu.VMEM((2, 32 // chunks, hidden // 32, width), bf16),
            pltpu.VMEM(g_low.shape, bf16),
            pltpu.VMEM((OWN, TILE, width), bf16), pltpu.VMEM((OWN, 2, TILE, width), bf16),
            pltpu.VMEM((chunks, 4, 4, width // 32, FFN_CHUNK), bf16), pltpu.VMEM((chunks, 4, hidden // 32, width), bf16),
            pltpu.VMEM((32, width // 32, width), bf16),
            dma(2, chunks), dma(2, chunks), dma(2, 2, 2), dma(2, 4), dma(2), dma(2),
            pltpu.SemaphoreType.DMA, pltpu.SemaphoreType.DMA, dma(chunks + 1, 5), dma(chunks + 1, 5),
            pltpu.VMEM((tok, 2 * tok), bf16),
        ],
        compiler_params=params(4),
    )(deal, x, att, wo, small, g_low, grd, wi, wu)


def tail(x, small, d_mid, dq, dk, dv, wq, wk, wv, g_two, g_rel):
    tok, width = x.shape
    block = (width // 32, width)
    blocks = [block, block, block, (16, 128)]
    count = len(blocks)
    return pl.pallas_call(
        tail_kernel,
        name="tail",
        out_shape=[shaped(2, 3, TILE, width), shaped(4, 16, 128)] + [shaped(4, *block)] * 3,
        in_specs=[VMEM] * 4 + [ANYWHERE] * 7,
        out_specs=[ANYWHERE] * 5,
        scratch_shapes=[
            pltpu.VMEM((tok, width), jnp.float32), pltpu.VMEM((3, width, width), jnp.bfloat16),
            pltpu.VMEM((3, OWN, TILE, width), jnp.bfloat16), pltpu.VMEM((tok, width), jnp.bfloat16),
            pltpu.VMEM((OWN, TILE, width), jnp.bfloat16),
            pltpu.VMEM((32, 16, 128), jnp.bfloat16),
        ]
        + [pltpu.VMEM((32, *block), jnp.bfloat16)] * 3
        + landing(blocks)
        + [dma(count, 10), dma(count, 10), dma(count, 1), dma(OWN), dma(2, 3), dma(4, PAIRS + 1)],
        compiler_params=params(3),
    )(x, small, g_two, g_rel, d_mid, dq, dk, dv, wq, wk, wv)


def last_sums(low, high, gin, terms):
    f32 = jnp.float32
    lines = lambda n: shaped(1, n, dtype=f32)
    return pl.pallas_call(
        sum_kernel,
        name="last_sums",
        out_shape=[shaped(*low.shape[:2], 2 * low.shape[2], dtype=f32), shaped(*gin.shape, dtype=f32), lines(24), lines(24), lines(H)]
        + [shaped(*t.shape[1:], dtype=f32) for t in terms[1:]],
        in_specs=[VMEM] * (3 + len(terms)),
        out_specs=[VMEM] * (4 + len(terms)),
        compiler_params=params(),
    )(low, high, gin, *terms)


def on_device_packed(
    hidden_in, grad_out, gain_attn, gain_ffn, rel_bias,
    w_query, w_key, w_value, w_output, w_inner, w_outer,
    dealing, lengths, bucket_table,
):
    micro_count, tok_rows, width = hidden_in.shape
    matrix = lambda w: w.reshape(-1, w.shape[-1])
    table = bucket_table[None]
    grd = grad_out.reshape(2, 2, tok_rows // 2, width)
    lens_u, deal_u, x_own, small, wq, wk, wv, wo = gather_all(
        lengths, dealing, hidden_in.reshape(2, 3, TILE, width),
        gain_attn[None], gain_ffn[None], rel_bias[None], (w_query, w_key, w_value, w_output),
    )
    wq, wk, wv = map(matrix, (wq, wk, wv))
    x_rows = matrix(x_own)
    q, k, v, att, log_total, g_low, wi, wu = attention_forward(
        lens_u, x_rows, small, table, wq, wk, wv, grd, w_inner, w_outer
    )
    d_mid, d_att, delta, g_wo, g_two, dealt, g_wi, g_wu, hid_low = feed_forward(
        deal_u, x_rows, att, matrix(wo), small, g_low, grd, matrix(wi), matrix(wu)
    )
    dq, dk, dv, g_rel, t_wo, t_wi, t_wu, hid_high = attention_backward(
        lens_u, q, k, v, log_total, d_att, delta, small, table, g_wo, g_wi, g_wu, dealt
    )
    gin, t_small, t_wq, t_wk, t_wv = tail(x_rows, small, d_mid, dq, dk, dv, wq, wk, wv, g_two, g_rel)
    hid, gin, s_one, s_two, s_rel, *grads = last_sums(hid_low, hid_high, gin, (t_small, t_wq, t_wk, t_wv, t_wo, t_wi, t_wu))
    return (hid, gin.reshape(2, tok_rows, width), s_one[0], s_two[0], s_rel[0], *grads)


def solution(mesh):
    axes = ("dp", "fsdp")
    tokens, matrix, vector = P(None, axes, None), P(axes, None), P(axes)
    packed = mesh.shape["fsdp"] == 4 and mesh.shape["dp"] == 8
    return jax.shard_map(
        on_device_packed if packed else on_device,
        mesh=mesh,
        in_specs=(tokens, tokens, vector, vector, vector)
        + (matrix,) * 6
        + (P(None, "dp", None), P(None, "dp", None), P()),
        out_specs=(tokens, tokens, vector, vector, vector) + (matrix,) * 6,
        check_vma=False,
    )
```

```python
import functools
import math

import jax
import jax.numpy as jnp
from jax import lax
from jax.experimental import pallas as pl
from jax.experimental.pallas import tpu as pltpu
from jax.sharding import PartitionSpec as P

H = 12
BUCKETS = 32
EPSILON = 1e-06
NEG_FILL = -1e30
MESH = pl.DeviceIdType.MESH
TILE = 128
PAIRS = 6
OWN = 6
TILES = 12
FAR = 6
SEQS = 4


def lane_index(shape):
    return lax.broadcasted_iota(jnp.int32, shape, len(shape) - 1)


def row_index(shape):
    return lax.broadcasted_iota(jnp.int32, shape, len(shape) - 2)


def dot_nn(left, right):
    return lax.dot_general(left, right, (((1,), (0,)), ((), ())), preferred_element_type=jnp.float32)


def dot_nt(left, right):
    return lax.dot_general(left, right, (((1,), (1,)), ((), ())), preferred_element_type=jnp.float32)


def dot_tn(left, right):
    return lax.dot_general(left, right, (((0,), (0,)), ((), ())), preferred_element_type=jnp.float32)


def segments_of(places, lens_ref, count):
    edge = jnp.int32(0)
    found = jnp.zeros(places.shape, jnp.int32)
    for s in range(count - 1):
        edge = edge + lens_ref[0, s]
        found = found + (places >= edge).astype(jnp.int32)
    return found


def segment_tags(places, lens_ref, count, of_key):
    lane = lane_index(places.shape)
    hit = segments_of(places, lens_ref, count) == lane
    if of_key:
        return jnp.where((lane < count) & jnp.logical_not(hit), NEG_FILL, 0.0).astype(jnp.bfloat16)
    return jnp.where(hit, 1.0, 0.0).astype(jnp.bfloat16)


def one_hot(rows, columns):
    return jnp.where(rows == columns, 1.0, 0.0).astype(jnp.bfloat16)


def small_lines(small_ref, kind):
    flat = small_ref[...].reshape(32 * 16, 128)
    pick = one_hot(16 * row_index((32, 512)) + kind, lane_index((32, 512)))
    return dot_nn(pick, flat).astype(jnp.bfloat16)


def gain_row(small_ref, kind, width):
    lines = dot_nn(
        small_lines(small_ref, kind), one_hot(row_index((128, width)), lax.rem(lane_index((128, width)), 24))
    )
    own = lane_index((32, width)) // 24 == row_index((32, width))
    return jnp.sum(jnp.where(own, lines, 0.0), axis=0, keepdims=True)


def bucket_picks(table_ref, places):
    span = table_ref.shape[0]
    picked = one_hot(row_index((BUCKETS, span)), jnp.broadcast_to(table_ref[...][None, :], (BUCKETS, span)))
    places = jnp.clip(places, 0, span - 1)
    return dot_nn(picked, one_hot(row_index((span, 256)), jnp.broadcast_to(places, (span, 256)))).astype(jnp.bfloat16)


def class_places(cls, sign):
    lane = lane_index((1, 256))
    if cls >= 3:
        return jnp.full((1, 256), 0 if cls == 3 else 2 * TILE, jnp.int32)
    turn = jnp.where(lane < TILE, lane, lane - 2 * TILE)
    return TILE * (cls - 1) + sign * turn + TILE


def fill_rows(small_ref, table_ref, rows_ref, sign):
    rel = small_lines(small_ref, 2)
    for cls in range(5):
        made = dot_tn(rel, bucket_picks(table_ref, class_places(cls, sign)))
        for h in range(2 * PAIRS):
            rows_ref[cls, h] = made[h : h + 1, :]


def bucket_sums(hist_ref, table_ref):
    total = None
    for cls in range(5):
        if cls >= 3:
            places = class_places(cls, 1)
        else:
            places = TILE * (cls - 1) + 2 * TILE - 1 - lane_index((1, 256))
        hist = jnp.concatenate([hist_ref[cls, h] for h in range(2 * PAIRS)] + [jnp.zeros((4, 256), jnp.float32)], axis=0)
        term = lax.dot_general(
            bucket_picks(table_ref, places).astype(jnp.float32), hist, (((1,), (1,)), ((), ())),
            precision=lax.Precision.HIGHEST, preferred_element_type=jnp.float32,
        )
        total = term if total is None else total + term
    return total


def key_range(i):
    return max(0, 2 * i - FAR), min(TILES, 2 * i + FAR + 2)


def fill_bias(rows_ref, tiles_ref, heads):
    def one_head(h, carry):
        for cls in range(3):
            row = rows_ref[cls, h]
            wide = pltpu.roll(
                jnp.broadcast_to(row, (TILE, 2 * TILE)), 0, 1, stride=1, stride_axis=0
            )
            tiles_ref[h, cls + 1] = wide[:, :TILE]
        left = rows_ref[3, h, :, :TILE]
        right = rows_ref[4, h, :, :TILE]
        tiles_ref[h, 0] = jnp.broadcast_to(left, (TILE, TILE))
        tiles_ref[h, 4] = jnp.broadcast_to(right, (TILE, TILE))
        return carry

    lax.fori_loop(0, heads, one_head, 0)


def bias_class(kt, i, core):
    return jnp.clip(kt - 2 * i - core, -2, 2) + 2


def make_tags(lens_ref, ext_q, ext_k):
    core = lax.rem(lax.axis_index("dp"), 2)
    for t in range(TILES):
        ext_k[t] = segment_tags(TILE * t + row_index((TILE, 128)), lens_ref, SEQS, True)
    for i in range(OWN):
        ext_q[i] = segment_tags(TILE * (2 * i + core) + row_index((TILE, 128)), lens_ref, SEQS, False)


def attn_fwd(
    lens_ref, x_ref, small_ref, table_ref, wq_ref, wk_ref, wv_ref, grd_in, wi_in, wu_in,
    q_ref, k_ref, v_ref, att_ref, log_ref, g_low, wi_all, wu_all,
    rows_ref, bias_ref, ext_q, ext_k, s_ref, log_acc, send_sem, recv_sem,
    w_send, w_recv, w_local, g_send, g_recv,
):
    y, x, core, z = coordinates()
    sibling = place(y, x, 1 - core, z)
    greet()
    pieces = []
    part_i, part_u = wi_in.shape[1] // FWD_PARTS, wu_in.shape[1] // FWD_PARTS
    for n in range(FWD_PARTS):
        pieces.append((wi_in, wi_all, (n * part_i, part_i), "xy"[(n + 1) % 2]))
        pieces.append((wu_in, wu_all, (n * part_u, part_u), "xy"[n % 2]))
    gather = Gather(pieces, w_send, w_recv, w_local)
    grads = list(grad_sends(grd_in, g_low, 0, g_send, g_recv))
    events = {}

    def plan(at, step, *args):
        events.setdefault(at, []).append(functools.partial(step, *args))

    for n in range(len(pieces)):
        plan(FWD_OWN[n], gather.spread_own, n)
        if n + FWD_AHEAD < len(pieces):
            plan(FWD_OWN[n], gather.start, n + FWD_AHEAD)
        plan(FWD_NEAR[n], gather.spread_near, n)
        plan(FWD_SIDE[n], gather.spread_side, n)
    plan(FWD_GRADS, start_all, grads)

    greeted()
    for n in range(FWD_AHEAD):
        gather.start(n)
    rows = x_ref[...].astype(jnp.float32)
    scale = lax.rsqrt(jnp.mean(rows * rows, axis=1, keepdims=True) + EPSILON)
    normed = (rows * scale * gain_row(small_ref, 0, rows.shape[1])).astype(jnp.bfloat16)

    def project(w_ref):
        return dot_nn(normed, w_ref[...]).astype(jnp.bfloat16)

    copies = []
    for n, (w_ref, all_ref) in enumerate(((wk_ref, k_ref), (wv_ref, v_ref))):
        made = project(w_ref)
        for hp in range(PAIRS):
            for i in range(OWN):
                all_ref[hp, i, core] = made[TILE * i : TILE * (i + 1), 128 * hp : 128 * (hp + 1)]
        copy = remote(all_ref.at[:, :, core], all_ref.at[:, :, core], send_sem.at[n], recv_sem.at[n], sibling)
        copy.start()
        copies.append(copy)
    made = project(wq_ref)
    for hp in range(PAIRS):
        for i in range(OWN):
            q_ref[hp, i] = made[TILE * i : TILE * (i + 1), 128 * hp : 128 * (hp + 1)]
    make_tags(lens_ref, ext_q, ext_k)
    for i in range(OWN):
        log_acc[i] = jnp.zeros((TILE, 128), jnp.float32)
    for step in events.pop(-1, ()):
        step()
    fill_rows(small_ref, table_ref, rows_ref, 1)
    fill_bias(rows_ref, bias_ref, 2 * PAIRS)
    for n, all_ref in enumerate((k_ref, v_ref)):
        block = all_ref.at[:, :, 1 - core]
        remote(block, block, send_sem.at[n], recv_sem.at[n], sibling).wait_recv()

    lane = lane_index((TILE, 128))

    def one_pair(hp, carry):
        for i in range(OWN):
            run_events(events, hp, i)
            lo, hi = key_range(i)
            width = (hi - lo) * TILE
            pair = q_ref[hp, i]
            tags = ext_q[i]
            zero = jnp.zeros_like(pair)
            left = jnp.concatenate(
                [
                    jnp.concatenate([jnp.where(lane < 64, pair, zero), tags], axis=1),
                    jnp.concatenate([jnp.where(lane < 64, zero, pair), tags], axis=1),
                ],
                axis=0,
            )
            keys = k_ref[hp, lo // 2 : hi // 2].reshape(width, 128)
            right = jnp.concatenate([keys, ext_k[lo:hi].reshape(width, 128)], axis=1)
            raw = dot_nt(left, right)
            tops = []
            for e in range(2):
                top = None
                for kt in range(lo, hi):
                    at = (kt - lo) * TILE
                    part = raw[e * TILE : (e + 1) * TILE, at : at + TILE]
                    if -1 <= kt - 2 * i <= 2:
                        part = part + bias_ref[2 * hp + e, bias_class(kt, i, core)]
                    else:
                        part = part + rows_ref[3 if kt < 2 * i else 4, 2 * hp + e, :, :TILE]
                    s_ref[e, :, at : at + TILE] = part
                    top = part if top is None else jnp.maximum(top, part)
                tops.append(jnp.max(top, axis=1, keepdims=True))
            outs = []
            for e in range(2):
                total = None
                found = []
                for kt in range(lo, hi):
                    at = (kt - lo) * TILE
                    weight = jnp.exp(s_ref[e, :, at : at + TILE] - tops[e])
                    total = weight if total is None else total + weight
                    found.append(weight.astype(jnp.bfloat16))
                total = jnp.sum(total, axis=1, keepdims=True)
                probs = jnp.concatenate(found, axis=1)
                values = v_ref[hp, lo // 2 : hi // 2].reshape(width, 128)
                outs.append(dot_nn(probs, values) / total)
                log_acc[i] = jnp.where(lane == 2 * hp + e, tops[e] + jnp.log(total), log_acc[i])
            att_ref[TILE * i : TILE * (i + 1), pl.ds(pl.multiple_of(128 * hp, 128), 128)] = jnp.where(
                lane < 64, outs[0], outs[1]
            ).astype(jnp.bfloat16)
        return carry

    lax.fori_loop(0, PAIRS, one_pair, 0)
    for i in range(OWN):
        turned = log_acc[i].T
        for h in range(2 * PAIRS):
            log_ref[i, h] = turned[h : h + 1, :]
    late(events)
    share_grads(g_low, g_send, g_recv)
    for n in range(len(pieces)):
        gather.finish(n)
    end_grads(grads, g_low, g_send, g_recv)
    for copy in copies:
        copy.wait_send()


def attn_bwd(
    lens_ref, q_ref, k_ref, v_ref, log_ref, do_ref, delta_ref, small_ref, table_ref, gwo, gwi, gwu, dealt,
    dq_ref, dk_ref, dv_ref, rel_ref, two, twi, twu, hid_out,
    rows_ref, hist_ref, bias_ref, acc_ref, ext_q, ext_k, dk_acc, dv_acc, out_k, out_v, got_k, got_v, send_sem, recv_sem,
    w_send, w_recv, w_local, h_send, h_recv, *landed,
):
    y, x, core, z = coordinates()
    sibling = place(y, x, 1 - core, z)
    greet()
    plain = []
    part_i, part_u = gwi.shape[3] // BWD_PARTS, gwu.shape[3] // BWD_PARTS
    for n in range(BWD_PARTS):
        plain.append((gwi, twi, (n * part_i, part_i), "xy"[n % 2]))
        plain.append((gwu, twu, (n * part_u, part_u), "xy"[(n + 1) % 2]))
    plain.append((gwo, two, None, "x"))
    count = len(plain)
    scatter = LateScatter(
        [item + tuple(landed[3 * n : 3 * n + 3]) for n, item in enumerate(plain)], w_send, w_recv, w_local
    )
    events = {}

    def plan(at, step, *args):
        events.setdefault(at, []).append(functools.partial(step, *args))

    for n in range(count):
        plan(BWD_SIDE[n], scatter.sum_side, n)
        if n + BWD_AHEAD < count:
            plan(BWD_SIDE[n], scatter.start, n + BWD_AHEAD)
        plan(BWD_NEAR[n], scatter.sum_near, n)
    make_tags(lens_ref, ext_q, ext_k)
    greeted()
    for n in range(BWD_AHEAD):
        scatter.start(n)
    deals = list(dealt_sends(dealt, hid_out, hid_out.shape[2], h_send, h_recv))
    start_all(deals)
    acc_ref[...] = jnp.zeros_like(acc_ref)
    fill_rows(small_ref, table_ref, rows_ref, -1)
    fill_bias(rows_ref, bias_ref, 2 * PAIRS)
    for step in events.pop(-1, ()):
        step()
    lane = lane_index((TILE, 128))

    def one_pair(hp, carry):
        dk_acc[...] = jnp.zeros_like(dk_acc)
        dv_acc[...] = jnp.zeros_like(dv_acc)
        for i in range(OWN):
            run_events(events, hp, i)
            lo, hi = key_range(i)
            width = (hi - lo) * TILE
            pair, d_pair = q_ref[hp, i], do_ref[hp, i]
            tags = ext_q[i]
            zero = jnp.zeros_like(pair)
            q_two = jnp.concatenate([jnp.where(lane < 64, pair, zero), jnp.where(lane < 64, zero, pair)], axis=0)
            d_two = jnp.concatenate([jnp.where(lane < 64, d_pair, zero), jnp.where(lane < 64, zero, d_pair)], axis=0)
            q_ext = jnp.concatenate([q_two, jnp.concatenate([tags, tags], axis=0)], axis=1)
            keys = k_ref[hp, lo // 2 : hi // 2].reshape(width, 128)
            values = v_ref[hp, lo // 2 : hi // 2].reshape(width, 128)
            k_ext = jnp.concatenate([keys, ext_k[lo:hi].reshape(width, 128)], axis=1)
            raw = dot_nt(k_ext, q_ext)
            d_probs = dot_nt(values, d_two)
            p_rows, s_rows = [], []
            for kt in range(lo, hi):
                at = (kt - lo) * TILE
                p_two, s_two = [], []
                for e in range(2):
                    head = 2 * hp + e
                    part = raw[at : at + TILE, e * TILE : (e + 1) * TILE]
                    near = -1 <= kt - 2 * i <= 2
                    cls = bias_class(kt, i, core) if near else (0 if kt < 2 * i else 4)
                    if near:
                        part = part + bias_ref[head, cls]
                    else:
                        part = part + rows_ref[3 if kt < 2 * i else 4, head, :, :TILE]
                    probs = jnp.exp(part - log_ref[i, head])
                    slope = probs * (
                        d_probs[at : at + TILE, e * TILE : (e + 1) * TILE] - delta_ref[i, head]
                    )
                    acc_ref[head, cls] += slope
                    p_two.append(probs.astype(jnp.bfloat16))
                    s_two.append(slope.astype(jnp.bfloat16))
                p_rows.append(jnp.concatenate(p_two, axis=1))
                s_rows.append(jnp.concatenate(s_two, axis=1))
            probs_t = jnp.concatenate(p_rows, axis=0)
            slopes_t = jnp.concatenate(s_rows, axis=0)
            dv_acc[lo * TILE : hi * TILE, :] += dot_nn(probs_t, d_two)
            dk_acc[lo * TILE : hi * TILE, :] += dot_nn(slopes_t, q_two)
            d_q = dot_tn(slopes_t, keys)
            dq_ref[hp, i] = jnp.where(lane < 64, d_q[:TILE], d_q[TILE:]).astype(jnp.bfloat16)
        for acc, own, out in ((dk_acc, dk_ref, out_k), (dv_acc, dv_ref, out_v)):
            for i in range(OWN):
                own[hp, i] = acc[pl.ds((2 * i + core) * TILE, TILE), :].astype(jnp.bfloat16)
                out[hp, i] = acc[pl.ds((2 * i + 1 - core) * TILE, TILE), :].astype(jnp.bfloat16)
        for n, (out, got) in enumerate(((out_k, got_k), (out_v, got_v))):
            pltpu.make_async_remote_copy(
                out.at[hp], got.at[hp], send_sem.at[n, hp], recv_sem.at[n, hp],
                device_id=sibling, device_id_type=MESH,
            ).start()
        return carry

    lax.fori_loop(0, PAIRS, one_pair, 0)
    flip = (row_index((TILE, TILE)) + lane == TILE - 1).astype(jnp.float32)

    def one_head(h, carry):
        for cls in range(3):
            tile = jnp.dot(flip, acc_ref[h, cls + 1], precision=lax.Precision.HIGHEST)
            wide = jnp.concatenate([tile, jnp.zeros((TILE, TILE), jnp.float32)], axis=1)
            wide = pltpu.roll(wide, 0, 1, stride=1, stride_axis=0)
            hist_ref[cls, h] = jnp.sum(wide, axis=0, keepdims=True)
        for n, cls in ((3, 0), (4, 4)):
            row = jnp.sum(acc_ref[h, cls], axis=0, keepdims=True)
            hist_ref[n, h] = jnp.concatenate([row, jnp.zeros_like(row)], axis=1)
        return carry

    lax.fori_loop(0, 2 * PAIRS, one_head, 0)

    rel_ref[...] = jnp.zeros_like(rel_ref)
    rel_ref[:, :16] = bucket_sums(hist_ref, table_ref)

    def finish(hp, carry):
        for n, (out, got, own) in enumerate(((out_k, got_k, dk_ref), (out_v, got_v, dv_ref))):
            copy = pltpu.make_async_remote_copy(
                out.at[hp], got.at[hp], send_sem.at[n, hp], recv_sem.at[n, hp],
                device_id=sibling, device_id_type=MESH,
            )
            copy.wait_send()
            copy.wait_recv()
            own[hp] = (own[hp].astype(jnp.float32) + got[hp].astype(jnp.float32)).astype(jnp.bfloat16)
        return carry

    lax.fori_loop(0, PAIRS, finish, 0)
    late(events)
    for n in range(count):
        scatter.finish(n)
    for item in deals:
        sent(*item)
    for m in range(2):
        remote(hid_out.at[m], hid_out.at[m], h_send.at[0], h_recv.at[m], sibling).wait_recv()


def norm_back(rows_in, scale, gain, grad_normed):
    scaled = grad_normed * gain
    grad_gain = jnp.sum(grad_normed * rows_in * scale, axis=0, keepdims=True)
    shared = jnp.mean(scaled * rows_in, axis=1, keepdims=True)
    return scale * scaled - rows_in * (scale * scale * scale * shared), grad_gain


def join_pairs(pairs_ref, joined_ref):
    for hp in range(PAIRS):
        joined_ref[:, 128 * hp : 128 * (hp + 1)] = (
            pairs_ref[hp].reshape(OWN * TILE, 128).astype(joined_ref.dtype)
        )


def gain_block(row):
    width = row.shape[1]
    lines = jnp.where(lane_index((32, width)) // 24 == row_index((32, width)), row, 0.0)
    pick = (lax.rem(row_index((width, 128)), 24) == lane_index((width, 128))).astype(jnp.float32)
    return jnp.dot(lines, pick, precision=lax.Precision.HIGHEST)


def ffn_kernel(
    deal_ref, x_ref, att_ref, wo_ref, small_ref, g_low, grd_in, wi_in, wu_in,
    dmid_ref, datt_ref, delta_ref, gwo_ref, two_ref, dealt, gwi, gwu, hid_out,
    grad_ref, mid_ref, normed_ref, total_ref, active_ref, slope_ref, wi_ref, wu_ref, gwi_two, gwu_two, g_high,
    res_ref, res_all, got_i, got_u, gwo_own, in_sem, out_sem, g_send, g_recv, h_send, h_recv, e_send, e_recv,
    c_send, c_recv,
):
    y, x, core, z = coordinates()
    sibling = place(y, x, 1 - core, z)
    greet()
    width = x_ref.shape[1]
    half = width // 2
    chunk = FFN_CHUNK
    chunks = wi_ref.shape[1] // chunk

    def bring(j):
        span = pl.ds(chunk * j, chunk)
        return (
            pltpu.make_async_copy(wi_in.at[:, span], wi_ref.at[:, span], in_sem.at[0, j]),
            pltpu.make_async_copy(wu_in.at[span], wu_ref.at[span], in_sem.at[1, j]),
        )

    for j in range(chunks):
        for copy in bring(j):
            copy.start()
    grads = list(grad_sends(grd_in, g_high, half, g_send, g_recv))
    gain = gain_row(small_ref, 1, width)
    mid = x_ref[...].astype(jnp.float32) + dot_nn(att_ref[...], wo_ref[...])
    mid_ref[...] = mid
    scale = lax.rsqrt(jnp.mean(mid * mid, axis=1, keepdims=True) + EPSILON)
    normed_ref[...] = (mid * scale * gain).astype(jnp.bfloat16)
    greeted()
    start_all(grads)

    def rows_of(i):
        return slice(TILE * i, TILE * (i + 1))

    picks = []
    for i in range(OWN):
        picks.append(one_hot((2 * i + core) * TILE + row_index((TILE, TILES * TILE)), deal_ref[...]))
        grad_ref[rows_of(i), :half] = dot_nn(
            picks[i], g_low[...].reshape(TILES * TILE, half)
        ).astype(jnp.bfloat16)
    for j in range(chunks):
        span = slice(chunk * j, chunk * (j + 1))
        for copy in bring(j):
            copy.wait()
        inner = dot_nn(normed_ref[...], wi_ref[:, span])
        cdf = 0.5 * (1.0 + lax.erf(inner * (1.0 / math.sqrt(2.0))))
        active = (inner * cdf).astype(jnp.bfloat16)
        active_ref[:, span] = active
        slope = cdf + inner * (jnp.exp(-0.5 * inner * inner) * (1.0 / math.sqrt(2.0 * math.pi)))
        slope_ref[:, span] = slope.astype(jnp.bfloat16)
        term = dot_nn(active, wu_ref[span, :])
        total_ref[...] = term if j == 0 else total_ref[...] + term
    result = (mid_ref[...] + total_ref[...]).astype(jnp.bfloat16).reshape(OWN, TILE, width)
    res_ref[...] = result
    res_copy = remote(res_ref, res_all.at[:, core], e_send, e_recv, sibling)
    res_copy.start()
    for i in range(OWN):
        res_all[i, core] = result[i]
    share_grads(g_high, g_send, g_recv)

    remote(res_ref, res_all.at[:, 1 - core], e_send, e_recv, sibling).wait_recv()
    lane = lane_index((TILE, TILE))
    for b in range(OWN):
        at = pl.multiple_of((OWN * core + b) * TILE, TILE)
        turned = jnp.broadcast_to(deal_ref[:, pl.ds(at, TILE)].astype(jnp.float32), (TILE, TILE)).T
        turned = turned.astype(jnp.int32)
        pick = jnp.concatenate([one_hot(turned, TILE * t + lane) for t in range(TILES)], axis=1)
        made = dot_nn(pick, res_all[...].reshape(TILES * TILE, width)).astype(jnp.bfloat16)
        dealt[b // 3, TILE * (b % 3) : TILE * (b % 3 + 1)] = made
    deals = list(dealt_sends(dealt, hid_out, 0, h_send, h_recv))
    start_all(deals)
    end_grads(grads, g_high, g_send, g_recv)
    for i in range(OWN):
        grad_ref[rows_of(i), half:] = dot_nn(
            picks[i], g_high[...].reshape(TILES * TILE, half)
        ).astype(jnp.bfloat16)

    def swap(j):
        slot, there = j % 2, 4 * (1 - core)
        copies = [remote(gwu_two.at[slot, pl.ds(there, 4)], got_u.at[j], c_send.at[j, 4], c_recv.at[j, 4], sibling)]
        for k in range(4):
            copies.append(
                remote(
                    gwi_two.at[slot, pl.ds(8 * k + there, 4)], got_i.at[j, k],
                    c_send.at[j, k], c_recv.at[j, k], sibling,
                )
            )
        return copies

    def take(j):
        return (
            pltpu.make_async_copy(got_i.at[j], gwi.at[:, :, :, pl.ds(chunk * j, chunk)], out_sem.at[0, j]),
            pltpu.make_async_copy(got_u.at[j], gwu.at[j], out_sem.at[1, j]),
        )

    def combine(j):
        slot, here = j % 2, 4 * core
        for copy in swap(j):
            copy.wait_recv()
        for n in range(4):
            got_u[j, n] = got_u[j, n] + gwu_two[slot, here + n]
            for k in range(4):
                got_i[j, k, n] = got_i[j, k, n] + gwi_two[slot, 8 * k + here + n]
        for copy in take(j):
            copy.start()
        for copy in swap(j):
            copy.wait_send()

    for j in range(chunks):
        span = slice(chunk * j, chunk * (j + 1))
        d_inner = (
            dot_nt(grad_ref[...], wu_ref[span, :]) * slope_ref[:, span].astype(jnp.float32)
        ).astype(jnp.bfloat16)
        made = dot_tn(active_ref[:, span], grad_ref[...])
        gwu_two[j % 2] = made.astype(jnp.bfloat16).reshape(gwu_two.shape[1:])
        made = dot_tn(normed_ref[...], d_inner)
        gwi_two[j % 2] = made.reshape(32, -1, chunk).astype(jnp.bfloat16)
        for copy in swap(j):
            copy.start()
        term = dot_nt(d_inner, wi_ref[:, span])
        total_ref[...] = term if j == 0 else total_ref[...] + term
        if j:
            combine(j - 1)

    mid = mid_ref[...]
    scale = lax.rsqrt(jnp.mean(mid * mid, axis=1, keepdims=True) + EPSILON)
    d_rows, d_gain = norm_back(mid, scale, gain, total_ref[...])
    two_ref[...] = gain_block(d_gain)
    d_mid = grad_ref[...].astype(jnp.float32) + d_rows
    dmid_ref[...] = d_mid
    branch = d_mid.astype(jnp.bfloat16)
    made = dot_tn(att_ref[...], branch)
    gwo_own[...] = made.reshape(32, -1, width).astype(jnp.bfloat16)
    swaps = [
        remote(
            gwo_own.at[pl.ds(8 * k + 4 * (1 - core), 4)], gwo_ref.at[k], c_send.at[chunks, k], c_recv.at[chunks, k], sibling
        )
        for k in range(4)
    ]
    for copy in swaps:
        copy.start()
    combine(chunks - 1)
    d_att = dot_nt(branch, wo_ref[...]).astype(jnp.bfloat16)
    pick = (lane_index((16, width)) // 64 == row_index((16, width))).astype(jnp.float32)
    prod = d_att.astype(jnp.float32) * att_ref[...].astype(jnp.float32)
    sums = lax.dot_general(
        pick, prod, (((1,), (1,)), ((), ())), precision=lax.Precision.HIGHEST, preferred_element_type=jnp.float32
    )
    for hp in range(PAIRS):
        datt_ref[hp] = d_att[:, 128 * hp : 128 * (hp + 1)].reshape(OWN, TILE, 128)
    for i in range(OWN):
        for h in range(2 * PAIRS):
            delta_ref[i, h] = sums[h : h + 1, TILE * i : TILE * (i + 1)]
    for k, copy in enumerate(swaps):
        copy.wait_recv()
        for n in range(4):
            gwo_ref[k, n] = gwo_ref[k, n] + gwo_own[8 * k + 4 * core + n]
        copy.wait_send()
    for j in range(chunks):
        for copy in take(j):
            copy.wait()
    res_copy.wait_send()
    for item in deals:
        sent(*item)
    for m in range(2):
        remote(hid_out.at[m], hid_out.at[m], h_send.at[0], h_recv.at[m], sibling).wait_recv()


def tail_kernel(
    x_ref, small_ref, g_two, g_rel, dmid_in, dq_in, dk_in, dv_in, wq_in, wk_in, wv_in,
    gin_out, tsmall, tq, tk, tv,
    dmid_ref, w_ref, join_ref, normed_ref, back_out, small, gq, gk, gv, *scratch,
):
    y, x, c, z = coordinates()
    sibling = place(y, x, 1 - c, z)
    owner, micro = z // 2, lax.rem(z, 2)
    greet()
    plain = [(gk, tk, None, "x"), (gv, tv, None, "y"), (gq, tq, None, "x"), (small, tsmall, None, "y")]
    count = len(plain)
    w_send, w_recv, w_local, b_send, b_recv, in_sem = scratch[3 * count :]
    scatter = Scatter(
        [item + tuple(scratch[3 * n : 3 * n + 3]) for n, item in enumerate(plain)], w_send, w_recv, w_local
    )
    grads_in = []
    for n, (w_in, pairs) in enumerate(((wq_in, dq_in), (wk_in, dk_in), (wv_in, dv_in))):
        copies = [pltpu.make_async_copy(w_in, w_ref.at[n], in_sem.at[n, PAIRS])]
        for hp in range(PAIRS):
            copies.append(
                pltpu.make_async_copy(
                    pairs.at[hp], join_ref.at[n, :, :, pl.ds(128 * hp, 128)], in_sem.at[n, hp]
                )
            )
        for copy in copies:
            copy.start()
        grads_in.append(copies)
    dmid_copy = pltpu.make_async_copy(dmid_in, dmid_ref, in_sem.at[3, 0])
    dmid_copy.start()

    def back_sends():
        for i in range(OWN):
            t = 2 * i + c
            z_to, l = t // 3, lax.rem(t, 3)
            yield (
                back_out.at[i], gin_out.at[micro, l], b_send.at[i], b_recv.at[micro, l],
                place(y, x, owner, z_to), (owner == c) & (z_to == z),
            )

    sends = list(back_sends())
    gain = gain_row(small_ref, 0, x_ref.shape[1])
    width = x_ref.shape[1]
    d_gain = None
    for half in range(2):
        tiles = slice(OWN // 2 * half, OWN // 2 * (half + 1))
        span = slice(TILE * tiles.start, TILE * tiles.stop)
        rows = x_ref[span, :].astype(jnp.float32)
        scale = lax.rsqrt(jnp.mean(rows * rows, axis=1, keepdims=True) + EPSILON)
        normed_ref[span, :] = (rows * scale * gain).astype(jnp.bfloat16)
        back = None
        for n in range(3):
            if half == 0:
                for copy in grads_in[n]:
                    copy.wait()
            term = dot_nt(join_ref[n, tiles].reshape(-1, width), w_ref[n])
            back = term if back is None else back + term
        d_rows, part = norm_back(rows, scale, gain, back)
        d_gain = part if d_gain is None else d_gain + part
        if half == 0:
            dmid_copy.wait()
        back_out[tiles] = (dmid_ref[span, :] + d_rows).astype(jnp.bfloat16).reshape(-1, TILE, width)
        if half == 0:
            greeted()
        start_all(sends[tiles])
    normed_t = normed_ref[...].T
    for n, (at, grad_ref) in enumerate(((1, gk), (2, gv), (0, gq))):
        made = dot_nn(normed_t, join_ref[at].reshape(-1, width))
        for r in range(32):
            grad_ref[r] = made[24 * r : 24 * (r + 1), :].astype(jnp.bfloat16)
        scatter.start(n)
    g_one = gain_block(d_gain)
    shape = (32, 16, 128)
    kind = lax.broadcasted_iota(jnp.int32, shape, 1)
    spread = lambda v: jnp.broadcast_to(v[:, None, :], shape)
    small[...] = jnp.where(
        kind == 0, spread(g_one), jnp.where(kind == 1, spread(g_two[...]), spread(g_rel[...]))
    ).astype(jnp.bfloat16)
    scatter.start(3)
    for n in range(count + 2):
        for back_by, stage in enumerate((scatter.sum_core, scatter.sum_side, scatter.sum_near)):
            if 0 <= n - back_by < count:
                stage(n - back_by)
    for n in range(count):
        scatter.finish(n)
    for item in sends:
        sent(*item)
    for m in range(2):
        for l in range(3):
            remote(back_out.at[0], gin_out.at[m, l], b_send.at[0], b_recv.at[m, l], sibling).wait_recv()


def coordinates():
    dp, z = lax.axis_index("dp"), lax.axis_index("fsdp")
    return dp // 4, lax.rem(dp // 2, 2), lax.rem(dp, 2), z


def place(y, x, c, z):
    return (4 * y + 2 * x + c, z)


def column(y, x, c):
    return 16 * y + 8 * x + 4 * c


def partners():
    y, x, c, z = coordinates()
    found = [place(1 - y, x, c, z), place(y, 1 - x, c, z)]
    for dc in range(2):
        for dz in range(4):
            if dc or dz:
                found.append(place(y, x, lax.rem(c + dc, 2), lax.rem(z + dz, 4)))
    return found


def greet():
    for partner in partners():
        pl.semaphore_signal(pltpu.get_barrier_semaphore(), inc=1, device_id=partner, device_id_type=MESH)


def greeted():
    pl.semaphore_wait(pltpu.get_barrier_semaphore(), len(partners()))


def remote(src, dst, send, recv, target):
    return pltpu.make_async_remote_copy(
        src, dst, send, recv, device_id=target, device_id_type=MESH
    )


def send_or_keep(src, dst, send, recv, target, here):
    @pl.when(jnp.logical_not(here))
    def _():
        remote(src, dst, send, recv, target).start()

    @pl.when(here)
    def _():
        pltpu.make_async_copy(src, dst, recv).start()


def sent(src, dst, send, recv, target, here):
    @pl.when(jnp.logical_not(here))
    def _():
        remote(src, dst, send, recv, target).wait_send()


def cut(ref, lead, part):
    return ref.at[lead] if part is None else ref.at[lead, slice(None), pl.ds(*part)]


def cut_shard(ref, part):
    return ref if part is None else ref.at[:, pl.ds(*part)]


class Gather:
    def __init__(self, pieces, send, recv, local):
        self.pieces, self.send, self.recv, self.local = pieces, send, recv, local
        self.y, self.x, self.c, self.z = coordinates()
        y, x, c, z = self.y, self.x, self.c, self.z
        self.sibling = place(y, x, 1 - c, z)
        self.mine = column(y, x, c)
        self.far = column(1 - y, 1 - x, c)
        by_x = (place(y, 1 - x, c, z), column(y, 1 - x, c))
        by_y = (place(1 - y, x, c, z), column(1 - y, x, c))
        self.sides = {"x": by_x + by_y, "y": by_y + by_x}

    def own_copy(self, n):
        shard, whole, part, _ = self.pieces[n]
        return pltpu.make_async_copy(
            cut_shard(shard, part), cut(whole, self.mine + self.z, part), self.local.at[n]
        )

    def z_copy(self, n, dz, came=False):
        shard, whole, part, _ = self.pieces[n]
        entry = self.mine + (lax.rem(self.z + 4 - dz, 4) if came else self.z)
        return remote(
            cut_shard(shard, part), cut(whole, entry, part), self.send.at[n, dz - 1], self.recv.at[n, dz - 1],
            place(self.y, self.x, self.c, lax.rem(self.z + dz, 4)),
        )

    def push(self, n, k, base, target):
        _, whole, part, _ = self.pieces[n]
        block = cut(whole, pl.ds(base, 4), part)
        return remote(block, block, self.send.at[n, k], self.recv.at[n, k], target)

    def start(self, n):
        self.own_copy(n).start()
        for dz in range(1, 4):
            self.z_copy(n, dz).start()

    def spread_own(self, n):
        near, _, side, _ = self.sides[self.pieces[n][3]]
        self.own_copy(n).wait()
        for dz in range(1, 4):
            self.z_copy(n, dz, True).wait_recv()
        for k, target in ((3, near), (4, side), (6, self.sibling)):
            self.push(n, k, self.mine, target).start()

    def spread_near(self, n):
        _, near_column, side, _ = self.sides[self.pieces[n][3]]
        self.push(n, 3, near_column, self.sibling).wait_recv()
        self.push(n, 5, near_column, side).start()
        self.push(n, 7, near_column, self.sibling).start()

    def spread_side(self, n):
        side_column = self.sides[self.pieces[n][3]][3]
        self.push(n, 4, side_column, self.sibling).wait_recv()
        self.push(n, 8, side_column, self.sibling).start()
        self.push(n, 5, self.far, self.sibling).wait_recv()
        self.push(n, 9, self.far, self.sibling).start()

    def finish(self, n):
        _, near_column, _, side_column = self.sides[self.pieces[n][3]]
        for k, base in ((6, self.mine), (7, near_column), (8, side_column), (9, self.far)):
            self.push(n, k, base + 4 - 8 * self.c, self.sibling).wait_recv()
        for dz in range(1, 4):
            self.z_copy(n, dz).wait_send()
        for k in range(3, 10):
            self.push(n, k, self.mine, self.sibling).wait_send()


class Scatter:
    def __init__(self, pieces, send, recv, local):
        self.pieces, self.send, self.recv, self.local = pieces, send, recv, local
        self.y, self.x, self.c, self.z = coordinates()
        y, x, c, z = self.y, self.x, self.c, self.z
        self.sibling = place(y, x, 1 - c, z)

    def sides(self, n):
        y, x, c, z = self.y, self.x, self.c, self.z
        by_x, by_y = place(y, 1 - x, c, z), place(1 - y, x, c, z)
        if self.pieces[n][3] == "x":
            return by_x, by_y, (lambda s, f: 2 * s + f), y, x
        return by_y, by_x, (lambda s, f: 2 * f + s), x, y

    def core_copy(self, n, k):
        grad, _, part, _, r1 = self.pieces[n][:5]
        return remote(
            cut(grad, pl.ds(8 * k + 4 * (1 - self.c), 4), part), r1.at[k],
            self.send.at[n, k], self.recv.at[n, k], self.sibling,
        )

    def side_copy(self, n, f_at):
        _, side, index, s, _ = self.sides(n)
        _, _, _, _, r1, r2, _ = self.pieces[n]
        return remote(
            r1.at[index(1 - s, f_at)], r2.at[f_at], self.send.at[n, 4 + f_at], self.recv.at[n, 4 + f_at], side
        )

    def near_copy(self, n):
        near, _, index, s, f = self.sides(n)
        _, _, _, _, r1, _, r3 = self.pieces[n]
        return remote(r1.at[index(s, 1 - f)], r3, self.send.at[n, 6], self.recv.at[n, 6], near)

    def z_copy(self, n, dz):
        _, _, index, s, f = self.sides(n)
        _, terms, part, _, r1, _, _ = self.pieces[n]
        z_to = lax.rem(self.z + dz, 4)
        return remote(
            r1.at[index(s, f), z_to], cut(terms, dz, part), self.send.at[n, 6 + dz], self.recv.at[n, 6 + dz],
            place(self.y, self.x, self.c, z_to),
        )

    def own_copy(self, n):
        _, _, index, s, f = self.sides(n)
        _, terms, part, _, r1, _, _ = self.pieces[n]
        return pltpu.make_async_copy(r1.at[index(s, f), self.z], cut(terms, 0, part), self.local.at[n, 0])

    def start(self, n):
        for k in range(4):
            self.core_copy(n, k).start()

    def sum_core(self, n):
        grad, _, part, _, r1 = self.pieces[n][:5]
        for k in range(4):
            self.core_copy(n, k).wait_recv()

            def one(j, carry, k=k):
                r1[k, j] = r1[k, j] + cut(grad, 8 * k + 4 * self.c + j, part)[...]
                return carry

            lax.fori_loop(0, 4, one, 0)
        for f_at in range(2):
            self.side_copy(n, f_at).start()

    def sum_side(self, n):
        _, _, index, s, _ = self.sides(n)
        _, _, _, _, r1, r2, _ = self.pieces[n]
        for f_at in range(2):
            self.side_copy(n, f_at).wait_recv()
            k = index(s, f_at)

            def one(j, carry, k=k, f_at=f_at):
                r1[k, j] = r1[k, j] + r2[f_at, j]
                return carry

            lax.fori_loop(0, 4, one, 0)
        self.near_copy(n).start()

    def sum_near(self, n):
        _, _, index, s, f = self.sides(n)
        _, _, _, _, r1, _, r3 = self.pieces[n]
        self.near_copy(n).wait_recv()
        k = index(s, f)

        def one(j, carry):
            r1[k, j] = r1[k, j] + r3[j]
            return carry

        lax.fori_loop(0, 4, one, 0)
        for dz in range(1, 4):
            self.z_copy(n, dz).start()
        self.own_copy(n).start()

    def finish(self, n):
        self.own_copy(n).wait()
        for dz in range(1, 4):
            self.z_copy(n, dz).wait_recv()
        for k in range(4):
            self.core_copy(n, k).wait_send()
        for f_at in range(2):
            self.side_copy(n, f_at).wait_send()
        self.near_copy(n).wait_send()
        for dz in range(1, 4):
            self.z_copy(n, dz).wait_send()


class LateScatter(Scatter):
    def side_copy(self, n, f_at):
        _, side, index, s, _ = self.sides(n)
        summed, _, part, _, _, r2, _ = self.pieces[n]
        return remote(
            cut(summed.at[index(1 - s, f_at)], pl.ds(0, 4), part), r2.at[f_at],
            self.send.at[n, 4 + f_at], self.recv.at[n, 4 + f_at], side,
        )

    def fetch(self, n, f_at):
        _, _, index, s, _ = self.sides(n)
        summed, _, part, _, own, _, _ = self.pieces[n]
        return pltpu.make_async_copy(
            cut(summed.at[index(s, f_at)], pl.ds(0, 4), part), own.at[f_at], self.local.at[n, 1 + f_at]
        )

    def near_copy(self, n):
        near, _, _, _, f = self.sides(n)
        _, _, _, _, _, r2, r3 = self.pieces[n]
        return remote(r2.at[1 - f], r3, self.send.at[n, 6], self.recv.at[n, 6], near)

    def z_copy(self, n, dz):
        f = self.sides(n)[4]
        _, terms, part, _, _, r2, _ = self.pieces[n]
        z_to = lax.rem(self.z + dz, 4)
        return remote(
            r2.at[f, z_to], cut(terms, dz, part), self.send.at[n, 6 + dz], self.recv.at[n, 6 + dz],
            place(self.y, self.x, self.c, z_to),
        )

    def own_copy(self, n):
        f = self.sides(n)[4]
        _, terms, part, _, _, r2, _ = self.pieces[n]
        return pltpu.make_async_copy(r2.at[f, self.z], cut(terms, 0, part), self.local.at[n, 0])

    def start(self, n):
        for f_at in range(2):
            self.side_copy(n, f_at).start()
            self.fetch(n, f_at).start()

    def sum_side(self, n):
        _, _, _, _, own, r2, _ = self.pieces[n]
        for f_at in range(2):
            self.side_copy(n, f_at).wait_recv()
            self.fetch(n, f_at).wait()

            def one(j, carry, f_at=f_at):
                r2[f_at, j] = r2[f_at, j] + own[f_at, j]
                return carry

            lax.fori_loop(0, 4, one, 0)
        self.near_copy(n).start()

    def sum_near(self, n):
        f = self.sides(n)[4]
        _, _, _, _, _, r2, r3 = self.pieces[n]
        self.near_copy(n).wait_recv()

        def one(j, carry):
            r2[f, j] = r2[f, j] + r3[j]
            return carry

        lax.fori_loop(0, 4, one, 0)
        for dz in range(1, 4):
            self.z_copy(n, dz).start()
        self.own_copy(n).start()

    def finish(self, n):
        self.own_copy(n).wait()
        for dz in range(1, 4):
            self.z_copy(n, dz).wait_recv()
        for f_at in range(2):
            self.side_copy(n, f_at).wait_send()
        self.near_copy(n).wait_send()
        for dz in range(1, 4):
            self.z_copy(n, dz).wait_send()


def run_events(events, hp, i):
    for at in range(PAIRS):
        todo = events.get(at * OWN + i, ())
        if todo:

            @pl.when(hp == at)
            def _(todo=todo):
                for step in todo:
                    step()


def late(events):
    for at in sorted(events):
        if at >= PAIRS * OWN:
            for step in events[at]:
                step()


def token_sends(hid_in, x_own, x_send, x_recv):
    y, x, c, z = coordinates()
    for m in range(2):
        for l in range(3):
            t = 3 * z + l
            core_to, z_to = lax.rem(t, 2), 2 * c + m
            yield (
                hid_in.at[m, l], x_own.at[t // 2], x_send.at[m, l], x_recv.at[t // 2],
                place(y, x, core_to, z_to), (core_to == c) & (z_to == z),
            )


def start_all(items):
    for item in items:
        send_or_keep(*item)


def grad_sends(grd_in, g_part, first, g_send, g_recv):
    y, x, c, z = coordinates()
    width = g_part.shape[2]
    for m in range(2):
        for half in range(2):
            z_to = 2 * c + m
            yield (
                grd_in.at[m, half, :, pl.ds(first, width)], g_part.at[2 * z + half], g_send.at[0, m, half],
                g_recv.at[0, z], place(y, x, half, z_to), (half == c) & (z_to == z),
            )


def dealt_sends(dealt, hid_part, first, h_send, h_recv):
    y, x, c, z = coordinates()
    owner, micro = z // 2, lax.rem(z, 2)
    for e in range(2):
        z_to = 2 * c + e
        yield (
            dealt.at[e, :, pl.ds(first, hid_part.shape[2])], hid_part.at[micro], h_send.at[e], h_recv.at[micro],
            place(y, x, owner, z_to), (owner == c) & (z_to == z),
        )


def share_copy(g_part, zs, core, g_send, g_recv):
    y, x, c, z = coordinates()
    block = g_part.at[2 * zs + core]
    return remote(
        block, block, g_send.at[1, zs // 2, zs % 2], g_recv.at[1, zs], place(y, x, 1 - c, z)
    )


def share_grads(g_part, g_send, g_recv):
    y, x, c, z = coordinates()
    for zs in range(4):
        block = g_part.at[2 * zs + c]
        remote(block, block, g_send.at[1, 0, 0], g_recv.at[0, zs], place(y, x, 1 - c, z)).wait_recv()
        share_copy(g_part, zs, c, g_send, g_recv).start()


def end_grads(items, g_part, g_send, g_recv):
    c = coordinates()[2]
    for zs in range(4):
        share_copy(g_part, zs, 1 - c, g_send, g_recv).wait_recv()
        share_copy(g_part, zs, c, g_send, g_recv).wait_send()
    for item in items:
        sent(*item)


def gather_kernel(first_axis, *refs):
    count = len(first_axis)
    lens_in, deal_in, hid_in, one_in, two_in, rel_in = refs[:6]
    shards = refs[6 : 5 + count]
    rest = refs[5 + count :]
    lens_u, deal_u, x_own = rest[:3]
    outs = rest[3 : 3 + count]
    lens_wide, rows_f, small, w_send, w_recv, w_local, x_send, x_recv, p_send, p_recv = rest[3 + count :]
    y, x, c, z = coordinates()
    sibling = place(y, x, 1 - c, z)
    greet()
    rows_f[...] = jnp.zeros_like(rows_f)
    rows_f[0:1, : one_in.shape[1]] = one_in[...].astype(jnp.float32)
    rows_f[1:2, : two_in.shape[1]] = two_in[...].astype(jnp.float32)
    rows_f[2:3, : rel_in.shape[1]] = rel_in[...].astype(jnp.float32)
    small[...] = rows_f[...].astype(jnp.bfloat16)
    lens_wide[...] = jnp.zeros_like(lens_wide)
    lens_wide[:, :, : lens_in.shape[2]] = lens_in[...]
    greeted()
    gather = Gather(
        [(s, o, None, a) for s, o, a in zip((small,) + tuple(shards), outs, first_axis)], w_send, w_recv, w_local
    )
    for n in range(count):
        gather.start(n)
    sends = list(token_sends(hid_in, x_own, x_send, x_recv))
    for item in sends:
        send_or_keep(*item)
    owner, micro = z // 2, lax.rem(z, 2)
    plans = []
    for n, (src, dst) in enumerate(((lens_wide, lens_u), (deal_in, deal_u))):
        plans.append((src.at[micro], dst, p_send.at[n], p_recv.at[n]))

    @pl.when(owner == c)
    def _():
        for src, dst, send, recv in plans:
            remote(src, dst, send, recv, sibling).start()
            pltpu.make_async_copy(src, dst, recv).start()

    for n in range(count):
        gather.spread_own(n)
    for n in range(count):
        gather.spread_near(n)
    for n in range(count):
        gather.spread_side(n)
    for n in range(count):
        gather.finish(n)
    for item in sends:
        sent(*item)
    for i in range(OWN):
        remote(hid_in.at[0, 0], x_own.at[i], x_send.at[0, 0], x_recv.at[i], sibling).wait_recv()
    for src, dst, send, recv in plans:
        remote(src, dst, send, recv, sibling).wait_recv()

    @pl.when(owner == c)
    def _():
        for src, dst, send, recv in plans:
            remote(src, dst, send, recv, sibling).wait_send()


def sum_terms(term):
    total = term[0].astype(jnp.float32)
    for dz in range(1, 4):
        total = total + term[dz].astype(jnp.float32)
    return total


def sum_kernel(
    hid_low, hid_high, gin_in, tsmall, tq, tk, tv, two, twi, twu,
    hid_out, gin_out, one_out, two_out, rel_out, gq, gk, gv, gwo, gwi, gwu,
):
    half = hid_low.shape[2]
    hid_out[:, :, :half] = hid_low[...].astype(jnp.float32)
    hid_out[:, :, half:] = hid_high[...].astype(jnp.float32)
    gin_out[...] = gin_in[...].astype(jnp.float32)

    @pl.when(pl.program_id(0) == 0)
    def _():
        small = sum_terms(tsmall)
        one_out[...] = small[0:1, : one_out.shape[1]]
        two_out[...] = small[1:2, : two_out.shape[1]]
        rel_out[...] = small[2:3, : rel_out.shape[1]]
        for term, out in ((tq, gq), (tk, gk), (tv, gv), (two, gwo), (twi, gwi), (twu, gwu)):
            out[...] = sum_terms(term)


def token_places(deal_order, lengths):
    seq_ends = jnp.cumsum(lengths)
    starts = seq_ends - lengths
    inside = (deal_order[:, None] >= starts[None, :]).astype(jnp.int32)
    segment = jnp.sum(inside, axis=1) - 1
    picked = (segment[:, None] == jnp.arange(lengths.shape[0], dtype=jnp.int32)[None, :]).astype(
        jnp.int32
    )
    position = deal_order - jnp.sum(picked * starts[None, :], axis=1)
    return (segment, position)


def rms_scale(rows_in):
    return lax.rsqrt(jnp.mean(rows_in * rows_in, axis=1, keepdims=True) + EPSILON)


def gelu_slope(values):
    normal_cdf = 0.5 * (1.0 + jax.scipy.special.erf(values * (1.0 / math.sqrt(2.0))))
    normal_pdf = jnp.exp(-0.5 * values * values) * (1.0 / math.sqrt(2.0 * math.pi))
    return normal_cdf + values * normal_pdf


def norm_back_rows(rows_in, scale, gain, grad_normed):
    scaled_grad = grad_normed * gain
    grad_gain = jnp.sum(grad_normed * rows_in * scale, axis=0)
    grad_rows = scale * scaled_grad - rows_in * scale * scale * scale * jnp.mean(
        scaled_grad * rows_in, axis=1, keepdims=True
    )
    return (grad_rows, grad_gain)


def key_layout(key_all, value_all, segment, position, head_count):
    rows_all = key_all.shape[0]
    block_rows = 512
    blocks = rows_all // block_rows
    return (
        key_all.reshape(blocks, block_rows, head_count, -1),
        value_all.reshape(blocks, block_rows, head_count, -1),
        segment.reshape(blocks, block_rows),
        position.reshape(blocks, block_rows),
    )


def block_scores(
    queries,
    key_block,
    seg_query,
    pos_query,
    seg_block,
    pos_block,
    rel_bucket,
    bucket_edges,
    max_offset,
):
    lower_edge, upper_edge = bucket_edges
    raw_scores = jnp.einsum("qhd,khd->hqk", queries, key_block, preferred_element_type=jnp.float32)
    offset = jnp.clip(pos_block[None, :] - pos_query[:, None], -max_offset, max_offset)
    bucket_hit = (
        (offset[:, :, None] >= lower_edge[None, None, :])
        & (offset[:, :, None] <= upper_edge[None, None, :])
    ).astype(jnp.float32)
    bias = jnp.einsum(
        "qkb,bh->hqk",
        bucket_hit,
        rel_bucket,
        precision=lax.Precision.HIGHEST,
        preferred_element_type=jnp.float32,
    )
    same_seq = (seg_query[:, None] == seg_block[None, :])[None]
    return (raw_scores + bias, same_seq, bucket_hit)


def attend(queries, layout, seg_query, pos_query, rel_bucket, bucket_edges, max_offset):
    key_blocks, value_blocks, seg_blocks, pos_blocks = layout
    query_count, head_count, head_size = queries.shape

    def measure(carry, block):
        row_top, row_total = carry
        key_block, seg_block, pos_block = block
        scores, same_seq, _ = block_scores(
            queries,
            key_block,
            seg_query,
            pos_query,
            seg_block,
            pos_block,
            rel_bucket,
            bucket_edges,
            max_offset,
        )
        scores = jnp.where(same_seq, scores, NEG_FILL)
        new_top = jnp.maximum(row_top, jnp.max(scores, axis=2))
        weights_now = jnp.where(same_seq, jnp.exp(scores - new_top[:, :, None]), 0.0)
        row_total = row_total * jnp.exp(row_top - new_top) + jnp.sum(weights_now, axis=2)
        return ((new_top, row_total), None)

    start = (
        jnp.full((head_count, query_count), NEG_FILL, jnp.float32),
        jnp.zeros((head_count, query_count), jnp.float32),
    )
    (row_top, row_total), _ = lax.scan(measure, start, (key_blocks, seg_blocks, pos_blocks))
    log_total = row_top + jnp.log(row_total)

    def collect(summed, block):
        key_block, value_block, seg_block, pos_block = block
        scores, same_seq, _ = block_scores(
            queries,
            key_block,
            seg_query,
            pos_query,
            seg_block,
            pos_block,
            rel_bucket,
            bucket_edges,
            max_offset,
        )
        probs = jnp.where(same_seq, jnp.exp(scores - log_total[:, :, None]), 0.0).astype(
            jnp.bfloat16
        )
        return (
            summed
            + jnp.einsum("hqk,khd->qhd", probs, value_block, preferred_element_type=jnp.float32),
            None,
        )

    attended_f, _ = lax.scan(
        collect, jnp.zeros((query_count, head_count, head_size), jnp.float32), layout
    )
    return (attended_f, log_total)


def attend_back(
    queries,
    layout,
    seg_query,
    pos_query,
    rel_bucket,
    bucket_edges,
    max_offset,
    log_total,
    d_attended,
    row_delta,
):

    def step(carry, block):
        d_queries, d_buckets = carry
        key_block, value_block, seg_block, pos_block = block
        scores, same_seq, bucket_hit = block_scores(
            queries,
            key_block,
            seg_query,
            pos_query,
            seg_block,
            pos_block,
            rel_bucket,
            bucket_edges,
            max_offset,
        )
        probs_f = jnp.where(same_seq, jnp.exp(scores - log_total[:, :, None]), 0.0)
        d_probs = jnp.einsum(
            "qhd,khd->hqk", d_attended, value_block, preferred_element_type=jnp.float32
        )
        d_scores = (probs_f * (d_probs - row_delta[:, :, None])).astype(jnp.bfloat16)
        d_queries = d_queries + jnp.einsum(
            "hqk,khd->qhd", d_scores, key_block, preferred_element_type=jnp.float32
        )
        d_buckets = d_buckets + jnp.einsum(
            "hqk,qkb->bh",
            d_scores,
            bucket_hit.astype(jnp.bfloat16),
            preferred_element_type=jnp.float32,
        )
        d_values = jnp.einsum(
            "hqk,qhd->khd",
            probs_f.astype(jnp.bfloat16),
            d_attended,
            preferred_element_type=jnp.float32,
        )
        d_keys = jnp.einsum("hqk,qhd->khd", d_scores, queries, preferred_element_type=jnp.float32)
        return ((d_queries, d_buckets), (d_keys, d_values))

    start = (jnp.zeros(queries.shape, jnp.float32), jnp.zeros(rel_bucket.shape, jnp.float32))
    (d_queries, d_buckets), key_terms = lax.scan(step, start, layout)
    return (d_queries, key_terms, d_buckets)


def on_device(
    hidden_in,
    grad_out,
    gain_attn,
    gain_ffn,
    rel_bias,
    w_query,
    w_key,
    w_value,
    w_output,
    w_inner,
    w_outer,
    dealing,
    lengths,
    bucket_table,
):
    micro_count, tok_rows, model_width = hidden_in.shape
    group_size = lax.axis_size("fsdp")
    slot_rows = tok_rows // group_size
    own_index = lax.axis_index("fsdp")
    max_offset = (bucket_table.shape[0] - 1) // 2
    bucket_count = BUCKETS
    head_count = H
    offsets_all = jnp.arange(bucket_table.shape[0], dtype=jnp.int32) - max_offset
    matches = bucket_table[:, None] == jnp.arange(bucket_count, dtype=jnp.int32)[None, :]
    lower_edge = jnp.min(jnp.where(matches, offsets_all[:, None], 2 * max_offset + 2), axis=0)
    upper_edge = jnp.max(jnp.where(matches, offsets_all[:, None], -2 * max_offset - 2), axis=0)
    bucket_edges = (lower_edge, upper_edge)
    hidden_units = w_inner.shape[1]
    acc_gain_one = jnp.zeros((model_width,), jnp.float32)
    acc_gain_two = jnp.zeros((model_width,), jnp.float32)
    acc_buckets = jnp.zeros((bucket_count, head_count), jnp.float32)
    acc_query = jnp.zeros((model_width, model_width), jnp.float32)
    acc_key = jnp.zeros((model_width, model_width), jnp.float32)
    acc_value = jnp.zeros((model_width, model_width), jnp.float32)
    acc_output = jnp.zeros((model_width, model_width), jnp.float32)
    acc_inner = jnp.zeros((model_width, hidden_units), jnp.float32)
    acc_outer = jnp.zeros((hidden_units, model_width), jnp.float32)
    outputs_list = []
    grads_list = []
    for micro_idx in range(micro_count):
        weights_now = (
            lax.all_gather(gain_attn, ("dp", "fsdp"), axis=0, tiled=True),
            lax.all_gather(gain_ffn, ("dp", "fsdp"), axis=0, tiled=True),
            lax.all_gather(rel_bias, ("dp", "fsdp"), axis=0, tiled=True),
            lax.all_gather(w_query, ("dp", "fsdp"), axis=0, tiled=True),
            lax.all_gather(w_key, ("dp", "fsdp"), axis=0, tiled=True),
            lax.all_gather(w_value, ("dp", "fsdp"), axis=0, tiled=True),
            lax.all_gather(w_output, ("dp", "fsdp"), axis=0, tiled=True),
            lax.all_gather(w_inner, ("dp", "fsdp"), axis=0, tiled=True),
            lax.all_gather(w_outer, ("dp", "fsdp"), axis=0, tiled=True),
        )
        gain_one = weights_now[0].astype(jnp.float32)
        gain_two = weights_now[1].astype(jnp.float32)
        rel_bucket = weights_now[2].astype(jnp.float32).reshape(bucket_count, head_count)
        query_weight, key_weight, value_weight, output_weight, inner_weight, outer_weight = (
            weights_now[3:]
        )
        deal_order = dealing[micro_idx, 0]
        segment, position = token_places(deal_order, lengths[micro_idx, 0])
        seg_query = lax.dynamic_slice_in_dim(segment, own_index * tok_rows, tok_rows)
        pos_query = lax.dynamic_slice_in_dim(position, own_index * tok_rows, tok_rows)
        take_rows = (
            lax.dynamic_slice_in_dim(
                deal_order.reshape(group_size, tok_rows), own_index * slot_rows, slot_rows, 1
            )
            - own_index * tok_rows
        ).reshape(tok_rows)
        dealt = lax.all_to_all(
            jnp.take(hidden_in[micro_idx], take_rows, axis=0),
            "fsdp",
            split_axis=0,
            concat_axis=0,
            tiled=True,
        )
        dealt_rows = dealt.astype(jnp.float32)
        scale_one = rms_scale(dealt_rows)
        normed1 = (dealt_rows * scale_one * gain_one).astype(jnp.bfloat16)
        queries = jnp.dot(normed1, query_weight, preferred_element_type=jnp.float32).astype(
            jnp.bfloat16
        )
        key_rows = jnp.dot(normed1, key_weight, preferred_element_type=jnp.float32).astype(
            jnp.bfloat16
        )
        value_rows = jnp.dot(normed1, value_weight, preferred_element_type=jnp.float32).astype(
            jnp.bfloat16
        )
        key_all, value_all = (
            lax.all_gather(key_rows, "fsdp", axis=0, tiled=True),
            lax.all_gather(value_rows, "fsdp", axis=0, tiled=True),
        )
        layout = key_layout(key_all, value_all, segment, position, head_count)
        queries_heads = queries.reshape(tok_rows, head_count, -1)
        attended_f, log_total = attend(
            queries_heads, layout, seg_query, pos_query, rel_bucket, bucket_edges, max_offset
        )
        attended = attended_f.reshape(tok_rows, model_width).astype(jnp.bfloat16)
        mid = dealt_rows + jnp.dot(attended, output_weight, preferred_element_type=jnp.float32)
        scale_two = rms_scale(mid)
        normed2 = (mid * scale_two * gain_two).astype(jnp.bfloat16)
        inner_act = jnp.dot(normed2, inner_weight, preferred_element_type=jnp.float32)
        active = jax.nn.gelu(inner_act, approximate=False).astype(jnp.bfloat16)
        result = mid + jnp.dot(active, outer_weight, preferred_element_type=jnp.float32)
        outputs_list.append(result)
        weights_back = (
            lax.all_gather(gain_attn, ("dp", "fsdp"), axis=0, tiled=True),
            lax.all_gather(gain_ffn, ("dp", "fsdp"), axis=0, tiled=True),
            lax.all_gather(rel_bias, ("dp", "fsdp"), axis=0, tiled=True),
            lax.all_gather(w_query, ("dp", "fsdp"), axis=0, tiled=True),
            lax.all_gather(w_key, ("dp", "fsdp"), axis=0, tiled=True),
            lax.all_gather(w_value, ("dp", "fsdp"), axis=0, tiled=True),
            lax.all_gather(w_output, ("dp", "fsdp"), axis=0, tiled=True),
            lax.all_gather(w_inner, ("dp", "fsdp"), axis=0, tiled=True),
            lax.all_gather(w_outer, ("dp", "fsdp"), axis=0, tiled=True),
        )
        query_weight, key_weight, value_weight, output_weight, inner_weight, outer_weight = (
            weights_back[3:]
        )
        grad_top = grad_out[micro_idx]
        acc_outer = acc_outer + jnp.einsum(
            "tf,td->fd", active, grad_top, preferred_element_type=jnp.float32
        )
        d_active = jnp.einsum(
            "td,fd->tf", grad_top, outer_weight, preferred_element_type=jnp.float32
        )
        d_inner = (d_active * gelu_slope(inner_act)).astype(jnp.bfloat16)
        acc_inner = acc_inner + jnp.einsum(
            "td,tf->df", normed2, d_inner, preferred_element_type=jnp.float32
        )
        d_normed2 = jnp.einsum(
            "tf,df->td", d_inner, inner_weight, preferred_element_type=jnp.float32
        )
        d_mid_norm, d_gain_two = norm_back_rows(mid, scale_two, gain_two, d_normed2)
        acc_gain_two = acc_gain_two + d_gain_two
        d_mid = grad_top.astype(jnp.float32) + d_mid_norm
        d_branch = d_mid.astype(jnp.bfloat16)
        acc_output = acc_output + jnp.einsum(
            "td,te->de", attended, d_branch, preferred_element_type=jnp.float32
        )
        d_attended = jnp.einsum(
            "te,de->td", d_branch, output_weight, preferred_element_type=jnp.float32
        ).astype(jnp.bfloat16)
        d_attended_heads = d_attended.reshape(tok_rows, head_count, -1)
        row_delta = jnp.sum(d_attended_heads.astype(jnp.float32) * attended_f, axis=2).T
        key_back, value_back = (
            lax.all_gather(key_rows, "fsdp", axis=0, tiled=True),
            lax.all_gather(value_rows, "fsdp", axis=0, tiled=True),
        )
        layout_back = key_layout(key_back, value_back, segment, position, head_count)
        d_queries, key_terms, d_buckets = attend_back(
            queries_heads,
            layout_back,
            seg_query,
            pos_query,
            rel_bucket,
            bucket_edges,
            max_offset,
            log_total,
            d_attended_heads,
            row_delta,
        )
        d_keys, d_values = key_terms
        group_rows = d_keys.shape[0] * d_keys.shape[1]
        d_keys_own, d_values_own = (
            lax.psum_scatter(
                d_keys.reshape(group_rows, model_width).astype(jnp.bfloat16),
                "fsdp",
                scatter_dimension=0,
                tiled=True,
            ).astype(jnp.float32),
            lax.psum_scatter(
                d_values.reshape(group_rows, model_width).astype(jnp.bfloat16),
                "fsdp",
                scatter_dimension=0,
                tiled=True,
            ).astype(jnp.float32),
        )
        acc_buckets = acc_buckets + d_buckets
        d_queries_low = d_queries.reshape(tok_rows, model_width).astype(jnp.bfloat16)
        d_keys_low = d_keys_own.astype(jnp.bfloat16)
        d_values_low = d_values_own.astype(jnp.bfloat16)
        acc_query = acc_query + jnp.einsum(
            "td,te->de", normed1, d_queries_low, preferred_element_type=jnp.float32
        )
        acc_key = acc_key + jnp.einsum(
            "td,te->de", normed1, d_keys_low, preferred_element_type=jnp.float32
        )
        acc_value = acc_value + jnp.einsum(
            "td,te->de", normed1, d_values_low, preferred_element_type=jnp.float32
        )
        d_normed1 = (
            jnp.einsum("te,de->td", d_queries_low, query_weight, preferred_element_type=jnp.float32)
            + jnp.einsum("te,de->td", d_keys_low, key_weight, preferred_element_type=jnp.float32)
            + jnp.einsum(
                "te,de->td", d_values_low, value_weight, preferred_element_type=jnp.float32
            )
        )
        d_rows_norm, d_gain_one = norm_back_rows(dealt_rows, scale_one, gain_one, d_normed1)
        acc_gain_one = acc_gain_one + d_gain_one
        d_dealt = d_mid + d_rows_norm
        returned = lax.all_to_all(
            d_dealt.astype(jnp.bfloat16), "fsdp", split_axis=0, concat_axis=0, tiled=True
        ).astype(d_dealt.dtype)
        grads_list.append(jnp.zeros_like(returned).at[take_rows].set(returned))
    acc_rel = acc_buckets.reshape(-1)
    summed = (
        lax.psum_scatter(acc_gain_one, ("dp", "fsdp"), scatter_dimension=0, tiled=True),
        lax.psum_scatter(acc_gain_two, ("dp", "fsdp"), scatter_dimension=0, tiled=True),
        lax.psum_scatter(acc_rel, ("dp", "fsdp"), scatter_dimension=0, tiled=True),
        lax.psum_scatter(acc_query, ("dp", "fsdp"), scatter_dimension=0, tiled=True),
        lax.psum_scatter(acc_key, ("dp", "fsdp"), scatter_dimension=0, tiled=True),
        lax.psum_scatter(acc_value, ("dp", "fsdp"), scatter_dimension=0, tiled=True),
        lax.psum_scatter(acc_output, ("dp", "fsdp"), scatter_dimension=0, tiled=True),
        lax.psum_scatter(acc_inner, ("dp", "fsdp"), scatter_dimension=0, tiled=True),
        lax.psum_scatter(acc_outer, ("dp", "fsdp"), scatter_dimension=0, tiled=True),
    )
    return (
        jnp.stack(outputs_list),
        jnp.stack(grads_list),
        summed[0],
        summed[1],
        summed[2],
        summed[3],
        summed[4],
        summed[5],
        summed[6],
        summed[7],
        summed[8],
    )


VMEM = pl.BlockSpec(memory_space=pltpu.VMEM)
SMEM = pl.BlockSpec(memory_space=pltpu.SMEM)
ANYWHERE = pl.BlockSpec(memory_space=pl.ANY)
LIMIT = 58 * 1024 * 1024
FIRST_AXIS = ("x", "x", "y", "x", "y")
FWD_PARTS = 3
FWD_AHEAD = 2
FWD_OWN = (-1, 0, 6, 12, 15, 21)
FWD_NEAR = (9, 12, 18, 24, 27, 33)
FWD_SIDE = (21, 24, 30, 36, 41, 41)
FWD_GRADS = 15
FFN_CHUNK = 768
BWD_PARTS = 3
BWD_AHEAD = 4
BWD_SIDE = (12, 14, 20, 20, 24, 26, 28)
BWD_NEAR = (18, 22, 26, 24, 28, 30, 34)


def shaped(*shape, dtype=jnp.bfloat16):
    return jax.ShapeDtypeStruct(shape, dtype)


def params(collective_id=None):
    if collective_id is None:
        return pltpu.CompilerParams(vmem_limit_bytes=LIMIT)
    return pltpu.CompilerParams(
        collective_id=collective_id, has_side_effects=True, vmem_limit_bytes=LIMIT
    )


def dma(*shape):
    return pltpu.SemaphoreType.DMA(shape)


def gather_all(lens, deal, hid, one, two, rel, shards):
    count = len(shards) + 1
    return pl.pallas_call(
        functools.partial(gather_kernel, FIRST_AXIS),
        name="gather_all",
        out_shape=[
            shaped(1, 128, dtype=jnp.int32),
            shaped(*deal.shape[1:], dtype=jnp.int32),
            shaped(OWN, TILE, hid.shape[-1]),
            shaped(32, 16, 128),
        ]
        + [shaped(32, *s.shape) for s in shards],
        in_specs=[VMEM] + [ANYWHERE] * 2 + [VMEM] * 3 + [ANYWHERE] * (count - 1),
        out_specs=[ANYWHERE] * (3 + count),
        scratch_shapes=[
            pltpu.VMEM((2, 1, 128), jnp.int32), pltpu.VMEM((16, 128), jnp.float32), pltpu.VMEM((16, 128), jnp.bfloat16),
            dma(count, 10), dma(count, 10), dma(count), dma(2, 3), dma(OWN), dma(2), dma(2),
        ],
        compiler_params=params(0),
    )(lens, deal, hid, one, two, rel, *shards)


def attention_forward(lens, x, small, table, wq, wk, wv, grd, wi, wu):
    heads, keys = (PAIRS, OWN, TILE, 128), (PAIRS, OWN, 2, TILE, 128)
    count = len(FWD_OWN)
    return pl.pallas_call(
        attn_fwd,
        name="attn_fwd",
        out_shape=[
            shaped(*heads), shaped(*keys), shaped(*keys), shaped(*x.shape),
            shaped(OWN, 2 * PAIRS, 1, TILE, dtype=jnp.float32),
            shaped(8, grd.shape[2], grd.shape[3] // 2),
            shaped(32, *wi.shape), shaped(32, *wu.shape),
        ],
        in_specs=[SMEM] + [VMEM] * 6 + [ANYWHERE] * 3,
        out_specs=[VMEM] * 5 + [ANYWHERE] * 3,
        scratch_shapes=[
            pltpu.VMEM((5, 2 * PAIRS, 1, 2 * TILE), jnp.float32),
            pltpu.VMEM((2 * PAIRS, 5, TILE, TILE), jnp.float32),
            pltpu.VMEM((OWN, TILE, 128), jnp.bfloat16),
            pltpu.VMEM((TILES, TILE, 128), jnp.bfloat16),
            pltpu.VMEM((2, TILE, TILES * TILE), jnp.float32),
            pltpu.VMEM((OWN, TILE, 128), jnp.float32),
            dma(2), dma(2),
            dma(count, 10), dma(count, 10), dma(count), dma(2, 2, 2), dma(2, 4),
        ],
        compiler_params=params(1),
    )(lens, x, small, table, wq, wk, wv, grd, wi, wu)


def landing(shapes, leads=((4, 4), (2, 4), (4,))):
    return [pltpu.VMEM((*lead, *b), jnp.bfloat16) for b in shapes for lead in leads]


def attention_backward(lens, q, k, v, log_total, d_att, delta, small, table, gwo, gwi, gwu, dealt):
    heads = (PAIRS, OWN, TILE, 128)
    block_i, block_u = (gwi.shape[2], gwi.shape[3] // BWD_PARTS), (gwu.shape[2], gwu.shape[3] // BWD_PARTS)
    blocks = [block_i, block_u] * BWD_PARTS + [gwo.shape[2:]]
    count = len(blocks)
    return pl.pallas_call(
        attn_bwd,
        name="attn_bwd",
        out_shape=[shaped(*heads)] * 3
        + [shaped(32, 128, dtype=jnp.float32)]
        + [shaped(4, *g.shape[2:]) for g in (gwo, gwi, gwu)]
        + [shaped(*dealt.shape[:2], dealt.shape[2] // 2)],
        in_specs=[SMEM] + [VMEM] * 8 + [ANYWHERE] * 4,
        out_specs=[VMEM] * 4 + [ANYWHERE] * 4,
        scratch_shapes=[pltpu.VMEM((5, 2 * PAIRS, 1, 2 * TILE), jnp.float32)] * 2
        + [pltpu.VMEM((2 * PAIRS, 5, TILE, TILE), jnp.float32)] * 2
        + [pltpu.VMEM((OWN, TILE, 128), jnp.bfloat16), pltpu.VMEM((TILES, TILE, 128), jnp.bfloat16)]
        + [pltpu.VMEM((TILES * TILE, 128), jnp.float32)] * 2
        + [pltpu.VMEM(heads, jnp.bfloat16)] * 4
        + [dma(2, PAIRS), dma(2, PAIRS), dma(count, 10), dma(count, 10), dma(count, 3), dma(2), dma(2)]
        + landing(blocks, ((2, 4), (2, 4), (4,))),
        compiler_params=params(2),
    )(lens, q, k, v, log_total, d_att, delta, small, table, gwo, gwi, gwu, dealt)


def feed_forward(deal, x, att, wo, small, g_low, grd, wi, wu):
    tok, width = x.shape
    hidden = wi.shape[1]
    f32, bf16 = jnp.float32, jnp.bfloat16
    heads, stats = (PAIRS, OWN, TILE, 128), (OWN, 2 * PAIRS, 1, TILE)
    block_i, block_u = (32, width // 32, hidden), (32, hidden // 32, width)
    chunks = hidden // FFN_CHUNK
    return pl.pallas_call(
        ffn_kernel,
        name="feed_forward",
        out_shape=[
            shaped(tok, width, dtype=f32), shaped(*heads), shaped(*stats, dtype=f32),
            shaped(4, 4, width // 32, width), shaped(32, 128, dtype=f32), shaped(2, 3 * TILE, width),
            shaped(4, 4, *block_i[1:]), shaped(4, 4, *block_u[1:]), shaped(2, 3 * TILE, width // 2),
        ],
        in_specs=[VMEM] * 6 + [ANYWHERE] * 3,
        out_specs=[VMEM] * 6 + [ANYWHERE] * 3,
        scratch_shapes=[
            pltpu.VMEM((tok, width), bf16), pltpu.VMEM((tok, width), f32), pltpu.VMEM((tok, width), bf16),
            pltpu.VMEM((tok, width), f32), pltpu.VMEM((tok, hidden), bf16), pltpu.VMEM((tok, hidden), bf16),
            pltpu.VMEM((width, hidden), bf16), pltpu.VMEM((hidden, width), bf16),
            pltpu.VMEM((2, 32, width // 32, FFN_CHUNK), bf16), pltpu.VMEM((2, 32 // chunks, hidden // 32, width), bf16),
            pltpu.VMEM(g_low.shape, bf16),
            pltpu.VMEM((OWN, TILE, width), bf16), pltpu.VMEM((OWN, 2, TILE, width), bf16),
            pltpu.VMEM((chunks, 4, 4, width // 32, FFN_CHUNK), bf16), pltpu.VMEM((chunks, 4, hidden // 32, width), bf16),
            pltpu.VMEM((32, width // 32, width), bf16),
            dma(2, chunks), dma(2, chunks), dma(2, 2, 2), dma(2, 4), dma(2), dma(2),
            pltpu.SemaphoreType.DMA, pltpu.SemaphoreType.DMA, dma(chunks + 1, 5), dma(chunks + 1, 5),
        ],
        compiler_params=params(4),
    )(deal, x, att, wo, small, g_low, grd, wi, wu)


def tail(x, small, d_mid, dq, dk, dv, wq, wk, wv, g_two, g_rel):
    tok, width = x.shape
    block = (width // 32, width)
    blocks = [block, block, block, (16, 128)]
    count = len(blocks)
    return pl.pallas_call(
        tail_kernel,
        name="tail",
        out_shape=[shaped(2, 3, TILE, width), shaped(4, 16, 128)] + [shaped(4, *block)] * 3,
        in_specs=[VMEM] * 4 + [ANYWHERE] * 7,
        out_specs=[ANYWHERE] * 5,
        scratch_shapes=[
            pltpu.VMEM((tok, width), jnp.float32), pltpu.VMEM((3, width, width), jnp.bfloat16),
            pltpu.VMEM((3, OWN, TILE, width), jnp.bfloat16), pltpu.VMEM((tok, width), jnp.bfloat16),
            pltpu.VMEM((OWN, TILE, width), jnp.bfloat16),
            pltpu.VMEM((32, 16, 128), jnp.bfloat16),
        ]
        + [pltpu.VMEM((32, *block), jnp.bfloat16)] * 3
        + landing(blocks)
        + [dma(count, 10), dma(count, 10), dma(count, 1), dma(OWN), dma(2, 3), dma(4, PAIRS + 1)],
        compiler_params=params(3),
    )(x, small, g_two, g_rel, d_mid, dq, dk, dv, wq, wk, wv)


def last_sums(low, high, gin, terms):
    f32 = jnp.float32
    lines = lambda n: shaped(1, n, dtype=f32)
    hid_shape = (*low.shape[:2], 2 * low.shape[2])

    def by_micro(shape):
        return pl.BlockSpec((1, *shape[1:]), lambda m: (m,) + (0,) * (len(shape) - 1))

    def whole(shape):
        return pl.BlockSpec(shape, lambda m: (0,) * len(shape))

    sums = [lines(24), lines(24), lines(H)] + [shaped(*t.shape[1:], dtype=f32) for t in terms[1:]]
    return pl.pallas_call(
        sum_kernel,
        name="last_sums",
        grid=(low.shape[0],),
        out_shape=[shaped(*hid_shape, dtype=f32), shaped(*gin.shape, dtype=f32)] + sums,
        in_specs=[by_micro(v.shape) for v in (low, high, gin)] + [whole(t.shape) for t in terms],
        out_specs=[by_micro(hid_shape), by_micro(gin.shape)] + [whole(s.shape) for s in sums],
        compiler_params=params(),
    )(low, high, gin, *terms)


def on_device_packed(
    hidden_in, grad_out, gain_attn, gain_ffn, rel_bias,
    w_query, w_key, w_value, w_output, w_inner, w_outer,
    dealing, lengths, bucket_table,
):
    micro_count, tok_rows, width = hidden_in.shape
    matrix = lambda w: w.reshape(-1, w.shape[-1])
    table = bucket_table
    grd = grad_out.reshape(2, 2, tok_rows // 2, width)
    lens_u, deal_u, x_own, small, wq, wk, wv, wo = gather_all(
        lengths, dealing, hidden_in.reshape(2, 3, TILE, width),
        gain_attn[None], gain_ffn[None], rel_bias[None], (w_query, w_key, w_value, w_output),
    )
    wq, wk, wv = map(matrix, (wq, wk, wv))
    x_rows = matrix(x_own)
    q, k, v, att, log_total, g_low, wi, wu = attention_forward(
        lens_u, x_rows, small, table, wq, wk, wv, grd, w_inner, w_outer
    )
    d_mid, d_att, delta, g_wo, g_two, dealt, g_wi, g_wu, hid_low = feed_forward(
        deal_u, x_rows, att, matrix(wo), small, g_low, grd, matrix(wi), matrix(wu)
    )
    dq, dk, dv, g_rel, t_wo, t_wi, t_wu, hid_high = attention_backward(
        lens_u, q, k, v, log_total, d_att, delta, small, table, g_wo, g_wi, g_wu, dealt
    )
    gin, t_small, t_wq, t_wk, t_wv = tail(x_rows, small, d_mid, dq, dk, dv, wq, wk, wv, g_two, g_rel)
    hid, gin, s_one, s_two, s_rel, *grads = last_sums(hid_low, hid_high, gin, (t_small, t_wq, t_wk, t_wv, t_wo, t_wi, t_wu))
    return (hid, gin.reshape(2, tok_rows, width), s_one[0], s_two[0], s_rel[0], *grads)


def solution(mesh):
    axes = ("dp", "fsdp")
    tokens, matrix, vector = P(None, axes, None), P(axes, None), P(axes)
    packed = mesh.shape["fsdp"] == 4 and mesh.shape["dp"] == 8
    return jax.shard_map(
        on_device_packed if packed else on_device,
        mesh=mesh,
        in_specs=(tokens, tokens, vector, vector, vector)
        + (matrix,) * 6
        + (P(None, "dp", None), P(None, "dp", None), P()),
        out_specs=(tokens, tokens, vector, vector, vector) + (matrix,) * 6,
        check_vma=False,
    )
```

```python
import functools
import math

import jax
import jax.numpy as jnp
from jax import lax
from jax.experimental import pallas as pl
from jax.experimental.pallas import tpu as pltpu
from jax.sharding import PartitionSpec as P

H = 12
BUCKETS = 32
EPSILON = 1e-06
NEG_FILL = -1e30
MESH = pl.DeviceIdType.MESH
TILE = 128
PAIRS = 6
OWN = 6
TILES = 12
FAR = 6
SEQS = 4


def lane_index(shape):
    return lax.broadcasted_iota(jnp.int32, shape, len(shape) - 1)


def row_index(shape):
    return lax.broadcasted_iota(jnp.int32, shape, len(shape) - 2)


def dot_nn(left, right):
    return lax.dot_general(left, right, (((1,), (0,)), ((), ())), preferred_element_type=jnp.float32)


def dot_nt(left, right):
    return lax.dot_general(left, right, (((1,), (1,)), ((), ())), preferred_element_type=jnp.float32)


def dot_tn(left, right):
    return lax.dot_general(left, right, (((0,), (0,)), ((), ())), preferred_element_type=jnp.float32)


def segments_of(places, lens_ref, count):
    edge = jnp.int32(0)
    found = jnp.zeros(places.shape, jnp.int32)
    for s in range(count - 1):
        edge = edge + lens_ref[0, s]
        found = found + (places >= edge).astype(jnp.int32)
    return found


def segment_tags(places, lens_ref, count, of_key):
    lane = lane_index(places.shape)
    hit = segments_of(places, lens_ref, count) == lane
    if of_key:
        return jnp.where((lane < count) & jnp.logical_not(hit), NEG_FILL, 0.0).astype(jnp.bfloat16)
    return jnp.where(hit, 1.0, 0.0).astype(jnp.bfloat16)


def one_hot(rows, columns):
    return jnp.where(rows == columns, 1.0, 0.0).astype(jnp.bfloat16)


def small_lines(small_ref, kind):
    flat = small_ref[...].reshape(32 * 16, 128)
    pick = one_hot(16 * row_index((32, 512)) + kind, lane_index((32, 512)))
    return dot_nn(pick, flat).astype(jnp.bfloat16)


def gain_row(small_ref, kind, width):
    lines = dot_nn(
        small_lines(small_ref, kind), one_hot(row_index((128, width)), lax.rem(lane_index((128, width)), 24))
    )
    own = lane_index((32, width)) // 24 == row_index((32, width))
    return jnp.sum(jnp.where(own, lines, 0.0), axis=0, keepdims=True)


def bucket_picks(table_ref, places):
    span = table_ref.shape[0]
    picked = one_hot(row_index((BUCKETS, span)), jnp.broadcast_to(table_ref[...][None, :], (BUCKETS, span)))
    places = jnp.clip(places, 0, span - 1)
    return dot_nn(picked, one_hot(row_index((span, 256)), jnp.broadcast_to(places, (span, 256)))).astype(jnp.bfloat16)


def class_places(cls, sign):
    lane = lane_index((1, 256))
    if cls >= 3:
        return jnp.full((1, 256), 0 if cls == 3 else 2 * TILE, jnp.int32)
    turn = jnp.where(lane < TILE, lane, lane - 2 * TILE)
    return TILE * (cls - 1) + sign * turn + TILE


def fill_rows(small_ref, table_ref, rows_ref, sign):
    rel = small_lines(small_ref, 2)
    for cls in range(5):
        made = dot_tn(rel, bucket_picks(table_ref, class_places(cls, sign)))
        for h in range(2 * PAIRS):
            rows_ref[cls, h] = made[h : h + 1, :]


def bucket_sums(hist_ref, table_ref):
    total = None
    for cls in range(5):
        if cls >= 3:
            places = class_places(cls, 1)
        else:
            places = TILE * (cls - 1) + 2 * TILE - 1 - lane_index((1, 256))
        hist = jnp.concatenate([hist_ref[cls, h] for h in range(2 * PAIRS)] + [jnp.zeros((4, 256), jnp.float32)], axis=0)
        term = lax.dot_general(
            bucket_picks(table_ref, places).astype(jnp.float32), hist, (((1,), (1,)), ((), ())),
            precision=lax.Precision.HIGHEST, preferred_element_type=jnp.float32,
        )
        total = term if total is None else total + term
    return total


def key_range(i):
    return max(0, 2 * i - FAR), min(TILES, 2 * i + FAR + 2)


def fill_bias(rows_ref, tiles_ref, heads):
    def one_head(h, carry):
        for cls in range(3):
            row = rows_ref[cls, h]
            wide = pltpu.roll(
                jnp.broadcast_to(row, (TILE, 2 * TILE)), 0, 1, stride=1, stride_axis=0
            )
            tiles_ref[h, cls + 1] = wide[:, :TILE]
        left = rows_ref[3, h, :, :TILE]
        right = rows_ref[4, h, :, :TILE]
        tiles_ref[h, 0] = jnp.broadcast_to(left, (TILE, TILE))
        tiles_ref[h, 4] = jnp.broadcast_to(right, (TILE, TILE))
        return carry

    lax.fori_loop(0, heads, one_head, 0)


def bias_class(kt, i, core):
    return jnp.clip(kt - 2 * i - core, -2, 2) + 2


def make_tags(lens_ref, ext_q, ext_k):
    core = lax.rem(lax.axis_index("dp"), 2)
    for t in range(TILES):
        ext_k[t] = segment_tags(TILE * t + row_index((TILE, 128)), lens_ref, SEQS, True)
    for i in range(OWN):
        ext_q[i] = segment_tags(TILE * (2 * i + core) + row_index((TILE, 128)), lens_ref, SEQS, False)


def attn_fwd(
    lens_ref, x_ref, small_ref, table_ref, wq_ref, wk_ref, wv_ref, grd_in, wi_in, wu_in,
    q_ref, k_ref, v_ref, att_ref, log_ref, g_low, wi_all, wu_all,
    rows_ref, bias_ref, ext_q, ext_k, s_ref, log_acc, send_sem, recv_sem,
    w_send, w_recv, w_local, g_send, g_recv,
):
    y, x, core, z = coordinates()
    sibling = place(y, x, 1 - core, z)
    greet()
    pieces = []
    part_i, part_u = wi_in.shape[1] // FWD_PARTS, wu_in.shape[1] // FWD_PARTS
    for n in range(FWD_PARTS):
        pieces.append((wi_in, wi_all, (n * part_i, part_i), "xy"[(n + 1) % 2]))
        pieces.append((wu_in, wu_all, (n * part_u, part_u), "xy"[n % 2]))
    gather = Gather(pieces, w_send, w_recv, w_local)
    grads = list(grad_sends(grd_in, g_low, 0, g_send, g_recv))
    events = {}

    def plan(at, step, *args):
        events.setdefault(at, []).append(functools.partial(step, *args))

    for n in range(len(pieces)):
        plan(FWD_OWN[n], gather.spread_own, n)
        if n + FWD_AHEAD < len(pieces):
            plan(FWD_OWN[n], gather.start, n + FWD_AHEAD)
        plan(FWD_NEAR[n], gather.spread_near, n)
        plan(FWD_SIDE[n], gather.spread_side, n)
    plan(FWD_GRADS, start_all, grads)

    greeted()
    for n in range(FWD_AHEAD):
        gather.start(n)
    rows = x_ref[...].astype(jnp.float32)
    scale = lax.rsqrt(jnp.mean(rows * rows, axis=1, keepdims=True) + EPSILON)
    normed = (rows * scale * gain_row(small_ref, 0, rows.shape[1])).astype(jnp.bfloat16)

    def project(w_ref):
        return dot_nn(normed, w_ref[...]).astype(jnp.bfloat16)

    copies = []
    for n, (w_ref, all_ref) in enumerate(((wk_ref, k_ref), (wv_ref, v_ref))):
        made = project(w_ref)
        for hp in range(PAIRS):
            for i in range(OWN):
                all_ref[hp, i, core] = made[TILE * i : TILE * (i + 1), 128 * hp : 128 * (hp + 1)]
        copy = remote(all_ref.at[:, :, core], all_ref.at[:, :, core], send_sem.at[n], recv_sem.at[n], sibling)
        copy.start()
        copies.append(copy)
    made = project(wq_ref)
    for hp in range(PAIRS):
        for i in range(OWN):
            q_ref[hp, i] = made[TILE * i : TILE * (i + 1), 128 * hp : 128 * (hp + 1)]
    make_tags(lens_ref, ext_q, ext_k)
    for i in range(OWN):
        log_acc[i] = jnp.zeros((TILE, 128), jnp.float32)
    for step in events.pop(-1, ()):
        step()
    fill_rows(small_ref, table_ref, rows_ref, 1)
    fill_bias(rows_ref, bias_ref, 2 * PAIRS)
    for n, all_ref in enumerate((k_ref, v_ref)):
        block = all_ref.at[:, :, 1 - core]
        remote(block, block, send_sem.at[n], recv_sem.at[n], sibling).wait_recv()

    lane = lane_index((TILE, 128))

    def one_pair(hp, carry):
        for i in range(OWN):
            run_events(events, hp, i)
            lo, hi = key_range(i)
            width = (hi - lo) * TILE
            pair = q_ref[hp, i]
            tags = ext_q[i]
            zero = jnp.zeros_like(pair)
            left = jnp.concatenate(
                [
                    jnp.concatenate([jnp.where(lane < 64, pair, zero), tags], axis=1),
                    jnp.concatenate([jnp.where(lane < 64, zero, pair), tags], axis=1),
                ],
                axis=0,
            )
            keys = k_ref[hp, lo // 2 : hi // 2].reshape(width, 128)
            right = jnp.concatenate([keys, ext_k[lo:hi].reshape(width, 128)], axis=1)
            raw = dot_nt(left, right)
            tops = []
            for e in range(2):
                top = None
                for kt in range(lo, hi):
                    at = (kt - lo) * TILE
                    part = raw[e * TILE : (e + 1) * TILE, at : at + TILE]
                    if -1 <= kt - 2 * i <= 2:
                        part = part + bias_ref[2 * hp + e, bias_class(kt, i, core)]
                    else:
                        part = part + rows_ref[3 if kt < 2 * i else 4, 2 * hp + e, :, :TILE]
                    s_ref[e, :, at : at + TILE] = part
                    top = part if top is None else jnp.maximum(top, part)
                tops.append(jnp.max(top, axis=1, keepdims=True))
            outs = []
            for e in range(2):
                total = None
                found = []
                for kt in range(lo, hi):
                    at = (kt - lo) * TILE
                    weight = jnp.exp(s_ref[e, :, at : at + TILE] - tops[e])
                    total = weight if total is None else total + weight
                    found.append(weight.astype(jnp.bfloat16))
                total = jnp.sum(total, axis=1, keepdims=True)
                probs = jnp.concatenate(found, axis=1)
                values = v_ref[hp, lo // 2 : hi // 2].reshape(width, 128)
                outs.append(dot_nn(probs, values) / total)
                log_acc[i] = jnp.where(lane == 2 * hp + e, tops[e] + jnp.log(total), log_acc[i])
            att_ref[TILE * i : TILE * (i + 1), pl.ds(pl.multiple_of(128 * hp, 128), 128)] = jnp.where(
                lane < 64, outs[0], outs[1]
            ).astype(jnp.bfloat16)
        return carry

    lax.fori_loop(0, PAIRS, one_pair, 0)
    late(events)
    share_grads(g_low, g_send, g_recv)
    for i in range(OWN):
        turned = log_acc[i].T
        for h in range(2 * PAIRS):
            log_ref[i, h] = turned[h : h + 1, :]
    for n in range(len(pieces)):
        gather.finish(n)
    end_grads(grads, g_low, g_send, g_recv)
    for copy in copies:
        copy.wait_send()


def attn_bwd(
    lens_ref, q_ref, k_ref, v_ref, log_ref, do_ref, delta_ref, small_ref, table_ref, gwo, gwi, gwu, dealt,
    dq_ref, dk_ref, dv_ref, rel_ref, two, twi, twu, hid_out,
    rows_ref, hist_ref, bias_ref, acc_ref, ext_q, ext_k, dk_acc, dv_acc, out_k, out_v, got_k, got_v, send_sem, recv_sem,
    w_send, w_recv, w_local, h_send, h_recv, *landed,
):
    y, x, core, z = coordinates()
    sibling = place(y, x, 1 - core, z)
    greet()
    plain = []
    part_i, part_u = gwi.shape[3] // BWD_PARTS, gwu.shape[3] // BWD_PARTS
    for n in range(BWD_PARTS):
        plain.append((gwi, twi, (n * part_i, part_i), "xy"[n % 2]))
        plain.append((gwu, twu, (n * part_u, part_u), "xy"[(n + 1) % 2]))
    plain.append((gwo, two, None, "x"))
    count = len(plain)
    scatter = LateScatter(
        [item + tuple(landed[3 * n : 3 * n + 3]) for n, item in enumerate(plain)], w_send, w_recv, w_local
    )
    events = {}

    def plan(at, step, *args):
        events.setdefault(at, []).append(functools.partial(step, *args))

    for n in range(count):
        plan(BWD_SIDE[n], scatter.sum_side, n)
        if n + BWD_AHEAD < count:
            plan(BWD_SIDE[n], scatter.start, n + BWD_AHEAD)
        plan(BWD_NEAR[n], scatter.sum_near, n)
    make_tags(lens_ref, ext_q, ext_k)
    greeted()
    for n in range(BWD_AHEAD):
        scatter.start(n)
    deals = list(dealt_sends(dealt, hid_out, hid_out.shape[2], h_send, h_recv))
    start_all(deals)
    acc_ref[...] = jnp.zeros_like(acc_ref)
    fill_rows(small_ref, table_ref, rows_ref, -1)
    fill_bias(rows_ref, bias_ref, 2 * PAIRS)
    for step in events.pop(-1, ()):
        step()
    lane = lane_index((TILE, 128))

    def one_pair(hp, carry):
        dk_acc[...] = jnp.zeros_like(dk_acc)
        dv_acc[...] = jnp.zeros_like(dv_acc)
        for i in range(OWN):
            run_events(events, hp, i)
            lo, hi = key_range(i)
            width = (hi - lo) * TILE
            pair, d_pair = q_ref[hp, i], do_ref[hp, i]
            tags = ext_q[i]
            zero = jnp.zeros_like(pair)
            q_two = jnp.concatenate([jnp.where(lane < 64, pair, zero), jnp.where(lane < 64, zero, pair)], axis=0)
            d_two = jnp.concatenate([jnp.where(lane < 64, d_pair, zero), jnp.where(lane < 64, zero, d_pair)], axis=0)
            q_ext = jnp.concatenate([q_two, jnp.concatenate([tags, tags], axis=0)], axis=1)
            keys = k_ref[hp, lo // 2 : hi // 2].reshape(width, 128)
            values = v_ref[hp, lo // 2 : hi // 2].reshape(width, 128)
            k_ext = jnp.concatenate([keys, ext_k[lo:hi].reshape(width, 128)], axis=1)
            raw = dot_nt(k_ext, q_ext)
            d_probs = dot_nt(values, d_two)
            p_rows, s_rows = [], []
            for kt in range(lo, hi):
                at = (kt - lo) * TILE
                p_two, s_two = [], []
                for e in range(2):
                    head = 2 * hp + e
                    part = raw[at : at + TILE, e * TILE : (e + 1) * TILE]
                    near = -1 <= kt - 2 * i <= 2
                    cls = bias_class(kt, i, core) if near else (0 if kt < 2 * i else 4)
                    if near:
                        part = part + bias_ref[head, cls]
                    else:
                        part = part + rows_ref[3 if kt < 2 * i else 4, head, :, :TILE]
                    probs = jnp.exp(part - log_ref[i, head])
                    slope = probs * (
                        d_probs[at : at + TILE, e * TILE : (e + 1) * TILE] - delta_ref[i, head]
                    )
                    acc_ref[head, cls] += slope
                    p_two.append(probs.astype(jnp.bfloat16))
                    s_two.append(slope.astype(jnp.bfloat16))
                p_rows.append(jnp.concatenate(p_two, axis=1))
                s_rows.append(jnp.concatenate(s_two, axis=1))
            probs_t = jnp.concatenate(p_rows, axis=0)
            slopes_t = jnp.concatenate(s_rows, axis=0)
            dv_acc[lo * TILE : hi * TILE, :] += dot_nn(probs_t, d_two)
            dk_acc[lo * TILE : hi * TILE, :] += dot_nn(slopes_t, q_two)
            d_q = dot_tn(slopes_t, keys)
            dq_ref[hp, i] = jnp.where(lane < 64, d_q[:TILE], d_q[TILE:]).astype(jnp.bfloat16)
        for acc, own, out in ((dk_acc, dk_ref, out_k), (dv_acc, dv_ref, out_v)):
            for i in range(OWN):
                own[hp, i] = acc[pl.ds((2 * i + core) * TILE, TILE), :].astype(jnp.bfloat16)
                out[hp, i] = acc[pl.ds((2 * i + 1 - core) * TILE, TILE), :].astype(jnp.bfloat16)
        for n, (out, got) in enumerate(((out_k, got_k), (out_v, got_v))):
            pltpu.make_async_remote_copy(
                out.at[hp], got.at[hp], send_sem.at[n, hp], recv_sem.at[n, hp],
                device_id=sibling, device_id_type=MESH,
            ).start()
        return carry

    lax.fori_loop(0, PAIRS, one_pair, 0)
    flip = (row_index((TILE, TILE)) + lane == TILE - 1).astype(jnp.float32)

    def one_head(h, carry):
        for cls in range(3):
            tile = jnp.dot(flip, acc_ref[h, cls + 1], precision=lax.Precision.HIGHEST)
            wide = jnp.concatenate([tile, jnp.zeros((TILE, TILE), jnp.float32)], axis=1)
            wide = pltpu.roll(wide, 0, 1, stride=1, stride_axis=0)
            hist_ref[cls, h] = jnp.sum(wide, axis=0, keepdims=True)
        for n, cls in ((3, 0), (4, 4)):
            row = jnp.sum(acc_ref[h, cls], axis=0, keepdims=True)
            hist_ref[n, h] = jnp.concatenate([row, jnp.zeros_like(row)], axis=1)
        return carry

    lax.fori_loop(0, 2 * PAIRS, one_head, 0)

    rel_ref[...] = jnp.zeros_like(rel_ref)
    rel_ref[:, :16] = bucket_sums(hist_ref, table_ref)

    def finish(hp, carry):
        for n, (out, got, own) in enumerate(((out_k, got_k, dk_ref), (out_v, got_v, dv_ref))):
            copy = pltpu.make_async_remote_copy(
                out.at[hp], got.at[hp], send_sem.at[n, hp], recv_sem.at[n, hp],
                device_id=sibling, device_id_type=MESH,
            )
            copy.wait_send()
            copy.wait_recv()
            own[hp] = (own[hp].astype(jnp.float32) + got[hp].astype(jnp.float32)).astype(jnp.bfloat16)
        return carry

    lax.fori_loop(0, PAIRS, finish, 0)
    late(events)
    for n in range(count):
        scatter.finish(n)
    for item in deals:
        sent(*item)
    for m in range(2):
        remote(hid_out.at[m], hid_out.at[m], h_send.at[0], h_recv.at[m], sibling).wait_recv()


def norm_back(rows_in, scale, gain, grad_normed):
    scaled = grad_normed * gain
    grad_gain = jnp.sum(grad_normed * rows_in * scale, axis=0, keepdims=True)
    shared = jnp.mean(scaled * rows_in, axis=1, keepdims=True)
    return scale * scaled - rows_in * (scale * scale * scale * shared), grad_gain


def join_pairs(pairs_ref, joined_ref):
    for hp in range(PAIRS):
        joined_ref[:, 128 * hp : 128 * (hp + 1)] = (
            pairs_ref[hp].reshape(OWN * TILE, 128).astype(joined_ref.dtype)
        )


def gain_block(row):
    width = row.shape[1]
    lines = jnp.where(lane_index((32, width)) // 24 == row_index((32, width)), row, 0.0)
    pick = (lax.rem(row_index((width, 128)), 24) == lane_index((width, 128))).astype(jnp.float32)
    return jnp.dot(lines, pick, precision=lax.Precision.HIGHEST)


def ffn_kernel(
    deal_ref, x_ref, att_ref, wo_ref, small_ref, g_low, grd_in, wi_in, wu_in,
    dmid_ref, datt_ref, delta_ref, gwo_ref, two_ref, dealt, gwi, gwu, hid_out,
    grad_ref, mid_ref, normed_ref, total_ref, active_ref, slope_ref, wi_ref, wu_ref, gwi_two, gwu_two, g_high,
    res_ref, res_all, got_i, got_u, gwo_own, in_sem, out_sem, g_send, g_recv, h_send, h_recv, e_send, e_recv,
    c_send, c_recv,
):
    y, x, core, z = coordinates()
    sibling = place(y, x, 1 - core, z)
    greet()
    width = x_ref.shape[1]
    half = width // 2
    chunk = FFN_CHUNK
    chunks = wi_ref.shape[1] // chunk

    def bring(j):
        span = pl.ds(chunk * j, chunk)
        return (
            pltpu.make_async_copy(wi_in.at[:, span], wi_ref.at[:, span], in_sem.at[0, j]),
            pltpu.make_async_copy(wu_in.at[span], wu_ref.at[span], in_sem.at[1, j]),
        )

    for j in range(chunks):
        for copy in bring(j):
            copy.start()
    grads = list(grad_sends(grd_in, g_high, half, g_send, g_recv))
    gain = gain_row(small_ref, 1, width)
    mid = x_ref[...].astype(jnp.float32) + dot_nn(att_ref[...], wo_ref[...])
    mid_ref[...] = mid
    scale = lax.rsqrt(jnp.mean(mid * mid, axis=1, keepdims=True) + EPSILON)
    normed_ref[...] = (mid * scale * gain).astype(jnp.bfloat16)
    greeted()
    start_all(grads)

    def rows_of(i):
        return slice(TILE * i, TILE * (i + 1))

    picks = []
    for i in range(OWN):
        picks.append(one_hot((2 * i + core) * TILE + row_index((TILE, TILES * TILE)), deal_ref[...]))
        grad_ref[rows_of(i), :half] = dot_nn(
            picks[i], g_low[...].reshape(TILES * TILE, half)
        ).astype(jnp.bfloat16)
    for j in range(chunks):
        span = slice(chunk * j, chunk * (j + 1))
        for copy in bring(j):
            copy.wait()
        inner = dot_nn(normed_ref[...], wi_ref[:, span])
        cdf = 0.5 * (1.0 + lax.erf(inner * (1.0 / math.sqrt(2.0))))
        active = (inner * cdf).astype(jnp.bfloat16)
        active_ref[:, span] = active
        slope = cdf + inner * (jnp.exp(-0.5 * inner * inner) * (1.0 / math.sqrt(2.0 * math.pi)))
        slope_ref[:, span] = slope.astype(jnp.bfloat16)
        term = dot_nn(active, wu_ref[span, :])
        total_ref[...] = term if j == 0 else total_ref[...] + term
    result = (mid_ref[...] + total_ref[...]).astype(jnp.bfloat16).reshape(OWN, TILE, width)
    res_ref[...] = result
    res_copy = remote(res_ref, res_all.at[:, core], e_send, e_recv, sibling)
    res_copy.start()
    for i in range(OWN):
        res_all[i, core] = result[i]
    share_grads(g_high, g_send, g_recv)

    remote(res_ref, res_all.at[:, 1 - core], e_send, e_recv, sibling).wait_recv()
    lane = lane_index((TILE, TILE))
    for b in range(OWN):
        at = pl.multiple_of((OWN * core + b) * TILE, TILE)
        turned = jnp.broadcast_to(deal_ref[:, pl.ds(at, TILE)].astype(jnp.float32), (TILE, TILE)).T
        turned = turned.astype(jnp.int32)
        pick = jnp.concatenate([one_hot(turned, TILE * t + lane) for t in range(TILES)], axis=1)
        made = dot_nn(pick, res_all[...].reshape(TILES * TILE, width)).astype(jnp.bfloat16)
        dealt[b // 3, TILE * (b % 3) : TILE * (b % 3 + 1)] = made
    deals = list(dealt_sends(dealt, hid_out, 0, h_send, h_recv))
    start_all(deals)
    end_grads(grads, g_high, g_send, g_recv)
    for i in range(OWN):
        grad_ref[rows_of(i), half:] = dot_nn(
            picks[i], g_high[...].reshape(TILES * TILE, half)
        ).astype(jnp.bfloat16)

    def swap(j):
        slot, there = j % 2, 4 * (1 - core)
        copies = [remote(gwu_two.at[slot, pl.ds(there, 4)], got_u.at[j], c_send.at[j, 4], c_recv.at[j, 4], sibling)]
        for k in range(4):
            copies.append(
                remote(
                    gwi_two.at[slot, pl.ds(8 * k + there, 4)], got_i.at[j, k],
                    c_send.at[j, k], c_recv.at[j, k], sibling,
                )
            )
        return copies

    def take(j):
        return (
            pltpu.make_async_copy(got_i.at[j], gwi.at[:, :, :, pl.ds(chunk * j, chunk)], out_sem.at[0, j]),
            pltpu.make_async_copy(got_u.at[j], gwu.at[j], out_sem.at[1, j]),
        )

    def combine(j):
        slot, here = j % 2, 4 * core
        for copy in swap(j):
            copy.wait_recv()
        for n in range(4):
            got_u[j, n] = got_u[j, n] + gwu_two[slot, here + n]
            for k in range(4):
                got_i[j, k, n] = got_i[j, k, n] + gwi_two[slot, 8 * k + here + n]
        for copy in take(j):
            copy.start()
        for copy in swap(j):
            copy.wait_send()

    for j in range(chunks):
        span = slice(chunk * j, chunk * (j + 1))
        d_inner = (
            dot_nt(grad_ref[...], wu_ref[span, :]) * slope_ref[:, span].astype(jnp.float32)
        ).astype(jnp.bfloat16)
        made = dot_tn(active_ref[:, span], grad_ref[...])
        gwu_two[j % 2] = made.astype(jnp.bfloat16).reshape(gwu_two.shape[1:])
        made = dot_tn(normed_ref[...], d_inner)
        gwi_two[j % 2] = made.reshape(32, -1, chunk).astype(jnp.bfloat16)
        for copy in swap(j):
            copy.start()
        term = dot_nt(d_inner, wi_ref[:, span])
        total_ref[...] = term if j == 0 else total_ref[...] + term
        if j:
            combine(j - 1)

    mid = mid_ref[...]
    scale = lax.rsqrt(jnp.mean(mid * mid, axis=1, keepdims=True) + EPSILON)
    d_rows, d_gain = norm_back(mid, scale, gain, total_ref[...])
    two_ref[...] = gain_block(d_gain)
    d_mid = grad_ref[...].astype(jnp.float32) + d_rows
    dmid_ref[...] = d_mid
    branch = d_mid.astype(jnp.bfloat16)
    made = dot_tn(att_ref[...], branch)
    gwo_own[...] = made.reshape(32, -1, width).astype(jnp.bfloat16)
    swaps = [
        remote(
            gwo_own.at[pl.ds(8 * k + 4 * (1 - core), 4)], gwo_ref.at[k], c_send.at[chunks, k], c_recv.at[chunks, k], sibling
        )
        for k in range(4)
    ]
    for copy in swaps:
        copy.start()
    combine(chunks - 1)
    d_att = dot_nt(branch, wo_ref[...]).astype(jnp.bfloat16)
    pick = (lane_index((16, width)) // 64 == row_index((16, width))).astype(jnp.float32)
    prod = d_att.astype(jnp.float32) * att_ref[...].astype(jnp.float32)
    sums = lax.dot_general(
        pick, prod, (((1,), (1,)), ((), ())), precision=lax.Precision.HIGHEST, preferred_element_type=jnp.float32
    )
    for hp in range(PAIRS):
        datt_ref[hp] = d_att[:, 128 * hp : 128 * (hp + 1)].reshape(OWN, TILE, 128)
    for i in range(OWN):
        for h in range(2 * PAIRS):
            delta_ref[i, h] = sums[h : h + 1, TILE * i : TILE * (i + 1)]
    for k, copy in enumerate(swaps):
        copy.wait_recv()
        for n in range(4):
            gwo_ref[k, n] = gwo_ref[k, n] + gwo_own[8 * k + 4 * core + n]
        copy.wait_send()
    for j in range(chunks):
        for copy in take(j):
            copy.wait()
    res_copy.wait_send()
    for item in deals:
        sent(*item)
    for m in range(2):
        remote(hid_out.at[m], hid_out.at[m], h_send.at[0], h_recv.at[m], sibling).wait_recv()


def tail_kernel(
    x_ref, small_ref, g_two, g_rel, dmid_in, dq_in, dk_in, dv_in, wq_in, wk_in, wv_in,
    gin_out, tsmall, tq, tk, tv,
    dmid_ref, w_ref, join_ref, normed_ref, back_out, small, gq, gk, gv, *scratch,
):
    y, x, c, z = coordinates()
    sibling = place(y, x, 1 - c, z)
    owner, micro = z // 2, lax.rem(z, 2)
    greet()
    plain = [(gk, tk, None, "x"), (gv, tv, None, "y"), (gq, tq, None, "x"), (small, tsmall, None, "y")]
    count = len(plain)
    w_send, w_recv, w_local, b_send, b_recv, in_sem = scratch[3 * count :]
    scatter = Scatter(
        [item + tuple(scratch[3 * n : 3 * n + 3]) for n, item in enumerate(plain)], w_send, w_recv, w_local
    )
    grads_in = []
    for n, (w_in, pairs) in enumerate(((wq_in, dq_in), (wk_in, dk_in), (wv_in, dv_in))):
        copies = [pltpu.make_async_copy(w_in, w_ref.at[n], in_sem.at[n, PAIRS])]
        for hp in range(PAIRS):
            copies.append(
                pltpu.make_async_copy(
                    pairs.at[hp], join_ref.at[n, :, :, pl.ds(128 * hp, 128)], in_sem.at[n, hp]
                )
            )
        for copy in copies:
            copy.start()
        grads_in.append(copies)
    dmid_copy = pltpu.make_async_copy(dmid_in, dmid_ref, in_sem.at[3, 0])
    dmid_copy.start()

    def back_sends():
        for i in range(OWN):
            t = 2 * i + c
            z_to, l = t // 3, lax.rem(t, 3)
            yield (
                back_out.at[i], gin_out.at[micro, l], b_send.at[i], b_recv.at[micro, l],
                place(y, x, owner, z_to), (owner == c) & (z_to == z),
            )

    sends = list(back_sends())
    gain = gain_row(small_ref, 0, x_ref.shape[1])
    width = x_ref.shape[1]
    d_gain = None
    for part_at in range(3):
        tiles = slice(OWN // 3 * part_at, OWN // 3 * (part_at + 1))
        span = slice(TILE * tiles.start, TILE * tiles.stop)
        rows = x_ref[span, :].astype(jnp.float32)
        scale = lax.rsqrt(jnp.mean(rows * rows, axis=1, keepdims=True) + EPSILON)
        normed_ref[span, :] = (rows * scale * gain).astype(jnp.bfloat16)
        back = None
        for n in range(3):
            if part_at == 0:
                for copy in grads_in[n]:
                    copy.wait()
            term = dot_nt(join_ref[n, tiles].reshape(-1, width), w_ref[n])
            back = term if back is None else back + term
        d_rows, part = norm_back(rows, scale, gain, back)
        d_gain = part if d_gain is None else d_gain + part
        if part_at == 0:
            dmid_copy.wait()
        back_out[tiles] = (dmid_ref[span, :] + d_rows).astype(jnp.bfloat16).reshape(-1, TILE, width)
        if part_at == 0:
            greeted()
        start_all(sends[tiles])
    normed_t = normed_ref[...].T
    for n, (at, grad_ref) in enumerate(((1, gk), (2, gv), (0, gq))):
        made = dot_nn(normed_t, join_ref[at].reshape(-1, width))
        for r in range(32):
            grad_ref[r] = made[24 * r : 24 * (r + 1), :].astype(jnp.bfloat16)
        scatter.start(n)
    g_one = gain_block(d_gain)
    shape = (32, 16, 128)
    kind = lax.broadcasted_iota(jnp.int32, shape, 1)
    spread = lambda v: jnp.broadcast_to(v[:, None, :], shape)
    small[...] = jnp.where(
        kind == 0, spread(g_one), jnp.where(kind == 1, spread(g_two[...]), spread(g_rel[...]))
    ).astype(jnp.bfloat16)
    scatter.start(3)
    for n in range(count + 2):
        for back_by, stage in enumerate((scatter.sum_core, scatter.sum_side, scatter.sum_near)):
            if 0 <= n - back_by < count:
                stage(n - back_by)
    for n in range(count):
        scatter.finish(n)
    for item in sends:
        sent(*item)
    for m in range(2):
        for l in range(3):
            remote(back_out.at[0], gin_out.at[m, l], b_send.at[0], b_recv.at[m, l], sibling).wait_recv()


def coordinates():
    dp, z = lax.axis_index("dp"), lax.axis_index("fsdp")
    return dp // 4, lax.rem(dp // 2, 2), lax.rem(dp, 2), z


def place(y, x, c, z):
    return (4 * y + 2 * x + c, z)


def column(y, x, c):
    return 16 * y + 8 * x + 4 * c


def partners():
    y, x, c, z = coordinates()
    found = [place(1 - y, x, c, z), place(y, 1 - x, c, z)]
    for dc in range(2):
        for dz in range(4):
            if dc or dz:
                found.append(place(y, x, lax.rem(c + dc, 2), lax.rem(z + dz, 4)))
    return found


def greet():
    for partner in partners():
        pl.semaphore_signal(pltpu.get_barrier_semaphore(), inc=1, device_id=partner, device_id_type=MESH)


def greeted():
    pl.semaphore_wait(pltpu.get_barrier_semaphore(), len(partners()))


def remote(src, dst, send, recv, target):
    return pltpu.make_async_remote_copy(
        src, dst, send, recv, device_id=target, device_id_type=MESH
    )


def send_or_keep(src, dst, send, recv, target, here):
    @pl.when(jnp.logical_not(here))
    def _():
        remote(src, dst, send, recv, target).start()

    @pl.when(here)
    def _():
        pltpu.make_async_copy(src, dst, recv).start()


def sent(src, dst, send, recv, target, here):
    @pl.when(jnp.logical_not(here))
    def _():
        remote(src, dst, send, recv, target).wait_send()


def cut(ref, lead, part):
    return ref.at[lead] if part is None else ref.at[lead, slice(None), pl.ds(*part)]


def cut_shard(ref, part):
    return ref if part is None else ref.at[:, pl.ds(*part)]


class Gather:
    def __init__(self, pieces, send, recv, local):
        self.pieces, self.send, self.recv, self.local = pieces, send, recv, local
        self.y, self.x, self.c, self.z = coordinates()
        y, x, c, z = self.y, self.x, self.c, self.z
        self.sibling = place(y, x, 1 - c, z)
        self.mine = column(y, x, c)
        self.far = column(1 - y, 1 - x, c)
        by_x = (place(y, 1 - x, c, z), column(y, 1 - x, c))
        by_y = (place(1 - y, x, c, z), column(1 - y, x, c))
        self.sides = {"x": by_x + by_y, "y": by_y + by_x}

    def own_copy(self, n):
        shard, whole, part, _ = self.pieces[n]
        return pltpu.make_async_copy(
            cut_shard(shard, part), cut(whole, self.mine + self.z, part), self.local.at[n]
        )

    def z_copy(self, n, dz, came=False):
        shard, whole, part, _ = self.pieces[n]
        entry = self.mine + (lax.rem(self.z + 4 - dz, 4) if came else self.z)
        return remote(
            cut_shard(shard, part), cut(whole, entry, part), self.send.at[n, dz - 1], self.recv.at[n, dz - 1],
            place(self.y, self.x, self.c, lax.rem(self.z + dz, 4)),
        )

    def push(self, n, k, base, target):
        _, whole, part, _ = self.pieces[n]
        block = cut(whole, pl.ds(base, 4), part)
        return remote(block, block, self.send.at[n, k], self.recv.at[n, k], target)

    def start(self, n):
        self.own_copy(n).start()
        for dz in range(1, 4):
            self.z_copy(n, dz).start()

    def spread_own(self, n):
        near, _, side, _ = self.sides[self.pieces[n][3]]
        self.own_copy(n).wait()
        for dz in range(1, 4):
            self.z_copy(n, dz, True).wait_recv()
        for k, target in ((3, near), (4, side), (6, self.sibling)):
            self.push(n, k, self.mine, target).start()

    def spread_near(self, n):
        _, near_column, side, _ = self.sides[self.pieces[n][3]]
        self.push(n, 3, near_column, self.sibling).wait_recv()
        self.push(n, 5, near_column, side).start()
        self.push(n, 7, near_column, self.sibling).start()

    def spread_side(self, n):
        side_column = self.sides[self.pieces[n][3]][3]
        self.push(n, 4, side_column, self.sibling).wait_recv()
        self.push(n, 8, side_column, self.sibling).start()
        self.push(n, 5, self.far, self.sibling).wait_recv()
        self.push(n, 9, self.far, self.sibling).start()

    def finish(self, n):
        _, near_column, _, side_column = self.sides[self.pieces[n][3]]
        for k, base in ((6, self.mine), (7, near_column), (8, side_column), (9, self.far)):
            self.push(n, k, base + 4 - 8 * self.c, self.sibling).wait_recv()
        for dz in range(1, 4):
            self.z_copy(n, dz).wait_send()
        for k in range(3, 10):
            self.push(n, k, self.mine, self.sibling).wait_send()


class Scatter:
    def __init__(self, pieces, send, recv, local):
        self.pieces, self.send, self.recv, self.local = pieces, send, recv, local
        self.y, self.x, self.c, self.z = coordinates()
        y, x, c, z = self.y, self.x, self.c, self.z
        self.sibling = place(y, x, 1 - c, z)

    def sides(self, n):
        y, x, c, z = self.y, self.x, self.c, self.z
        by_x, by_y = place(y, 1 - x, c, z), place(1 - y, x, c, z)
        if self.pieces[n][3] == "x":
            return by_x, by_y, (lambda s, f: 2 * s + f), y, x
        return by_y, by_x, (lambda s, f: 2 * f + s), x, y

    def core_copy(self, n, k):
        grad, _, part, _, r1 = self.pieces[n][:5]
        return remote(
            cut(grad, pl.ds(8 * k + 4 * (1 - self.c), 4), part), r1.at[k],
            self.send.at[n, k], self.recv.at[n, k], self.sibling,
        )

    def side_copy(self, n, f_at):
        _, side, index, s, _ = self.sides(n)
        _, _, _, _, r1, r2, _ = self.pieces[n]
        return remote(
            r1.at[index(1 - s, f_at)], r2.at[f_at], self.send.at[n, 4 + f_at], self.recv.at[n, 4 + f_at], side
        )

    def near_copy(self, n):
        near, _, index, s, f = self.sides(n)
        _, _, _, _, r1, _, r3 = self.pieces[n]
        return remote(r1.at[index(s, 1 - f)], r3, self.send.at[n, 6], self.recv.at[n, 6], near)

    def z_copy(self, n, dz):
        _, _, index, s, f = self.sides(n)
        _, terms, part, _, r1, _, _ = self.pieces[n]
        z_to = lax.rem(self.z + dz, 4)
        return remote(
            r1.at[index(s, f), z_to], cut(terms, dz, part), self.send.at[n, 6 + dz], self.recv.at[n, 6 + dz],
            place(self.y, self.x, self.c, z_to),
        )

    def own_copy(self, n):
        _, _, index, s, f = self.sides(n)
        _, terms, part, _, r1, _, _ = self.pieces[n]
        return pltpu.make_async_copy(r1.at[index(s, f), self.z], cut(terms, 0, part), self.local.at[n, 0])

    def start(self, n):
        for k in range(4):
            self.core_copy(n, k).start()

    def sum_core(self, n):
        grad, _, part, _, r1 = self.pieces[n][:5]
        for k in range(4):
            self.core_copy(n, k).wait_recv()

            def one(j, carry, k=k):
                r1[k, j] = r1[k, j] + cut(grad, 8 * k + 4 * self.c + j, part)[...]
                return carry

            lax.fori_loop(0, 4, one, 0)
        for f_at in range(2):
            self.side_copy(n, f_at).start()

    def sum_side(self, n):
        _, _, index, s, _ = self.sides(n)
        _, _, _, _, r1, r2, _ = self.pieces[n]
        for f_at in range(2):
            self.side_copy(n, f_at).wait_recv()
            k = index(s, f_at)

            def one(j, carry, k=k, f_at=f_at):
                r1[k, j] = r1[k, j] + r2[f_at, j]
                return carry

            lax.fori_loop(0, 4, one, 0)
        self.near_copy(n).start()

    def sum_near(self, n):
        _, _, index, s, f = self.sides(n)
        _, _, _, _, r1, _, r3 = self.pieces[n]
        self.near_copy(n).wait_recv()
        k = index(s, f)

        def one(j, carry):
            r1[k, j] = r1[k, j] + r3[j]
            return carry

        lax.fori_loop(0, 4, one, 0)
        for dz in range(1, 4):
            self.z_copy(n, dz).start()
        self.own_copy(n).start()

    def finish(self, n):
        self.own_copy(n).wait()
        for dz in range(1, 4):
            self.z_copy(n, dz).wait_recv()
        for k in range(4):
            self.core_copy(n, k).wait_send()
        for f_at in range(2):
            self.side_copy(n, f_at).wait_send()
        self.near_copy(n).wait_send()
        for dz in range(1, 4):
            self.z_copy(n, dz).wait_send()


class LateScatter(Scatter):
    def side_copy(self, n, f_at):
        _, side, index, s, _ = self.sides(n)
        summed, _, part, _, _, r2, _ = self.pieces[n]
        return remote(
            cut(summed.at[index(1 - s, f_at)], pl.ds(0, 4), part), r2.at[f_at],
            self.send.at[n, 4 + f_at], self.recv.at[n, 4 + f_at], side,
        )

    def fetch(self, n, f_at):
        _, _, index, s, _ = self.sides(n)
        summed, _, part, _, own, _, _ = self.pieces[n]
        return pltpu.make_async_copy(
            cut(summed.at[index(s, f_at)], pl.ds(0, 4), part), own.at[f_at], self.local.at[n, 1 + f_at]
        )

    def near_copy(self, n):
        near, _, _, _, f = self.sides(n)
        _, _, _, _, _, r2, r3 = self.pieces[n]
        return remote(r2.at[1 - f], r3, self.send.at[n, 6], self.recv.at[n, 6], near)

    def z_copy(self, n, dz):
        f = self.sides(n)[4]
        _, terms, part, _, _, r2, _ = self.pieces[n]
        z_to = lax.rem(self.z + dz, 4)
        return remote(
            r2.at[f, z_to], cut(terms, dz, part), self.send.at[n, 6 + dz], self.recv.at[n, 6 + dz],
            place(self.y, self.x, self.c, z_to),
        )

    def own_copy(self, n):
        f = self.sides(n)[4]
        _, terms, part, _, _, r2, _ = self.pieces[n]
        return pltpu.make_async_copy(r2.at[f, self.z], cut(terms, 0, part), self.local.at[n, 0])

    def start(self, n):
        for f_at in range(2):
            self.side_copy(n, f_at).start()
            self.fetch(n, f_at).start()

    def sum_side(self, n):
        _, _, _, _, own, r2, _ = self.pieces[n]
        for f_at in range(2):
            self.side_copy(n, f_at).wait_recv()
            self.fetch(n, f_at).wait()

            def one(j, carry, f_at=f_at):
                r2[f_at, j] = r2[f_at, j] + own[f_at, j]
                return carry

            lax.fori_loop(0, 4, one, 0)
        self.near_copy(n).start()

    def sum_near(self, n):
        f = self.sides(n)[4]
        _, _, _, _, _, r2, r3 = self.pieces[n]
        self.near_copy(n).wait_recv()

        def one(j, carry):
            r2[f, j] = r2[f, j] + r3[j]
            return carry

        lax.fori_loop(0, 4, one, 0)
        for dz in range(1, 4):
            self.z_copy(n, dz).start()
        self.own_copy(n).start()

    def finish(self, n):
        self.own_copy(n).wait()
        for dz in range(1, 4):
            self.z_copy(n, dz).wait_recv()
        for f_at in range(2):
            self.side_copy(n, f_at).wait_send()
        self.near_copy(n).wait_send()
        for dz in range(1, 4):
            self.z_copy(n, dz).wait_send()


def run_events(events, hp, i):
    for at in range(PAIRS):
        todo = events.get(at * OWN + i, ())
        if todo:

            @pl.when(hp == at)
            def _(todo=todo):
                for step in todo:
                    step()


def late(events):
    for at in sorted(events):
        if at >= PAIRS * OWN:
            for step in events[at]:
                step()


def token_sends(hid_in, x_own, x_send, x_recv):
    y, x, c, z = coordinates()
    for m in range(2):
        for l in range(3):
            t = 3 * z + l
            core_to, z_to = lax.rem(t, 2), 2 * c + m
            yield (
                hid_in.at[m, l], x_own.at[t // 2], x_send.at[m, l], x_recv.at[t // 2],
                place(y, x, core_to, z_to), (core_to == c) & (z_to == z),
            )


def start_all(items):
    for item in items:
        send_or_keep(*item)


def grad_sends(grd_in, g_part, first, g_send, g_recv):
    y, x, c, z = coordinates()
    width = g_part.shape[2]
    for m in range(2):
        for half in range(2):
            z_to = 2 * c + m
            yield (
                grd_in.at[m, half, :, pl.ds(first, width)], g_part.at[2 * z + half], g_send.at[0, m, half],
                g_recv.at[0, z], place(y, x, half, z_to), (half == c) & (z_to == z),
            )


def dealt_sends(dealt, hid_part, first, h_send, h_recv):
    y, x, c, z = coordinates()
    owner, micro = z // 2, lax.rem(z, 2)
    for e in range(2):
        z_to = 2 * c + e
        yield (
            dealt.at[e, :, pl.ds(first, hid_part.shape[2])], hid_part.at[micro], h_send.at[e], h_recv.at[micro],
            place(y, x, owner, z_to), (owner == c) & (z_to == z),
        )


def share_copy(g_part, zs, core, g_send, g_recv):
    y, x, c, z = coordinates()
    block = g_part.at[2 * zs + core]
    return remote(
        block, block, g_send.at[1, zs // 2, zs % 2], g_recv.at[1, zs], place(y, x, 1 - c, z)
    )


def share_grads(g_part, g_send, g_recv):
    y, x, c, z = coordinates()
    for zs in range(4):
        block = g_part.at[2 * zs + c]
        remote(block, block, g_send.at[1, 0, 0], g_recv.at[0, zs], place(y, x, 1 - c, z)).wait_recv()
        share_copy(g_part, zs, c, g_send, g_recv).start()


def end_grads(items, g_part, g_send, g_recv):
    c = coordinates()[2]
    for zs in range(4):
        share_copy(g_part, zs, 1 - c, g_send, g_recv).wait_recv()
        share_copy(g_part, zs, c, g_send, g_recv).wait_send()
    for item in items:
        sent(*item)


def gather_kernel(first_axis, *refs):
    count = len(first_axis)
    lens_in, deal_in, hid_in, one_in, two_in, rel_in = refs[:6]
    shards = refs[6 : 5 + count]
    rest = refs[5 + count :]
    lens_u, deal_u, x_own = rest[:3]
    outs = rest[3 : 3 + count]
    lens_wide, rows_f, small, w_send, w_recv, w_local, x_send, x_recv, p_send, p_recv = rest[3 + count :]
    y, x, c, z = coordinates()
    sibling = place(y, x, 1 - c, z)
    greet()
    rows_f[...] = jnp.zeros_like(rows_f)
    rows_f[0:1, : one_in.shape[1]] = one_in[...].astype(jnp.float32)
    rows_f[1:2, : two_in.shape[1]] = two_in[...].astype(jnp.float32)
    rows_f[2:3, : rel_in.shape[1]] = rel_in[...].astype(jnp.float32)
    small[...] = rows_f[...].astype(jnp.bfloat16)
    lens_wide[...] = jnp.zeros_like(lens_wide)
    lens_wide[:, :, : lens_in.shape[2]] = lens_in[...]
    greeted()
    gather = Gather(
        [(s, o, None, a) for s, o, a in zip((small,) + tuple(shards), outs, first_axis)], w_send, w_recv, w_local
    )
    for n in range(count):
        gather.start(n)
    sends = list(token_sends(hid_in, x_own, x_send, x_recv))
    for item in sends:
        send_or_keep(*item)
    owner, micro = z // 2, lax.rem(z, 2)
    plans = []
    for n, (src, dst) in enumerate(((lens_wide, lens_u), (deal_in, deal_u))):
        plans.append((src.at[micro], dst, p_send.at[n], p_recv.at[n]))

    @pl.when(owner == c)
    def _():
        for src, dst, send, recv in plans:
            remote(src, dst, send, recv, sibling).start()
            pltpu.make_async_copy(src, dst, recv).start()

    for n in range(count):
        gather.spread_own(n)
    for n in range(count):
        gather.spread_near(n)
    for n in range(count):
        gather.spread_side(n)
    for n in range(count):
        gather.finish(n)
    for item in sends:
        sent(*item)
    for i in range(OWN):
        remote(hid_in.at[0, 0], x_own.at[i], x_send.at[0, 0], x_recv.at[i], sibling).wait_recv()
    for src, dst, send, recv in plans:
        remote(src, dst, send, recv, sibling).wait_recv()

    @pl.when(owner == c)
    def _():
        for src, dst, send, recv in plans:
            remote(src, dst, send, recv, sibling).wait_send()


def sum_terms(term):
    total = term[0].astype(jnp.float32)
    for dz in range(1, 4):
        total = total + term[dz].astype(jnp.float32)
    return total


def sum_kernel(
    hid_low, hid_high, gin_in, tsmall, tq, tk, tv, two, twi, twu,
    hid_out, gin_out, one_out, two_out, rel_out, gq, gk, gv, gwo, gwi, gwu,
):
    half = hid_low.shape[2]
    hid_out[:, :, :half] = hid_low[...].astype(jnp.float32)
    hid_out[:, :, half:] = hid_high[...].astype(jnp.float32)
    gin_out[...] = gin_in[...].astype(jnp.float32)

    @pl.when(pl.program_id(0) == 0)
    def _():
        small = sum_terms(tsmall)
        one_out[...] = small[0:1, : one_out.shape[1]]
        two_out[...] = small[1:2, : two_out.shape[1]]
        rel_out[...] = small[2:3, : rel_out.shape[1]]
        for term, out in ((tq, gq), (tk, gk), (tv, gv), (two, gwo), (twi, gwi), (twu, gwu)):
            out[...] = sum_terms(term)


def token_places(deal_order, lengths):
    seq_ends = jnp.cumsum(lengths)
    starts = seq_ends - lengths
    inside = (deal_order[:, None] >= starts[None, :]).astype(jnp.int32)
    segment = jnp.sum(inside, axis=1) - 1
    picked = (segment[:, None] == jnp.arange(lengths.shape[0], dtype=jnp.int32)[None, :]).astype(
        jnp.int32
    )
    position = deal_order - jnp.sum(picked * starts[None, :], axis=1)
    return (segment, position)


def rms_scale(rows_in):
    return lax.rsqrt(jnp.mean(rows_in * rows_in, axis=1, keepdims=True) + EPSILON)


def gelu_slope(values):
    normal_cdf = 0.5 * (1.0 + jax.scipy.special.erf(values * (1.0 / math.sqrt(2.0))))
    normal_pdf = jnp.exp(-0.5 * values * values) * (1.0 / math.sqrt(2.0 * math.pi))
    return normal_cdf + values * normal_pdf


def norm_back_rows(rows_in, scale, gain, grad_normed):
    scaled_grad = grad_normed * gain
    grad_gain = jnp.sum(grad_normed * rows_in * scale, axis=0)
    grad_rows = scale * scaled_grad - rows_in * scale * scale * scale * jnp.mean(
        scaled_grad * rows_in, axis=1, keepdims=True
    )
    return (grad_rows, grad_gain)


def key_layout(key_all, value_all, segment, position, head_count):
    rows_all = key_all.shape[0]
    block_rows = 512
    blocks = rows_all // block_rows
    return (
        key_all.reshape(blocks, block_rows, head_count, -1),
        value_all.reshape(blocks, block_rows, head_count, -1),
        segment.reshape(blocks, block_rows),
        position.reshape(blocks, block_rows),
    )


def block_scores(
    queries,
    key_block,
    seg_query,
    pos_query,
    seg_block,
    pos_block,
    rel_bucket,
    bucket_edges,
    max_offset,
):
    lower_edge, upper_edge = bucket_edges
    raw_scores = jnp.einsum("qhd,khd->hqk", queries, key_block, preferred_element_type=jnp.float32)
    offset = jnp.clip(pos_block[None, :] - pos_query[:, None], -max_offset, max_offset)
    bucket_hit = (
        (offset[:, :, None] >= lower_edge[None, None, :])
        & (offset[:, :, None] <= upper_edge[None, None, :])
    ).astype(jnp.float32)
    bias = jnp.einsum(
        "qkb,bh->hqk",
        bucket_hit,
        rel_bucket,
        precision=lax.Precision.HIGHEST,
        preferred_element_type=jnp.float32,
    )
    same_seq = (seg_query[:, None] == seg_block[None, :])[None]
    return (raw_scores + bias, same_seq, bucket_hit)


def attend(queries, layout, seg_query, pos_query, rel_bucket, bucket_edges, max_offset):
    key_blocks, value_blocks, seg_blocks, pos_blocks = layout
    query_count, head_count, head_size = queries.shape

    def measure(carry, block):
        row_top, row_total = carry
        key_block, seg_block, pos_block = block
        scores, same_seq, _ = block_scores(
            queries,
            key_block,
            seg_query,
            pos_query,
            seg_block,
            pos_block,
            rel_bucket,
            bucket_edges,
            max_offset,
        )
        scores = jnp.where(same_seq, scores, NEG_FILL)
        new_top = jnp.maximum(row_top, jnp.max(scores, axis=2))
        weights_now = jnp.where(same_seq, jnp.exp(scores - new_top[:, :, None]), 0.0)
        row_total = row_total * jnp.exp(row_top - new_top) + jnp.sum(weights_now, axis=2)
        return ((new_top, row_total), None)

    start = (
        jnp.full((head_count, query_count), NEG_FILL, jnp.float32),
        jnp.zeros((head_count, query_count), jnp.float32),
    )
    (row_top, row_total), _ = lax.scan(measure, start, (key_blocks, seg_blocks, pos_blocks))
    log_total = row_top + jnp.log(row_total)

    def collect(summed, block):
        key_block, value_block, seg_block, pos_block = block
        scores, same_seq, _ = block_scores(
            queries,
            key_block,
            seg_query,
            pos_query,
            seg_block,
            pos_block,
            rel_bucket,
            bucket_edges,
            max_offset,
        )
        probs = jnp.where(same_seq, jnp.exp(scores - log_total[:, :, None]), 0.0).astype(
            jnp.bfloat16
        )
        return (
            summed
            + jnp.einsum("hqk,khd->qhd", probs, value_block, preferred_element_type=jnp.float32),
            None,
        )

    attended_f, _ = lax.scan(
        collect, jnp.zeros((query_count, head_count, head_size), jnp.float32), layout
    )
    return (attended_f, log_total)


def attend_back(
    queries,
    layout,
    seg_query,
    pos_query,
    rel_bucket,
    bucket_edges,
    max_offset,
    log_total,
    d_attended,
    row_delta,
):

    def step(carry, block):
        d_queries, d_buckets = carry
        key_block, value_block, seg_block, pos_block = block
        scores, same_seq, bucket_hit = block_scores(
            queries,
            key_block,
            seg_query,
            pos_query,
            seg_block,
            pos_block,
            rel_bucket,
            bucket_edges,
            max_offset,
        )
        probs_f = jnp.where(same_seq, jnp.exp(scores - log_total[:, :, None]), 0.0)
        d_probs = jnp.einsum(
            "qhd,khd->hqk", d_attended, value_block, preferred_element_type=jnp.float32
        )
        d_scores = (probs_f * (d_probs - row_delta[:, :, None])).astype(jnp.bfloat16)
        d_queries = d_queries + jnp.einsum(
            "hqk,khd->qhd", d_scores, key_block, preferred_element_type=jnp.float32
        )
        d_buckets = d_buckets + jnp.einsum(
            "hqk,qkb->bh",
            d_scores,
            bucket_hit.astype(jnp.bfloat16),
            preferred_element_type=jnp.float32,
        )
        d_values = jnp.einsum(
            "hqk,qhd->khd",
            probs_f.astype(jnp.bfloat16),
            d_attended,
            preferred_element_type=jnp.float32,
        )
        d_keys = jnp.einsum("hqk,qhd->khd", d_scores, queries, preferred_element_type=jnp.float32)
        return ((d_queries, d_buckets), (d_keys, d_values))

    start = (jnp.zeros(queries.shape, jnp.float32), jnp.zeros(rel_bucket.shape, jnp.float32))
    (d_queries, d_buckets), key_terms = lax.scan(step, start, layout)
    return (d_queries, key_terms, d_buckets)


def on_device(
    hidden_in,
    grad_out,
    gain_attn,
    gain_ffn,
    rel_bias,
    w_query,
    w_key,
    w_value,
    w_output,
    w_inner,
    w_outer,
    dealing,
    lengths,
    bucket_table,
):
    micro_count, tok_rows, model_width = hidden_in.shape
    group_size = lax.axis_size("fsdp")
    slot_rows = tok_rows // group_size
    own_index = lax.axis_index("fsdp")
    max_offset = (bucket_table.shape[0] - 1) // 2
    bucket_count = BUCKETS
    head_count = H
    offsets_all = jnp.arange(bucket_table.shape[0], dtype=jnp.int32) - max_offset
    matches = bucket_table[:, None] == jnp.arange(bucket_count, dtype=jnp.int32)[None, :]
    lower_edge = jnp.min(jnp.where(matches, offsets_all[:, None], 2 * max_offset + 2), axis=0)
    upper_edge = jnp.max(jnp.where(matches, offsets_all[:, None], -2 * max_offset - 2), axis=0)
    bucket_edges = (lower_edge, upper_edge)
    hidden_units = w_inner.shape[1]
    acc_gain_one = jnp.zeros((model_width,), jnp.float32)
    acc_gain_two = jnp.zeros((model_width,), jnp.float32)
    acc_buckets = jnp.zeros((bucket_count, head_count), jnp.float32)
    acc_query = jnp.zeros((model_width, model_width), jnp.float32)
    acc_key = jnp.zeros((model_width, model_width), jnp.float32)
    acc_value = jnp.zeros((model_width, model_width), jnp.float32)
    acc_output = jnp.zeros((model_width, model_width), jnp.float32)
    acc_inner = jnp.zeros((model_width, hidden_units), jnp.float32)
    acc_outer = jnp.zeros((hidden_units, model_width), jnp.float32)
    outputs_list = []
    grads_list = []
    for micro_idx in range(micro_count):
        weights_now = (
            lax.all_gather(gain_attn, ("dp", "fsdp"), axis=0, tiled=True),
            lax.all_gather(gain_ffn, ("dp", "fsdp"), axis=0, tiled=True),
            lax.all_gather(rel_bias, ("dp", "fsdp"), axis=0, tiled=True),
            lax.all_gather(w_query, ("dp", "fsdp"), axis=0, tiled=True),
            lax.all_gather(w_key, ("dp", "fsdp"), axis=0, tiled=True),
            lax.all_gather(w_value, ("dp", "fsdp"), axis=0, tiled=True),
            lax.all_gather(w_output, ("dp", "fsdp"), axis=0, tiled=True),
            lax.all_gather(w_inner, ("dp", "fsdp"), axis=0, tiled=True),
            lax.all_gather(w_outer, ("dp", "fsdp"), axis=0, tiled=True),
        )
        gain_one = weights_now[0].astype(jnp.float32)
        gain_two = weights_now[1].astype(jnp.float32)
        rel_bucket = weights_now[2].astype(jnp.float32).reshape(bucket_count, head_count)
        query_weight, key_weight, value_weight, output_weight, inner_weight, outer_weight = (
            weights_now[3:]
        )
        deal_order = dealing[micro_idx, 0]
        segment, position = token_places(deal_order, lengths[micro_idx, 0])
        seg_query = lax.dynamic_slice_in_dim(segment, own_index * tok_rows, tok_rows)
        pos_query = lax.dynamic_slice_in_dim(position, own_index * tok_rows, tok_rows)
        take_rows = (
            lax.dynamic_slice_in_dim(
                deal_order.reshape(group_size, tok_rows), own_index * slot_rows, slot_rows, 1
            )
            - own_index * tok_rows
        ).reshape(tok_rows)
        dealt = lax.all_to_all(
            jnp.take(hidden_in[micro_idx], take_rows, axis=0),
            "fsdp",
            split_axis=0,
            concat_axis=0,
            tiled=True,
        )
        dealt_rows = dealt.astype(jnp.float32)
        scale_one = rms_scale(dealt_rows)
        normed1 = (dealt_rows * scale_one * gain_one).astype(jnp.bfloat16)
        queries = jnp.dot(normed1, query_weight, preferred_element_type=jnp.float32).astype(
            jnp.bfloat16
        )
        key_rows = jnp.dot(normed1, key_weight, preferred_element_type=jnp.float32).astype(
            jnp.bfloat16
        )
        value_rows = jnp.dot(normed1, value_weight, preferred_element_type=jnp.float32).astype(
            jnp.bfloat16
        )
        key_all, value_all = (
            lax.all_gather(key_rows, "fsdp", axis=0, tiled=True),
            lax.all_gather(value_rows, "fsdp", axis=0, tiled=True),
        )
        layout = key_layout(key_all, value_all, segment, position, head_count)
        queries_heads = queries.reshape(tok_rows, head_count, -1)
        attended_f, log_total = attend(
            queries_heads, layout, seg_query, pos_query, rel_bucket, bucket_edges, max_offset
        )
        attended = attended_f.reshape(tok_rows, model_width).astype(jnp.bfloat16)
        mid = dealt_rows + jnp.dot(attended, output_weight, preferred_element_type=jnp.float32)
        scale_two = rms_scale(mid)
        normed2 = (mid * scale_two * gain_two).astype(jnp.bfloat16)
        inner_act = jnp.dot(normed2, inner_weight, preferred_element_type=jnp.float32)
        active = jax.nn.gelu(inner_act, approximate=False).astype(jnp.bfloat16)
        result = mid + jnp.dot(active, outer_weight, preferred_element_type=jnp.float32)
        outputs_list.append(result)
        weights_back = (
            lax.all_gather(gain_attn, ("dp", "fsdp"), axis=0, tiled=True),
            lax.all_gather(gain_ffn, ("dp", "fsdp"), axis=0, tiled=True),
            lax.all_gather(rel_bias, ("dp", "fsdp"), axis=0, tiled=True),
            lax.all_gather(w_query, ("dp", "fsdp"), axis=0, tiled=True),
            lax.all_gather(w_key, ("dp", "fsdp"), axis=0, tiled=True),
            lax.all_gather(w_value, ("dp", "fsdp"), axis=0, tiled=True),
            lax.all_gather(w_output, ("dp", "fsdp"), axis=0, tiled=True),
            lax.all_gather(w_inner, ("dp", "fsdp"), axis=0, tiled=True),
            lax.all_gather(w_outer, ("dp", "fsdp"), axis=0, tiled=True),
        )
        query_weight, key_weight, value_weight, output_weight, inner_weight, outer_weight = (
            weights_back[3:]
        )
        grad_top = grad_out[micro_idx]
        acc_outer = acc_outer + jnp.einsum(
            "tf,td->fd", active, grad_top, preferred_element_type=jnp.float32
        )
        d_active = jnp.einsum(
            "td,fd->tf", grad_top, outer_weight, preferred_element_type=jnp.float32
        )
        d_inner = (d_active * gelu_slope(inner_act)).astype(jnp.bfloat16)
        acc_inner = acc_inner + jnp.einsum(
            "td,tf->df", normed2, d_inner, preferred_element_type=jnp.float32
        )
        d_normed2 = jnp.einsum(
            "tf,df->td", d_inner, inner_weight, preferred_element_type=jnp.float32
        )
        d_mid_norm, d_gain_two = norm_back_rows(mid, scale_two, gain_two, d_normed2)
        acc_gain_two = acc_gain_two + d_gain_two
        d_mid = grad_top.astype(jnp.float32) + d_mid_norm
        d_branch = d_mid.astype(jnp.bfloat16)
        acc_output = acc_output + jnp.einsum(
            "td,te->de", attended, d_branch, preferred_element_type=jnp.float32
        )
        d_attended = jnp.einsum(
            "te,de->td", d_branch, output_weight, preferred_element_type=jnp.float32
        ).astype(jnp.bfloat16)
        d_attended_heads = d_attended.reshape(tok_rows, head_count, -1)
        row_delta = jnp.sum(d_attended_heads.astype(jnp.float32) * attended_f, axis=2).T
        key_back, value_back = (
            lax.all_gather(key_rows, "fsdp", axis=0, tiled=True),
            lax.all_gather(value_rows, "fsdp", axis=0, tiled=True),
        )
        layout_back = key_layout(key_back, value_back, segment, position, head_count)
        d_queries, key_terms, d_buckets = attend_back(
            queries_heads,
            layout_back,
            seg_query,
            pos_query,
            rel_bucket,
            bucket_edges,
            max_offset,
            log_total,
            d_attended_heads,
            row_delta,
        )
        d_keys, d_values = key_terms
        group_rows = d_keys.shape[0] * d_keys.shape[1]
        d_keys_own, d_values_own = (
            lax.psum_scatter(
                d_keys.reshape(group_rows, model_width).astype(jnp.bfloat16),
                "fsdp",
                scatter_dimension=0,
                tiled=True,
            ).astype(jnp.float32),
            lax.psum_scatter(
                d_values.reshape(group_rows, model_width).astype(jnp.bfloat16),
                "fsdp",
                scatter_dimension=0,
                tiled=True,
            ).astype(jnp.float32),
        )
        acc_buckets = acc_buckets + d_buckets
        d_queries_low = d_queries.reshape(tok_rows, model_width).astype(jnp.bfloat16)
        d_keys_low = d_keys_own.astype(jnp.bfloat16)
        d_values_low = d_values_own.astype(jnp.bfloat16)
        acc_query = acc_query + jnp.einsum(
            "td,te->de", normed1, d_queries_low, preferred_element_type=jnp.float32
        )
        acc_key = acc_key + jnp.einsum(
            "td,te->de", normed1, d_keys_low, preferred_element_type=jnp.float32
        )
        acc_value = acc_value + jnp.einsum(
            "td,te->de", normed1, d_values_low, preferred_element_type=jnp.float32
        )
        d_normed1 = (
            jnp.einsum("te,de->td", d_queries_low, query_weight, preferred_element_type=jnp.float32)
            + jnp.einsum("te,de->td", d_keys_low, key_weight, preferred_element_type=jnp.float32)
            + jnp.einsum(
                "te,de->td", d_values_low, value_weight, preferred_element_type=jnp.float32
            )
        )
        d_rows_norm, d_gain_one = norm_back_rows(dealt_rows, scale_one, gain_one, d_normed1)
        acc_gain_one = acc_gain_one + d_gain_one
        d_dealt = d_mid + d_rows_norm
        returned = lax.all_to_all(
            d_dealt.astype(jnp.bfloat16), "fsdp", split_axis=0, concat_axis=0, tiled=True
        ).astype(d_dealt.dtype)
        grads_list.append(jnp.zeros_like(returned).at[take_rows].set(returned))
    acc_rel = acc_buckets.reshape(-1)
    summed = (
        lax.psum_scatter(acc_gain_one, ("dp", "fsdp"), scatter_dimension=0, tiled=True),
        lax.psum_scatter(acc_gain_two, ("dp", "fsdp"), scatter_dimension=0, tiled=True),
        lax.psum_scatter(acc_rel, ("dp", "fsdp"), scatter_dimension=0, tiled=True),
        lax.psum_scatter(acc_query, ("dp", "fsdp"), scatter_dimension=0, tiled=True),
        lax.psum_scatter(acc_key, ("dp", "fsdp"), scatter_dimension=0, tiled=True),
        lax.psum_scatter(acc_value, ("dp", "fsdp"), scatter_dimension=0, tiled=True),
        lax.psum_scatter(acc_output, ("dp", "fsdp"), scatter_dimension=0, tiled=True),
        lax.psum_scatter(acc_inner, ("dp", "fsdp"), scatter_dimension=0, tiled=True),
        lax.psum_scatter(acc_outer, ("dp", "fsdp"), scatter_dimension=0, tiled=True),
    )
    return (
        jnp.stack(outputs_list),
        jnp.stack(grads_list),
        summed[0],
        summed[1],
        summed[2],
        summed[3],
        summed[4],
        summed[5],
        summed[6],
        summed[7],
        summed[8],
    )


VMEM = pl.BlockSpec(memory_space=pltpu.VMEM)
SMEM = pl.BlockSpec(memory_space=pltpu.SMEM)
ANYWHERE = pl.BlockSpec(memory_space=pl.ANY)
LIMIT = 58 * 1024 * 1024
FIRST_AXIS = ("x", "x", "y", "x", "y")
FWD_PARTS = 3
FWD_AHEAD = 2
FWD_OWN = (-1, 0, 6, 12, 15, 21)
FWD_NEAR = (9, 12, 18, 24, 27, 33)
FWD_SIDE = (21, 24, 30, 36, 41, 41)
FWD_GRADS = 15
FFN_CHUNK = 768
BWD_PARTS = 3
BWD_AHEAD = 4
BWD_SIDE = (12, 14, 20, 20, 24, 26, 28)
BWD_NEAR = (18, 22, 26, 24, 28, 30, 34)


def shaped(*shape, dtype=jnp.bfloat16):
    return jax.ShapeDtypeStruct(shape, dtype)


def params(collective_id=None):
    if collective_id is None:
        return pltpu.CompilerParams(vmem_limit_bytes=LIMIT)
    return pltpu.CompilerParams(
        collective_id=collective_id, has_side_effects=True, vmem_limit_bytes=LIMIT
    )


def dma(*shape):
    return pltpu.SemaphoreType.DMA(shape)


def gather_all(lens, deal, hid, one, two, rel, shards):
    count = len(shards) + 1
    return pl.pallas_call(
        functools.partial(gather_kernel, FIRST_AXIS),
        name="gather_all",
        out_shape=[
            shaped(1, 128, dtype=jnp.int32),
            shaped(*deal.shape[1:], dtype=jnp.int32),
            shaped(OWN, TILE, hid.shape[-1]),
            shaped(32, 16, 128),
        ]
        + [shaped(32, *s.shape) for s in shards],
        in_specs=[VMEM] + [ANYWHERE] * 2 + [VMEM] * 3 + [ANYWHERE] * (count - 1),
        out_specs=[ANYWHERE] * (3 + count),
        scratch_shapes=[
            pltpu.VMEM((2, 1, 128), jnp.int32), pltpu.VMEM((16, 128), jnp.float32), pltpu.VMEM((16, 128), jnp.bfloat16),
            dma(count, 10), dma(count, 10), dma(count), dma(2, 3), dma(OWN), dma(2), dma(2),
        ],
        compiler_params=params(0),
    )(lens, deal, hid, one, two, rel, *shards)


def attention_forward(lens, x, small, table, wq, wk, wv, grd, wi, wu):
    heads, keys = (PAIRS, OWN, TILE, 128), (PAIRS, OWN, 2, TILE, 128)
    count = len(FWD_OWN)
    return pl.pallas_call(
        attn_fwd,
        name="attn_fwd",
        out_shape=[
            shaped(*heads), shaped(*keys), shaped(*keys), shaped(*x.shape),
            shaped(OWN, 2 * PAIRS, 1, TILE, dtype=jnp.float32),
            shaped(8, grd.shape[2], grd.shape[3] // 2),
            shaped(32, *wi.shape), shaped(32, *wu.shape),
        ],
        in_specs=[SMEM] + [VMEM] * 6 + [ANYWHERE] * 3,
        out_specs=[VMEM] * 5 + [ANYWHERE] * 3,
        scratch_shapes=[
            pltpu.VMEM((5, 2 * PAIRS, 1, 2 * TILE), jnp.float32),
            pltpu.VMEM((2 * PAIRS, 5, TILE, TILE), jnp.float32),
            pltpu.VMEM((OWN, TILE, 128), jnp.bfloat16),
            pltpu.VMEM((TILES, TILE, 128), jnp.bfloat16),
            pltpu.VMEM((2, TILE, TILES * TILE), jnp.float32),
            pltpu.VMEM((OWN, TILE, 128), jnp.float32),
            dma(2), dma(2),
            dma(count, 10), dma(count, 10), dma(count), dma(2, 2, 2), dma(2, 4),
        ],
        compiler_params=params(1),
    )(lens, x, small, table, wq, wk, wv, grd, wi, wu)


def landing(shapes, leads=((4, 4), (2, 4), (4,))):
    return [pltpu.VMEM((*lead, *b), jnp.bfloat16) for b in shapes for lead in leads]


def attention_backward(lens, q, k, v, log_total, d_att, delta, small, table, gwo, gwi, gwu, dealt):
    heads = (PAIRS, OWN, TILE, 128)
    block_i, block_u = (gwi.shape[2], gwi.shape[3] // BWD_PARTS), (gwu.shape[2], gwu.shape[3] // BWD_PARTS)
    blocks = [block_i, block_u] * BWD_PARTS + [gwo.shape[2:]]
    count = len(blocks)
    return pl.pallas_call(
        attn_bwd,
        name="attn_bwd",
        out_shape=[shaped(*heads)] * 3
        + [shaped(32, 128, dtype=jnp.float32)]
        + [shaped(4, *g.shape[2:]) for g in (gwo, gwi, gwu)]
        + [shaped(*dealt.shape[:2], dealt.shape[2] // 2)],
        in_specs=[SMEM] + [VMEM] * 8 + [ANYWHERE] * 4,
        out_specs=[VMEM] * 4 + [ANYWHERE] * 4,
        scratch_shapes=[pltpu.VMEM((5, 2 * PAIRS, 1, 2 * TILE), jnp.float32)] * 2
        + [pltpu.VMEM((2 * PAIRS, 5, TILE, TILE), jnp.float32)] * 2
        + [pltpu.VMEM((OWN, TILE, 128), jnp.bfloat16), pltpu.VMEM((TILES, TILE, 128), jnp.bfloat16)]
        + [pltpu.VMEM((TILES * TILE, 128), jnp.float32)] * 2
        + [pltpu.VMEM(heads, jnp.bfloat16)] * 4
        + [dma(2, PAIRS), dma(2, PAIRS), dma(count, 10), dma(count, 10), dma(count, 3), dma(2), dma(2)]
        + landing(blocks, ((2, 4), (2, 4), (4,))),
        compiler_params=params(2),
    )(lens, q, k, v, log_total, d_att, delta, small, table, gwo, gwi, gwu, dealt)


def feed_forward(deal, x, att, wo, small, g_low, grd, wi, wu):
    tok, width = x.shape
    hidden = wi.shape[1]
    f32, bf16 = jnp.float32, jnp.bfloat16
    heads, stats = (PAIRS, OWN, TILE, 128), (OWN, 2 * PAIRS, 1, TILE)
    block_i, block_u = (32, width // 32, hidden), (32, hidden // 32, width)
    chunks = hidden // FFN_CHUNK
    return pl.pallas_call(
        ffn_kernel,
        name="feed_forward",
        out_shape=[
            shaped(tok, width, dtype=f32), shaped(*heads), shaped(*stats, dtype=f32),
            shaped(4, 4, width // 32, width), shaped(32, 128, dtype=f32), shaped(2, 3 * TILE, width),
            shaped(4, 4, *block_i[1:]), shaped(4, 4, *block_u[1:]), shaped(2, 3 * TILE, width // 2),
        ],
        in_specs=[VMEM] * 6 + [ANYWHERE] * 3,
        out_specs=[VMEM] * 6 + [ANYWHERE] * 3,
        scratch_shapes=[
            pltpu.VMEM((tok, width), bf16), pltpu.VMEM((tok, width), f32), pltpu.VMEM((tok, width), bf16),
            pltpu.VMEM((tok, width), f32), pltpu.VMEM((tok, hidden), bf16), pltpu.VMEM((tok, hidden), bf16),
            pltpu.VMEM((width, hidden), bf16), pltpu.VMEM((hidden, width), bf16),
            pltpu.VMEM((2, 32, width // 32, FFN_CHUNK), bf16), pltpu.VMEM((2, 32 // chunks, hidden // 32, width), bf16),
            pltpu.VMEM(g_low.shape, bf16),
            pltpu.VMEM((OWN, TILE, width), bf16), pltpu.VMEM((OWN, 2, TILE, width), bf16),
            pltpu.VMEM((chunks, 4, 4, width // 32, FFN_CHUNK), bf16), pltpu.VMEM((chunks, 4, hidden // 32, width), bf16),
            pltpu.VMEM((32, width // 32, width), bf16),
            dma(2, chunks), dma(2, chunks), dma(2, 2, 2), dma(2, 4), dma(2), dma(2),
            pltpu.SemaphoreType.DMA, pltpu.SemaphoreType.DMA, dma(chunks + 1, 5), dma(chunks + 1, 5),
        ],
        compiler_params=params(4),
    )(deal, x, att, wo, small, g_low, grd, wi, wu)


def tail(x, small, d_mid, dq, dk, dv, wq, wk, wv, g_two, g_rel):
    tok, width = x.shape
    block = (width // 32, width)
    blocks = [block, block, block, (16, 128)]
    count = len(blocks)
    return pl.pallas_call(
        tail_kernel,
        name="tail",
        out_shape=[shaped(2, 3, TILE, width), shaped(4, 16, 128)] + [shaped(4, *block)] * 3,
        in_specs=[VMEM] * 4 + [ANYWHERE] * 7,
        out_specs=[ANYWHERE] * 5,
        scratch_shapes=[
            pltpu.VMEM((tok, width), jnp.float32), pltpu.VMEM((3, width, width), jnp.bfloat16),
            pltpu.VMEM((3, OWN, TILE, width), jnp.bfloat16), pltpu.VMEM((tok, width), jnp.bfloat16),
            pltpu.VMEM((OWN, TILE, width), jnp.bfloat16),
            pltpu.VMEM((32, 16, 128), jnp.bfloat16),
        ]
        + [pltpu.VMEM((32, *block), jnp.bfloat16)] * 3
        + landing(blocks)
        + [dma(count, 10), dma(count, 10), dma(count, 1), dma(OWN), dma(2, 3), dma(4, PAIRS + 1)],
        compiler_params=params(3),
    )(x, small, g_two, g_rel, d_mid, dq, dk, dv, wq, wk, wv)


def last_sums(low, high, gin, terms):
    f32 = jnp.float32
    lines = lambda n: shaped(1, n, dtype=f32)
    hid_shape = (*low.shape[:2], 2 * low.shape[2])

    def by_micro(shape):
        return pl.BlockSpec((1, *shape[1:]), lambda m: (m,) + (0,) * (len(shape) - 1))

    def whole(shape):
        return pl.BlockSpec(shape, lambda m: (0,) * len(shape))

    sums = [lines(24), lines(24), lines(H)] + [shaped(*t.shape[1:], dtype=f32) for t in terms[1:]]
    return pl.pallas_call(
        sum_kernel,
        name="last_sums",
        grid=(low.shape[0],),
        out_shape=[shaped(*hid_shape, dtype=f32), shaped(*gin.shape, dtype=f32)] + sums,
        in_specs=[by_micro(v.shape) for v in (low, high, gin)] + [whole(t.shape) for t in terms],
        out_specs=[by_micro(hid_shape), by_micro(gin.shape)] + [whole(s.shape) for s in sums],
        compiler_params=params(),
    )(low, high, gin, *terms)


def on_device_packed(
    hidden_in, grad_out, gain_attn, gain_ffn, rel_bias,
    w_query, w_key, w_value, w_output, w_inner, w_outer,
    dealing, lengths, bucket_table,
):
    micro_count, tok_rows, width = hidden_in.shape
    matrix = lambda w: w.reshape(-1, w.shape[-1])
    table = bucket_table
    grd = grad_out.reshape(2, 2, tok_rows // 2, width)
    lens_u, deal_u, x_own, small, wq, wk, wv, wo = gather_all(
        lengths, dealing, hidden_in.reshape(2, 3, TILE, width),
        gain_attn[None], gain_ffn[None], rel_bias[None], (w_query, w_key, w_value, w_output),
    )
    wq, wk, wv = map(matrix, (wq, wk, wv))
    x_rows = matrix(x_own)
    q, k, v, att, log_total, g_low, wi, wu = attention_forward(
        lens_u, x_rows, small, table, wq, wk, wv, grd, w_inner, w_outer
    )
    d_mid, d_att, delta, g_wo, g_two, dealt, g_wi, g_wu, hid_low = feed_forward(
        deal_u, x_rows, att, matrix(wo), small, g_low, grd, matrix(wi), matrix(wu)
    )
    dq, dk, dv, g_rel, t_wo, t_wi, t_wu, hid_high = attention_backward(
        lens_u, q, k, v, log_total, d_att, delta, small, table, g_wo, g_wi, g_wu, dealt
    )
    gin, t_small, t_wq, t_wk, t_wv = tail(x_rows, small, d_mid, dq, dk, dv, wq, wk, wv, g_two, g_rel)
    hid, gin, s_one, s_two, s_rel, *grads = last_sums(hid_low, hid_high, gin, (t_small, t_wq, t_wk, t_wv, t_wo, t_wi, t_wu))
    return (hid, gin.reshape(2, tok_rows, width), s_one[0], s_two[0], s_rel[0], *grads)


def solution(mesh):
    axes = ("dp", "fsdp")
    tokens, matrix, vector = P(None, axes, None), P(axes, None), P(axes)
    packed = mesh.shape["fsdp"] == 4 and mesh.shape["dp"] == 8
    return jax.shard_map(
        on_device_packed if packed else on_device,
        mesh=mesh,
        in_specs=(tokens, tokens, vector, vector, vector)
        + (matrix,) * 6
        + (P(None, "dp", None), P(None, "dp", None), P()),
        out_specs=(tokens, tokens, vector, vector, vector) + (matrix,) * 6,
        check_vma=False,
    )
```

```python
import functools
import math

import jax
import jax.numpy as jnp
from jax import lax
from jax.experimental import pallas as pl
from jax.experimental.pallas import tpu as pltpu
from jax.sharding import PartitionSpec as P

H = 12
BUCKETS = 32
EPSILON = 1e-06
NEG_FILL = -1e30
MESH = pl.DeviceIdType.MESH
TILE = 128
PAIRS = 6
OWN = 6
TILES = 12
FAR = 6
SEQS = 4


def lane_index(shape):
    return lax.broadcasted_iota(jnp.int32, shape, len(shape) - 1)


def row_index(shape):
    return lax.broadcasted_iota(jnp.int32, shape, len(shape) - 2)


def dot_nn(left, right):
    return lax.dot_general(left, right, (((1,), (0,)), ((), ())), preferred_element_type=jnp.float32)


def dot_nt(left, right):
    return lax.dot_general(left, right, (((1,), (1,)), ((), ())), preferred_element_type=jnp.float32)


def dot_tn(left, right):
    return lax.dot_general(left, right, (((0,), (0,)), ((), ())), preferred_element_type=jnp.float32)


def segments_of(places, lens_ref, count):
    edge = jnp.int32(0)
    found = jnp.zeros(places.shape, jnp.int32)
    for s in range(count - 1):
        edge = edge + lens_ref[0, s]
        found = found + (places >= edge).astype(jnp.int32)
    return found


def segment_tags(places, lens_ref, count, of_key):
    lane = lane_index(places.shape)
    hit = segments_of(places, lens_ref, count) == lane
    if of_key:
        return jnp.where((lane < count) & jnp.logical_not(hit), NEG_FILL, 0.0).astype(jnp.bfloat16)
    return jnp.where(hit, 1.0, 0.0).astype(jnp.bfloat16)


def one_hot(rows, columns):
    return jnp.where(rows == columns, 1.0, 0.0).astype(jnp.bfloat16)


def small_lines(small_ref, kind):
    flat = small_ref[...].reshape(32 * 16, 128)
    pick = one_hot(16 * row_index((32, 512)) + kind, lane_index((32, 512)))
    return dot_nn(pick, flat).astype(jnp.bfloat16)


def gain_row(small_ref, kind, width):
    lines = dot_nn(
        small_lines(small_ref, kind), one_hot(row_index((128, width)), lax.rem(lane_index((128, width)), 24))
    )
    own = lane_index((32, width)) // 24 == row_index((32, width))
    return jnp.sum(jnp.where(own, lines, 0.0), axis=0, keepdims=True)


def bucket_picks(table_ref, places):
    span = table_ref.shape[0]
    picked = one_hot(row_index((BUCKETS, span)), jnp.broadcast_to(table_ref[...][None, :], (BUCKETS, span)))
    places = jnp.clip(places, 0, span - 1)
    return dot_nn(picked, one_hot(row_index((span, 256)), jnp.broadcast_to(places, (span, 256)))).astype(jnp.bfloat16)


def class_places(cls, sign):
    lane = lane_index((1, 256))
    if cls >= 3:
        return jnp.full((1, 256), 0 if cls == 3 else 2 * TILE, jnp.int32)
    turn = jnp.where(lane < TILE, lane, lane - 2 * TILE)
    return TILE * (cls - 1) + sign * turn + TILE


def fill_rows(small_ref, table_ref, rows_ref, sign):
    rel = small_lines(small_ref, 2)
    for cls in range(5):
        made = dot_tn(rel, bucket_picks(table_ref, class_places(cls, sign)))
        for h in range(2 * PAIRS):
            rows_ref[cls, h] = made[h : h + 1, :]


def bucket_sums(hist_ref, table_ref):
    total = None
    for cls in range(5):
        if cls >= 3:
            places = class_places(cls, 1)
        else:
            places = TILE * (cls - 1) + 2 * TILE - 1 - lane_index((1, 256))
        hist = jnp.concatenate([hist_ref[cls, h] for h in range(2 * PAIRS)] + [jnp.zeros((4, 256), jnp.float32)], axis=0)
        term = lax.dot_general(
            bucket_picks(table_ref, places).astype(jnp.float32), hist, (((1,), (1,)), ((), ())),
            precision=lax.Precision.HIGHEST, preferred_element_type=jnp.float32,
        )
        total = term if total is None else total + term
    return total


def key_range(i):
    return max(0, 2 * i - FAR), min(TILES, 2 * i + FAR + 2)


def fill_bias(rows_ref, tiles_ref, heads):
    def one_head(h, carry):
        for cls in range(3):
            row = rows_ref[cls, h]
            wide = pltpu.roll(
                jnp.broadcast_to(row, (TILE, 2 * TILE)), 0, 1, stride=1, stride_axis=0
            )
            tiles_ref[h, cls + 1] = wide[:, :TILE]
        left = rows_ref[3, h, :, :TILE]
        right = rows_ref[4, h, :, :TILE]
        tiles_ref[h, 0] = jnp.broadcast_to(left, (TILE, TILE))
        tiles_ref[h, 4] = jnp.broadcast_to(right, (TILE, TILE))
        return carry

    lax.fori_loop(0, heads, one_head, 0)


def bias_class(kt, i, core):
    return jnp.clip(kt - 2 * i - core, -2, 2) + 2


def make_tags(lens_ref, ext_q, ext_k):
    core = lax.rem(lax.axis_index("dp"), 2)
    for t in range(TILES):
        ext_k[t] = segment_tags(TILE * t + row_index((TILE, 128)), lens_ref, SEQS, True)
    for i in range(OWN):
        ext_q[i] = segment_tags(TILE * (2 * i + core) + row_index((TILE, 128)), lens_ref, SEQS, False)


def attn_fwd(
    lens_ref, x_ref, small_ref, table_ref, wq_ref, wk_ref, wv_ref, grd_in, wi_in, wu_in,
    q_ref, k_ref, v_ref, att_ref, log_ref, g_low, wi_all, wu_all,
    rows_ref, bias_ref, ext_q, ext_k, s_ref, log_acc, send_sem, recv_sem,
    w_send, w_recv, w_local, g_send, g_recv,
):
    y, x, core, z = coordinates()
    sibling = place(y, x, 1 - core, z)
    greet()
    pieces = []
    part_i, part_u = wi_in.shape[1] // FWD_PARTS, wu_in.shape[1] // FWD_PARTS
    for n in range(FWD_PARTS):
        pieces.append((wi_in, wi_all, (n * part_i, part_i), "xy"[(n + 1) % 2]))
        pieces.append((wu_in, wu_all, (n * part_u, part_u), "xy"[n % 2]))
    gather = Gather(pieces, w_send, w_recv, w_local)
    grads = list(grad_sends(grd_in, g_low, 0, g_send, g_recv))
    events = {}

    def plan(at, step, *args):
        events.setdefault(at, []).append(functools.partial(step, *args))

    for n in range(len(pieces)):
        plan(FWD_OWN[n], gather.spread_own, n)
        if n + FWD_AHEAD < len(pieces):
            plan(FWD_OWN[n], gather.start, n + FWD_AHEAD)
        plan(FWD_NEAR[n], gather.spread_near, n)
        plan(FWD_SIDE[n], gather.spread_side, n)
    plan(FWD_GRADS, start_all, grads)

    greeted()
    for n in range(FWD_AHEAD):
        gather.start(n)
    rows = x_ref[...].astype(jnp.float32)
    scale = lax.rsqrt(jnp.mean(rows * rows, axis=1, keepdims=True) + EPSILON)
    normed = (rows * scale * gain_row(small_ref, 0, rows.shape[1])).astype(jnp.bfloat16)

    def project(w_ref):
        return dot_nn(normed, w_ref[...]).astype(jnp.bfloat16)

    copies = []
    for n, (w_ref, all_ref) in enumerate(((wk_ref, k_ref), (wv_ref, v_ref))):
        made = project(w_ref)
        for hp in range(PAIRS):
            for i in range(OWN):
                all_ref[hp, i, core] = made[TILE * i : TILE * (i + 1), 128 * hp : 128 * (hp + 1)]
        copy = remote(all_ref.at[:, :, core], all_ref.at[:, :, core], send_sem.at[n], recv_sem.at[n], sibling)
        copy.start()
        copies.append(copy)
    made = project(wq_ref)
    for hp in range(PAIRS):
        for i in range(OWN):
            q_ref[hp, i] = made[TILE * i : TILE * (i + 1), 128 * hp : 128 * (hp + 1)]
    make_tags(lens_ref, ext_q, ext_k)
    for i in range(OWN):
        log_acc[i] = jnp.zeros((TILE, 128), jnp.float32)
    for step in events.pop(-1, ()):
        step()
    fill_rows(small_ref, table_ref, rows_ref, 1)
    fill_bias(rows_ref, bias_ref, 2 * PAIRS)
    for n, all_ref in enumerate((k_ref, v_ref)):
        block = all_ref.at[:, :, 1 - core]
        remote(block, block, send_sem.at[n], recv_sem.at[n], sibling).wait_recv()

    lane = lane_index((TILE, 128))

    def one_pair(hp, carry):
        for i in range(OWN):
            run_events(events, hp, i)
            lo, hi = key_range(i)
            width = (hi - lo) * TILE
            pair = q_ref[hp, i]
            tags = ext_q[i]
            zero = jnp.zeros_like(pair)
            left = jnp.concatenate(
                [
                    jnp.concatenate([jnp.where(lane < 64, pair, zero), tags], axis=1),
                    jnp.concatenate([jnp.where(lane < 64, zero, pair), tags], axis=1),
                ],
                axis=0,
            )
            keys = k_ref[hp, lo // 2 : hi // 2].reshape(width, 128)
            right = jnp.concatenate([keys, ext_k[lo:hi].reshape(width, 128)], axis=1)
            raw = dot_nt(left, right)
            tops = []
            for e in range(2):
                top = None
                for kt in range(lo, hi):
                    at = (kt - lo) * TILE
                    part = raw[e * TILE : (e + 1) * TILE, at : at + TILE]
                    if -1 <= kt - 2 * i <= 2:
                        part = part + bias_ref[2 * hp + e, bias_class(kt, i, core)]
                    else:
                        part = part + rows_ref[3 if kt < 2 * i else 4, 2 * hp + e, :, :TILE]
                    s_ref[e, :, at : at + TILE] = part
                    top = part if top is None else jnp.maximum(top, part)
                tops.append(jnp.max(top, axis=1, keepdims=True))
            outs = []
            for e in range(2):
                total = None
                found = []
                for kt in range(lo, hi):
                    at = (kt - lo) * TILE
                    weight = jnp.exp(s_ref[e, :, at : at + TILE] - tops[e])
                    total = weight if total is None else total + weight
                    found.append(weight.astype(jnp.bfloat16))
                total = jnp.sum(total, axis=1, keepdims=True)
                probs = jnp.concatenate(found, axis=1)
                values = v_ref[hp, lo // 2 : hi // 2].reshape(width, 128)
                outs.append(dot_nn(probs, values) / total)
                log_acc[i] = jnp.where(lane == 2 * hp + e, tops[e] + jnp.log(total), log_acc[i])
            att_ref[TILE * i : TILE * (i + 1), pl.ds(pl.multiple_of(128 * hp, 128), 128)] = jnp.where(
                lane < 64, outs[0], outs[1]
            ).astype(jnp.bfloat16)
        return carry

    lax.fori_loop(0, PAIRS, one_pair, 0)
    late(events)
    share_grads(g_low, g_send, g_recv)
    for i in range(OWN):
        turned = log_acc[i].T
        for h in range(2 * PAIRS):
            log_ref[i, h] = turned[h : h + 1, :]
    for n in range(len(pieces)):
        gather.finish(n)
    end_grads(grads, g_low, g_send, g_recv)
    for copy in copies:
        copy.wait_send()


def attn_bwd(
    lens_ref, q_ref, k_ref, v_ref, log_ref, do_ref, delta_ref, small_ref, table_ref, gwo, gwi, gwu, dealt,
    dq_ref, dk_ref, dv_ref, rel_ref, two, twi, twu, hid_out,
    rows_ref, hist_ref, bias_ref, acc_ref, ext_q, ext_k, dk_acc, dv_acc, out_k, out_v, got_k, got_v, send_sem, recv_sem,
    w_send, w_recv, w_local, h_send, h_recv, *landed,
):
    y, x, core, z = coordinates()
    sibling = place(y, x, 1 - core, z)
    greet()
    plain = []
    part_i, part_u = gwi.shape[3] // BWD_PARTS, gwu.shape[3] // BWD_PARTS
    for n in range(BWD_PARTS):
        plain.append((gwi, twi, (n * part_i, part_i), "xy"[n % 2]))
        plain.append((gwu, twu, (n * part_u, part_u), "xy"[(n + 1) % 2]))
    plain.append((gwo, two, None, "x"))
    count = len(plain)
    scatter = LateScatter(
        [item + tuple(landed[3 * n : 3 * n + 3]) for n, item in enumerate(plain)], w_send, w_recv, w_local
    )
    events = {}

    def plan(at, step, *args):
        events.setdefault(at, []).append(functools.partial(step, *args))

    for n in range(count):
        plan(BWD_SIDE[n], scatter.sum_side, n)
        if n + BWD_AHEAD < count:
            plan(BWD_SIDE[n], scatter.start, n + BWD_AHEAD)
        plan(BWD_NEAR[n], scatter.sum_near, n)
    make_tags(lens_ref, ext_q, ext_k)
    greeted()
    for n in range(BWD_AHEAD):
        scatter.start(n)
    deals = list(dealt_sends(dealt, hid_out, hid_out.shape[2], h_send, h_recv))
    start_all(deals)
    acc_ref[...] = jnp.zeros_like(acc_ref)
    fill_rows(small_ref, table_ref, rows_ref, -1)
    fill_bias(rows_ref, bias_ref, 2 * PAIRS)
    for step in events.pop(-1, ()):
        step()
    lane = lane_index((TILE, 128))

    def one_pair(hp, carry):
        dk_acc[...] = jnp.zeros_like(dk_acc)
        dv_acc[...] = jnp.zeros_like(dv_acc)
        for i in range(OWN):
            run_events(events, hp, i)
            lo, hi = key_range(i)
            width = (hi - lo) * TILE
            pair, d_pair = q_ref[hp, i], do_ref[hp, i]
            tags = ext_q[i]
            zero = jnp.zeros_like(pair)
            q_two = jnp.concatenate([jnp.where(lane < 64, pair, zero), jnp.where(lane < 64, zero, pair)], axis=0)
            d_two = jnp.concatenate([jnp.where(lane < 64, d_pair, zero), jnp.where(lane < 64, zero, d_pair)], axis=0)
            q_ext = jnp.concatenate([q_two, jnp.concatenate([tags, tags], axis=0)], axis=1)
            keys = k_ref[hp, lo // 2 : hi // 2].reshape(width, 128)
            values = v_ref[hp, lo // 2 : hi // 2].reshape(width, 128)
            k_ext = jnp.concatenate([keys, ext_k[lo:hi].reshape(width, 128)], axis=1)
            raw = dot_nt(k_ext, q_ext)
            d_probs = dot_nt(values, d_two)
            p_rows, s_rows = [], []
            for kt in range(lo, hi):
                at = (kt - lo) * TILE
                p_two, s_two = [], []
                for e in range(2):
                    head = 2 * hp + e
                    part = raw[at : at + TILE, e * TILE : (e + 1) * TILE]
                    near = -1 <= kt - 2 * i <= 2
                    cls = bias_class(kt, i, core) if near else (0 if kt < 2 * i else 4)
                    if near:
                        part = part + bias_ref[head, cls]
                    else:
                        part = part + rows_ref[3 if kt < 2 * i else 4, head, :, :TILE]
                    probs = jnp.exp(part - log_ref[i, head])
                    slope = probs * (
                        d_probs[at : at + TILE, e * TILE : (e + 1) * TILE] - delta_ref[i, head]
                    )
                    acc_ref[head, cls] += slope
                    p_two.append(probs.astype(jnp.bfloat16))
                    s_two.append(slope.astype(jnp.bfloat16))
                p_rows.append(jnp.concatenate(p_two, axis=1))
                s_rows.append(jnp.concatenate(s_two, axis=1))
            probs_t = jnp.concatenate(p_rows, axis=0)
            slopes_t = jnp.concatenate(s_rows, axis=0)
            dv_acc[lo * TILE : hi * TILE, :] += dot_nn(probs_t, d_two)
            dk_acc[lo * TILE : hi * TILE, :] += dot_nn(slopes_t, q_two)
            d_q = dot_tn(slopes_t, keys)
            dq_ref[hp, i] = jnp.where(lane < 64, d_q[:TILE], d_q[TILE:]).astype(jnp.bfloat16)
        for acc, own, out in ((dk_acc, dk_ref, out_k), (dv_acc, dv_ref, out_v)):
            for i in range(OWN):
                own[hp, i] = acc[pl.ds((2 * i + core) * TILE, TILE), :].astype(jnp.bfloat16)
                out[hp, i] = acc[pl.ds((2 * i + 1 - core) * TILE, TILE), :].astype(jnp.bfloat16)
        for n, (out, got) in enumerate(((out_k, got_k), (out_v, got_v))):
            pltpu.make_async_remote_copy(
                out.at[hp], got.at[hp], send_sem.at[n, hp], recv_sem.at[n, hp],
                device_id=sibling, device_id_type=MESH,
            ).start()
        return carry

    lax.fori_loop(0, PAIRS, one_pair, 0)
    flip = (row_index((TILE, TILE)) + lane == TILE - 1).astype(jnp.float32)

    def one_head(h, carry):
        for cls in range(3):
            tile = jnp.dot(flip, acc_ref[h, cls + 1], precision=lax.Precision.HIGHEST)
            wide = jnp.concatenate([tile, jnp.zeros((TILE, TILE), jnp.float32)], axis=1)
            wide = pltpu.roll(wide, 0, 1, stride=1, stride_axis=0)
            hist_ref[cls, h] = jnp.sum(wide, axis=0, keepdims=True)
        for n, cls in ((3, 0), (4, 4)):
            row = jnp.sum(acc_ref[h, cls], axis=0, keepdims=True)
            hist_ref[n, h] = jnp.concatenate([row, jnp.zeros_like(row)], axis=1)
        return carry

    lax.fori_loop(0, 2 * PAIRS, one_head, 0)

    rel_ref[...] = jnp.zeros_like(rel_ref)
    rel_ref[:, :16] = bucket_sums(hist_ref, table_ref)

    def finish(hp, carry):
        for n, (out, got, own) in enumerate(((out_k, got_k, dk_ref), (out_v, got_v, dv_ref))):
            copy = pltpu.make_async_remote_copy(
                out.at[hp], got.at[hp], send_sem.at[n, hp], recv_sem.at[n, hp],
                device_id=sibling, device_id_type=MESH,
            )
            copy.wait_send()
            copy.wait_recv()
            own[hp] = (own[hp].astype(jnp.float32) + got[hp].astype(jnp.float32)).astype(jnp.bfloat16)
        return carry

    lax.fori_loop(0, PAIRS, finish, 0)
    late(events)
    for n in range(count):
        scatter.finish(n)
    for item in deals:
        sent(*item)
    for m in range(2):
        remote(hid_out.at[m], hid_out.at[m], h_send.at[0], h_recv.at[m], sibling).wait_recv()


def norm_back(rows_in, scale, gain, grad_normed):
    scaled = grad_normed * gain
    grad_gain = jnp.sum(grad_normed * rows_in * scale, axis=0, keepdims=True)
    shared = jnp.mean(scaled * rows_in, axis=1, keepdims=True)
    return scale * scaled - rows_in * (scale * scale * scale * shared), grad_gain


def join_pairs(pairs_ref, joined_ref):
    for hp in range(PAIRS):
        joined_ref[:, 128 * hp : 128 * (hp + 1)] = (
            pairs_ref[hp].reshape(OWN * TILE, 128).astype(joined_ref.dtype)
        )


def gain_block(row):
    width = row.shape[1]
    lines = jnp.where(lane_index((32, width)) // 24 == row_index((32, width)), row, 0.0)
    pick = (lax.rem(row_index((width, 128)), 24) == lane_index((width, 128))).astype(jnp.float32)
    return jnp.dot(lines, pick, precision=lax.Precision.HIGHEST)


def ffn_kernel(
    deal_ref, x_ref, att_ref, wo_ref, small_ref, g_low, grd_in, wi_in, wu_in,
    dmid_ref, datt_ref, delta_ref, gwo_ref, two_ref, dealt, gwi, gwu, hid_out,
    grad_ref, mid_ref, normed_ref, total_ref, active_ref, slope_ref, wi_ref, wu_ref, gwi_two, gwu_two, g_high,
    res_ref, res_all, got_i, got_u, gwo_own, in_sem, out_sem, g_send, g_recv, h_send, h_recv, e_send, e_recv,
    c_send, c_recv,
):
    y, x, core, z = coordinates()
    sibling = place(y, x, 1 - core, z)
    greet()
    width = x_ref.shape[1]
    half = width // 2
    chunk = FFN_CHUNK
    chunks = wi_ref.shape[1] // chunk

    def bring(j):
        span = pl.ds(chunk * j, chunk)
        return (
            pltpu.make_async_copy(wi_in.at[:, span], wi_ref.at[:, span], in_sem.at[0, j]),
            pltpu.make_async_copy(wu_in.at[span], wu_ref.at[span], in_sem.at[1, j]),
        )

    for j in range(chunks):
        for copy in bring(j):
            copy.start()
    grads = list(grad_sends(grd_in, g_high, half, g_send, g_recv))
    gain = gain_row(small_ref, 1, width)
    mid = x_ref[...].astype(jnp.float32) + dot_nn(att_ref[...], wo_ref[...])
    mid_ref[...] = mid
    scale = lax.rsqrt(jnp.mean(mid * mid, axis=1, keepdims=True) + EPSILON)
    normed_ref[...] = (mid * scale * gain).astype(jnp.bfloat16)
    greeted()
    start_all(grads)

    def rows_of(i):
        return slice(TILE * i, TILE * (i + 1))

    picks = []
    for i in range(OWN):
        picks.append(one_hot((2 * i + core) * TILE + row_index((TILE, TILES * TILE)), deal_ref[...]))
        grad_ref[rows_of(i), :half] = dot_nn(
            picks[i], g_low[...].reshape(TILES * TILE, half)
        ).astype(jnp.bfloat16)
    for j in range(chunks):
        span = slice(chunk * j, chunk * (j + 1))
        for copy in bring(j):
            copy.wait()
        inner = dot_nn(normed_ref[...], wi_ref[:, span])
        cdf = 0.5 * (1.0 + lax.erf(inner * (1.0 / math.sqrt(2.0))))
        active = (inner * cdf).astype(jnp.bfloat16)
        active_ref[:, span] = active
        slope = cdf + inner * (jnp.exp(-0.5 * inner * inner) * (1.0 / math.sqrt(2.0 * math.pi)))
        slope_ref[:, span] = slope.astype(jnp.bfloat16)
        term = dot_nn(active, wu_ref[span, :])
        total_ref[...] = term if j == 0 else total_ref[...] + term
    result = (mid_ref[...] + total_ref[...]).astype(jnp.bfloat16).reshape(OWN, TILE, width)
    res_ref[...] = result
    res_copy = remote(res_ref, res_all.at[:, core], e_send, e_recv, sibling)
    res_copy.start()
    for i in range(OWN):
        res_all[i, core] = result[i]
    share_grads(g_high, g_send, g_recv)

    remote(res_ref, res_all.at[:, 1 - core], e_send, e_recv, sibling).wait_recv()
    lane = lane_index((TILE, TILE))
    for b in range(OWN):
        at = pl.multiple_of((OWN * core + b) * TILE, TILE)
        turned = jnp.broadcast_to(deal_ref[:, pl.ds(at, TILE)].astype(jnp.float32), (TILE, TILE)).T
        turned = turned.astype(jnp.int32)
        pick = jnp.concatenate([one_hot(turned, TILE * t + lane) for t in range(TILES)], axis=1)
        made = dot_nn(pick, res_all[...].reshape(TILES * TILE, width)).astype(jnp.bfloat16)
        dealt[b // 3, TILE * (b % 3) : TILE * (b % 3 + 1)] = made
    deals = list(dealt_sends(dealt, hid_out, 0, h_send, h_recv))
    start_all(deals)
    end_grads(grads, g_high, g_send, g_recv)
    for i in range(OWN):
        grad_ref[rows_of(i), half:] = dot_nn(
            picks[i], g_high[...].reshape(TILES * TILE, half)
        ).astype(jnp.bfloat16)

    def swap(j):
        slot, there = j % 2, 4 * (1 - core)
        copies = [remote(gwu_two.at[slot, pl.ds(there, 4)], got_u.at[j], c_send.at[j, 4], c_recv.at[j, 4], sibling)]
        for k in range(4):
            copies.append(
                remote(
                    gwi_two.at[slot, pl.ds(8 * k + there, 4)], got_i.at[j, k],
                    c_send.at[j, k], c_recv.at[j, k], sibling,
                )
            )
        return copies

    def take(j):
        return (
            pltpu.make_async_copy(got_i.at[j], gwi.at[:, :, :, pl.ds(chunk * j, chunk)], out_sem.at[0, j]),
            pltpu.make_async_copy(got_u.at[j], gwu.at[j], out_sem.at[1, j]),
        )

    def combine(j):
        slot, here = j % 2, 4 * core
        for copy in swap(j):
            copy.wait_recv()
        for n in range(4):
            got_u[j, n] = got_u[j, n] + gwu_two[slot, here + n]
            for k in range(4):
                got_i[j, k, n] = got_i[j, k, n] + gwi_two[slot, 8 * k + here + n]
        for copy in take(j):
            copy.start()
        for copy in swap(j):
            copy.wait_send()

    for j in range(chunks):
        span = slice(chunk * j, chunk * (j + 1))
        d_inner = (
            dot_nt(grad_ref[...], wu_ref[span, :]) * slope_ref[:, span].astype(jnp.float32)
        ).astype(jnp.bfloat16)
        made = dot_tn(active_ref[:, span], grad_ref[...])
        gwu_two[j % 2] = made.astype(jnp.bfloat16).reshape(gwu_two.shape[1:])
        made = dot_tn(normed_ref[...], d_inner)
        gwi_two[j % 2] = made.reshape(32, -1, chunk).astype(jnp.bfloat16)
        for copy in swap(j):
            copy.start()
        term = dot_nt(d_inner, wi_ref[:, span])
        total_ref[...] = term if j == 0 else total_ref[...] + term
        if j:
            combine(j - 1)

    mid = mid_ref[...]
    scale = lax.rsqrt(jnp.mean(mid * mid, axis=1, keepdims=True) + EPSILON)
    d_rows, d_gain = norm_back(mid, scale, gain, total_ref[...])
    two_ref[...] = gain_block(d_gain)
    d_mid = grad_ref[...].astype(jnp.float32) + d_rows
    dmid_ref[...] = d_mid
    branch = d_mid.astype(jnp.bfloat16)
    made = dot_tn(att_ref[...], branch)
    gwo_own[...] = made.reshape(32, -1, width).astype(jnp.bfloat16)
    swaps = [
        remote(
            gwo_own.at[pl.ds(8 * k + 4 * (1 - core), 4)], gwo_ref.at[k], c_send.at[chunks, k], c_recv.at[chunks, k], sibling
        )
        for k in range(4)
    ]
    for copy in swaps:
        copy.start()
    combine(chunks - 1)
    d_att = dot_nt(branch, wo_ref[...]).astype(jnp.bfloat16)
    pick = (lane_index((16, width)) // 64 == row_index((16, width))).astype(jnp.float32)
    prod = d_att.astype(jnp.float32) * att_ref[...].astype(jnp.float32)
    sums = lax.dot_general(
        pick, prod, (((1,), (1,)), ((), ())), precision=lax.Precision.HIGHEST, preferred_element_type=jnp.float32
    )
    for hp in range(PAIRS):
        datt_ref[hp] = d_att[:, 128 * hp : 128 * (hp + 1)].reshape(OWN, TILE, 128)
    for i in range(OWN):
        for h in range(2 * PAIRS):
            delta_ref[i, h] = sums[h : h + 1, TILE * i : TILE * (i + 1)]
    for k, copy in enumerate(swaps):
        copy.wait_recv()
        for n in range(4):
            gwo_ref[k, n] = gwo_ref[k, n] + gwo_own[8 * k + 4 * core + n]
        copy.wait_send()
    for j in range(chunks):
        for copy in take(j):
            copy.wait()
    res_copy.wait_send()
    for item in deals:
        sent(*item)
    for m in range(2):
        remote(hid_out.at[m], hid_out.at[m], h_send.at[0], h_recv.at[m], sibling).wait_recv()


def tail_kernel(
    x_ref, small_ref, g_two, g_rel, dmid_in, dq_in, dk_in, dv_in, wq_in, wk_in, wv_in,
    gin_out, tsmall, tq, tk, tv,
    dmid_ref, w_ref, join_ref, normed_ref, back_out, small, gq, gk, gv, *scratch,
):
    y, x, c, z = coordinates()
    sibling = place(y, x, 1 - c, z)
    owner, micro = z // 2, lax.rem(z, 2)
    greet()
    plain = [(gk, tk, None, "x"), (gv, tv, None, "y"), (gq, tq, None, "x"), (small, tsmall, None, "y")]
    count = len(plain)
    w_send, w_recv, w_local, b_send, b_recv, in_sem = scratch[3 * count :]
    scatter = Scatter(
        [item + tuple(scratch[3 * n : 3 * n + 3]) for n, item in enumerate(plain)], w_send, w_recv, w_local
    )
    grads_in = []
    for n, (w_in, pairs) in enumerate(((wq_in, dq_in), (wk_in, dk_in), (wv_in, dv_in))):
        copies = [pltpu.make_async_copy(w_in, w_ref.at[n], in_sem.at[n, PAIRS])]
        for hp in range(PAIRS):
            copies.append(
                pltpu.make_async_copy(
                    pairs.at[hp], join_ref.at[n, :, :, pl.ds(128 * hp, 128)], in_sem.at[n, hp]
                )
            )
        for copy in copies:
            copy.start()
        grads_in.append(copies)
    dmid_copy = pltpu.make_async_copy(dmid_in, dmid_ref, in_sem.at[3, 0])
    dmid_copy.start()

    def back_sends():
        for i in range(OWN):
            t = 2 * i + c
            z_to, l = t // 3, lax.rem(t, 3)
            yield (
                back_out.at[i], gin_out.at[micro, l], b_send.at[i], b_recv.at[micro, l],
                place(y, x, owner, z_to), (owner == c) & (z_to == z),
            )

    sends = list(back_sends())
    gain = gain_row(small_ref, 0, x_ref.shape[1])
    width = x_ref.shape[1]
    d_gain = None
    for part_at in range(3):
        tiles = slice(OWN // 3 * part_at, OWN // 3 * (part_at + 1))
        span = slice(TILE * tiles.start, TILE * tiles.stop)
        rows = x_ref[span, :].astype(jnp.float32)
        scale = lax.rsqrt(jnp.mean(rows * rows, axis=1, keepdims=True) + EPSILON)
        normed_ref[span, :] = (rows * scale * gain).astype(jnp.bfloat16)
        back = None
        for n in range(3):
            if part_at == 0:
                for copy in grads_in[n]:
                    copy.wait()
            term = dot_nt(join_ref[n, tiles].reshape(-1, width), w_ref[n])
            back = term if back is None else back + term
        d_rows, part = norm_back(rows, scale, gain, back)
        d_gain = part if d_gain is None else d_gain + part
        if part_at == 0:
            dmid_copy.wait()
        back_out[tiles] = (dmid_ref[span, :] + d_rows).astype(jnp.bfloat16).reshape(-1, TILE, width)
        if part_at == 0:
            greeted()
        start_all(sends[tiles])
    normed_t = normed_ref[...].T
    for n, (at, grad_ref) in enumerate(((1, gk), (2, gv), (0, gq))):
        made = dot_nn(normed_t, join_ref[at].reshape(-1, width))
        for r in range(32):
            grad_ref[r] = made[24 * r : 24 * (r + 1), :].astype(jnp.bfloat16)
        scatter.start(n)
    g_one = gain_block(d_gain)
    shape = (32, 16, 128)
    kind = lax.broadcasted_iota(jnp.int32, shape, 1)
    spread = lambda v: jnp.broadcast_to(v[:, None, :], shape)
    small[...] = jnp.where(
        kind == 0, spread(g_one), jnp.where(kind == 1, spread(g_two[...]), spread(g_rel[...]))
    ).astype(jnp.bfloat16)
    scatter.start(3)
    for n in range(count + 2):
        for back_by, stage in enumerate((scatter.sum_core, scatter.sum_side, scatter.sum_near)):
            if 0 <= n - back_by < count:
                stage(n - back_by)
    for n in range(count):
        scatter.finish(n)
    for item in sends:
        sent(*item)
    for m in range(2):
        for l in range(3):
            remote(back_out.at[0], gin_out.at[m, l], b_send.at[0], b_recv.at[m, l], sibling).wait_recv()


def coordinates():
    dp, z = lax.axis_index("dp"), lax.axis_index("fsdp")
    return dp // 4, lax.rem(dp // 2, 2), lax.rem(dp, 2), z


def place(y, x, c, z):
    return (4 * y + 2 * x + c, z)


def column(y, x, c):
    return 16 * y + 8 * x + 4 * c


def partners():
    y, x, c, z = coordinates()
    found = [place(1 - y, x, c, z), place(y, 1 - x, c, z)]
    for dc in range(2):
        for dz in range(4):
            if dc or dz:
                found.append(place(y, x, lax.rem(c + dc, 2), lax.rem(z + dz, 4)))
    return found


def greet():
    for partner in partners():
        pl.semaphore_signal(pltpu.get_barrier_semaphore(), inc=1, device_id=partner, device_id_type=MESH)


def greeted():
    pl.semaphore_wait(pltpu.get_barrier_semaphore(), len(partners()))


def remote(src, dst, send, recv, target):
    return pltpu.make_async_remote_copy(
        src, dst, send, recv, device_id=target, device_id_type=MESH
    )


def send_or_keep(src, dst, send, recv, target, here):
    @pl.when(jnp.logical_not(here))
    def _():
        remote(src, dst, send, recv, target).start()

    @pl.when(here)
    def _():
        pltpu.make_async_copy(src, dst, recv).start()


def sent(src, dst, send, recv, target, here):
    @pl.when(jnp.logical_not(here))
    def _():
        remote(src, dst, send, recv, target).wait_send()


def cut(ref, lead, part):
    return ref.at[lead] if part is None else ref.at[lead, slice(None), pl.ds(*part)]


def cut_shard(ref, part):
    return ref if part is None else ref.at[:, pl.ds(*part)]


class Gather:
    def __init__(self, pieces, send, recv, local):
        self.pieces, self.send, self.recv, self.local = pieces, send, recv, local
        self.y, self.x, self.c, self.z = coordinates()
        y, x, c, z = self.y, self.x, self.c, self.z
        self.sibling = place(y, x, 1 - c, z)
        self.mine = column(y, x, c)
        self.far = column(1 - y, 1 - x, c)
        by_x = (place(y, 1 - x, c, z), column(y, 1 - x, c))
        by_y = (place(1 - y, x, c, z), column(1 - y, x, c))
        self.sides = {"x": by_x + by_y, "y": by_y + by_x}

    def own_copy(self, n):
        shard, whole, part, _ = self.pieces[n]
        return pltpu.make_async_copy(
            cut_shard(shard, part), cut(whole, self.mine + self.z, part), self.local.at[n]
        )

    def z_copy(self, n, dz, came=False):
        shard, whole, part, _ = self.pieces[n]
        entry = self.mine + (lax.rem(self.z + 4 - dz, 4) if came else self.z)
        return remote(
            cut_shard(shard, part), cut(whole, entry, part), self.send.at[n, dz - 1], self.recv.at[n, dz - 1],
            place(self.y, self.x, self.c, lax.rem(self.z + dz, 4)),
        )

    def push(self, n, k, base, target):
        _, whole, part, _ = self.pieces[n]
        block = cut(whole, pl.ds(base, 4), part)
        return remote(block, block, self.send.at[n, k], self.recv.at[n, k], target)

    def start(self, n):
        self.own_copy(n).start()
        for dz in range(1, 4):
            self.z_copy(n, dz).start()

    def spread_own(self, n):
        near, _, side, _ = self.sides[self.pieces[n][3]]
        self.own_copy(n).wait()
        for dz in range(1, 4):
            self.z_copy(n, dz, True).wait_recv()
        for k, target in ((3, near), (4, side), (6, self.sibling)):
            self.push(n, k, self.mine, target).start()

    def spread_near(self, n):
        _, near_column, side, _ = self.sides[self.pieces[n][3]]
        self.push(n, 3, near_column, self.sibling).wait_recv()
        self.push(n, 5, near_column, side).start()
        self.push(n, 7, near_column, self.sibling).start()

    def spread_side(self, n):
        side_column = self.sides[self.pieces[n][3]][3]
        self.push(n, 4, side_column, self.sibling).wait_recv()
        self.push(n, 8, side_column, self.sibling).start()
        self.push(n, 5, self.far, self.sibling).wait_recv()
        self.push(n, 9, self.far, self.sibling).start()

    def finish(self, n):
        _, near_column, _, side_column = self.sides[self.pieces[n][3]]
        for k, base in ((6, self.mine), (7, near_column), (8, side_column), (9, self.far)):
            self.push(n, k, base + 4 - 8 * self.c, self.sibling).wait_recv()
        for dz in range(1, 4):
            self.z_copy(n, dz).wait_send()
        for k in range(3, 10):
            self.push(n, k, self.mine, self.sibling).wait_send()


class Scatter:
    def __init__(self, pieces, send, recv, local):
        self.pieces, self.send, self.recv, self.local = pieces, send, recv, local
        self.y, self.x, self.c, self.z = coordinates()
        y, x, c, z = self.y, self.x, self.c, self.z
        self.sibling = place(y, x, 1 - c, z)

    def sides(self, n):
        y, x, c, z = self.y, self.x, self.c, self.z
        by_x, by_y = place(y, 1 - x, c, z), place(1 - y, x, c, z)
        if self.pieces[n][3] == "x":
            return by_x, by_y, (lambda s, f: 2 * s + f), y, x
        return by_y, by_x, (lambda s, f: 2 * f + s), x, y

    def core_copy(self, n, k):
        grad, _, part, _, r1 = self.pieces[n][:5]
        return remote(
            cut(grad, pl.ds(8 * k + 4 * (1 - self.c), 4), part), r1.at[k],
            self.send.at[n, k], self.recv.at[n, k], self.sibling,
        )

    def side_copy(self, n, f_at):
        _, side, index, s, _ = self.sides(n)
        _, _, _, _, r1, r2, _ = self.pieces[n]
        return remote(
            r1.at[index(1 - s, f_at)], r2.at[f_at], self.send.at[n, 4 + f_at], self.recv.at[n, 4 + f_at], side
        )

    def near_copy(self, n):
        near, _, index, s, f = self.sides(n)
        _, _, _, _, r1, _, r3 = self.pieces[n]
        return remote(r1.at[index(s, 1 - f)], r3, self.send.at[n, 6], self.recv.at[n, 6], near)

    def z_copy(self, n, dz):
        _, _, index, s, f = self.sides(n)
        _, terms, part, _, r1, _, _ = self.pieces[n]
        z_to = lax.rem(self.z + dz, 4)
        return remote(
            r1.at[index(s, f), z_to], cut(terms, dz, part), self.send.at[n, 6 + dz], self.recv.at[n, 6 + dz],
            place(self.y, self.x, self.c, z_to),
        )

    def own_copy(self, n):
        _, _, index, s, f = self.sides(n)
        _, terms, part, _, r1, _, _ = self.pieces[n]
        return pltpu.make_async_copy(r1.at[index(s, f), self.z], cut(terms, 0, part), self.local.at[n, 0])

    def start(self, n):
        for k in range(4):
            self.core_copy(n, k).start()

    def sum_core(self, n):
        grad, _, part, _, r1 = self.pieces[n][:5]
        for k in range(4):
            self.core_copy(n, k).wait_recv()

            def one(j, carry, k=k):
                r1[k, j] = r1[k, j] + cut(grad, 8 * k + 4 * self.c + j, part)[...]
                return carry

            lax.fori_loop(0, 4, one, 0)
        for f_at in range(2):
            self.side_copy(n, f_at).start()

    def sum_side(self, n):
        _, _, index, s, _ = self.sides(n)
        _, _, _, _, r1, r2, _ = self.pieces[n]
        for f_at in range(2):
            self.side_copy(n, f_at).wait_recv()
            k = index(s, f_at)

            def one(j, carry, k=k, f_at=f_at):
                r1[k, j] = r1[k, j] + r2[f_at, j]
                return carry

            lax.fori_loop(0, 4, one, 0)
        self.near_copy(n).start()

    def sum_near(self, n):
        _, _, index, s, f = self.sides(n)
        _, _, _, _, r1, _, r3 = self.pieces[n]
        self.near_copy(n).wait_recv()
        k = index(s, f)

        def one(j, carry):
            r1[k, j] = r1[k, j] + r3[j]
            return carry

        lax.fori_loop(0, 4, one, 0)
        for dz in range(1, 4):
            self.z_copy(n, dz).start()
        self.own_copy(n).start()

    def finish(self, n):
        self.own_copy(n).wait()
        for dz in range(1, 4):
            self.z_copy(n, dz).wait_recv()
        for k in range(4):
            self.core_copy(n, k).wait_send()
        for f_at in range(2):
            self.side_copy(n, f_at).wait_send()
        self.near_copy(n).wait_send()
        for dz in range(1, 4):
            self.z_copy(n, dz).wait_send()


class LateScatter(Scatter):
    def side_copy(self, n, f_at):
        _, side, index, s, _ = self.sides(n)
        summed, _, part, _, _, r2, _ = self.pieces[n]
        return remote(
            cut(summed.at[index(1 - s, f_at)], pl.ds(0, 4), part), r2.at[f_at],
            self.send.at[n, 4 + f_at], self.recv.at[n, 4 + f_at], side,
        )

    def fetch(self, n, f_at):
        _, _, index, s, _ = self.sides(n)
        summed, _, part, _, own, _, _ = self.pieces[n]
        return pltpu.make_async_copy(
            cut(summed.at[index(s, f_at)], pl.ds(0, 4), part), own.at[f_at], self.local.at[n, 1 + f_at]
        )

    def near_copy(self, n):
        near, _, _, _, f = self.sides(n)
        _, _, _, _, _, r2, r3 = self.pieces[n]
        return remote(r2.at[1 - f], r3, self.send.at[n, 6], self.recv.at[n, 6], near)

    def z_copy(self, n, dz):
        f = self.sides(n)[4]
        _, terms, part, _, _, r2, _ = self.pieces[n]
        z_to = lax.rem(self.z + dz, 4)
        return remote(
            r2.at[f, z_to], cut(terms, dz, part), self.send.at[n, 6 + dz], self.recv.at[n, 6 + dz],
            place(self.y, self.x, self.c, z_to),
        )

    def own_copy(self, n):
        f = self.sides(n)[4]
        _, terms, part, _, _, r2, _ = self.pieces[n]
        return pltpu.make_async_copy(r2.at[f, self.z], cut(terms, 0, part), self.local.at[n, 0])

    def start(self, n):
        for f_at in range(2):
            self.side_copy(n, f_at).start()
            self.fetch(n, f_at).start()

    def sum_side(self, n):
        _, _, _, _, own, r2, _ = self.pieces[n]
        for f_at in range(2):
            self.side_copy(n, f_at).wait_recv()
            self.fetch(n, f_at).wait()

            def one(j, carry, f_at=f_at):
                r2[f_at, j] = r2[f_at, j] + own[f_at, j]
                return carry

            lax.fori_loop(0, 4, one, 0)
        self.near_copy(n).start()

    def sum_near(self, n):
        f = self.sides(n)[4]
        _, _, _, _, _, r2, r3 = self.pieces[n]
        self.near_copy(n).wait_recv()

        def one(j, carry):
            r2[f, j] = r2[f, j] + r3[j]
            return carry

        lax.fori_loop(0, 4, one, 0)
        for dz in range(1, 4):
            self.z_copy(n, dz).start()
        self.own_copy(n).start()

    def finish(self, n):
        self.own_copy(n).wait()
        for dz in range(1, 4):
            self.z_copy(n, dz).wait_recv()
        for f_at in range(2):
            self.side_copy(n, f_at).wait_send()
        self.near_copy(n).wait_send()
        for dz in range(1, 4):
            self.z_copy(n, dz).wait_send()


def run_events(events, hp, i):
    for at in range(PAIRS):
        todo = events.get(at * OWN + i, ())
        if todo:

            @pl.when(hp == at)
            def _(todo=todo):
                for step in todo:
                    step()


def late(events):
    for at in sorted(events):
        if at >= PAIRS * OWN:
            for step in events[at]:
                step()


def token_sends(hid_in, x_own, x_send, x_recv):
    y, x, c, z = coordinates()
    for m in range(2):
        for l in range(3):
            t = 3 * z + l
            core_to, z_to = lax.rem(t, 2), 2 * c + m
            yield (
                hid_in.at[m, l], x_own.at[t // 2], x_send.at[m, l], x_recv.at[t // 2],
                place(y, x, core_to, z_to), (core_to == c) & (z_to == z),
            )


def start_all(items):
    for item in items:
        send_or_keep(*item)


def grad_sends(grd_in, g_part, first, g_send, g_recv):
    y, x, c, z = coordinates()
    width = g_part.shape[2]
    for m in range(2):
        for half in range(2):
            z_to = 2 * c + m
            yield (
                grd_in.at[m, half, :, pl.ds(first, width)], g_part.at[2 * z + half], g_send.at[0, m, half],
                g_recv.at[0, z], place(y, x, half, z_to), (half == c) & (z_to == z),
            )


def dealt_sends(dealt, hid_part, first, h_send, h_recv):
    y, x, c, z = coordinates()
    owner, micro = z // 2, lax.rem(z, 2)
    for e in range(2):
        z_to = 2 * c + e
        yield (
            dealt.at[e, :, pl.ds(first, hid_part.shape[2])], hid_part.at[micro], h_send.at[e], h_recv.at[micro],
            place(y, x, owner, z_to), (owner == c) & (z_to == z),
        )


def share_copy(g_part, zs, core, g_send, g_recv):
    y, x, c, z = coordinates()
    block = g_part.at[2 * zs + core]
    return remote(
        block, block, g_send.at[1, zs // 2, zs % 2], g_recv.at[1, zs], place(y, x, 1 - c, z)
    )


def share_grads(g_part, g_send, g_recv):
    y, x, c, z = coordinates()
    for zs in range(4):
        block = g_part.at[2 * zs + c]
        remote(block, block, g_send.at[1, 0, 0], g_recv.at[0, zs], place(y, x, 1 - c, z)).wait_recv()
        share_copy(g_part, zs, c, g_send, g_recv).start()


def end_grads(items, g_part, g_send, g_recv):
    c = coordinates()[2]
    for zs in range(4):
        share_copy(g_part, zs, 1 - c, g_send, g_recv).wait_recv()
        share_copy(g_part, zs, c, g_send, g_recv).wait_send()
    for item in items:
        sent(*item)


def gather_kernel(first_axis, *refs):
    count = len(first_axis)
    lens_in, deal_in, hid_in, one_in, two_in, rel_in = refs[:6]
    shards = refs[6 : 5 + count]
    rest = refs[5 + count :]
    lens_u, deal_u, x_own = rest[:3]
    outs = rest[3 : 3 + count]
    lens_wide, rows_f, small, w_send, w_recv, w_local, x_send, x_recv, p_send, p_recv = rest[3 + count :]
    y, x, c, z = coordinates()
    sibling = place(y, x, 1 - c, z)
    greet()
    rows_f[...] = jnp.zeros_like(rows_f)
    rows_f[0:1, : one_in.shape[1]] = one_in[...].astype(jnp.float32)
    rows_f[1:2, : two_in.shape[1]] = two_in[...].astype(jnp.float32)
    rows_f[2:3, : rel_in.shape[1]] = rel_in[...].astype(jnp.float32)
    small[...] = rows_f[...].astype(jnp.bfloat16)
    lens_wide[...] = jnp.zeros_like(lens_wide)
    lens_wide[:, :, : lens_in.shape[2]] = lens_in[...]
    greeted()
    gather = Gather(
        [(s, o, None, a) for s, o, a in zip((small,) + tuple(shards), outs, first_axis)], w_send, w_recv, w_local
    )
    for n in range(count):
        gather.start(n)
    sends = list(token_sends(hid_in, x_own, x_send, x_recv))
    for item in sends:
        send_or_keep(*item)
    owner, micro = z // 2, lax.rem(z, 2)
    plans = []
    for n, (src, dst) in enumerate(((lens_wide, lens_u), (deal_in, deal_u))):
        plans.append((src.at[micro], dst, p_send.at[n], p_recv.at[n]))

    @pl.when(owner == c)
    def _():
        for src, dst, send, recv in plans:
            remote(src, dst, send, recv, sibling).start()
            pltpu.make_async_copy(src, dst, recv).start()

    for n in range(count):
        gather.spread_own(n)
    for n in range(count):
        gather.spread_near(n)
    for n in range(count):
        gather.spread_side(n)
    for n in range(count):
        gather.finish(n)
    for item in sends:
        sent(*item)
    for i in range(OWN):
        remote(hid_in.at[0, 0], x_own.at[i], x_send.at[0, 0], x_recv.at[i], sibling).wait_recv()
    for src, dst, send, recv in plans:
        remote(src, dst, send, recv, sibling).wait_recv()

    @pl.when(owner == c)
    def _():
        for src, dst, send, recv in plans:
            remote(src, dst, send, recv, sibling).wait_send()


def sum_terms(term):
    total = term[0].astype(jnp.float32)
    for dz in range(1, 4):
        total = total + term[dz].astype(jnp.float32)
    return total


def sum_kernel(
    hid_low, hid_high, gin_in, tsmall, tq, tk, tv, two, twi, twu,
    hid_out, gin_out, one_out, two_out, rel_out, gq, gk, gv, gwo, gwi, gwu,
):
    half = hid_low.shape[2]
    hid_out[:, :, :half] = hid_low[...].astype(jnp.float32)
    hid_out[:, :, half:] = hid_high[...].astype(jnp.float32)
    gin_out[...] = gin_in[...].astype(jnp.float32)

    @pl.when(pl.program_id(0) == 0)
    def _():
        small = sum_terms(tsmall)
        one_out[...] = small[0:1, : one_out.shape[1]]
        two_out[...] = small[1:2, : two_out.shape[1]]
        rel_out[...] = small[2:3, : rel_out.shape[1]]
        for term, out in ((tq, gq), (tk, gk), (tv, gv), (two, gwo), (twi, gwi), (twu, gwu)):
            out[...] = sum_terms(term)


def token_places(deal_order, lengths):
    seq_ends = jnp.cumsum(lengths)
    starts = seq_ends - lengths
    inside = (deal_order[:, None] >= starts[None, :]).astype(jnp.int32)
    segment = jnp.sum(inside, axis=1) - 1
    picked = (segment[:, None] == jnp.arange(lengths.shape[0], dtype=jnp.int32)[None, :]).astype(
        jnp.int32
    )
    position = deal_order - jnp.sum(picked * starts[None, :], axis=1)
    return (segment, position)


def rms_scale(rows_in):
    return lax.rsqrt(jnp.mean(rows_in * rows_in, axis=1, keepdims=True) + EPSILON)


def gelu_slope(values):
    normal_cdf = 0.5 * (1.0 + jax.scipy.special.erf(values * (1.0 / math.sqrt(2.0))))
    normal_pdf = jnp.exp(-0.5 * values * values) * (1.0 / math.sqrt(2.0 * math.pi))
    return normal_cdf + values * normal_pdf


def norm_back_rows(rows_in, scale, gain, grad_normed):
    scaled_grad = grad_normed * gain
    grad_gain = jnp.sum(grad_normed * rows_in * scale, axis=0)
    grad_rows = scale * scaled_grad - rows_in * scale * scale * scale * jnp.mean(
        scaled_grad * rows_in, axis=1, keepdims=True
    )
    return (grad_rows, grad_gain)


def key_layout(key_all, value_all, segment, position, head_count):
    rows_all = key_all.shape[0]
    block_rows = 512
    blocks = rows_all // block_rows
    return (
        key_all.reshape(blocks, block_rows, head_count, -1),
        value_all.reshape(blocks, block_rows, head_count, -1),
        segment.reshape(blocks, block_rows),
        position.reshape(blocks, block_rows),
    )


def block_scores(
    queries,
    key_block,
    seg_query,
    pos_query,
    seg_block,
    pos_block,
    rel_bucket,
    bucket_edges,
    max_offset,
):
    lower_edge, upper_edge = bucket_edges
    raw_scores = jnp.einsum("qhd,khd->hqk", queries, key_block, preferred_element_type=jnp.float32)
    offset = jnp.clip(pos_block[None, :] - pos_query[:, None], -max_offset, max_offset)
    bucket_hit = (
        (offset[:, :, None] >= lower_edge[None, None, :])
        & (offset[:, :, None] <= upper_edge[None, None, :])
    ).astype(jnp.float32)
    bias = jnp.einsum(
        "qkb,bh->hqk",
        bucket_hit,
        rel_bucket,
        precision=lax.Precision.HIGHEST,
        preferred_element_type=jnp.float32,
    )
    same_seq = (seg_query[:, None] == seg_block[None, :])[None]
    return (raw_scores + bias, same_seq, bucket_hit)


def attend(queries, layout, seg_query, pos_query, rel_bucket, bucket_edges, max_offset):
    key_blocks, value_blocks, seg_blocks, pos_blocks = layout
    query_count, head_count, head_size = queries.shape

    def measure(carry, block):
        row_top, row_total = carry
        key_block, seg_block, pos_block = block
        scores, same_seq, _ = block_scores(
            queries,
            key_block,
            seg_query,
            pos_query,
            seg_block,
            pos_block,
            rel_bucket,
            bucket_edges,
            max_offset,
        )
        scores = jnp.where(same_seq, scores, NEG_FILL)
        new_top = jnp.maximum(row_top, jnp.max(scores, axis=2))
        weights_now = jnp.where(same_seq, jnp.exp(scores - new_top[:, :, None]), 0.0)
        row_total = row_total * jnp.exp(row_top - new_top) + jnp.sum(weights_now, axis=2)
        return ((new_top, row_total), None)

    start = (
        jnp.full((head_count, query_count), NEG_FILL, jnp.float32),
        jnp.zeros((head_count, query_count), jnp.float32),
    )
    (row_top, row_total), _ = lax.scan(measure, start, (key_blocks, seg_blocks, pos_blocks))
    log_total = row_top + jnp.log(row_total)

    def collect(summed, block):
        key_block, value_block, seg_block, pos_block = block
        scores, same_seq, _ = block_scores(
            queries,
            key_block,
            seg_query,
            pos_query,
            seg_block,
            pos_block,
            rel_bucket,
            bucket_edges,
            max_offset,
        )
        probs = jnp.where(same_seq, jnp.exp(scores - log_total[:, :, None]), 0.0).astype(
            jnp.bfloat16
        )
        return (
            summed
            + jnp.einsum("hqk,khd->qhd", probs, value_block, preferred_element_type=jnp.float32),
            None,
        )

    attended_f, _ = lax.scan(
        collect, jnp.zeros((query_count, head_count, head_size), jnp.float32), layout
    )
    return (attended_f, log_total)


def attend_back(
    queries,
    layout,
    seg_query,
    pos_query,
    rel_bucket,
    bucket_edges,
    max_offset,
    log_total,
    d_attended,
    row_delta,
):

    def step(carry, block):
        d_queries, d_buckets = carry
        key_block, value_block, seg_block, pos_block = block
        scores, same_seq, bucket_hit = block_scores(
            queries,
            key_block,
            seg_query,
            pos_query,
            seg_block,
            pos_block,
            rel_bucket,
            bucket_edges,
            max_offset,
        )
        probs_f = jnp.where(same_seq, jnp.exp(scores - log_total[:, :, None]), 0.0)
        d_probs = jnp.einsum(
            "qhd,khd->hqk", d_attended, value_block, preferred_element_type=jnp.float32
        )
        d_scores = (probs_f * (d_probs - row_delta[:, :, None])).astype(jnp.bfloat16)
        d_queries = d_queries + jnp.einsum(
            "hqk,khd->qhd", d_scores, key_block, preferred_element_type=jnp.float32
        )
        d_buckets = d_buckets + jnp.einsum(
            "hqk,qkb->bh",
            d_scores,
            bucket_hit.astype(jnp.bfloat16),
            preferred_element_type=jnp.float32,
        )
        d_values = jnp.einsum(
            "hqk,qhd->khd",
            probs_f.astype(jnp.bfloat16),
            d_attended,
            preferred_element_type=jnp.float32,
        )
        d_keys = jnp.einsum("hqk,qhd->khd", d_scores, queries, preferred_element_type=jnp.float32)
        return ((d_queries, d_buckets), (d_keys, d_values))

    start = (jnp.zeros(queries.shape, jnp.float32), jnp.zeros(rel_bucket.shape, jnp.float32))
    (d_queries, d_buckets), key_terms = lax.scan(step, start, layout)
    return (d_queries, key_terms, d_buckets)


def on_device(
    hidden_in,
    grad_out,
    gain_attn,
    gain_ffn,
    rel_bias,
    w_query,
    w_key,
    w_value,
    w_output,
    w_inner,
    w_outer,
    dealing,
    lengths,
    bucket_table,
):
    micro_count, tok_rows, model_width = hidden_in.shape
    group_size = lax.axis_size("fsdp")
    slot_rows = tok_rows // group_size
    own_index = lax.axis_index("fsdp")
    max_offset = (bucket_table.shape[0] - 1) // 2
    bucket_count = BUCKETS
    head_count = H
    offsets_all = jnp.arange(bucket_table.shape[0], dtype=jnp.int32) - max_offset
    matches = bucket_table[:, None] == jnp.arange(bucket_count, dtype=jnp.int32)[None, :]
    lower_edge = jnp.min(jnp.where(matches, offsets_all[:, None], 2 * max_offset + 2), axis=0)
    upper_edge = jnp.max(jnp.where(matches, offsets_all[:, None], -2 * max_offset - 2), axis=0)
    bucket_edges = (lower_edge, upper_edge)
    hidden_units = w_inner.shape[1]
    acc_gain_one = jnp.zeros((model_width,), jnp.float32)
    acc_gain_two = jnp.zeros((model_width,), jnp.float32)
    acc_buckets = jnp.zeros((bucket_count, head_count), jnp.float32)
    acc_query = jnp.zeros((model_width, model_width), jnp.float32)
    acc_key = jnp.zeros((model_width, model_width), jnp.float32)
    acc_value = jnp.zeros((model_width, model_width), jnp.float32)
    acc_output = jnp.zeros((model_width, model_width), jnp.float32)
    acc_inner = jnp.zeros((model_width, hidden_units), jnp.float32)
    acc_outer = jnp.zeros((hidden_units, model_width), jnp.float32)
    outputs_list = []
    grads_list = []
    for micro_idx in range(micro_count):
        weights_now = (
            lax.all_gather(gain_attn, ("dp", "fsdp"), axis=0, tiled=True),
            lax.all_gather(gain_ffn, ("dp", "fsdp"), axis=0, tiled=True),
            lax.all_gather(rel_bias, ("dp", "fsdp"), axis=0, tiled=True),
            lax.all_gather(w_query, ("dp", "fsdp"), axis=0, tiled=True),
            lax.all_gather(w_key, ("dp", "fsdp"), axis=0, tiled=True),
            lax.all_gather(w_value, ("dp", "fsdp"), axis=0, tiled=True),
            lax.all_gather(w_output, ("dp", "fsdp"), axis=0, tiled=True),
            lax.all_gather(w_inner, ("dp", "fsdp"), axis=0, tiled=True),
            lax.all_gather(w_outer, ("dp", "fsdp"), axis=0, tiled=True),
        )
        gain_one = weights_now[0].astype(jnp.float32)
        gain_two = weights_now[1].astype(jnp.float32)
        rel_bucket = weights_now[2].astype(jnp.float32).reshape(bucket_count, head_count)
        query_weight, key_weight, value_weight, output_weight, inner_weight, outer_weight = (
            weights_now[3:]
        )
        deal_order = dealing[micro_idx, 0]
        segment, position = token_places(deal_order, lengths[micro_idx, 0])
        seg_query = lax.dynamic_slice_in_dim(segment, own_index * tok_rows, tok_rows)
        pos_query = lax.dynamic_slice_in_dim(position, own_index * tok_rows, tok_rows)
        take_rows = (
            lax.dynamic_slice_in_dim(
                deal_order.reshape(group_size, tok_rows), own_index * slot_rows, slot_rows, 1
            )
            - own_index * tok_rows
        ).reshape(tok_rows)
        dealt = lax.all_to_all(
            jnp.take(hidden_in[micro_idx], take_rows, axis=0),
            "fsdp",
            split_axis=0,
            concat_axis=0,
            tiled=True,
        )
        dealt_rows = dealt.astype(jnp.float32)
        scale_one = rms_scale(dealt_rows)
        normed1 = (dealt_rows * scale_one * gain_one).astype(jnp.bfloat16)
        queries = jnp.dot(normed1, query_weight, preferred_element_type=jnp.float32).astype(
            jnp.bfloat16
        )
        key_rows = jnp.dot(normed1, key_weight, preferred_element_type=jnp.float32).astype(
            jnp.bfloat16
        )
        value_rows = jnp.dot(normed1, value_weight, preferred_element_type=jnp.float32).astype(
            jnp.bfloat16
        )
        key_all, value_all = (
            lax.all_gather(key_rows, "fsdp", axis=0, tiled=True),
            lax.all_gather(value_rows, "fsdp", axis=0, tiled=True),
        )
        layout = key_layout(key_all, value_all, segment, position, head_count)
        queries_heads = queries.reshape(tok_rows, head_count, -1)
        attended_f, log_total = attend(
            queries_heads, layout, seg_query, pos_query, rel_bucket, bucket_edges, max_offset
        )
        attended = attended_f.reshape(tok_rows, model_width).astype(jnp.bfloat16)
        mid = dealt_rows + jnp.dot(attended, output_weight, preferred_element_type=jnp.float32)
        scale_two = rms_scale(mid)
        normed2 = (mid * scale_two * gain_two).astype(jnp.bfloat16)
        inner_act = jnp.dot(normed2, inner_weight, preferred_element_type=jnp.float32)
        active = jax.nn.gelu(inner_act, approximate=False).astype(jnp.bfloat16)
        result = mid + jnp.dot(active, outer_weight, preferred_element_type=jnp.float32)
        outputs_list.append(result)
        weights_back = (
            lax.all_gather(gain_attn, ("dp", "fsdp"), axis=0, tiled=True),
            lax.all_gather(gain_ffn, ("dp", "fsdp"), axis=0, tiled=True),
            lax.all_gather(rel_bias, ("dp", "fsdp"), axis=0, tiled=True),
            lax.all_gather(w_query, ("dp", "fsdp"), axis=0, tiled=True),
            lax.all_gather(w_key, ("dp", "fsdp"), axis=0, tiled=True),
            lax.all_gather(w_value, ("dp", "fsdp"), axis=0, tiled=True),
            lax.all_gather(w_output, ("dp", "fsdp"), axis=0, tiled=True),
            lax.all_gather(w_inner, ("dp", "fsdp"), axis=0, tiled=True),
            lax.all_gather(w_outer, ("dp", "fsdp"), axis=0, tiled=True),
        )
        query_weight, key_weight, value_weight, output_weight, inner_weight, outer_weight = (
            weights_back[3:]
        )
        grad_top = grad_out[micro_idx]
        acc_outer = acc_outer + jnp.einsum(
            "tf,td->fd", active, grad_top, preferred_element_type=jnp.float32
        )
        d_active = jnp.einsum(
            "td,fd->tf", grad_top, outer_weight, preferred_element_type=jnp.float32
        )
        d_inner = (d_active * gelu_slope(inner_act)).astype(jnp.bfloat16)
        acc_inner = acc_inner + jnp.einsum(
            "td,tf->df", normed2, d_inner, preferred_element_type=jnp.float32
        )
        d_normed2 = jnp.einsum(
            "tf,df->td", d_inner, inner_weight, preferred_element_type=jnp.float32
        )
        d_mid_norm, d_gain_two = norm_back_rows(mid, scale_two, gain_two, d_normed2)
        acc_gain_two = acc_gain_two + d_gain_two
        d_mid = grad_top.astype(jnp.float32) + d_mid_norm
        d_branch = d_mid.astype(jnp.bfloat16)
        acc_output = acc_output + jnp.einsum(
            "td,te->de", attended, d_branch, preferred_element_type=jnp.float32
        )
        d_attended = jnp.einsum(
            "te,de->td", d_branch, output_weight, preferred_element_type=jnp.float32
        ).astype(jnp.bfloat16)
        d_attended_heads = d_attended.reshape(tok_rows, head_count, -1)
        row_delta = jnp.sum(d_attended_heads.astype(jnp.float32) * attended_f, axis=2).T
        key_back, value_back = (
            lax.all_gather(key_rows, "fsdp", axis=0, tiled=True),
            lax.all_gather(value_rows, "fsdp", axis=0, tiled=True),
        )
        layout_back = key_layout(key_back, value_back, segment, position, head_count)
        d_queries, key_terms, d_buckets = attend_back(
            queries_heads,
            layout_back,
            seg_query,
            pos_query,
            rel_bucket,
            bucket_edges,
            max_offset,
            log_total,
            d_attended_heads,
            row_delta,
        )
        d_keys, d_values = key_terms
        group_rows = d_keys.shape[0] * d_keys.shape[1]
        d_keys_own, d_values_own = (
            lax.psum_scatter(
                d_keys.reshape(group_rows, model_width).astype(jnp.bfloat16),
                "fsdp",
                scatter_dimension=0,
                tiled=True,
            ).astype(jnp.float32),
            lax.psum_scatter(
                d_values.reshape(group_rows, model_width).astype(jnp.bfloat16),
                "fsdp",
                scatter_dimension=0,
                tiled=True,
            ).astype(jnp.float32),
        )
        acc_buckets = acc_buckets + d_buckets
        d_queries_low = d_queries.reshape(tok_rows, model_width).astype(jnp.bfloat16)
        d_keys_low = d_keys_own.astype(jnp.bfloat16)
        d_values_low = d_values_own.astype(jnp.bfloat16)
        acc_query = acc_query + jnp.einsum(
            "td,te->de", normed1, d_queries_low, preferred_element_type=jnp.float32
        )
        acc_key = acc_key + jnp.einsum(
            "td,te->de", normed1, d_keys_low, preferred_element_type=jnp.float32
        )
        acc_value = acc_value + jnp.einsum(
            "td,te->de", normed1, d_values_low, preferred_element_type=jnp.float32
        )
        d_normed1 = (
            jnp.einsum("te,de->td", d_queries_low, query_weight, preferred_element_type=jnp.float32)
            + jnp.einsum("te,de->td", d_keys_low, key_weight, preferred_element_type=jnp.float32)
            + jnp.einsum(
                "te,de->td", d_values_low, value_weight, preferred_element_type=jnp.float32
            )
        )
        d_rows_norm, d_gain_one = norm_back_rows(dealt_rows, scale_one, gain_one, d_normed1)
        acc_gain_one = acc_gain_one + d_gain_one
        d_dealt = d_mid + d_rows_norm
        returned = lax.all_to_all(
            d_dealt.astype(jnp.bfloat16), "fsdp", split_axis=0, concat_axis=0, tiled=True
        ).astype(d_dealt.dtype)
        grads_list.append(jnp.zeros_like(returned).at[take_rows].set(returned))
    acc_rel = acc_buckets.reshape(-1)
    summed = (
        lax.psum_scatter(acc_gain_one, ("dp", "fsdp"), scatter_dimension=0, tiled=True),
        lax.psum_scatter(acc_gain_two, ("dp", "fsdp"), scatter_dimension=0, tiled=True),
        lax.psum_scatter(acc_rel, ("dp", "fsdp"), scatter_dimension=0, tiled=True),
        lax.psum_scatter(acc_query, ("dp", "fsdp"), scatter_dimension=0, tiled=True),
        lax.psum_scatter(acc_key, ("dp", "fsdp"), scatter_dimension=0, tiled=True),
        lax.psum_scatter(acc_value, ("dp", "fsdp"), scatter_dimension=0, tiled=True),
        lax.psum_scatter(acc_output, ("dp", "fsdp"), scatter_dimension=0, tiled=True),
        lax.psum_scatter(acc_inner, ("dp", "fsdp"), scatter_dimension=0, tiled=True),
        lax.psum_scatter(acc_outer, ("dp", "fsdp"), scatter_dimension=0, tiled=True),
    )
    return (
        jnp.stack(outputs_list),
        jnp.stack(grads_list),
        summed[0],
        summed[1],
        summed[2],
        summed[3],
        summed[4],
        summed[5],
        summed[6],
        summed[7],
        summed[8],
    )


VMEM = pl.BlockSpec(memory_space=pltpu.VMEM)
SMEM = pl.BlockSpec(memory_space=pltpu.SMEM)
ANYWHERE = pl.BlockSpec(memory_space=pl.ANY)
LIMIT = 58 * 1024 * 1024
FIRST_AXIS = ("x", "x", "y", "x", "y")
FWD_PARTS = 3
FWD_AHEAD = 2
FWD_OWN = (-1, 0, 6, 12, 15, 21)
FWD_NEAR = (9, 12, 18, 24, 27, 33)
FWD_SIDE = (21, 24, 30, 36, 41, 41)
FWD_GRADS = 15
FFN_CHUNK = 768
BWD_PARTS = 3
BWD_AHEAD = 2
BWD_SIDE = (4, 4, 14, 14, 24, 28, 30)
BWD_NEAR = (16, 12, 26, 22, 28, 32, 34)


def shaped(*shape, dtype=jnp.bfloat16):
    return jax.ShapeDtypeStruct(shape, dtype)


def params(collective_id=None):
    if collective_id is None:
        return pltpu.CompilerParams(vmem_limit_bytes=LIMIT)
    return pltpu.CompilerParams(
        collective_id=collective_id, has_side_effects=True, vmem_limit_bytes=LIMIT
    )


def dma(*shape):
    return pltpu.SemaphoreType.DMA(shape)


def gather_all(lens, deal, hid, one, two, rel, shards):
    count = len(shards) + 1
    return pl.pallas_call(
        functools.partial(gather_kernel, FIRST_AXIS),
        name="gather_all",
        out_shape=[
            shaped(1, 128, dtype=jnp.int32),
            shaped(*deal.shape[1:], dtype=jnp.int32),
            shaped(OWN, TILE, hid.shape[-1]),
            shaped(32, 16, 128),
        ]
        + [shaped(32, *s.shape) for s in shards],
        in_specs=[VMEM] + [ANYWHERE] * 2 + [VMEM] * 3 + [ANYWHERE] * (count - 1),
        out_specs=[ANYWHERE] * (3 + count),
        scratch_shapes=[
            pltpu.VMEM((2, 1, 128), jnp.int32), pltpu.VMEM((16, 128), jnp.float32), pltpu.VMEM((16, 128), jnp.bfloat16),
            dma(count, 10), dma(count, 10), dma(count), dma(2, 3), dma(OWN), dma(2), dma(2),
        ],
        compiler_params=params(0),
    )(lens, deal, hid, one, two, rel, *shards)


def attention_forward(lens, x, small, table, wq, wk, wv, grd, wi, wu):
    heads, keys = (PAIRS, OWN, TILE, 128), (PAIRS, OWN, 2, TILE, 128)
    count = len(FWD_OWN)
    return pl.pallas_call(
        attn_fwd,
        name="attn_fwd",
        out_shape=[
            shaped(*heads), shaped(*keys), shaped(*keys), shaped(*x.shape),
            shaped(OWN, 2 * PAIRS, 1, TILE, dtype=jnp.float32),
            shaped(8, grd.shape[2], grd.shape[3] // 2),
            shaped(32, *wi.shape), shaped(32, *wu.shape),
        ],
        in_specs=[SMEM] + [VMEM] * 6 + [ANYWHERE] * 3,
        out_specs=[VMEM] * 5 + [ANYWHERE] * 3,
        scratch_shapes=[
            pltpu.VMEM((5, 2 * PAIRS, 1, 2 * TILE), jnp.float32),
            pltpu.VMEM((2 * PAIRS, 5, TILE, TILE), jnp.float32),
            pltpu.VMEM((OWN, TILE, 128), jnp.bfloat16),
            pltpu.VMEM((TILES, TILE, 128), jnp.bfloat16),
            pltpu.VMEM((2, TILE, TILES * TILE), jnp.float32),
            pltpu.VMEM((OWN, TILE, 128), jnp.float32),
            dma(2), dma(2),
            dma(count, 10), dma(count, 10), dma(count), dma(2, 2, 2), dma(2, 4),
        ],
        compiler_params=params(1),
    )(lens, x, small, table, wq, wk, wv, grd, wi, wu)


def landing(shapes, leads=((4, 4), (2, 4), (4,))):
    return [pltpu.VMEM((*lead, *b), jnp.bfloat16) for b in shapes for lead in leads]


def attention_backward(lens, q, k, v, log_total, d_att, delta, small, table, gwo, gwi, gwu, dealt):
    heads = (PAIRS, OWN, TILE, 128)
    block_i, block_u = (gwi.shape[2], gwi.shape[3] // BWD_PARTS), (gwu.shape[2], gwu.shape[3] // BWD_PARTS)
    blocks = [block_i, block_u] * BWD_PARTS + [gwo.shape[2:]]
    count = len(blocks)
    return pl.pallas_call(
        attn_bwd,
        name="attn_bwd",
        out_shape=[shaped(*heads)] * 3
        + [shaped(32, 128, dtype=jnp.float32)]
        + [shaped(4, *g.shape[2:]) for g in (gwo, gwi, gwu)]
        + [shaped(*dealt.shape[:2], dealt.shape[2] // 2)],
        in_specs=[SMEM] + [VMEM] * 8 + [ANYWHERE] * 4,
        out_specs=[VMEM] * 4 + [ANYWHERE] * 4,
        scratch_shapes=[pltpu.VMEM((5, 2 * PAIRS, 1, 2 * TILE), jnp.float32)] * 2
        + [pltpu.VMEM((2 * PAIRS, 5, TILE, TILE), jnp.float32)] * 2
        + [pltpu.VMEM((OWN, TILE, 128), jnp.bfloat16), pltpu.VMEM((TILES, TILE, 128), jnp.bfloat16)]
        + [pltpu.VMEM((TILES * TILE, 128), jnp.float32)] * 2
        + [pltpu.VMEM(heads, jnp.bfloat16)] * 4
        + [dma(2, PAIRS), dma(2, PAIRS), dma(count, 10), dma(count, 10), dma(count, 3), dma(2), dma(2)]
        + landing(blocks, ((2, 4), (2, 4), (4,))),
        compiler_params=params(2),
    )(lens, q, k, v, log_total, d_att, delta, small, table, gwo, gwi, gwu, dealt)


def feed_forward(deal, x, att, wo, small, g_low, grd, wi, wu):
    tok, width = x.shape
    hidden = wi.shape[1]
    f32, bf16 = jnp.float32, jnp.bfloat16
    heads, stats = (PAIRS, OWN, TILE, 128), (OWN, 2 * PAIRS, 1, TILE)
    block_i, block_u = (32, width // 32, hidden), (32, hidden // 32, width)
    chunks = hidden // FFN_CHUNK
    return pl.pallas_call(
        ffn_kernel,
        name="feed_forward",
        out_shape=[
            shaped(tok, width, dtype=f32), shaped(*heads), shaped(*stats, dtype=f32),
            shaped(4, 4, width // 32, width), shaped(32, 128, dtype=f32), shaped(2, 3 * TILE, width),
            shaped(4, 4, *block_i[1:]), shaped(4, 4, *block_u[1:]), shaped(2, 3 * TILE, width // 2),
        ],
        in_specs=[VMEM] * 6 + [ANYWHERE] * 3,
        out_specs=[VMEM] * 6 + [ANYWHERE] * 3,
        scratch_shapes=[
            pltpu.VMEM((tok, width), bf16), pltpu.VMEM((tok, width), f32), pltpu.VMEM((tok, width), bf16),
            pltpu.VMEM((tok, width), f32), pltpu.VMEM((tok, hidden), bf16), pltpu.VMEM((tok, hidden), bf16),
            pltpu.VMEM((width, hidden), bf16), pltpu.VMEM((hidden, width), bf16),
            pltpu.VMEM((2, 32, width // 32, FFN_CHUNK), bf16), pltpu.VMEM((2, 32 // chunks, hidden // 32, width), bf16),
            pltpu.VMEM(g_low.shape, bf16),
            pltpu.VMEM((OWN, TILE, width), bf16), pltpu.VMEM((OWN, 2, TILE, width), bf16),
            pltpu.VMEM((chunks, 4, 4, width // 32, FFN_CHUNK), bf16), pltpu.VMEM((chunks, 4, hidden // 32, width), bf16),
            pltpu.VMEM((32, width // 32, width), bf16),
            dma(2, chunks), dma(2, chunks), dma(2, 2, 2), dma(2, 4), dma(2), dma(2),
            pltpu.SemaphoreType.DMA, pltpu.SemaphoreType.DMA, dma(chunks + 1, 5), dma(chunks + 1, 5),
        ],
        compiler_params=params(4),
    )(deal, x, att, wo, small, g_low, grd, wi, wu)


def tail(x, small, d_mid, dq, dk, dv, wq, wk, wv, g_two, g_rel):
    tok, width = x.shape
    block = (width // 32, width)
    blocks = [block, block, block, (16, 128)]
    count = len(blocks)
    return pl.pallas_call(
        tail_kernel,
        name="tail",
        out_shape=[shaped(2, 3, TILE, width), shaped(4, 16, 128)] + [shaped(4, *block)] * 3,
        in_specs=[VMEM] * 4 + [ANYWHERE] * 7,
        out_specs=[ANYWHERE] * 5,
        scratch_shapes=[
            pltpu.VMEM((tok, width), jnp.float32), pltpu.VMEM((3, width, width), jnp.bfloat16),
            pltpu.VMEM((3, OWN, TILE, width), jnp.bfloat16), pltpu.VMEM((tok, width), jnp.bfloat16),
            pltpu.VMEM((OWN, TILE, width), jnp.bfloat16),
            pltpu.VMEM((32, 16, 128), jnp.bfloat16),
        ]
        + [pltpu.VMEM((32, *block), jnp.bfloat16)] * 3
        + landing(blocks)
        + [dma(count, 10), dma(count, 10), dma(count, 1), dma(OWN), dma(2, 3), dma(4, PAIRS + 1)],
        compiler_params=params(3),
    )(x, small, g_two, g_rel, d_mid, dq, dk, dv, wq, wk, wv)


def last_sums(low, high, gin, terms):
    f32 = jnp.float32
    lines = lambda n: shaped(1, n, dtype=f32)
    hid_shape = (*low.shape[:2], 2 * low.shape[2])

    def by_micro(shape):
        return pl.BlockSpec((1, *shape[1:]), lambda m: (m,) + (0,) * (len(shape) - 1))

    def whole(shape):
        return pl.BlockSpec(shape, lambda m: (0,) * len(shape))

    sums = [lines(24), lines(24), lines(H)] + [shaped(*t.shape[1:], dtype=f32) for t in terms[1:]]
    return pl.pallas_call(
        sum_kernel,
        name="last_sums",
        grid=(low.shape[0],),
        out_shape=[shaped(*hid_shape, dtype=f32), shaped(*gin.shape, dtype=f32)] + sums,
        in_specs=[by_micro(v.shape) for v in (low, high, gin)] + [whole(t.shape) for t in terms],
        out_specs=[by_micro(hid_shape), by_micro(gin.shape)] + [whole(s.shape) for s in sums],
        compiler_params=params(),
    )(low, high, gin, *terms)


def on_device_packed(
    hidden_in, grad_out, gain_attn, gain_ffn, rel_bias,
    w_query, w_key, w_value, w_output, w_inner, w_outer,
    dealing, lengths, bucket_table,
):
    micro_count, tok_rows, width = hidden_in.shape
    matrix = lambda w: w.reshape(-1, w.shape[-1])
    table = bucket_table
    grd = grad_out.reshape(2, 2, tok_rows // 2, width)
    lens_u, deal_u, x_own, small, wq, wk, wv, wo = gather_all(
        lengths, dealing, hidden_in.reshape(2, 3, TILE, width),
        gain_attn[None], gain_ffn[None], rel_bias[None], (w_query, w_key, w_value, w_output),
    )
    wq, wk, wv = map(matrix, (wq, wk, wv))
    x_rows = matrix(x_own)
    q, k, v, att, log_total, g_low, wi, wu = attention_forward(
        lens_u, x_rows, small, table, wq, wk, wv, grd, w_inner, w_outer
    )
    d_mid, d_att, delta, g_wo, g_two, dealt, g_wi, g_wu, hid_low = feed_forward(
        deal_u, x_rows, att, matrix(wo), small, g_low, grd, matrix(wi), matrix(wu)
    )
    dq, dk, dv, g_rel, t_wo, t_wi, t_wu, hid_high = attention_backward(
        lens_u, q, k, v, log_total, d_att, delta, small, table, g_wo, g_wi, g_wu, dealt
    )
    gin, t_small, t_wq, t_wk, t_wv = tail(x_rows, small, d_mid, dq, dk, dv, wq, wk, wv, g_two, g_rel)
    hid, gin, s_one, s_two, s_rel, *grads = last_sums(hid_low, hid_high, gin, (t_small, t_wq, t_wk, t_wv, t_wo, t_wi, t_wu))
    return (hid, gin.reshape(2, tok_rows, width), s_one[0], s_two[0], s_rel[0], *grads)


def solution(mesh):
    axes = ("dp", "fsdp")
    tokens, matrix, vector = P(None, axes, None), P(axes, None), P(axes)
    packed = mesh.shape["fsdp"] == 4 and mesh.shape["dp"] == 8
    return jax.shard_map(
        on_device_packed if packed else on_device,
        mesh=mesh,
        in_specs=(tokens, tokens, vector, vector, vector)
        + (matrix,) * 6
        + (P(None, "dp", None), P(None, "dp", None), P()),
        out_specs=(tokens, tokens, vector, vector, vector) + (matrix,) * 6,
        check_vma=False,
    )
```
